32 devices in a mesh: node: 4 (over x, core), local: 8 (over z, y).
Axes of the slice: x: 2, y: 2, z: 4, core: 2. Of those that a mesh axis runs over, the one named last changes fastest.
Arguments:
- tokens: bfloat16 [2048, 4096], P('local'), may hold values from -6 to 6
- norm_gain: bfloat16 [4096], replicated, may hold values from 0.099609375 to 1.8984375
- w_quant: bfloat16 [3, 4096, 4096], P(None, 'local', 'node'), may hold values from -1 to 1
- w_scale: bfloat16 [3, 32, 4096], P(None, 'local', 'node'), as said below
- d_out: bfloat16 [2048, 4096], P('local', 'node'), may hold values from -4 to 4
Outputs:
- attn_out: bfloat16 [2048, 4096], P('local', 'node')
- d_tokens: bfloat16 [2048, 4096], P('local', 'node')
- weight_grads: float32 [3, 4096, 4096], P(None, 'local', 'node')
The draws below stay inside these ranges and needn't reach their ends.
Inputs may be any that keep to these rules, and one draw needn't show every extreme that they name: `w_scale`: positive.
All inputs are finite; a program needn't handle non-finite values. Where the reference program divides by a largest or mean magnitude, that divisor is 1e-20 or more.
Results may differ from the reference program's by a relative error of at most 0.017.
Values may be sent and summed in bfloat16 or wider, within the bound.
No kernel may reach another device: no remote copies, remote signals or barrier semaphores. Data moves between devices by JAX's collectives and lax.ppermute only.
A program may use at most 320 MiB of HBM per device.

```python
import math
import jax
import jax.numpy as jnp
from jax import lax

D = 4096
HEADS = 32
HEAD_DIM = 128
QB = 128
TOK_DEV = 256
HD = 4096
GROUP_HEADS = 8
SEQS = 8
TOKENS = 2048


def draw_w_scale(key, part):
    key = jax.random.fold_in(key, 23)
    spread = jax.random.uniform(key, (3, D // QB, HEADS * HEAD_DIM), jnp.float32, -0.7, 0.7)
    return (jnp.exp(spread) * (1.72 / math.sqrt(D))).astype(jnp.bfloat16)


def block_scale(rng, extent, cuts, low, high):
    level, own = 1.0, jax.random.fold_in(rng, 6)
    for dim, parts in cuts:
        steps = jnp.exp(jax.random.uniform(jax.random.fold_in(own, dim), (parts,), jnp.float32, low / len(cuts), high / len(cuts)))
        level = level * jnp.repeat(steps, extent[dim] // parts).reshape([-1 if axis == dim else 1 for axis in range(len(extent))])
    return level


def gaussian(key, shape, deviation, bound, split=(), kind=jnp.bfloat16):
    level = block_scale(key, shape, split, -0.22, 0.18) if split else 1.0
    drawn = jax.random.normal(key, shape, jnp.float32) * deviation * level
    return jnp.minimum(jnp.maximum(drawn, -bound), bound).astype(kind)


def setup_inputs(seed: int = 0) -> dict:
    splits = jax.random.split(jax.random.key(seed), 6)
    tokens = gaussian(splits[0], (TOKENS, D), 1.0, 6.0, ((0, 8),))
    norm_gain = jnp.clip(1.0 + 0.18 * jax.random.normal(splits[1], (D,), jnp.float32), 0.099609375, 1.8984375).astype(jnp.bfloat16)
    w_quant = jnp.clip(jax.random.uniform(splits[2], (3, D, HD), jnp.float32, -1.0, 1.0) * block_scale(splits[2], (3, D, HD), ((1, 8), (2, 4)), -0.4, 0.0), -1.0, 1.0).astype(jnp.bfloat16)
    w_scale = draw_w_scale(jax.random.fold_in(splits[5], 71), 0)
    d_out = gaussian(splits[4], (TOKENS, HD), 0.25, 4.0, ((0, 8), (1, 4)))
    return {"tokens": tokens, "norm_gain": norm_gain, "w_quant": w_quant, "w_scale": w_scale, "d_out": d_out}


NORM_EPS = 1e-05
SCALE_EPS = 1e-06

def rope_tables(length, width):
    position = jnp.arange(length).astype(jnp.float32)[:, None]
    frequency = jnp.exp(jnp.arange(width // 2).astype(jnp.float32) * (-2.0 * math.log(10000.0) / width))
    angle = position * frequency[None, :]
    return (jnp.cos(angle), jnp.sin(angle))

def rotate(tensor, cosine, sine):
    half = tensor.shape[-1] // 2
    first = tensor[..., :half]
    second = tensor[..., half:]
    cosine = cosine[:, None, :]
    sine = sine[:, None, :]
    return jnp.concatenate([first * cosine - second * sine, second * cosine + first * sine], axis=-1)

def attend(query, key_rows, value):
    length = query.shape[0]
    scores = jnp.einsum('shd,thd->hst', query.astype(jnp.float32), key_rows.astype(jnp.float32)) / math.sqrt(query.shape[-1])
    causal = jnp.arange(length)[:, None] >= jnp.arange(length)[None, :]
    scores = jnp.where(causal[None], scores, jnp.float32(-1e+30))
    probs = jax.nn.softmax(scores, axis=-1).astype(jnp.bfloat16)
    return jnp.einsum('hst,thd->shd', probs.astype(jnp.float32), value.astype(jnp.float32)).astype(jnp.bfloat16)

def normed(rows, gain):
    values = rows.astype(jnp.float32)
    inverse_rms = lax.rsqrt(lax.optimization_barrier(jnp.mean(values * values, axis=-1, keepdims=True)) + NORM_EPS)
    return ((values * inverse_rms * gain.astype(jnp.float32)).astype(jnp.bfloat16), inverse_rms)

def expand_blocks(quant, scale):
    widened = quant.astype(jnp.float32) * scale.astype(jnp.float32)[:, :, None, :]
    return widened.reshape(quant.shape[0], quant.shape[1] * quant.shape[2], quant.shape[3])

def quantize(grad, block):
    blocks = grad.reshape(grad.shape[0], grad.shape[1] // block, block, grad.shape[2])
    scale = (lax.optimization_barrier(jnp.max(jnp.abs(blocks), axis=2)) + SCALE_EPS).astype(jnp.bfloat16)
    quant = (blocks / scale.astype(jnp.float32)[:, :, None, :]).astype(jnp.bfloat16)
    return (quant, scale)

def reference(tokens, norm_gain, w_quant, w_scale, d_out):
    block = w_quant.shape[1] // w_scale.shape[1]
    quant_blocks = w_quant.reshape(3, w_scale.shape[1], block, HD)
    weights = expand_blocks(quant_blocks, w_scale).astype(jnp.bfloat16)
    groups = HEADS // GROUP_HEADS
    weight_groups = weights.astype(jnp.float32).reshape(3, D, groups, GROUP_HEADS * HEAD_DIM)
    cosine, sine = rope_tables(TOK_DEV, HEAD_DIM)
    rows_all = tokens.reshape(SEQS, TOK_DEV, D)
    upstream_all = d_out.reshape(SEQS, TOK_DEV, HD)
    gains = norm_gain.astype(jnp.float32)

    def one_sequence(grads, pair):
        rows, upstream = pair
        normed_rows, inverse_rms = normed(rows, norm_gain)
        query_pre = jnp.dot(normed_rows, weights[0], preferred_element_type=jnp.float32).reshape(TOK_DEV, HEADS, HEAD_DIM)
        key_pre = jnp.dot(normed_rows, weights[1], preferred_element_type=jnp.float32).reshape(TOK_DEV, HEADS, HEAD_DIM)
        value_pre = jnp.dot(normed_rows, weights[2], preferred_element_type=jnp.float32).reshape(TOK_DEV, HEADS, HEAD_DIM)
        query = rotate(query_pre, cosine, sine).astype(jnp.bfloat16)
        key_rows = rotate(key_pre, cosine, sine).astype(jnp.bfloat16)
        value = value_pre.astype(jnp.bfloat16)
        output, pull = jax.vjp(attend, query, key_rows, value)
        d_query, d_key, d_value = pull(upstream.reshape(TOK_DEV, HEADS, HEAD_DIM))
        pre_query = rotate(d_query.astype(jnp.float32), cosine, -sine).astype(jnp.bfloat16)
        pre_key = rotate(d_key.astype(jnp.float32), cosine, -sine).astype(jnp.bfloat16)
        pre = jnp.stack([pre_query, pre_key, d_value]).reshape(3, TOK_DEV, HD)
        partial_value = jnp.einsum('sr,msc->mrc', normed_rows.astype(jnp.float32), pre.astype(jnp.float32))
        quant, scale = quantize(partial_value, block)
        dequant = expand_blocks(quant, scale).astype(jnp.bfloat16)
        grads = grads + lax.optimization_barrier(dequant).astype(jnp.float32)
        pre_groups = pre.astype(jnp.float32).reshape(3, TOK_DEV, groups, GROUP_HEADS * HEAD_DIM)
        terms = jnp.einsum('msgc,mdgc->gsd', pre_groups, weight_groups).astype(jnp.bfloat16)
        upstream_norm = lax.optimization_barrier(jnp.sum(terms.astype(jnp.float32), axis=0))
        values = rows.astype(jnp.float32)
        dots = lax.optimization_barrier(jnp.sum(gains * upstream_norm * values, axis=-1, keepdims=True))
        d_rows = inverse_rms * gains * upstream_norm - values * inverse_rms ** 3 * dots / D
        return (grads, (output.reshape(TOK_DEV, HD), d_rows.astype(jnp.bfloat16)))
    grads, (outputs, d_rows) = lax.scan(one_sequence, jnp.zeros((3, D, HD), jnp.float32), (rows_all, upstream_all))
    return (outputs.reshape(TOKENS, HD), d_rows.reshape(TOKENS, D), grads)
```

```python
import functools
import math

import jax
import jax.numpy as jnp
from jax import lax
from jax.experimental import pallas as pl
from jax.experimental.pallas import tpu as pltpu
from jax.sharding import PartitionSpec as P

HEAD_DIM = 128
NORM_EPS = 1e-05
CHUNKS = 2
VMEM = 40 * 1024 * 1024


def params(*semantics):
    return pltpu.CompilerParams(dimension_semantics=semantics, vmem_limit_bytes=VMEM)


def cost(flops, moved):
    return pl.CostEstimate(flops=flops, bytes_accessed=moved, transcendentals=0)


def mm(a, b):
    return jnp.dot(a, b, preferred_element_type=jnp.float32)


def mm_nt(a, b):
    return lax.dot_general(a, b, (((1,), (1,)), ((), ())), preferred_element_type=jnp.float32)


def mm_tn(a, b):
    return lax.dot_general(a, b, (((0,), (0,)), ((), ())), preferred_element_type=jnp.float32)


def rope_tables(length, width):
    position = jnp.arange(length).astype(jnp.float32)[:, None]
    frequency = jnp.exp(
        jnp.arange(width // 2).astype(jnp.float32) * (-2.0 * math.log(10000.0) / width)
    )
    angle = position * frequency[None, :]
    cosine, sine = jnp.cos(angle), jnp.sin(angle)
    return (
        jnp.concatenate([cosine, cosine], axis=-1),
        jnp.concatenate([-sine, sine], axis=-1),
    )


def ring_order(size):
    return [*range(0, size, 2), *reversed(range(1, size, 2))]


def sum_first_kernel(idx, rows, weight, right, left):
    half = right.shape[1]
    product = mm(rows[0], weight[0])
    right[0] = product[:half].astype(jnp.bfloat16)
    left[0] = product[half:].astype(jnp.bfloat16)


def sum_step_kernel(idx, rows_r, rows_l, weight, from_left, from_right, right, left):
    length, part = right.shape[1], from_left.shape[1]
    product = mm(rows_r[0], weight[0])
    right[0, :part] = (product[:part] + from_left[0].astype(jnp.float32)).astype(jnp.bfloat16)
    if part < length:
        right[0, part:] = product[part:].astype(jnp.bfloat16)
    product = mm(rows_l[0], weight[0])
    rest = length - part
    left[0, rest:] = (product[rest:] + from_right[0].astype(jnp.float32)).astype(jnp.bfloat16)
    if rest:
        left[0, :rest] = product[:rest].astype(jnp.bfloat16)


def sum_first(seq, rows, weights, chunk, wide):
    _, length, depth = rows.shape
    half = length // 2
    part = jax.ShapeDtypeStruct((3, half, wide), jnp.bfloat16)
    return pl.pallas_call(
        sum_first_kernel,
        grid_spec=pltpu.PrefetchScalarGridSpec(
            num_scalar_prefetch=1,
            grid=(3,),
            in_specs=[
                pl.BlockSpec((1, length, depth), lambda m, idx: (idx[0], 0, 0)),
                pl.BlockSpec((1, depth, wide), lambda m, idx: (m, 0, chunk)),
            ],
            out_specs=[pl.BlockSpec((1, half, wide), lambda m, idx: (m, 0, 0))] * 2,
        ),
        out_shape=[part, part],
        compiler_params=params("arbitrary"),
        cost_estimate=cost(6 * length * depth * wide, 8 * depth * wide),
        name="sum_first",
    )(seq, rows, weights)


def sum_step(seqs, rows, weights, from_left, from_right, chunk, wide):
    _, length, depth = rows.shape
    whole = jax.ShapeDtypeStruct((3, length, wide), jnp.bfloat16)
    part = from_left.shape[1]
    return pl.pallas_call(
        sum_step_kernel,
        grid_spec=pltpu.PrefetchScalarGridSpec(
            num_scalar_prefetch=1,
            grid=(3,),
            in_specs=[
                pl.BlockSpec((1, length, depth), lambda m, idx: (idx[0], 0, 0)),
                pl.BlockSpec((1, length, depth), lambda m, idx: (idx[1], 0, 0)),
                pl.BlockSpec((1, depth, wide), lambda m, idx: (m, 0, chunk)),
                pl.BlockSpec((1, part, wide), lambda m, idx: (m, 0, 0)),
                pl.BlockSpec((1, part, wide), lambda m, idx: (m, 0, 0)),
            ],
            out_specs=[pl.BlockSpec((1, length, wide), lambda m, idx: (m, 0, 0))] * 2,
        ),
        out_shape=[whole, whole],
        compiler_params=params("arbitrary"),
        cost_estimate=cost(12 * length * depth * wide, 12 * depth * wide),
        name="sum_step",
    )(seqs, rows, rows, weights, from_left, from_right)


def attention_kernel(
    idx, rows, weight, from_left, from_right, d_out, cosine, sine, output, pre, dots
):
    length = rows.shape[1]
    proj = [
        mm(rows[0], weight[m])
        + (from_left[m].astype(jnp.float32) + from_right[m].astype(jnp.float32))
        for m in range(3)
    ]
    cos, sin = cosine[...], sine[...]
    half = HEAD_DIM // 2

    def rotate(tensor, angle):
        return tensor * cos + pltpu.roll(tensor, half, 1) * angle

    query = rotate(proj[0], sin).astype(jnp.bfloat16)
    key_rows = rotate(proj[1], sin).astype(jnp.bfloat16)
    value = proj[2].astype(jnp.bfloat16)
    scores = mm_nt(query, key_rows) * (1.0 / math.sqrt(HEAD_DIM))
    causal = lax.broadcasted_iota(jnp.int32, (length, length), 0) >= lax.broadcasted_iota(
        jnp.int32, (length, length), 1
    )
    scores = jnp.where(causal, scores, jnp.float32(-1e30))
    powers = jnp.exp(scores - jnp.max(scores, axis=-1, keepdims=True))
    probs = powers * (1.0 / jnp.sum(powers, axis=-1, keepdims=True))
    probs_low = probs.astype(jnp.bfloat16)
    output[...] = mm(probs_low, value).astype(jnp.bfloat16)
    cotangent = d_out[...]
    d_value = mm_tn(probs_low, cotangent).astype(jnp.bfloat16)
    d_probs = mm_nt(cotangent, value).astype(jnp.bfloat16).astype(jnp.float32)
    inner = jnp.sum(d_probs * probs, axis=-1, keepdims=True)
    d_scores = (probs * (d_probs - inner) * (1.0 / math.sqrt(HEAD_DIM))).astype(jnp.bfloat16)
    d_query = mm(d_scores, key_rows).astype(jnp.bfloat16).astype(jnp.float32)
    d_key = mm_tn(d_scores, query).astype(jnp.bfloat16).astype(jnp.float32)
    pre_query = rotate(d_query, -sin).astype(jnp.bfloat16)
    pre_key = rotate(d_key, -sin).astype(jnp.bfloat16)
    pre[0] = pre_query
    pre[1] = pre_key
    pre[2] = d_value
    product = (
        pre_query.astype(jnp.float32) * proj[0]
        + pre_key.astype(jnp.float32) * proj[1]
        + d_value.astype(jnp.float32) * proj[2]
    )

    @pl.when(pl.program_id(0) == 0)
    def _():
        dots[...] = product

    @pl.when(pl.program_id(0) > 0)
    def _():
        dots[...] += product


def attention(seq, rows, weights, from_left, from_right, d_out, tables, chunk, wide):
    _, length, depth = rows.shape
    heads = wide // HEAD_DIM
    first = chunk * heads
    table = pl.BlockSpec((length, HEAD_DIM), lambda h, idx: (0, 0))
    stack = pl.BlockSpec((3, length, HEAD_DIM), lambda h, idx: (0, 0, h))
    return pl.pallas_call(
        attention_kernel,
        grid_spec=pltpu.PrefetchScalarGridSpec(
            num_scalar_prefetch=1,
            grid=(heads,),
            in_specs=[
                pl.BlockSpec((1, length, depth), lambda h, idx: (idx[0], 0, 0)),
                pl.BlockSpec((3, depth, HEAD_DIM), lambda h, idx: (0, 0, first + h)),
                stack,
                stack,
                pl.BlockSpec((length, HEAD_DIM), lambda h, idx: (0, first + h)),
                table,
                table,
            ],
            out_specs=[
                pl.BlockSpec((length, HEAD_DIM), lambda h, idx: (0, h)),
                stack,
                table,
            ],
        ),
        out_shape=[
            jax.ShapeDtypeStruct((length, wide), jnp.bfloat16),
            jax.ShapeDtypeStruct((3, length, wide), jnp.bfloat16),
            jax.ShapeDtypeStruct((length, HEAD_DIM), jnp.float32),
        ],
        compiler_params=params("arbitrary"),
        cost_estimate=cost(6 * length * depth * wide, 12 * depth * wide),
        name="attention",
    )(seq, rows, weights, from_left, from_right, d_out, *tables)


def grads_kernel(count, idx, rows_t, *refs):
    pieces, far, out = refs[: count - 1], refs[count - 1 : count + 1], refs[-1]
    total = mm(rows_t[idx[0]], pieces[0][0])
    for place in range(1, count - 1):
        total += mm(rows_t[idx[place]], pieces[place][0])
    half = far[0].shape[1]
    last = rows_t[idx[count - 1]]
    total += mm(last[:, :half], far[0][0])
    total += mm(last[:, half:], far[1][0])
    out[0] = total


def grads_chunk(seqs, rows_t, pieces, far, before, chunk, wide, columns):
    size, depth, length = rows_t.shape
    block = pl.BlockSpec((1, length, wide), lambda m, idx: (m, 0, 0))
    half = pl.BlockSpec((1, length // 2, wide), lambda m, idx: (m, 0, 0))
    in_specs = [
        pl.BlockSpec((size, depth, length), lambda m, idx: (0, 0, 0)),
        *[block] * (size - 1),
        half,
        half,
    ]
    operands = [seqs, rows_t, *pieces, *far]
    aliases = {}
    if before is not None:
        aliases = {len(operands): 0}
        operands.append(before)
        in_specs.append(pl.BlockSpec(memory_space=pl.ANY))
    return pl.pallas_call(
        functools.partial(grads_kernel, size),
        grid_spec=pltpu.PrefetchScalarGridSpec(
            num_scalar_prefetch=1,
            grid=(3,),
            in_specs=in_specs,
            out_specs=pl.BlockSpec((1, depth, wide), lambda m, idx: (m, 0, chunk)),
        ),
        out_shape=jax.ShapeDtypeStruct((3, depth, columns), jnp.float32),
        input_output_aliases=aliases,
        compiler_params=params("arbitrary"),
        cost_estimate=cost(6 * size * length * depth * wide, 12 * size * length * wide),
        name="grads",
    )(*operands)


def term_kernel(count, has_before, idx, weight, *refs):
    pieces, far = refs[: count - 1], refs[count - 1 : count + 1]
    before, out = refs[count + 1] if has_before else None, refs[-1]

    def back(piece):
        total = mm_nt(piece[0], weight[0])
        for m in range(1, 3):
            total += mm_nt(piece[m], weight[m])
        return total

    def put(place, low, high, total):
        if has_before:
            total += before[place, low:high]
        out[place, low:high] = total.astype(out.dtype)

    length = pieces[0].shape[1]
    for index in range(count - 1):
        put(idx[index], 0, length, back(pieces[index]))
    put(idx[count - 1], 0, length // 2, back(far[0]))
    put(idx[count - 1], length // 2, length, back(far[1]))


def term_chunk(seqs, weights, pieces, far, before, kind, chunk, wide):
    size = len(pieces) + 1
    length = pieces[0].shape[1]
    depth = weights.shape[1]
    block = pl.BlockSpec((3, length, wide), lambda i, idx: (0, 0, 0))
    half = pl.BlockSpec((3, length // 2, wide), lambda i, idx: (0, 0, 0))
    result = pl.BlockSpec((size, length, depth), lambda i, idx: (0, 0, 0))
    in_specs = [
        pl.BlockSpec((3, depth, wide), lambda i, idx: (0, 0, chunk)),
        *[block] * (size - 1),
        half,
        half,
    ]
    operands = [seqs, weights, *pieces, *far]
    if before is not None:
        operands.append(before)
        in_specs.append(result)
    return pl.pallas_call(
        functools.partial(term_kernel, size, before is not None),
        grid_spec=pltpu.PrefetchScalarGridSpec(
            num_scalar_prefetch=1, grid=(1,), in_specs=in_specs, out_specs=result
        ),
        out_shape=jax.ShapeDtypeStruct((size, length, depth), kind),
        compiler_params=params("arbitrary"),
        cost_estimate=cost(6 * size * length * depth * wide, 12 * size * length * wide),
        name="term",
    )(*operands)


def local(tokens, norm_gain, w_quant, w_scale, d_out):
    length, width = tokens.shape
    depth, columns = w_quant.shape[1:]
    size, nodes = lax.axis_size("local"), lax.axis_size("node")
    here, node = lax.axis_index("local"), lax.axis_index("node")
    wide = columns // CHUNKS
    far = size // 2

    order = ring_order(size)
    to_right = [(order[i], order[(i + 1) % size]) for i in range(size)]
    to_left = [(b, a) for a, b in to_right]
    table = jnp.array(order, jnp.int32)
    place = jnp.where(here % 2 == 0, here // 2, size - (here + 1) // 2)

    def sequence(distance):
        return table[(place + distance + size) % size]

    values = tokens.astype(jnp.float32)
    gains = norm_gain.astype(jnp.float32)
    inverse_rms = lax.rsqrt(jnp.mean(values * values, axis=-1, keepdims=True) + NORM_EPS)
    normed = (values * inverse_rms * gains).astype(jnp.bfloat16)
    core = node % 2
    pairs = [(n, n ^ 1) for n in range(nodes)]
    shares = normed.reshape(length, size, 2, depth // 2)
    mine = lax.dynamic_index_in_dim(shares, core, 2, keepdims=False).transpose(1, 0, 2)
    mine = lax.all_to_all(mine, "local", split_axis=0, concat_axis=0, tiled=True)
    other = lax.ppermute(mine, "node", pairs)
    rows = jnp.where(
        core == 0,
        jnp.concatenate([mine, other], axis=-1),
        jnp.concatenate([other, mine], axis=-1),
    )
    rows_t = rows.transpose(0, 2, 1)

    blocks = w_quant.reshape(3, w_scale.shape[1], -1, columns).astype(jnp.float32)
    weights = (blocks * w_scale.astype(jnp.float32)[:, :, None, :]).astype(jnp.bfloat16)
    weights = weights.reshape(3, depth, columns)

    tables = rope_tables(length, HEAD_DIM)
    arrived = []
    for chunk in range(CHUNKS):
        right, left = sum_first(sequence(far)[None], rows, weights, chunk, wide)
        for distance in range(far - 1, -1, -1):
            from_left = lax.ppermute(right, "local", to_right)
            from_right = lax.ppermute(left, "local", to_left)
            if distance:
                seqs = jnp.stack([sequence(distance), sequence(-distance)])
                right, left = sum_step(seqs, rows, weights, from_left, from_right, chunk, wide)
        arrived.append((from_left, from_right))

    outputs, pres, dots = [], [], 0.0
    for chunk in range(CHUNKS):
        output, pre, product = attention(
            here[None], rows, weights, *arrived[chunk], d_out, tables, chunk, wide
        )
        outputs.append(output)
        pres.append(pre)
        dots += jnp.sum(product, axis=-1, keepdims=True)
    dots = lax.psum(dots, "node")

    distances = [0]
    for step in range(1, far):
        distances += [-step, step]
    distances.append(far)
    seqs = jnp.stack([sequence(distance) for distance in distances])
    grads, term = None, None
    half = length // 2
    for chunk in range(CHUNKS):
        right = left = pres[chunk]
        pieces = [pres[chunk]]
        for step in range(1, far + 1):
            if step == far:
                right, left = right[:, :half], left[:, half:]
            right = lax.ppermute(right, "local", to_right)
            left = lax.ppermute(left, "local", to_left)
            if step < far:
                pieces += [right, left]
        kind = jnp.bfloat16 if chunk == CHUNKS - 1 else jnp.float32
        term = term_chunk(seqs, weights, pieces, (right, left), term, kind, chunk, wide)
        grads = grads_chunk(
            seqs, rows_t, pieces, (right, left), grads, chunk, wide, columns
        )

    group = size // nodes
    summed = lax.all_to_all(
        term.reshape(nodes, group, length, depth), "node", split_axis=0, concat_axis=0, tiled=True
    )
    summed = jnp.sum(summed.astype(jnp.float32), axis=0).astype(jnp.bfloat16)
    came = []
    for turn in range(group):
        block = lax.dynamic_index_in_dim(summed, (here + turn) % group, 0, keepdims=False)
        moves = [
            (n * size + s, (s // group) * size + n * group + (s + turn) % group)
            for n in range(nodes)
            for s in range(size)
        ]
        came.append(lax.ppermute(block, ("node", "local"), moves))
    came = jnp.stack(came)
    upstream = jnp.concatenate(
        [
            lax.dynamic_index_in_dim(came, (here + group - i) % group, 0, keepdims=False)
            for i in range(group)
        ],
        axis=-1,
    ).astype(jnp.float32)
    share = width // nodes
    values_part = lax.dynamic_slice_in_dim(tokens, node * share, share, 1).astype(jnp.float32)
    gains_part = lax.dynamic_slice_in_dim(gains, node * share, share, 0)
    d_tokens = (
        inverse_rms * gains_part * upstream - values_part * inverse_rms**2 * dots / width
    )
    return (jnp.concatenate(outputs, axis=-1), d_tokens.astype(jnp.bfloat16), grads)


def solution(mesh):
    placed = (
        P("local", None),
        P(),
        P(None, "local", "node"),
        P(None, "local", "node"),
        P("local", "node"),
    )
    return jax.shard_map(
        local,
        mesh=mesh,
        in_specs=placed,
        out_specs=(P("local", "node"), P("local", "node"), P(None, "local", "node")),
        check_vma=False,
    )
```

```python
import functools
import math

import jax
import jax.numpy as jnp
from jax import lax
from jax.experimental import pallas as pl
from jax.experimental.pallas import tpu as pltpu
from jax.sharding import PartitionSpec as P

HEAD_DIM = 128
NORM_EPS = 1e-05
VMEM = 60 * 1024 * 1024


def params(*semantics):
    return pltpu.CompilerParams(dimension_semantics=semantics, vmem_limit_bytes=VMEM)


def cost(flops, moved):
    return pl.CostEstimate(flops=flops, bytes_accessed=moved, transcendentals=0)


def mm(a, b):
    return jnp.dot(a, b, preferred_element_type=jnp.float32)


def mm_nt(a, b):
    return lax.dot_general(a, b, (((1,), (1,)), ((), ())), preferred_element_type=jnp.float32)


def mm_tn(a, b):
    return lax.dot_general(a, b, (((0,), (0,)), ((), ())), preferred_element_type=jnp.float32)


def rope_tables(length, width):
    position = jnp.arange(length).astype(jnp.float32)[:, None]
    frequency = jnp.exp(
        jnp.arange(width // 2).astype(jnp.float32) * (-2.0 * math.log(10000.0) / width)
    )
    angle = position * frequency[None, :]
    cosine, sine = jnp.cos(angle), jnp.sin(angle)
    return (
        jnp.concatenate([cosine, cosine], axis=-1),
        jnp.concatenate([-sine, sine], axis=-1),
    )


def ring_order(size):
    return [*range(0, size, 2), *reversed(range(1, size, 2))]


def normed_kernel(idx, tokens, gain, *outs):
    width, part = tokens.shape[1], outs[0].shape[1]
    values = tokens[...].astype(jnp.float32)
    inverse = lax.rsqrt(jnp.mean(values * values, axis=-1, keepdims=True) + NORM_EPS)
    size = len(outs) - 1
    for distance in range(size):
        start = pl.multiple_of(idx[distance] * (width // size) + idx[size] * part, part)
        block = tokens[:, pl.ds(start, part)].astype(jnp.float32)
        scale = gain[:, pl.ds(start, part)]
        outs[distance][...] = (block * inverse * scale).astype(jnp.bfloat16)
    outs[size][...] = jnp.broadcast_to(inverse, outs[size].shape)


def normed_blocks(idx, tokens, gain, size, part):
    length, width = tokens.shape
    tile = length // 4
    block = pl.BlockSpec((tile, part), lambda i, idx: (i, 0))
    *blocks, inverse = pl.pallas_call(
        normed_kernel,
        grid_spec=pltpu.PrefetchScalarGridSpec(
            num_scalar_prefetch=1,
            grid=(4,),
            in_specs=[
                pl.BlockSpec((tile, width), lambda i, idx: (i, 0)),
                pl.BlockSpec((1, width), lambda i, idx: (0, 0)),
            ],
            out_specs=[block] * size + [pl.BlockSpec((tile, 128), lambda i, idx: (i, 0))],
        ),
        out_shape=[jax.ShapeDtypeStruct((length, part), jnp.bfloat16)] * size
        + [jax.ShapeDtypeStruct((length, 128), jnp.float32)],
        compiler_params=params("arbitrary"),
        cost_estimate=cost(8 * length * width, 4 * length * width),
        name="normed_blocks",
    )(idx, tokens, gain)
    return blocks, inverse[:, :1]


def sum_first_kernel(core, mine, other, weight, weight_other, right, left):
    half = right.shape[1]
    product = mm(mine[...], weight[0]) + mm(other[...], weight_other[0])
    right[0] = product[:half].astype(jnp.bfloat16)
    left[0] = product[half:].astype(jnp.bfloat16)


def sum_step_kernel(
    core, mine_r, other_r, mine_l, other_l, weight, weight_other, from_left, from_right, right, left
):
    length, part = right.shape[1], from_left.shape[1]
    product = mm(mine_r[...], weight[0]) + mm(other_r[...], weight_other[0])
    right[0, :part] = (product[:part] + from_left[0].astype(jnp.float32)).astype(jnp.bfloat16)
    if part < length:
        right[0, part:] = product[part:].astype(jnp.bfloat16)
    product = mm(mine_l[...], weight[0]) + mm(other_l[...], weight_other[0])
    rest = length - part
    left[0, rest:] = (product[rest:] + from_right[0].astype(jnp.float32)).astype(jnp.bfloat16)
    if rest:
        left[0, :rest] = product[:rest].astype(jnp.bfloat16)


def weight_halves(depth, wide, chunk):
    return [
        pl.BlockSpec((1, depth // 2, wide), lambda m, core: (m, core[0], chunk)),
        pl.BlockSpec((1, depth // 2, wide), lambda m, core: (m, 1 - core[0], chunk)),
    ]


def sum_first(core, rows, weights, chunk, wide):
    length, part = rows[0].shape
    half = length // 2
    block = pl.BlockSpec((length, part), lambda m, core: (0, 0))
    result = jax.ShapeDtypeStruct((3, half, wide), jnp.bfloat16)
    return pl.pallas_call(
        sum_first_kernel,
        grid_spec=pltpu.PrefetchScalarGridSpec(
            num_scalar_prefetch=1,
            grid=(3,),
            in_specs=[block, block, *weight_halves(2 * part, wide, chunk)],
            out_specs=[pl.BlockSpec((1, half, wide), lambda m, core: (m, 0, 0))] * 2,
        ),
        out_shape=[result, result],
        compiler_params=params("arbitrary"),
        cost_estimate=cost(12 * length * part * wide, 16 * part * wide),
        name="sum_first",
    )(core, *rows, weights, weights)


def sum_step(core, rows_r, rows_l, weights, from_left, from_right, chunk, wide):
    length, part = rows_r[0].shape
    block = pl.BlockSpec((length, part), lambda m, core: (0, 0))
    whole = jax.ShapeDtypeStruct((3, length, wide), jnp.bfloat16)
    came = from_left.shape[1]
    return pl.pallas_call(
        sum_step_kernel,
        grid_spec=pltpu.PrefetchScalarGridSpec(
            num_scalar_prefetch=1,
            grid=(3,),
            in_specs=[
                *[block] * 4,
                *weight_halves(2 * part, wide, chunk),
                pl.BlockSpec((1, came, wide), lambda m, core: (m, 0, 0)),
                pl.BlockSpec((1, came, wide), lambda m, core: (m, 0, 0)),
            ],
            out_specs=[pl.BlockSpec((1, length, wide), lambda m, core: (m, 0, 0))] * 2,
        ),
        out_shape=[whole, whole],
        compiler_params=params("arbitrary"),
        cost_estimate=cost(24 * length * part * wide, 24 * part * wide),
        name="sum_step",
    )(core, *rows_r, *rows_l, weights, weights, from_left, from_right)


def attention_kernel(
    core, mine, other, weight, weight_other, from_left, from_right, d_out, cosine, sine,
    output, pre, dots,
):
    length = mine.shape[0]
    proj = [
        mm(mine[...], weight[m])
        + mm(other[...], weight_other[m])
        + (from_left[m].astype(jnp.float32) + from_right[m].astype(jnp.float32))
        for m in range(3)
    ]
    cos, sin = cosine[...], sine[...]
    half = HEAD_DIM // 2

    def rotate(tensor, angle):
        return tensor * cos + pltpu.roll(tensor, half, 1) * angle

    query = rotate(proj[0], sin).astype(jnp.bfloat16)
    key_rows = rotate(proj[1], sin).astype(jnp.bfloat16)
    value = proj[2].astype(jnp.bfloat16)
    scores = mm_nt(query, key_rows) * (1.0 / math.sqrt(HEAD_DIM))
    causal = lax.broadcasted_iota(jnp.int32, (length, length), 0) >= lax.broadcasted_iota(
        jnp.int32, (length, length), 1
    )
    scores = jnp.where(causal, scores, jnp.float32(-1e30))
    powers = jnp.exp(scores - jnp.max(scores, axis=-1, keepdims=True))
    probs = powers * (1.0 / jnp.sum(powers, axis=-1, keepdims=True))
    probs_low = probs.astype(jnp.bfloat16)
    output[...] = mm(probs_low, value).astype(jnp.bfloat16)
    cotangent = d_out[...]
    d_value = mm_tn(probs_low, cotangent).astype(jnp.bfloat16)
    d_probs = mm_nt(cotangent, value).astype(jnp.bfloat16).astype(jnp.float32)
    inner = jnp.sum(d_probs * probs, axis=-1, keepdims=True)
    d_scores = (probs * (d_probs - inner) * (1.0 / math.sqrt(HEAD_DIM))).astype(jnp.bfloat16)
    d_query = mm(d_scores, key_rows).astype(jnp.bfloat16).astype(jnp.float32)
    d_key = mm_tn(d_scores, query).astype(jnp.bfloat16).astype(jnp.float32)
    pre_query = rotate(d_query, -sin).astype(jnp.bfloat16)
    pre_key = rotate(d_key, -sin).astype(jnp.bfloat16)
    pre[0] = pre_query
    pre[1] = pre_key
    pre[2] = d_value
    product = (
        pre_query.astype(jnp.float32) * proj[0]
        + pre_key.astype(jnp.float32) * proj[1]
        + d_value.astype(jnp.float32) * proj[2]
    )

    @pl.when(pl.program_id(0) == 0)
    def _():
        dots[...] = product

    @pl.when(pl.program_id(0) > 0)
    def _():
        dots[...] += product


def attention(core, rows, weights, from_left, from_right, d_out, tables, chunk, wide):
    length, part = rows[0].shape
    heads = wide // HEAD_DIM
    first = chunk * heads
    block = pl.BlockSpec((length, part), lambda h, core: (0, 0))
    table = pl.BlockSpec((length, HEAD_DIM), lambda h, core: (0, 0))
    stack = pl.BlockSpec((3, length, HEAD_DIM), lambda h, core: (0, 0, h))
    return pl.pallas_call(
        attention_kernel,
        grid_spec=pltpu.PrefetchScalarGridSpec(
            num_scalar_prefetch=1,
            grid=(heads,),
            in_specs=[
                block,
                block,
                pl.BlockSpec((3, part, HEAD_DIM), lambda h, core: (0, core[0], first + h)),
                pl.BlockSpec((3, part, HEAD_DIM), lambda h, core: (0, 1 - core[0], first + h)),
                stack,
                stack,
                pl.BlockSpec((length, HEAD_DIM), lambda h, core: (0, first + h)),
                table,
                table,
            ],
            out_specs=[
                pl.BlockSpec((length, HEAD_DIM), lambda h, core: (0, h)),
                stack,
                table,
            ],
        ),
        out_shape=[
            jax.ShapeDtypeStruct((length, wide), jnp.bfloat16),
            jax.ShapeDtypeStruct((3, length, wide), jnp.bfloat16),
            jax.ShapeDtypeStruct((length, HEAD_DIM), jnp.float32),
        ],
        compiler_params=params("arbitrary"),
        cost_estimate=cost(12 * length * part * wide, 24 * part * wide),
        name="attention",
    )(core, *rows, weights, weights, from_left, from_right, d_out, *tables)


def grads_kernel(count, sets, core, *refs):
    mine, other = refs[:count], refs[count : 2 * count]
    pieces, out, turned = refs[2 * count : -2], refs[-2], refs[-1]
    length, part = mine[0].shape

    @pl.when(pl.program_id(0) == 0)
    def _():
        for place in range(count):
            span = slice(place * length, (place + 1) * length)
            turned[:part, span] = mine[place][...].T
            turned[part:, span] = other[place][...].T

    totals = [None, None]
    start = 0
    for position in range(sets):
        group = pieces[position * (count + 1) : (position + 1) * (count + 1)]
        rows = group[0].shape[1]
        for place in range(count):
            if place < count - 1:
                block = group[place][0]
            else:
                block = jnp.concatenate([group[place][0], group[place + 1][0]], axis=0)
            low = place * length + start
            for side in range(2):
                product = mm(turned[side * part : (side + 1) * part, low : low + rows], block)
                totals[side] = product if totals[side] is None else totals[side] + product
        start += rows
    out[0, pl.ds(pl.multiple_of(core[0] * part, part), part)] = totals[0]
    out[0, pl.ds(pl.multiple_of((1 - core[0]) * part, part), part)] = totals[1]


def grads_chunk(core, mine, other, gathered, before, chunk, wide, columns):
    count = len(mine)
    length, part = mine[0].shape
    block = pl.BlockSpec((length, part), lambda m, core: (0, 0))
    in_specs = [block] * (2 * count)
    operands = [core, *mine, *other]
    for pieces in gathered:
        for piece in pieces:
            in_specs.append(pl.BlockSpec((1, *piece.shape[1:]), lambda m, core: (m, 0, 0)))
            operands.append(piece)
    aliases = {}
    kernel = functools.partial(grads_kernel, count, len(gathered))
    if before is not None:
        aliases = {len(operands): 0}
        operands.append(before)
        in_specs.append(pl.BlockSpec(memory_space=pl.ANY))
        inner = kernel

        def kernel(*refs):
            inner(*refs[:-3], *refs[-2:])

    return pl.pallas_call(
        kernel,
        grid_spec=pltpu.PrefetchScalarGridSpec(
            num_scalar_prefetch=1,
            grid=(3,),
            in_specs=in_specs,
            out_specs=pl.BlockSpec((1, 2 * part, wide), lambda m, core: (m, 0, chunk)),
            scratch_shapes=[pltpu.VMEM((2 * part, count * length), jnp.bfloat16)],
        ),
        out_shape=jax.ShapeDtypeStruct((3, 2 * part, columns), jnp.float32),
        input_output_aliases=aliases,
        compiler_params=params("arbitrary"),
        cost_estimate=cost(12 * count * length * part * wide, 12 * count * length * wide),
        name="grads",
    )(*operands)


def back(pieces, weight, place, count):
    def one(piece):
        total = mm_nt(piece[0], weight[0])
        for m in range(1, 3):
            total += mm_nt(piece[m], weight[m])
        return total

    if place < count - 1:
        return one(pieces[place])
    return jnp.concatenate([one(pieces[place]), one(pieces[place + 1])], axis=0)


def term_first_kernel(count, idx, weight, *refs):
    for place in range(count):
        refs[-1][idx[place]] = back(refs, weight, place, count)


def term_first(seqs, weights, pieces, chunk, wide):
    count = len(pieces) - 1
    length = pieces[0].shape[1]
    depth = weights.shape[1]
    return pl.pallas_call(
        functools.partial(term_first_kernel, count),
        grid_spec=pltpu.PrefetchScalarGridSpec(
            num_scalar_prefetch=1,
            grid=(1,),
            in_specs=[
                pl.BlockSpec((3, depth, wide), lambda i, idx: (0, 0, chunk)),
                *[pl.BlockSpec(piece.shape, lambda i, idx: (0, 0, 0)) for piece in pieces],
            ],
            out_specs=pl.BlockSpec((count, length, depth), lambda i, idx: (0, 0, 0)),
        ),
        out_shape=jax.ShapeDtypeStruct((count, length, depth), jnp.float32),
        compiler_params=params("arbitrary"),
        cost_estimate=cost(6 * count * length * depth * wide, 6 * count * length * wide),
        name="term_first",
    )(seqs, weights, *pieces)


def term_last_kernel(count, idx, weight, before, *refs):
    keep, send = refs[-2], refs[-1]
    for place in range(count):
        total = back(refs, weight, place, count) + before[idx[place]]

        @pl.when(idx[count + place] == 0)
        def _():
            keep[idx[2 * count + place]] = total.astype(jnp.bfloat16).astype(jnp.float32)

        @pl.when(idx[count + place] == 1)
        def _():
            send[idx[2 * count + place]] = total.astype(jnp.bfloat16)


def term_last(idx, weights, before, pieces, part, chunk, wide):
    count, _, depth = before.shape
    rows = pieces[0].shape[1]
    result = pl.BlockSpec((count // 2, rows, depth), lambda i, idx: (0, 0, 0))
    return pl.pallas_call(
        functools.partial(term_last_kernel, count),
        grid_spec=pltpu.PrefetchScalarGridSpec(
            num_scalar_prefetch=1,
            grid=(1,),
            in_specs=[
                pl.BlockSpec((3, depth, wide), lambda i, idx: (0, 0, chunk)),
                pl.BlockSpec((count, rows, depth), lambda i, idx: (0, part, 0)),
                *[pl.BlockSpec(piece.shape, lambda i, idx: (0, 0, 0)) for piece in pieces],
            ],
            out_specs=[result, result],
        ),
        out_shape=[
            jax.ShapeDtypeStruct((count // 2, rows, depth), jnp.float32),
            jax.ShapeDtypeStruct((count // 2, rows, depth), jnp.bfloat16),
        ],
        compiler_params=params("arbitrary"),
        cost_estimate=cost(6 * count * rows * depth * wide, 6 * count * rows * wide),
        name="term_last",
    )(idx, weights, before, *pieces)


def after(first, *arrays):
    tied = lax.optimization_barrier((first, *arrays))
    return tied[1:]


def local(tokens, norm_gain, w_quant, w_scale, d_out):
    length, width = tokens.shape
    depth, columns = w_quant.shape[1:]
    size, nodes = lax.axis_size("local"), lax.axis_size("node")
    here, node = lax.axis_index("local"), lax.axis_index("node")
    wide = columns // 2
    far = size // 2
    group = size // nodes
    core = node % 2

    order = ring_order(size)
    table = jnp.array(order, jnp.int32)
    place = jnp.where(here % 2 == 0, here // 2, size - (here + 1) // 2)

    def shift(array, distance):
        moves = [(order[i], order[(i + distance) % size]) for i in range(size)]
        return lax.ppermute(array, "local", moves)

    def swap(array, bit):
        return lax.ppermute(array, "node", [(n, n ^ bit) for n in range(nodes)])

    def sequence(distance):
        return table[(place + distance + size) % size]

    targets = jnp.stack([sequence(distance) for distance in range(size)] + [core])
    gains = norm_gain.astype(jnp.float32)
    blocks, inverse_rms = normed_blocks(
        targets.astype(jnp.int32), tokens, gains[None], size, depth // 2
    )
    mine, other = {0: blocks[0]}, {}
    mine[far] = shift(blocks[far], far)
    other[far] = swap(mine[far], 1)
    previous = mine[far]
    for distance in range(far - 1, 0, -1):
        tied = after(previous, blocks[distance], blocks[size - distance])
        mine[-distance] = shift(tied[0], distance)
        mine[distance] = shift(tied[1], -distance)
        for sign in (-1, 1):
            other[sign * distance] = swap(mine[sign * distance], 1)
        previous = mine[distance]
    other[0] = swap(mine[0], 1)

    scaled = w_quant.reshape(3, w_scale.shape[1], -1, columns).astype(jnp.float32)
    weights = (scaled * w_scale.astype(jnp.float32)[:, :, None, :]).astype(jnp.bfloat16)
    weights = weights.reshape(3, depth, columns)

    tables = rope_tables(length, HEAD_DIM)
    core_index = core[None].astype(jnp.int32)
    arrived = []
    for chunk in range(2):
        right, left = sum_first(core_index, (mine[far], other[far]), weights, chunk, wide)
        for distance in range(far - 1, -1, -1):
            from_left, from_right = shift(right, 1), shift(left, -1)
            if distance:
                right, left = sum_step(
                    core_index,
                    (mine[distance], other[distance]),
                    (mine[-distance], other[-distance]),
                    weights,
                    from_left,
                    from_right,
                    chunk,
                    wide,
                )
        arrived.append((from_left, from_right))

    outputs, pres, dots = [], [], 0.0
    for chunk in range(2):
        output, pre, product = attention(
            core_index, (mine[0], other[0]), weights, *arrived[chunk], d_out, tables, chunk, wide
        )
        outputs.append(output)
        pres.append(pre)
        dots += jnp.sum(product, axis=-1, keepdims=True)
    bit = 1
    while bit < nodes:
        dots = dots + swap(dots, bit)
        bit *= 2

    half = length // 2
    sets = [pres[0], pres[1][:, :half], pres[1][:, half:]]
    gathered = [[block] for block in sets]
    moving = [(block, block) for block in sets]
    schedule = [(0, 1)]
    for step in range(2, far + 1):
        schedule += [(0, step), (1, step - 1)]
    schedule += [(2, 1), (1, far)] + [(2, step) for step in range(2, far + 1)]

    distances = [0]
    for step in range(1, far):
        distances += [-step, step]
    distances.append(far)
    seqs = jnp.stack([sequence(distance) for distance in distances]).astype(jnp.int32)
    owner = seqs // group
    position = (owner // 2) * group + seqs % group
    idx = jnp.concatenate([seqs, (owner % 2) ^ core, position]).astype(jnp.int32)

    share = width // nodes
    values_part = lax.dynamic_slice_in_dim(tokens, node * share, share, 1).astype(jnp.float32)
    gains_part = lax.dynamic_slice_in_dim(gains, node * share, share, 0)

    def start_term(before, part):
        keep, send = term_last(idx, weights, before, gathered[1 + part], part, 1, wide)
        return keep + swap(send, 1).astype(jnp.float32)

    def end_term(summed, part):
        bit = 2
        while bit < nodes:
            pair = summed.reshape(-1, 2, group, *summed.shape[1:])
            own = (node // bit) % 2
            keep = lax.dynamic_index_in_dim(pair, own, 1, keepdims=False)
            send = lax.dynamic_index_in_dim(pair, 1 - own, 1, keepdims=False)
            summed = keep + swap(send.astype(jnp.bfloat16), bit).astype(jnp.float32)
            summed = summed.reshape(-1, *pair.shape[3:])
            bit *= 2
        summed = summed.astype(jnp.bfloat16)
        came = []
        for turn in range(group):
            block = lax.dynamic_index_in_dim(summed, (here + turn) % group, 0, keepdims=False)
            moves = [
                (n * size + s, (s // group) * size + n * group + (s + turn) % group)
                for n in range(nodes)
                for s in range(size)
            ]
            came.append(lax.ppermute(block, ("node", "local"), moves))
        came = jnp.stack(came)
        upstream = jnp.concatenate(
            [
                lax.dynamic_index_in_dim(came, (here + group - i) % group, 0, keepdims=False)
                for i in range(group)
            ],
            axis=-1,
        ).astype(jnp.float32)
        rows = slice(part * half, (part + 1) * half)
        d_rows = (
            inverse_rms[rows] * gains_part * upstream
            - values_part[rows] * inverse_rms[rows] ** 2 * dots[rows] / width
        )
        return d_rows.astype(jnp.bfloat16)

    term = early = None
    for ring, step in schedule:
        right, left = moving[ring]
        if step == far:
            middle = right.shape[1] // 2
            right, left = right[:, :middle], left[:, middle:]
        if (ring, step) == (1, 1):
            right, left = after(moving[0][0], right, left)
        if (ring, step) == (2, 1):
            right, left = after(moving[0][0], right, left)
        if (ring, step) == (2, min(2, far)):
            right, left = after(term, right, left)
        if (ring, step) == (2, far):
            right, left = after(early, right, left)
        right, left = shift(right, 1), shift(left, -1)
        moving[ring] = right, left
        gathered[ring] += [right, left]
        if (ring, step) == (0, far):
            term = term_first(seqs, weights, gathered[0], 0, wide)
        if (ring, step) == (1, far):
            early = start_term(term, 0)
    late = start_term(term, 1)
    d_tokens = jnp.concatenate([end_term(early, 0), end_term(late, 1)], axis=0)

    rows = [mine[distance] for distance in distances], [other[distance] for distance in distances]
    grads = grads_chunk(core_index, *rows, gathered[:1], None, 0, wide, columns)
    grads = grads_chunk(core_index, *rows, gathered[1:], grads, 1, wide, columns)
    return (jnp.concatenate(outputs, axis=-1), d_tokens, grads)


def solution(mesh):
    placed = (
        P("local", None),
        P(),
        P(None, "local", "node"),
        P(None, "local", "node"),
        P("local", "node"),
    )
    return jax.shard_map(
        local,
        mesh=mesh,
        in_specs=placed,
        out_specs=(P("local", "node"), P("local", "node"), P(None, "local", "node")),
        check_vma=False,
    )
```

```python
import functools
import math

import jax
import jax.numpy as jnp
import numpy as np
from jax import lax
from jax.experimental import pallas as pl
from jax.experimental.pallas import tpu as pltpu
from jax.sharding import PartitionSpec as P

HEAD_DIM = 128
NORM_EPS = 1e-05
SMALL, LARGE = 20 * 1024 * 1024, 56 * 1024 * 1024


def params(limit):
    return pltpu.CompilerParams(dimension_semantics=("arbitrary",), vmem_limit_bytes=limit)


def cost(flops, moved):
    return pl.CostEstimate(flops=flops, bytes_accessed=moved, transcendentals=0)


def mm(a, b):
    return jnp.dot(a, b, preferred_element_type=jnp.float32)


def mm_nt(a, b):
    return lax.dot_general(a, b, (((1,), (1,)), ((), ())), preferred_element_type=jnp.float32)


def mm_tn(a, b):
    return lax.dot_general(a, b, (((0,), (0,)), ((), ())), preferred_element_type=jnp.float32)


def rope_tables(length, width):
    position = jnp.arange(length).astype(jnp.float32)[:, None]
    frequency = jnp.exp(
        jnp.arange(width // 2).astype(jnp.float32) * (-2.0 * math.log(10000.0) / width)
    )
    angle = position * frequency[None, :]
    cosine, sine = jnp.cos(angle), jnp.sin(angle)
    return (
        jnp.concatenate([cosine, cosine], axis=-1),
        jnp.concatenate([-sine, sine], axis=-1),
    )


def ring_order(size):
    return [*range(0, size, 2), *reversed(range(1, size, 2))]


def ring_distances(size):
    far = size // 2
    distances = [0]
    for step in range(1, far):
        distances += [-step, step]
    return [*distances, far]


def index_table(size, nodes):
    order, group = ring_order(size), size // nodes
    rows = []
    for node in range(nodes):
        for here in range(size):
            place = order.index(here)
            seqs = [order[(place + distance) % size] for distance in ring_distances(size)]
            owner = [seq // group for seq in seqs]
            rows.append(
                [order[(place + distance) % size] for distance in range(size)]
                + [node % 2]
                + seqs
                + [owner_ % 2 ^ node % 2 for owner_ in owner]
                + [(o // 2) * group + seq % group for o, seq in zip(owner, seqs)]
            )
    return np.array(rows, np.int32)


def weights_kernel(quant, scale, out, turned):
    blocks = scale.shape[1]
    rows = quant.shape[1] // blocks
    scales = scale[0].astype(jnp.float32)
    for block in range(blocks):
        span = slice(block * rows, (block + 1) * rows)
        scaled = (quant[0, span].astype(jnp.float32) * scales[block : block + 1]).astype(jnp.bfloat16)
        out[0, span] = scaled
        turned[0, :, span] = scaled.T


def scaled_weights(w_quant, w_scale):
    _, depth, columns = w_quant.shape
    blocks = w_scale.shape[1]
    return pl.pallas_call(
        weights_kernel,
        grid=(3,),
        in_specs=[
            pl.BlockSpec((1, depth, columns), lambda m: (m, 0, 0)),
            pl.BlockSpec((1, blocks, columns), lambda m: (m, 0, 0)),
        ],
        out_specs=[
            pl.BlockSpec((1, depth, columns), lambda m: (m, 0, 0)),
            pl.BlockSpec((1, columns, depth), lambda m: (m, 0, 0)),
        ],
        out_shape=[
            jax.ShapeDtypeStruct((3, depth, columns), jnp.bfloat16),
            jax.ShapeDtypeStruct((3, columns, depth), jnp.bfloat16),
        ],
        compiler_params=params(SMALL),
        cost_estimate=cost(3 * depth * columns, 18 * depth * columns),
        name="scaled_weights",
    )(w_quant, w_scale)


def normed_kernel(idx, tokens, gain, *refs):
    outs, gains = refs[:-1], refs[-1]
    width, part = tokens.shape[1], outs[0].shape[1]
    gains[...] = gain[...].astype(jnp.float32)
    values = tokens[...].astype(jnp.float32)
    inverse = lax.rsqrt(jnp.mean(values * values, axis=-1, keepdims=True) + NORM_EPS)
    size = len(outs) - 1
    for distance in range(size):
        start = pl.multiple_of(idx[distance] * (width // size) + idx[size] * part, part)
        block = tokens[:, pl.ds(start, part)].astype(jnp.float32)
        scale = gains[:, pl.ds(start, part)]
        outs[distance][...] = (block * inverse * scale).astype(jnp.bfloat16)
    outs[size][...] = jnp.broadcast_to(inverse, outs[size].shape)


def normed_blocks(idx, tokens, gain, size, part):
    length, width = tokens.shape
    tile = length // 4
    block = pl.BlockSpec((tile, part), lambda i, idx: (i, 0))
    *blocks, inverse = pl.pallas_call(
        normed_kernel,
        grid_spec=pltpu.PrefetchScalarGridSpec(
            num_scalar_prefetch=1,
            grid=(4,),
            in_specs=[
                pl.BlockSpec((tile, width), lambda i, idx: (i, 0)),
                pl.BlockSpec((1, width), lambda i, idx: (0, 0)),
            ],
            out_specs=[block] * size + [pl.BlockSpec((tile, 128), lambda i, idx: (i, 0))],
            scratch_shapes=[pltpu.VMEM((1, width), jnp.float32)],
        ),
        out_shape=[jax.ShapeDtypeStruct((length, part), jnp.bfloat16)] * size
        + [jax.ShapeDtypeStruct((length, 128), jnp.float32)],
        compiler_params=params(SMALL),
        cost_estimate=cost(8 * length * width, 4 * length * width),
        name="normed_blocks",
    )(idx, tokens, gain)
    return blocks, inverse


def turn_kernel(count, idx, mine, other, mine_far, other_far, out):
    length, part = mine_far.shape
    for side, near, last in ((0, mine, mine_far), (1, other, other_far)):
        half = idx[count] * (1 - side) + (1 - idx[count]) * side
        rows = pl.ds(pl.multiple_of(half * part, part), part)
        for place in range(count):
            block = near[place] if place < count - 1 else last[...]
            out[rows, place * length : (place + 1) * length] = block.T


def turn(idx, mine, other, mine_far, other_far):
    near, length, part = mine.shape
    count = near + 1
    stack = pl.BlockSpec(mine.shape, lambda i, idx: (0, 0, 0))
    last = pl.BlockSpec((length, part), lambda i, idx: (0, 0))
    shape = (2 * part, count * length)
    return pl.pallas_call(
        functools.partial(turn_kernel, count),
        grid_spec=pltpu.PrefetchScalarGridSpec(
            num_scalar_prefetch=1,
            grid=(1,),
            in_specs=[stack, stack, last, last],
            out_specs=pl.BlockSpec(shape, lambda i, idx: (0, 0)),
        ),
        out_shape=jax.ShapeDtypeStruct(shape, jnp.bfloat16),
        compiler_params=params(SMALL),
        cost_estimate=cost(2 * count * length * part, 8 * count * length * part),
        name="turn",
    )(idx, mine, other, mine_far, other_far)


def sum_first_kernel(idx, mine, other, weight, weight_other, *outs):
    half, wide = outs[0].shape[1:]
    for chunk in range(2):
        span = slice(chunk * wide, (chunk + 1) * wide)
        product = mm(mine[...], weight[0, :, span]) + mm(other[...], weight_other[0, :, span])
        outs[2 * chunk][0] = product[:half].astype(jnp.bfloat16)
        outs[2 * chunk + 1][0] = product[half:].astype(jnp.bfloat16)


def sum_step_kernel(
    idx, mine_r, other_r, mine_l, other_l, weight, weight_other, from_left, from_right, right, left
):
    length, part = right.shape[1], from_left.shape[1]
    product = mm(mine_r[0], weight[0]) + mm(other_r[0], weight_other[0])
    right[0, :part] = (product[:part] + from_left[0].astype(jnp.float32)).astype(jnp.bfloat16)
    if part < length:
        right[0, part:] = product[part:].astype(jnp.bfloat16)
    product = mm(mine_l[0], weight[0]) + mm(other_l[0], weight_other[0])
    rest = length - part
    left[0, rest:] = (product[rest:] + from_right[0].astype(jnp.float32)).astype(jnp.bfloat16)
    if rest:
        left[0, :rest] = product[:rest].astype(jnp.bfloat16)


def weight_halves(size, part, wide, chunk):
    return [
        pl.BlockSpec((1, part, wide), lambda m, idx: (m, idx[size], chunk)),
        pl.BlockSpec((1, part, wide), lambda m, idx: (m, 1 - idx[size], chunk)),
    ]


def sum_first(idx, size, mine, other, weights):
    length, part = mine.shape
    columns = weights.shape[2]
    half, wide = length // 2, columns // 2
    block = pl.BlockSpec((length, part), lambda m, idx: (0, 0))
    result = jax.ShapeDtypeStruct((3, half, wide), jnp.bfloat16)
    return pl.pallas_call(
        sum_first_kernel,
        grid_spec=pltpu.PrefetchScalarGridSpec(
            num_scalar_prefetch=1,
            grid=(3,),
            in_specs=[block, block, *weight_halves(size, part, columns, 0)],
            out_specs=[pl.BlockSpec((1, half, wide), lambda m, idx: (m, 0, 0))] * 4,
        ),
        out_shape=[result] * 4,
        compiler_params=params(SMALL),
        cost_estimate=cost(12 * length * part * columns, 16 * part * columns),
        name="sum_first",
    )(idx, mine, other, weights, weights)


def sum_step(idx, size, mine, other, places, weights, from_left, from_right, chunk, wide):
    _, length, part = mine.shape
    block_r = pl.BlockSpec((1, length, part), lambda m, idx: (places[0], 0, 0))
    block_l = pl.BlockSpec((1, length, part), lambda m, idx: (places[1], 0, 0))
    came = pl.BlockSpec((1, from_left.shape[1], wide), lambda m, idx: (m, 0, 0))
    whole = jax.ShapeDtypeStruct((3, length, wide), jnp.bfloat16)
    return pl.pallas_call(
        sum_step_kernel,
        grid_spec=pltpu.PrefetchScalarGridSpec(
            num_scalar_prefetch=1,
            grid=(3,),
            in_specs=[
                block_r,
                block_r,
                block_l,
                block_l,
                *weight_halves(size, part, wide, chunk),
                came,
                came,
            ],
            out_specs=[pl.BlockSpec((1, length, wide), lambda m, idx: (m, 0, 0))] * 2,
        ),
        out_shape=[whole, whole],
        compiler_params=params(SMALL),
        cost_estimate=cost(24 * length * part * wide, 24 * part * wide),
        name="sum_step",
    )(idx, mine, other, mine, other, weights, weights, from_left, from_right)


def attention_kernel(
    idx, mine, other, weight, weight_other, from_left, from_right, d_out, cosine, sine,
    output, pre, dots,
):
    length = mine.shape[1]
    proj = [
        mm(mine[0], weight[m])
        + mm(other[0], weight_other[m])
        + (from_left[m].astype(jnp.float32) + from_right[m].astype(jnp.float32))
        for m in range(3)
    ]
    cos, sin = cosine[...], sine[...]
    half = HEAD_DIM // 2

    def rotate(tensor, angle):
        return tensor * cos + pltpu.roll(tensor, half, 1) * angle

    query = rotate(proj[0], sin).astype(jnp.bfloat16)
    key_rows = rotate(proj[1], sin).astype(jnp.bfloat16)
    value = proj[2].astype(jnp.bfloat16)
    scores = mm_nt(query, key_rows) * (1.0 / math.sqrt(HEAD_DIM))
    causal = lax.broadcasted_iota(jnp.int32, (length, length), 0) >= lax.broadcasted_iota(
        jnp.int32, (length, length), 1
    )
    scores = jnp.where(causal, scores, jnp.float32(-1e30))
    powers = jnp.exp(scores - jnp.max(scores, axis=-1, keepdims=True))
    probs = powers * (1.0 / jnp.sum(powers, axis=-1, keepdims=True))
    probs_low = probs.astype(jnp.bfloat16)
    output[...] = mm(probs_low, value).astype(jnp.bfloat16)
    cotangent = d_out[...]
    d_value = mm_tn(probs_low, cotangent).astype(jnp.bfloat16)
    d_probs = mm_nt(cotangent, value).astype(jnp.bfloat16).astype(jnp.float32)
    inner = jnp.sum(d_probs * probs, axis=-1, keepdims=True)
    d_scores = (probs * (d_probs - inner) * (1.0 / math.sqrt(HEAD_DIM))).astype(jnp.bfloat16)
    d_query = mm(d_scores, key_rows).astype(jnp.bfloat16).astype(jnp.float32)
    d_key = mm_tn(d_scores, query).astype(jnp.bfloat16).astype(jnp.float32)
    pre_query = rotate(d_query, -sin).astype(jnp.bfloat16)
    pre_key = rotate(d_key, -sin).astype(jnp.bfloat16)
    pre[0] = pre_query
    pre[1] = pre_key
    pre[2] = d_value
    product = (
        pre_query.astype(jnp.float32) * proj[0]
        + pre_key.astype(jnp.float32) * proj[1]
        + d_value.astype(jnp.float32) * proj[2]
    )

    @pl.when(pl.program_id(0) == 0)
    def _():
        dots[...] = product

    @pl.when(pl.program_id(0) > 0)
    def _():
        dots[...] += product


def attention(idx, size, mine, other, weights, from_left, from_right, d_out, tables, chunk, wide):
    _, length, part = mine.shape
    heads = wide // HEAD_DIM
    first = chunk * heads
    block = pl.BlockSpec((1, length, part), lambda h, idx: (0, 0, 0))
    table = pl.BlockSpec((length, HEAD_DIM), lambda h, idx: (0, 0))
    stack = pl.BlockSpec((3, length, HEAD_DIM), lambda h, idx: (0, 0, h))
    return pl.pallas_call(
        attention_kernel,
        grid_spec=pltpu.PrefetchScalarGridSpec(
            num_scalar_prefetch=1,
            grid=(heads,),
            in_specs=[
                block,
                block,
                pl.BlockSpec((3, part, HEAD_DIM), lambda h, idx: (0, idx[size], first + h)),
                pl.BlockSpec((3, part, HEAD_DIM), lambda h, idx: (0, 1 - idx[size], first + h)),
                stack,
                stack,
                pl.BlockSpec((length, HEAD_DIM), lambda h, idx: (0, first + h)),
                table,
                table,
            ],
            out_specs=[
                pl.BlockSpec((length, HEAD_DIM), lambda h, idx: (0, h)),
                stack,
                table,
            ],
        ),
        out_shape=[
            jax.ShapeDtypeStruct((length, wide), jnp.bfloat16),
            jax.ShapeDtypeStruct((3, length, wide), jnp.bfloat16),
            jax.ShapeDtypeStruct((length, HEAD_DIM), jnp.float32),
        ],
        compiler_params=params(SMALL),
        cost_estimate=cost(12 * length * part * wide, 24 * part * wide),
        name="attention",
    )(idx, mine, other, weights, weights, from_left, from_right, d_out, *tables)


def grads_kernel(count, sets, turned, *refs):
    pieces, out = refs[:-1], refs[-1]
    length = turned.shape[1] // count
    total, start = None, 0
    for position in range(sets):
        group = pieces[position * (count + 1) : (position + 1) * (count + 1)]
        rows = group[0].shape[1]
        for place in range(count):
            if place < count - 1:
                block = group[place][0]
            else:
                block = jnp.concatenate([group[place][0], group[place + 1][0]], axis=0)
            low = place * length + start
            product = mm(turned[:, low : low + rows], block)
            total = product if total is None else total + product
        start += rows
    out[0] = total


def grads_chunk(count, turned, gathered, before, chunk, wide, columns):
    depth, span = turned.shape
    in_specs = [pl.BlockSpec((depth, span), lambda m: (0, 0))]
    operands = [turned]
    for pieces in gathered:
        for piece in pieces:
            in_specs.append(pl.BlockSpec((1, *piece.shape[1:]), lambda m: (m, 0, 0)))
            operands.append(piece)
    aliases = {}
    kernel = functools.partial(grads_kernel, count, len(gathered))
    if before is not None:
        aliases = {len(operands): 0}
        operands.append(before)
        in_specs.append(pl.BlockSpec(memory_space=pl.ANY))
        inner = kernel

        def kernel(*refs):
            inner(*refs[:-2], refs[-1])

    return pl.pallas_call(
        kernel,
        grid=(3,),
        in_specs=in_specs,
        out_specs=pl.BlockSpec((1, depth, wide), lambda m: (m, 0, chunk)),
        out_shape=jax.ShapeDtypeStruct((3, depth, columns), jnp.float32),
        input_output_aliases=aliases,
        compiler_params=params(LARGE),
        cost_estimate=cost(6 * span * depth * wide, 6 * span * wide + 12 * depth * wide),
        name="grads",
    )(*operands)


def back(pieces, turned, place, count):
    def one(piece):
        total = mm(piece[0], turned[0])
        for m in range(1, 3):
            total += mm(piece[m], turned[m])
        return total

    if place < count - 1:
        return one(pieces[place])
    return jnp.concatenate([one(pieces[place]), one(pieces[place + 1])], axis=0)


def term_first_kernel(count, idx, turned, *refs):
    for place in range(count):
        refs[-1][idx[count + 1 + place]] = back(refs, turned, place, count)


def term_first(idx, turned, pieces, chunk, wide):
    count = len(pieces) - 1
    length = pieces[0].shape[1]
    depth = turned.shape[2]
    return pl.pallas_call(
        functools.partial(term_first_kernel, count),
        grid_spec=pltpu.PrefetchScalarGridSpec(
            num_scalar_prefetch=1,
            grid=(1,),
            in_specs=[
                pl.BlockSpec((3, wide, depth), lambda i, idx: (0, chunk, 0)),
                *[pl.BlockSpec(piece.shape, lambda i, idx: (0, 0, 0)) for piece in pieces],
            ],
            out_specs=pl.BlockSpec((count, length, depth), lambda i, idx: (0, 0, 0)),
        ),
        out_shape=jax.ShapeDtypeStruct((count, length, depth), jnp.float32),
        compiler_params=params(LARGE),
        cost_estimate=cost(6 * count * length * depth * wide, 6 * count * length * wide),
        name="term_first",
    )(idx, turned, *pieces)


def term_last_kernel(count, idx, turned, before, *refs):
    keep, send = refs[-2], refs[-1]
    for place in range(count):
        total = back(refs, turned, place, count) + before[idx[count + 1 + place]]

        @pl.when(idx[2 * count + 1 + place] == 0)
        def _():
            keep[idx[3 * count + 1 + place]] = total

        @pl.when(idx[2 * count + 1 + place] == 1)
        def _():
            send[idx[3 * count + 1 + place]] = total.astype(jnp.bfloat16)


def term_last(idx, turned, before, pieces, part, chunk, wide):
    count, _, depth = before.shape
    rows = pieces[0].shape[1]
    result = pl.BlockSpec((count // 2, rows, depth), lambda i, idx: (0, 0, 0))
    return pl.pallas_call(
        functools.partial(term_last_kernel, count),
        grid_spec=pltpu.PrefetchScalarGridSpec(
            num_scalar_prefetch=1,
            grid=(1,),
            in_specs=[
                pl.BlockSpec((3, wide, depth), lambda i, idx: (0, chunk, 0)),
                pl.BlockSpec((count, rows, depth), lambda i, idx: (0, part, 0)),
                *[pl.BlockSpec(piece.shape, lambda i, idx: (0, 0, 0)) for piece in pieces],
            ],
            out_specs=[result, result],
        ),
        out_shape=[
            jax.ShapeDtypeStruct((count // 2, rows, depth), jnp.float32),
            jax.ShapeDtypeStruct((count // 2, rows, depth), jnp.bfloat16),
        ],
        compiler_params=params(LARGE),
        cost_estimate=cost(6 * count * rows * depth * wide, 6 * count * rows * wide),
        name="term_last",
    )(idx, turned, before, *pieces)


def after(first, *arrays):
    tied = lax.optimization_barrier((first, *arrays))
    return tied[1:]


def local(tokens, norm_gain, w_quant, w_scale, d_out):
    length, width = tokens.shape
    depth, columns = w_quant.shape[1:]
    size, nodes = lax.axis_size("local"), lax.axis_size("node")
    here, node = lax.axis_index("local"), lax.axis_index("node")
    wide = columns // 2
    far = size // 2
    group = size // nodes
    core = node % 2

    order = ring_order(size)
    distances = ring_distances(size)
    table = jnp.asarray(index_table(size, nodes))
    idx = lax.dynamic_index_in_dim(table, node * size + here, 0, keepdims=False)

    def shift(array, distance):
        moves = [(order[i], order[(i + distance) % size]) for i in range(size)]
        return lax.ppermute(array, "local", moves)

    def swap(array, bit):
        return lax.ppermute(array, "node", [(n, n ^ bit) for n in range(nodes)])

    blocks, inverse_rms = normed_blocks(idx, tokens, norm_gain[None], size, depth // 2)
    mine_far = shift(blocks[far], far)
    other_far = swap(mine_far, 1)
    weights, turned = scaled_weights(w_quant, w_scale)
    firsts = sum_first(idx, size, mine_far, other_far, weights)
    mine = jnp.stack([shift(blocks[-d % size], -d) if d else blocks[0] for d in distances[:-1]])
    other = swap(mine, 1)

    tables = rope_tables(length, HEAD_DIM)
    arrived = []
    for chunk in range(2):
        right, left = firsts[2 * chunk : 2 * chunk + 2]
        for distance in range(far - 1, -1, -1):
            from_left, from_right = shift(right, 1), shift(left, -1)
            if distance:
                places = distances.index(distance), distances.index(-distance)
                right, left = sum_step(
                    idx, size, mine, other, places, weights, from_left, from_right, chunk, wide
                )
        arrived.append((from_left, from_right))

    outputs, pres, dots = [], [], 0.0
    for chunk in range(2):
        output, pre, product = attention(
            idx, size, mine, other, weights, *arrived[chunk], d_out, tables, chunk, wide
        )
        outputs.append(output)
        pres.append(pre)
        dots += jnp.sum(product, axis=-1, keepdims=True)
    bit = 1
    while bit < nodes:
        dots = dots + swap(dots, bit)
        bit *= 2
    rows_turned = turn(idx, mine, other, mine_far, other_far)

    half = length // 2
    sets = [pres[0], pres[1][:, :half], pres[1][:, half:]]
    gathered = [[block] for block in sets]
    moving = [(block, block) for block in sets]
    schedule = [(0, 1)]
    for step in range(2, far + 1):
        schedule += [(0, step), (1, step - 1)]
    schedule += [(2, 1), (1, far)] + [(2, step) for step in range(2, far + 1)]

    share = width // nodes
    values_part = lax.dynamic_slice_in_dim(tokens, node * share, share, 1).astype(jnp.float32)
    gains_part = lax.dynamic_slice_in_dim(norm_gain, node * share, share, 0).astype(jnp.float32)
    inverse_rms = inverse_rms[:, :1]

    def start_term(before, part):
        keep, send = term_last(idx, turned, before, gathered[1 + part], part, 1, wide)
        return keep + swap(send, 1).astype(jnp.float32)

    def end_term(summed, part):
        bit = 2
        while bit < nodes:
            pair = summed.reshape(-1, 2, group, *summed.shape[1:])
            own = (node // bit) % 2
            keep = lax.dynamic_index_in_dim(pair, own, 1, keepdims=False)
            send = lax.dynamic_index_in_dim(pair, 1 - own, 1, keepdims=False)
            summed = keep + swap(send.astype(jnp.bfloat16), bit).astype(jnp.float32)
            summed = summed.reshape(-1, *pair.shape[3:])
            bit *= 2
        summed = summed.astype(jnp.bfloat16)
        came = []
        for turn in range(group):
            block = lax.dynamic_index_in_dim(summed, (here + turn) % group, 0, keepdims=False)
            moves = [
                (n * size + s, (s // group) * size + n * group + (s + turn) % group)
                for n in range(nodes)
                for s in range(size)
            ]
            came.append(lax.ppermute(block, ("node", "local"), moves))
        came = jnp.stack(came)
        upstream = jnp.concatenate(
            [
                lax.dynamic_index_in_dim(came, (here + group - i) % group, 0, keepdims=False)
                for i in range(group)
            ],
            axis=-1,
        ).astype(jnp.float32)
        rows = slice(part * half, (part + 1) * half)
        d_rows = (
            inverse_rms[rows] * gains_part * upstream
            - values_part[rows] * inverse_rms[rows] ** 2 * dots[rows] / width
        )
        return d_rows.astype(jnp.bfloat16)

    term = early = None
    for ring, step in schedule:
        right, left = moving[ring]
        if step == far:
            middle = right.shape[1] // 2
            right, left = right[:, :middle], left[:, middle:]
        if (ring, step) == (1, 1):
            right, left = after(moving[0][0], right, left)
        if (ring, step) == (2, 1):
            right, left = after(moving[0][0], right, left)
        if (ring, step) == (2, min(2, far)):
            right, left = after(term, right, left)
        if (ring, step) == (2, far):
            right, left = after(early, right, left)
        right, left = shift(right, 1), shift(left, -1)
        moving[ring] = right, left
        gathered[ring] += [right, left]
        if (ring, step) == (0, far):
            term = term_first(idx, turned, gathered[0], 0, wide)
        if (ring, step) == (1, far):
            early = start_term(term, 0)
    late = start_term(term, 1)
    d_tokens = jnp.concatenate([end_term(early, 0), end_term(late, 1)], axis=0)

    grads = grads_chunk(size, rows_turned, gathered[:1], None, 0, wide, columns)
    grads = grads_chunk(size, rows_turned, gathered[1:], grads, 1, wide, columns)
    return (jnp.concatenate(outputs, axis=-1), d_tokens, grads)


def solution(mesh):
    placed = (
        P("local", None),
        P(),
        P(None, "local", "node"),
        P(None, "local", "node"),
        P("local", "node"),
    )
    return jax.shard_map(
        local,
        mesh=mesh,
        in_specs=placed,
        out_specs=(P("local", "node"), P("local", "node"), P(None, "local", "node")),
        check_vma=False,
    )
```

```python
import functools
import math

import jax
import jax.numpy as jnp
import numpy as np
from jax import lax
from jax.experimental import pallas as pl
from jax.experimental.pallas import tpu as pltpu
from jax.sharding import PartitionSpec as P

HEAD_DIM = 128
NORM_EPS = 1e-05
SMALL, LARGE = 20 * 1024 * 1024, 56 * 1024 * 1024


def params(limit):
    return pltpu.CompilerParams(dimension_semantics=("arbitrary",), vmem_limit_bytes=limit)


def cost(flops, moved):
    return pl.CostEstimate(flops=flops, bytes_accessed=moved, transcendentals=0)


def mm(a, b):
    return jnp.dot(a, b, preferred_element_type=jnp.float32)


def mm_nt(a, b):
    return lax.dot_general(a, b, (((1,), (1,)), ((), ())), preferred_element_type=jnp.float32)


def mm_tn(a, b):
    return lax.dot_general(a, b, (((0,), (0,)), ((), ())), preferred_element_type=jnp.float32)


def rope_tables(length, width):
    position = jnp.arange(length).astype(jnp.float32)[:, None]
    frequency = jnp.exp(
        jnp.arange(width // 2).astype(jnp.float32) * (-2.0 * math.log(10000.0) / width)
    )
    angle = position * frequency[None, :]
    cosine, sine = jnp.cos(angle), jnp.sin(angle)
    return (
        jnp.concatenate([cosine, cosine], axis=-1),
        jnp.concatenate([-sine, sine], axis=-1),
    )


def ring_order(size):
    return [*range(0, size, 2), *reversed(range(1, size, 2))]


def ring_distances(size):
    far = size // 2
    distances = [0]
    for step in range(1, far):
        distances += [-step, step]
    return [*distances, far]


def index_table(size, nodes):
    order, group = ring_order(size), size // nodes
    rows = []
    for node in range(nodes):
        for here in range(size):
            place = order.index(here)
            seqs = [order[(place + distance) % size] for distance in ring_distances(size)]
            owner = [seq // group for seq in seqs]
            rows.append(
                [order[(place + distance) % size] for distance in range(size)]
                + [node % 2]
                + seqs
                + [owner_ % 2 ^ node % 2 for owner_ in owner]
                + [(o // 2) * group + seq % group for o, seq in zip(owner, seqs)]
            )
    return np.array(rows, np.int32)


def weights_kernel(quant, scale, out, turned):
    blocks = scale.shape[1]
    rows = quant.shape[1] // blocks
    scales = scale[0].astype(jnp.float32)
    for block in range(blocks):
        span = slice(block * rows, (block + 1) * rows)
        scaled = (quant[0, span].astype(jnp.float32) * scales[block : block + 1]).astype(jnp.bfloat16)
        out[0, span] = scaled
        turned[0, :, span] = scaled.T


def scaled_weights(w_quant, w_scale):
    _, depth, columns = w_quant.shape
    blocks = w_scale.shape[1]
    return pl.pallas_call(
        weights_kernel,
        grid=(3,),
        in_specs=[
            pl.BlockSpec((1, depth, columns), lambda m: (m, 0, 0)),
            pl.BlockSpec((1, blocks, columns), lambda m: (m, 0, 0)),
        ],
        out_specs=[
            pl.BlockSpec((1, depth, columns), lambda m: (m, 0, 0)),
            pl.BlockSpec((1, columns, depth), lambda m: (m, 0, 0)),
        ],
        out_shape=[
            jax.ShapeDtypeStruct((3, depth, columns), jnp.bfloat16),
            jax.ShapeDtypeStruct((3, columns, depth), jnp.bfloat16),
        ],
        compiler_params=params(SMALL),
        cost_estimate=cost(3 * depth * columns, 18 * depth * columns),
        name="scaled_weights",
    )(w_quant, w_scale)


def normed_kernel(idx, tokens, gain, *refs):
    outs, gains = refs[:-1], refs[-1]
    width, part = tokens.shape[1], outs[0].shape[1]
    gains[...] = gain[...].astype(jnp.float32)
    values = tokens[...].astype(jnp.float32)
    inverse = lax.rsqrt(jnp.mean(values * values, axis=-1, keepdims=True) + NORM_EPS)
    size = len(outs) - 1
    for distance in range(size):
        start = pl.multiple_of(idx[distance] * (width // size) + idx[size] * part, part)
        block = tokens[:, pl.ds(start, part)].astype(jnp.float32)
        scale = gains[:, pl.ds(start, part)]
        outs[distance][...] = (block * inverse * scale).astype(jnp.bfloat16)
    outs[size][...] = jnp.broadcast_to(inverse, outs[size].shape)


def normed_blocks(idx, tokens, gain, size, part):
    length, width = tokens.shape
    tile = length // 4
    block = pl.BlockSpec((tile, part), lambda i, idx: (i, 0))
    *blocks, inverse = pl.pallas_call(
        normed_kernel,
        grid_spec=pltpu.PrefetchScalarGridSpec(
            num_scalar_prefetch=1,
            grid=(4,),
            in_specs=[
                pl.BlockSpec((tile, width), lambda i, idx: (i, 0)),
                pl.BlockSpec((1, width), lambda i, idx: (0, 0)),
            ],
            out_specs=[block] * size + [pl.BlockSpec((tile, 128), lambda i, idx: (i, 0))],
            scratch_shapes=[pltpu.VMEM((1, width), jnp.float32)],
        ),
        out_shape=[jax.ShapeDtypeStruct((length, part), jnp.bfloat16)] * size
        + [jax.ShapeDtypeStruct((length, 128), jnp.float32)],
        compiler_params=params(SMALL),
        cost_estimate=cost(8 * length * width, 4 * length * width),
        name="normed_blocks",
    )(idx, tokens, gain)
    return blocks, inverse


def turn_kernel(count, idx, mine, other, mine_far, other_far, out):
    length, part = mine_far.shape
    for side, near, last in ((0, mine, mine_far), (1, other, other_far)):
        half = idx[count] * (1 - side) + (1 - idx[count]) * side
        rows = pl.ds(pl.multiple_of(half * part, part), part)
        for place in range(count):
            block = near[place] if place < count - 1 else last[...]
            out[rows, place * length : (place + 1) * length] = block.T


def turn(idx, mine, other, mine_far, other_far):
    near, length, part = mine.shape
    count = near + 1
    stack = pl.BlockSpec(mine.shape, lambda i, idx: (0, 0, 0))
    last = pl.BlockSpec((length, part), lambda i, idx: (0, 0))
    shape = (2 * part, count * length)
    return pl.pallas_call(
        functools.partial(turn_kernel, count),
        grid_spec=pltpu.PrefetchScalarGridSpec(
            num_scalar_prefetch=1,
            grid=(1,),
            in_specs=[stack, stack, last, last],
            out_specs=pl.BlockSpec(shape, lambda i, idx: (0, 0)),
        ),
        out_shape=jax.ShapeDtypeStruct(shape, jnp.bfloat16),
        compiler_params=params(SMALL),
        cost_estimate=cost(2 * count * length * part, 8 * count * length * part),
        name="turn",
    )(idx, mine, other, mine_far, other_far)


def sum_first_kernel(idx, mine, other, weight, weight_other, *outs):
    half, wide = outs[0].shape[1:]
    for chunk in range(2):
        span = slice(chunk * wide, (chunk + 1) * wide)
        product = mm(mine[...], weight[0, :, span]) + mm(other[...], weight_other[0, :, span])
        outs[2 * chunk][0] = product[:half].astype(jnp.bfloat16)
        outs[2 * chunk + 1][0] = product[half:].astype(jnp.bfloat16)


def sum_step_kernel(
    idx, mine_r, other_r, mine_l, other_l, weight, weight_other, from_left, from_right, right, left
):
    length, part = right.shape[1], from_left.shape[1]
    product = mm(mine_r[0], weight[0]) + mm(other_r[0], weight_other[0])
    right[0, :part] = (product[:part] + from_left[0].astype(jnp.float32)).astype(jnp.bfloat16)
    if part < length:
        right[0, part:] = product[part:].astype(jnp.bfloat16)
    product = mm(mine_l[0], weight[0]) + mm(other_l[0], weight_other[0])
    rest = length - part
    left[0, rest:] = (product[rest:] + from_right[0].astype(jnp.float32)).astype(jnp.bfloat16)
    if rest:
        left[0, :rest] = product[:rest].astype(jnp.bfloat16)


def weight_halves(size, part, wide, chunk):
    return [
        pl.BlockSpec((1, part, wide), lambda m, idx: (m, idx[size], chunk)),
        pl.BlockSpec((1, part, wide), lambda m, idx: (m, 1 - idx[size], chunk)),
    ]


def sum_first(idx, size, mine, other, weights):
    length, part = mine.shape
    columns = weights.shape[2]
    half, wide = length // 2, columns // 2
    block = pl.BlockSpec((length, part), lambda m, idx: (0, 0))
    result = jax.ShapeDtypeStruct((3, half, wide), jnp.bfloat16)
    return pl.pallas_call(
        sum_first_kernel,
        grid_spec=pltpu.PrefetchScalarGridSpec(
            num_scalar_prefetch=1,
            grid=(3,),
            in_specs=[block, block, *weight_halves(size, part, columns, 0)],
            out_specs=[pl.BlockSpec((1, half, wide), lambda m, idx: (m, 0, 0))] * 4,
        ),
        out_shape=[result] * 4,
        compiler_params=params(SMALL),
        cost_estimate=cost(12 * length * part * columns, 16 * part * columns),
        name="sum_first",
    )(idx, mine, other, weights, weights)


def sum_step(idx, size, mine, other, places, weights, from_left, from_right, chunk, wide):
    _, length, part = mine.shape
    block_r = pl.BlockSpec((1, length, part), lambda m, idx: (places[0], 0, 0))
    block_l = pl.BlockSpec((1, length, part), lambda m, idx: (places[1], 0, 0))
    came = pl.BlockSpec((1, from_left.shape[1], wide), lambda m, idx: (m, 0, 0))
    whole = jax.ShapeDtypeStruct((3, length, wide), jnp.bfloat16)
    return pl.pallas_call(
        sum_step_kernel,
        grid_spec=pltpu.PrefetchScalarGridSpec(
            num_scalar_prefetch=1,
            grid=(3,),
            in_specs=[
                block_r,
                block_r,
                block_l,
                block_l,
                *weight_halves(size, part, wide, chunk),
                came,
                came,
            ],
            out_specs=[pl.BlockSpec((1, length, wide), lambda m, idx: (m, 0, 0))] * 2,
        ),
        out_shape=[whole, whole],
        compiler_params=params(SMALL),
        cost_estimate=cost(24 * length * part * wide, 24 * part * wide),
        name="sum_step",
    )(idx, mine, other, mine, other, weights, weights, from_left, from_right)


def attention_kernel(
    idx, mine, other, weight, weight_other, from_left, from_right, d_out, cosine, sine,
    output, pre, dots,
):
    length = mine.shape[1]
    proj = [
        mm(mine[0], weight[m])
        + mm(other[0], weight_other[m])
        + (from_left[m].astype(jnp.float32) + from_right[m].astype(jnp.float32))
        for m in range(3)
    ]
    cos, sin = cosine[...], sine[...]
    half = HEAD_DIM // 2

    def rotate(tensor, angle):
        return tensor * cos + pltpu.roll(tensor, half, 1) * angle

    query = rotate(proj[0], sin).astype(jnp.bfloat16)
    key_rows = rotate(proj[1], sin).astype(jnp.bfloat16)
    value = proj[2].astype(jnp.bfloat16)
    scores = mm_nt(query, key_rows) * (1.0 / math.sqrt(HEAD_DIM))
    causal = lax.broadcasted_iota(jnp.int32, (length, length), 0) >= lax.broadcasted_iota(
        jnp.int32, (length, length), 1
    )
    scores = jnp.where(causal, scores, jnp.float32(-1e30))
    powers = jnp.exp(scores - jnp.max(scores, axis=-1, keepdims=True))
    probs = powers * (1.0 / jnp.sum(powers, axis=-1, keepdims=True))
    probs_low = probs.astype(jnp.bfloat16)
    output[...] = mm(probs_low, value).astype(jnp.bfloat16)
    cotangent = d_out[...]
    d_value = mm_tn(probs_low, cotangent).astype(jnp.bfloat16)
    d_probs = mm_nt(cotangent, value).astype(jnp.bfloat16).astype(jnp.float32)
    inner = jnp.sum(d_probs * probs, axis=-1, keepdims=True)
    d_scores = (probs * (d_probs - inner) * (1.0 / math.sqrt(HEAD_DIM))).astype(jnp.bfloat16)
    d_query = mm(d_scores, key_rows).astype(jnp.bfloat16).astype(jnp.float32)
    d_key = mm_tn(d_scores, query).astype(jnp.bfloat16).astype(jnp.float32)
    pre_query = rotate(d_query, -sin).astype(jnp.bfloat16)
    pre_key = rotate(d_key, -sin).astype(jnp.bfloat16)
    pre[0] = pre_query
    pre[1] = pre_key
    pre[2] = d_value
    product = (
        pre_query.astype(jnp.float32) * proj[0]
        + pre_key.astype(jnp.float32) * proj[1]
        + d_value.astype(jnp.float32) * proj[2]
    )

    @pl.when(pl.program_id(0) == 0)
    def _():
        dots[...] = product

    @pl.when(pl.program_id(0) > 0)
    def _():
        dots[...] += product


def attention(idx, size, mine, other, weights, from_left, from_right, d_out, tables, chunk, wide):
    _, length, part = mine.shape
    heads = wide // HEAD_DIM
    first = chunk * heads
    block = pl.BlockSpec((1, length, part), lambda h, idx: (0, 0, 0))
    table = pl.BlockSpec((length, HEAD_DIM), lambda h, idx: (0, 0))
    stack = pl.BlockSpec((3, length, HEAD_DIM), lambda h, idx: (0, 0, h))
    return pl.pallas_call(
        attention_kernel,
        grid_spec=pltpu.PrefetchScalarGridSpec(
            num_scalar_prefetch=1,
            grid=(heads,),
            in_specs=[
                block,
                block,
                pl.BlockSpec((3, part, HEAD_DIM), lambda h, idx: (0, idx[size], first + h)),
                pl.BlockSpec((3, part, HEAD_DIM), lambda h, idx: (0, 1 - idx[size], first + h)),
                stack,
                stack,
                pl.BlockSpec((length, HEAD_DIM), lambda h, idx: (0, first + h)),
                table,
                table,
            ],
            out_specs=[
                pl.BlockSpec((length, HEAD_DIM), lambda h, idx: (0, h)),
                stack,
                table,
            ],
        ),
        out_shape=[
            jax.ShapeDtypeStruct((length, wide), jnp.bfloat16),
            jax.ShapeDtypeStruct((3, length, wide), jnp.bfloat16),
            jax.ShapeDtypeStruct((length, HEAD_DIM), jnp.float32),
        ],
        compiler_params=params(SMALL),
        cost_estimate=cost(12 * length * part * wide, 24 * part * wide),
        name="attention",
    )(idx, mine, other, weights, weights, from_left, from_right, d_out, *tables)


def grads_chunk(count, turned, pieces, start, before, add, chunk, wide, columns):
    depth, span = turned.shape
    in_specs = [pl.BlockSpec((depth, span), lambda m: (0, 0))]
    operands = [turned]
    for piece in pieces:
        in_specs.append(pl.BlockSpec((1, *piece.shape[1:]), lambda m: (m, 0, 0)))
        operands.append(piece)
    result = pl.BlockSpec((1, depth, wide), lambda m: (m, 0, chunk))
    aliases = {}
    if before is not None:
        aliases = {len(operands): 0}
        operands.append(before)
        in_specs.append(result if add else pl.BlockSpec(memory_space=pl.ANY))
    length = span // count
    rows = pieces[0].shape[1]

    def kernel(turned_ref, *refs):
        blocks = jnp.concatenate([piece[0] for piece in refs[: count + 1]], axis=0)
        left = [
            turned_ref[:, place * length + start : place * length + start + rows]
            for place in range(count)
        ]
        total = mm(jnp.concatenate(left, axis=1), blocks)
        refs[-1][0] = total + refs[-2][0] if add else total

    return pl.pallas_call(
        kernel,
        grid=(3,),
        in_specs=in_specs,
        out_specs=result,
        out_shape=jax.ShapeDtypeStruct((3, depth, columns), jnp.float32),
        input_output_aliases=aliases,
        compiler_params=params(LARGE),
        cost_estimate=cost(
            6 * count * rows * depth * wide, 6 * count * rows * wide + 12 * depth * wide
        ),
        name="grads",
    )(*operands)


def back(pieces, turned):
    wide, depth = turned.shape[1:]
    rows = [jnp.concatenate([piece[m] for m in range(3)], axis=1) for piece in pieces]
    return mm(jnp.concatenate(rows, axis=0), turned[...].reshape(3 * wide, depth))


def term_step(turned, pieces, befores, part, chunk, wide):
    depth = turned.shape[2]
    count = len(pieces)
    rows = pieces[0].shape[1]
    results = [pl.BlockSpec((rows, depth), lambda i: (0, 0))] * count
    takes = [
        pl.BlockSpec((rows, depth), lambda i, row=(part if before.shape[0] > rows else 0): (row, 0))
        for before in befores
    ]

    def kernel(turned_ref, *refs):
        total = back(refs[:count], turned_ref)
        for place in range(count):
            block = total[place * rows : (place + 1) * rows]
            if befores:
                block += refs[count + place][...]
            refs[len(refs) - count + place][...] = block

    return pl.pallas_call(
        kernel,
        grid=(1,),
        in_specs=[
            pl.BlockSpec((3, wide, depth), lambda i: (0, chunk, 0)),
            *[pl.BlockSpec(piece.shape, lambda i: (0, 0, 0)) for piece in pieces],
            *takes,
        ],
        out_specs=results,
        out_shape=[jax.ShapeDtypeStruct((rows, depth), jnp.float32)] * count,
        compiler_params=params(SMALL),
        cost_estimate=cost(6 * count * rows * depth * wide, 12 * count * rows * wide),
        name="term_step",
    )(turned, *pieces, *befores)


def term_last_kernel(count, idx, turned, before, far_r, far_l, *refs):
    nears, keep, send = refs[:-2], refs[-2], refs[-1]
    last = back([far_r, far_l], turned) + before[...]
    for place in range(count):
        total = nears[place][...] if place < count - 1 else last

        @pl.when(idx[2 * count + 1 + place] == 0)
        def _():
            keep[idx[3 * count + 1 + place]] = total

        @pl.when(idx[2 * count + 1 + place] == 1)
        def _():
            send[idx[3 * count + 1 + place]] = total.astype(jnp.bfloat16)


def term_last(idx, turned, before, pieces, nears, chunk, wide):
    count = len(nears) + 1
    rows, depth = before.shape
    result = pl.BlockSpec((count // 2, rows, depth), lambda i, idx: (0, 0, 0))
    block = pl.BlockSpec((rows, depth), lambda i, idx: (0, 0))
    return pl.pallas_call(
        functools.partial(term_last_kernel, count),
        grid_spec=pltpu.PrefetchScalarGridSpec(
            num_scalar_prefetch=1,
            grid=(1,),
            in_specs=[
                pl.BlockSpec((3, wide, depth), lambda i, idx: (0, chunk, 0)),
                block,
                *[pl.BlockSpec(piece.shape, lambda i, idx: (0, 0, 0)) for piece in pieces],
                *[block] * (count - 1),
            ],
            out_specs=[result, result],
        ),
        out_shape=[
            jax.ShapeDtypeStruct((count // 2, rows, depth), jnp.float32),
            jax.ShapeDtypeStruct((count // 2, rows, depth), jnp.bfloat16),
        ],
        compiler_params=params(SMALL),
        cost_estimate=cost(6 * rows * depth * wide, 12 * count * rows * depth),
        name="term_last",
    )(idx, turned, before, *pieces, *nears)


def after(first, *arrays):
    tied = lax.optimization_barrier((first, *arrays))
    return tied[1:]


def local(tokens, norm_gain, w_quant, w_scale, d_out):
    length, width = tokens.shape
    depth, columns = w_quant.shape[1:]
    size, nodes = lax.axis_size("local"), lax.axis_size("node")
    here, node = lax.axis_index("local"), lax.axis_index("node")
    wide = columns // 2
    far = size // 2
    group = size // nodes
    core = node % 2

    order = ring_order(size)
    distances = ring_distances(size)
    table = jnp.asarray(index_table(size, nodes))
    idx = lax.dynamic_index_in_dim(table, node * size + here, 0, keepdims=False)

    def shift(array, distance):
        moves = [(order[i], order[(i + distance) % size]) for i in range(size)]
        return lax.ppermute(array, "local", moves)

    def swap(array, bit):
        return lax.ppermute(array, "node", [(n, n ^ bit) for n in range(nodes)])

    blocks, inverse_rms = normed_blocks(idx, tokens, norm_gain[None], size, depth // 2)
    mine_far = shift(blocks[far], far)
    other_far = swap(mine_far, 1)
    weights, turned = scaled_weights(w_quant, w_scale)
    firsts = sum_first(idx, size, mine_far, other_far, weights)
    nears = after(mine_far, *blocks[:far], *blocks[far + 1 :])
    nears = [*nears[:far], None, *nears[far:]]
    mine = jnp.stack([shift(nears[-d % size], -d) if d else blocks[0] for d in distances[:-1]])
    other = swap(mine, 1)

    tables = rope_tables(length, HEAD_DIM)
    arrived = []
    for chunk in range(2):
        right, left = firsts[2 * chunk : 2 * chunk + 2]
        for distance in range(far - 1, -1, -1):
            from_left, from_right = shift(right, 1), shift(left, -1)
            if distance:
                places = distances.index(distance), distances.index(-distance)
                right, left = sum_step(
                    idx, size, mine, other, places, weights, from_left, from_right, chunk, wide
                )
        arrived.append((from_left, from_right))

    outputs, pres, dots = [], [], 0.0
    for chunk in range(2):
        output, pre, product = attention(
            idx, size, mine, other, weights, *arrived[chunk], d_out, tables, chunk, wide
        )
        outputs.append(output)
        pres.append(pre)
        dots += jnp.sum(product, axis=-1, keepdims=True)
    bit = 1
    while bit < nodes:
        dots = dots + swap(dots, bit)
        bit *= 2
    rows_turned = turn(idx, mine, other, mine_far, other_far)

    half = length // 2
    sets = [pres[0], pres[1][:, :half], pres[1][:, half:]]
    gathered = [[block] for block in sets]
    moving = [(block, block) for block in sets]
    schedule = [(0, 1)]
    for step in range(2, far):
        schedule += [(0, step), (1, step - 1)]
    schedule += [(2, 1), (0, far), (1, far - 1), (1, far)]
    schedule += [(2, step) for step in range(2, far + 1)]

    share = width // nodes
    values_part = lax.dynamic_slice_in_dim(tokens, node * share, share, 1).astype(jnp.float32)
    gains_part = lax.dynamic_slice_in_dim(norm_gain, node * share, share, 0).astype(jnp.float32)
    inverse_rms = inverse_rms[:, :1]

    def start_term(part):
        keep, send = term_last(
            idx, turned, lasts[0][part], gathered[1 + part][-2:], terms[1 + part], 1, wide
        )
        return keep + swap(send, 1).astype(jnp.float32)

    def sum_nodes(summed):
        bit = 2
        while bit < nodes:
            pair = summed.reshape(-1, 2, group, *summed.shape[1:])
            own = (node // bit) % 2
            keep = lax.dynamic_index_in_dim(pair, own, 1, keepdims=False)
            send = lax.dynamic_index_in_dim(pair, 1 - own, 1, keepdims=False)
            summed = keep + swap(send.astype(jnp.bfloat16), bit).astype(jnp.float32)
            summed = summed.reshape(-1, *pair.shape[3:])
            bit *= 2
        return summed.astype(jnp.bfloat16)

    def end_term(summed, part):
        came = []
        for turn in range(group):
            block = lax.dynamic_index_in_dim(summed, (here + turn) % group, 0, keepdims=False)
            moves = [
                (n * size + s, (s // group) * size + n * group + (s + turn) % group)
                for n in range(nodes)
                for s in range(size)
            ]
            came.append(lax.ppermute(block, ("node", "local"), moves))
        came = jnp.stack(came)
        upstream = jnp.concatenate(
            [
                lax.dynamic_index_in_dim(came, (here + group - i) % group, 0, keepdims=False)
                for i in range(group)
            ],
            axis=-1,
        ).astype(jnp.float32)
        rows = slice(part * half, (part + 1) * half)
        d_rows = (
            inverse_rms[rows] * gains_part * upstream
            - values_part[rows] * inverse_rms[rows] ** 2 * dots[rows] / width
        )
        return d_rows.astype(jnp.bfloat16)

    terms = [[], [], []]
    lasts = [None]
    first_grads = half_grads = early = None
    for ring, step in schedule:
        right, left = moving[ring]
        if step == far:
            middle = right.shape[1] // 2
            right, left = right[:, :middle], left[:, middle:]
        if (ring, step) == (1, 1):
            right, left = after(moving[0][0], right, left)
        if (ring, step) == (2, 1):
            right, left = after(moving[0][0], right, left)
        if (ring, step) == (2, far - 1):
            right, left = after((first_grads, early), right, left)
        if (ring, step) == (2, far):
            right, left = after((half_grads, summed), right, left)
        right, left = shift(right, 1), shift(left, -1)
        moving[ring] = right, left
        gathered[ring] += [right, left]
        chunk, part = min(ring, 1), max(ring - 1, 0)
        if step < far:
            pieces = gathered[ring] if step == 1 else [right, left]
            known = len(terms[ring])
            befores = terms[0][known : known + len(pieces)] if ring else []
            terms[ring] += term_step(turned, pieces, befores, part, chunk, wide)
        elif ring == 0:
            lasts[0] = term_step(turned, [right, left], [], 0, 0, wide)
            first_grads = grads_chunk(
                size, rows_turned, gathered[0], 0, None, False, 0, wide, columns
            )
        elif ring == 1:
            early = start_term(0)
            half_grads = grads_chunk(
                size, rows_turned, gathered[1], 0, first_grads, False, 1, wide, columns
            )
            summed = sum_nodes(early)
    late = start_term(1)
    d_tokens = jnp.concatenate([end_term(summed, 0), end_term(sum_nodes(late), 1)], axis=0)
    grads = grads_chunk(size, rows_turned, gathered[2], half, half_grads, True, 1, wide, columns)
    return (jnp.concatenate(outputs, axis=-1), d_tokens, grads)


def solution(mesh):
    placed = (
        P("local", None),
        P(),
        P(None, "local", "node"),
        P(None, "local", "node"),
        P("local", "node"),
    )
    return jax.shard_map(
        local,
        mesh=mesh,
        in_specs=placed,
        out_specs=(P("local", "node"), P("local", "node"), P(None, "local", "node")),
        check_vma=False,
    )
```

```python
import functools
import math

import jax
import jax.numpy as jnp
import numpy as np
from jax import lax
from jax.experimental import pallas as pl
from jax.experimental.pallas import tpu as pltpu
from jax.sharding import PartitionSpec as P

HEAD_DIM = 128
NORM_EPS = 1e-05
VMEM = 24 * 1024 * 1024


def params():
    return pltpu.CompilerParams(dimension_semantics=("arbitrary",), vmem_limit_bytes=VMEM)


def tied(kernel, inputs, ties):
    def inner(*refs):
        kernel(*refs[:inputs], *refs[inputs + ties :])

    return inner


def tie_specs(ties):
    return [pl.BlockSpec(memory_space=pl.ANY)] * len(ties)


def cost(flops, moved):
    return pl.CostEstimate(flops=flops, bytes_accessed=moved, transcendentals=0)


def mm(a, b):
    return jnp.dot(a, b, preferred_element_type=jnp.float32)


def mm_nt(a, b):
    return lax.dot_general(a, b, (((1,), (1,)), ((), ())), preferred_element_type=jnp.float32)


def mm_tn(a, b):
    return lax.dot_general(a, b, (((0,), (0,)), ((), ())), preferred_element_type=jnp.float32)


def rope_tables(length, width):
    position = jnp.arange(length).astype(jnp.float32)[:, None]
    frequency = jnp.exp(
        jnp.arange(width // 2).astype(jnp.float32) * (-2.0 * math.log(10000.0) / width)
    )
    angle = position * frequency[None, :]
    cosine, sine = jnp.cos(angle), jnp.sin(angle)
    return (
        jnp.concatenate([cosine, cosine], axis=-1),
        jnp.concatenate([-sine, sine], axis=-1),
    )


def ring_order(size):
    return [*range(0, size, 2), *reversed(range(1, size, 2))]


def ring_distances(size):
    far = size // 2
    distances = [0]
    for step in range(1, far):
        distances += [-step, step]
    return [*distances, far]


def index_table(size, nodes):
    order, group = ring_order(size), size // nodes
    rows = []
    for node in range(nodes):
        for here in range(size):
            place = order.index(here)
            seqs = [order[(place + distance) % size] for distance in ring_distances(size)]
            owner = [seq // group for seq in seqs]
            rows.append(
                [order[(place + distance) % size] for distance in range(size)]
                + [node % 2]
                + seqs
                + [owner_ % 2 ^ node % 2 for owner_ in owner]
                + [(o // 2) * group + seq % group for o, seq in zip(owner, seqs)]
            )
    return np.array(rows, np.int32)


def weights_kernel(quant, scale, out, turned):
    blocks = scale.shape[1]
    rows = quant.shape[1] // blocks
    scales = scale[0].astype(jnp.float32)
    for block in range(blocks):
        span = slice(block * rows, (block + 1) * rows)
        scaled = (quant[0, span].astype(jnp.float32) * scales[block : block + 1]).astype(jnp.bfloat16)
        out[0, span] = scaled
        turned[0, :, span] = scaled.T


def scaled_weights(w_quant, w_scale):
    _, depth, columns = w_quant.shape
    blocks = w_scale.shape[1]
    return pl.pallas_call(
        weights_kernel,
        grid=(3,),
        in_specs=[
            pl.BlockSpec((1, depth, columns), lambda m: (m, 0, 0)),
            pl.BlockSpec((1, blocks, columns), lambda m: (m, 0, 0)),
        ],
        out_specs=[
            pl.BlockSpec((1, depth, columns), lambda m: (m, 0, 0)),
            pl.BlockSpec((1, columns, depth), lambda m: (m, 0, 0)),
        ],
        out_shape=[
            jax.ShapeDtypeStruct((3, depth, columns), jnp.bfloat16),
            jax.ShapeDtypeStruct((3, columns, depth), jnp.bfloat16),
        ],
        compiler_params=params(),
        cost_estimate=cost(3 * depth * columns, 18 * depth * columns),
        name="scaled_weights",
    )(w_quant, w_scale)


def normed_kernel(idx, tokens, gain, *refs):
    outs, gains = refs[:-1], refs[-1]
    width, part = tokens.shape[1], outs[0].shape[1]
    gains[...] = gain[...].astype(jnp.float32)
    values = tokens[...].astype(jnp.float32)
    inverse = lax.rsqrt(jnp.mean(values * values, axis=-1, keepdims=True) + NORM_EPS)
    size = len(outs) - 1
    for distance in range(size):
        start = pl.multiple_of(idx[distance] * (width // size) + idx[size] * part, part)
        block = tokens[:, pl.ds(start, part)].astype(jnp.float32)
        scale = gains[:, pl.ds(start, part)]
        outs[distance][...] = (block * inverse * scale).astype(jnp.bfloat16)
    outs[size][...] = jnp.broadcast_to(inverse, outs[size].shape)


def normed_blocks(idx, tokens, gain, size, part):
    length, width = tokens.shape
    tile = length // 4
    block = pl.BlockSpec((tile, part), lambda i, idx: (i, 0))
    *blocks, inverse = pl.pallas_call(
        normed_kernel,
        grid_spec=pltpu.PrefetchScalarGridSpec(
            num_scalar_prefetch=1,
            grid=(4,),
            in_specs=[
                pl.BlockSpec((tile, width), lambda i, idx: (i, 0)),
                pl.BlockSpec((1, width), lambda i, idx: (0, 0)),
            ],
            out_specs=[block] * size + [pl.BlockSpec((tile, 128), lambda i, idx: (i, 0))],
            scratch_shapes=[pltpu.VMEM((1, width), jnp.float32)],
        ),
        out_shape=[jax.ShapeDtypeStruct((length, part), jnp.bfloat16)] * size
        + [jax.ShapeDtypeStruct((length, 128), jnp.float32)],
        compiler_params=params(),
        cost_estimate=cost(8 * length * width, 4 * length * width),
        name="normed_blocks",
    )(idx, tokens, gain)
    return blocks, inverse


def stack_kernel(*refs):
    for place, block in enumerate(refs[:-1]):
        refs[-1][place] = block[...]


def stack(blocks, ties):
    count, shape = len(blocks), blocks[0].shape
    block = pl.BlockSpec(shape, lambda i: (0, 0))
    return pl.pallas_call(
        tied(stack_kernel, count, len(ties)),
        grid=(1,),
        in_specs=[block] * count + tie_specs(ties),
        out_specs=pl.BlockSpec((count, *shape), lambda i: (0, 0, 0)),
        out_shape=jax.ShapeDtypeStruct((count, *shape), blocks[0].dtype),
        compiler_params=params(),
        cost_estimate=cost(0, 4 * count * shape[0] * shape[1]),
        name="stack",
    )(*blocks, *ties)


def pass_kernel(right, left, right_out, left_out):
    rows, sent = right.shape[1], right_out.shape[1]
    right_out[...] = right[:, :sent]
    left_out[...] = left[:, rows - sent :]


def pass_on(right, left, halve, ties):
    _, rows, wide = right.shape
    sent = rows // 2 if halve else rows
    result = jax.ShapeDtypeStruct((3, sent, wide), right.dtype)
    return pl.pallas_call(
        tied(pass_kernel, 2, len(ties)),
        grid=(1,),
        in_specs=[pl.BlockSpec(right.shape, lambda i: (0, 0, 0))] * 2 + tie_specs(ties),
        out_specs=[pl.BlockSpec(result.shape, lambda i: (0, 0, 0))] * 2,
        out_shape=[result, result],
        compiler_params=params(),
        cost_estimate=cost(0, 12 * sent * wide),
        name="pass_on",
    )(right, left, *ties)


def turn_kernel(count, idx, mine, other, mine_far, other_far, out):
    length, part = mine_far.shape
    for side, near, last in ((0, mine, mine_far), (1, other, other_far)):
        half = idx[count] * (1 - side) + (1 - idx[count]) * side
        rows = pl.ds(pl.multiple_of(half * part, part), part)
        for place in range(count):
            block = near[place] if place < count - 1 else last[...]
            out[rows, place * length : (place + 1) * length] = block.T


def turn(idx, mine, other, mine_far, other_far):
    near, length, part = mine.shape
    count = near + 1
    stack = pl.BlockSpec(mine.shape, lambda i, idx: (0, 0, 0))
    last = pl.BlockSpec((length, part), lambda i, idx: (0, 0))
    shape = (2 * part, count * length)
    return pl.pallas_call(
        functools.partial(turn_kernel, count),
        grid_spec=pltpu.PrefetchScalarGridSpec(
            num_scalar_prefetch=1,
            grid=(1,),
            in_specs=[stack, stack, last, last],
            out_specs=pl.BlockSpec(shape, lambda i, idx: (0, 0)),
        ),
        out_shape=jax.ShapeDtypeStruct(shape, jnp.bfloat16),
        compiler_params=params(),
        cost_estimate=cost(2 * count * length * part, 8 * count * length * part),
        name="turn",
    )(idx, mine, other, mine_far, other_far)


def sum_first_kernel(idx, mine, other, weight, weight_other, *outs):
    half, wide = outs[0].shape[1:]
    for chunk in range(2):
        span = slice(chunk * wide, (chunk + 1) * wide)
        product = mm(mine[...], weight[0, :, span]) + mm(other[...], weight_other[0, :, span])
        outs[2 * chunk][0] = product[:half].astype(jnp.bfloat16)
        outs[2 * chunk + 1][0] = product[half:].astype(jnp.bfloat16)


def sum_step_kernel(
    idx, mine_r, other_r, mine_l, other_l, weight, weight_other, from_left, from_right, right, left
):
    length, part = right.shape[1], from_left.shape[1]
    product = mm(mine_r[0], weight[0]) + mm(other_r[0], weight_other[0])
    right[0, :part] = (product[:part] + from_left[0].astype(jnp.float32)).astype(jnp.bfloat16)
    if part < length:
        right[0, part:] = product[part:].astype(jnp.bfloat16)
    product = mm(mine_l[0], weight[0]) + mm(other_l[0], weight_other[0])
    rest = length - part
    left[0, rest:] = (product[rest:] + from_right[0].astype(jnp.float32)).astype(jnp.bfloat16)
    if rest:
        left[0, :rest] = product[:rest].astype(jnp.bfloat16)


def weight_halves(size, part, wide, chunk):
    return [
        pl.BlockSpec((1, part, wide), lambda m, idx: (m, idx[size], chunk)),
        pl.BlockSpec((1, part, wide), lambda m, idx: (m, 1 - idx[size], chunk)),
    ]


def sum_first(idx, size, mine, other, weights):
    length, part = mine.shape
    columns = weights.shape[2]
    half, wide = length // 2, columns // 2
    block = pl.BlockSpec((length, part), lambda m, idx: (0, 0))
    result = jax.ShapeDtypeStruct((3, half, wide), jnp.bfloat16)
    return pl.pallas_call(
        sum_first_kernel,
        grid_spec=pltpu.PrefetchScalarGridSpec(
            num_scalar_prefetch=1,
            grid=(3,),
            in_specs=[block, block, *weight_halves(size, part, columns, 0)],
            out_specs=[pl.BlockSpec((1, half, wide), lambda m, idx: (m, 0, 0))] * 4,
        ),
        out_shape=[result] * 4,
        compiler_params=params(),
        cost_estimate=cost(12 * length * part * columns, 16 * part * columns),
        name="sum_first",
    )(idx, mine, other, weights, weights)


def sum_step(idx, size, mine, other, places, weights, from_left, from_right, chunk, wide, ties):
    _, length, part = mine.shape
    block_r = pl.BlockSpec((1, length, part), lambda m, idx: (places[0], 0, 0))
    block_l = pl.BlockSpec((1, length, part), lambda m, idx: (places[1], 0, 0))
    came = pl.BlockSpec((1, from_left.shape[1], wide), lambda m, idx: (m, 0, 0))
    whole = jax.ShapeDtypeStruct((3, length, wide), jnp.bfloat16)
    return pl.pallas_call(
        tied(sum_step_kernel, 9, len(ties)),
        grid_spec=pltpu.PrefetchScalarGridSpec(
            num_scalar_prefetch=1,
            grid=(3,),
            in_specs=[
                block_r,
                block_r,
                block_l,
                block_l,
                *weight_halves(size, part, wide, chunk),
                came,
                came,
                *tie_specs(ties),
            ],
            out_specs=[pl.BlockSpec((1, length, wide), lambda m, idx: (m, 0, 0))] * 2,
        ),
        out_shape=[whole, whole],
        compiler_params=params(),
        cost_estimate=cost(24 * length * part * wide, 24 * part * wide),
        name="sum_step",
    )(idx, mine, other, mine, other, weights, weights, from_left, from_right, *ties)


def attention_kernel(
    idx, mine, other, weight, weight_other, from_left, from_right, d_out, cosine, sine,
    output, dots, *pres,
):
    length = mine.shape[1]
    proj = [
        mm(mine[0], weight[m])
        + mm(other[0], weight_other[m])
        + (from_left[m].astype(jnp.float32) + from_right[m].astype(jnp.float32))
        for m in range(3)
    ]
    cos, sin = cosine[...], sine[...]
    half = HEAD_DIM // 2

    def rotate(tensor, angle):
        return tensor * cos + pltpu.roll(tensor, half, 1) * angle

    query = rotate(proj[0], sin).astype(jnp.bfloat16)
    key_rows = rotate(proj[1], sin).astype(jnp.bfloat16)
    value = proj[2].astype(jnp.bfloat16)
    scores = mm_nt(query, key_rows) * (1.0 / math.sqrt(HEAD_DIM))
    causal = lax.broadcasted_iota(jnp.int32, (length, length), 0) >= lax.broadcasted_iota(
        jnp.int32, (length, length), 1
    )
    scores = jnp.where(causal, scores, jnp.float32(-1e30))
    powers = jnp.exp(scores - jnp.max(scores, axis=-1, keepdims=True))
    probs = powers * (1.0 / jnp.sum(powers, axis=-1, keepdims=True))
    probs_low = probs.astype(jnp.bfloat16)
    output[...] = mm(probs_low, value).astype(jnp.bfloat16)
    cotangent = d_out[...]
    d_value = mm_tn(probs_low, cotangent).astype(jnp.bfloat16)
    d_probs = mm_nt(cotangent, value).astype(jnp.bfloat16).astype(jnp.float32)
    inner = jnp.sum(d_probs * probs, axis=-1, keepdims=True)
    d_scores = (probs * (d_probs - inner) * (1.0 / math.sqrt(HEAD_DIM))).astype(jnp.bfloat16)
    d_query = mm(d_scores, key_rows).astype(jnp.bfloat16).astype(jnp.float32)
    d_key = mm_tn(d_scores, query).astype(jnp.bfloat16).astype(jnp.float32)
    pre_query = rotate(d_query, -sin).astype(jnp.bfloat16)
    pre_key = rotate(d_key, -sin).astype(jnp.bfloat16)
    rows = length // len(pres)
    for position, pre in enumerate(pres):
        span = slice(position * rows, (position + 1) * rows)
        pre[0] = pre_query[span]
        pre[1] = pre_key[span]
        pre[2] = d_value[span]
    product = (
        pre_query.astype(jnp.float32) * proj[0]
        + pre_key.astype(jnp.float32) * proj[1]
        + d_value.astype(jnp.float32) * proj[2]
    )

    @pl.when(pl.program_id(0) == 0)
    def _():
        dots[...] = product

    @pl.when(pl.program_id(0) > 0)
    def _():
        dots[...] += product


def attention(idx, size, mine, other, weights, from_left, from_right, d_out, tables, chunk, wide, parts):
    _, length, part = mine.shape
    heads = wide // HEAD_DIM
    first = chunk * heads
    block = pl.BlockSpec((1, length, part), lambda h, idx: (0, 0, 0))
    table = pl.BlockSpec((length, HEAD_DIM), lambda h, idx: (0, 0))
    stack = pl.BlockSpec((3, length, HEAD_DIM), lambda h, idx: (0, 0, h))
    return pl.pallas_call(
        attention_kernel,
        grid_spec=pltpu.PrefetchScalarGridSpec(
            num_scalar_prefetch=1,
            grid=(heads,),
            in_specs=[
                block,
                block,
                pl.BlockSpec((3, part, HEAD_DIM), lambda h, idx: (0, idx[size], first + h)),
                pl.BlockSpec((3, part, HEAD_DIM), lambda h, idx: (0, 1 - idx[size], first + h)),
                stack,
                stack,
                pl.BlockSpec((length, HEAD_DIM), lambda h, idx: (0, first + h)),
                table,
                table,
            ],
            out_specs=[
                pl.BlockSpec((length, HEAD_DIM), lambda h, idx: (0, h)),
                table,
                *[pl.BlockSpec((3, length // parts, HEAD_DIM), lambda h, idx: (0, 0, h))] * parts,
            ],
        ),
        out_shape=[
            jax.ShapeDtypeStruct((length, wide), jnp.bfloat16),
            jax.ShapeDtypeStruct((length, HEAD_DIM), jnp.float32),
            *[jax.ShapeDtypeStruct((3, length // parts, wide), jnp.bfloat16)] * parts,
        ],
        compiler_params=params(),
        cost_estimate=cost(12 * length * part * wide, 24 * part * wide),
        name="attention",
    )(idx, mine, other, weights, weights, from_left, from_right, d_out, *tables)


def grads_chunk(count, turned, pieces, start, before, add, chunk, wide, columns):
    depth, span = turned.shape
    in_specs = [pl.BlockSpec((depth, span), lambda m: (0, 0))]
    operands = [turned]
    for piece in pieces:
        in_specs.append(pl.BlockSpec((1, *piece.shape[1:]), lambda m: (m, 0, 0)))
        operands.append(piece)
    result = pl.BlockSpec((1, depth, wide), lambda m: (m, 0, chunk))
    aliases = {}
    if before is not None:
        aliases = {len(operands): 0}
        operands.append(before)
        in_specs.append(result if add else pl.BlockSpec(memory_space=pl.ANY))
    length = span // count
    rows = pieces[0].shape[1]

    def kernel(turned_ref, *refs):
        blocks = jnp.concatenate([piece[0] for piece in refs[: count + 1]], axis=0)
        left = [
            turned_ref[:, place * length + start : place * length + start + rows]
            for place in range(count)
        ]
        total = mm(jnp.concatenate(left, axis=1), blocks)
        refs[-1][0] = total + refs[-2][0] if add else total

    return pl.pallas_call(
        kernel,
        grid=(3,),
        in_specs=in_specs,
        out_specs=result,
        out_shape=jax.ShapeDtypeStruct((3, depth, columns), jnp.float32),
        input_output_aliases=aliases,
        compiler_params=params(),
        cost_estimate=cost(
            6 * count * rows * depth * wide, 6 * count * rows * wide + 12 * depth * wide
        ),
        name="grads",
    )(*operands)


def back(pieces, turned):
    wide, depth = turned.shape[1:]
    rows = [jnp.concatenate([piece[m] for m in range(3)], axis=1) for piece in pieces]
    return mm(jnp.concatenate(rows, axis=0), turned[...].reshape(3 * wide, depth))


def term_step(turned, pieces, befores, part, chunk, wide):
    depth = turned.shape[2]
    count = len(pieces)
    rows = pieces[0].shape[1]
    results = [pl.BlockSpec((rows, depth), lambda i: (0, 0))] * count
    takes = [
        pl.BlockSpec((rows, depth), lambda i, row=(part if before.shape[0] > rows else 0): (row, 0))
        for before in befores
    ]

    def kernel(turned_ref, *refs):
        total = back(refs[:count], turned_ref)
        for place in range(count):
            block = total[place * rows : (place + 1) * rows]
            if befores:
                block += refs[count + place][...]
            refs[len(refs) - count + place][...] = block

    return pl.pallas_call(
        kernel,
        grid=(1,),
        in_specs=[
            pl.BlockSpec((3, wide, depth), lambda i: (0, chunk, 0)),
            *[pl.BlockSpec(piece.shape, lambda i: (0, 0, 0)) for piece in pieces],
            *takes,
        ],
        out_specs=results,
        out_shape=[jax.ShapeDtypeStruct((rows, depth), jnp.float32)] * count,
        compiler_params=params(),
        cost_estimate=cost(6 * count * rows * depth * wide, 12 * count * rows * wide),
        name="term_step",
    )(turned, *pieces, *befores)


def term_last_kernel(count, idx, turned, before, far_r, far_l, *refs):
    nears, keep, send = refs[:-2], refs[-2], refs[-1]
    last = back([far_r, far_l], turned) + before[...]
    for place in range(count):
        total = nears[place][...] if place < count - 1 else last

        @pl.when(idx[2 * count + 1 + place] == 0)
        def _():
            keep[idx[3 * count + 1 + place]] = total

        @pl.when(idx[2 * count + 1 + place] == 1)
        def _():
            send[idx[3 * count + 1 + place]] = total.astype(jnp.bfloat16)


def term_last(idx, turned, before, pieces, nears, chunk, wide, ties):
    count = len(nears) + 1
    rows, depth = before.shape
    result = pl.BlockSpec((count // 2, rows, depth), lambda i, idx: (0, 0, 0))
    block = pl.BlockSpec((rows, depth), lambda i, idx: (0, 0))
    return pl.pallas_call(
        tied(functools.partial(term_last_kernel, count), count + 4, len(ties)),
        grid_spec=pltpu.PrefetchScalarGridSpec(
            num_scalar_prefetch=1,
            grid=(1,),
            in_specs=[
                pl.BlockSpec((3, wide, depth), lambda i, idx: (0, chunk, 0)),
                block,
                *[pl.BlockSpec(piece.shape, lambda i, idx: (0, 0, 0)) for piece in pieces],
                *[block] * (count - 1),
                *tie_specs(ties),
            ],
            out_specs=[result, result],
        ),
        out_shape=[
            jax.ShapeDtypeStruct((count // 2, rows, depth), jnp.float32),
            jax.ShapeDtypeStruct((count // 2, rows, depth), jnp.bfloat16),
        ],
        compiler_params=params(),
        cost_estimate=cost(6 * rows * depth * wide, 12 * count * rows * depth),
        name="term_last",
    )(idx, turned, before, *pieces, *nears, *ties)


def local(tokens, norm_gain, w_quant, w_scale, d_out):
    length, width = tokens.shape
    depth, columns = w_quant.shape[1:]
    size, nodes = lax.axis_size("local"), lax.axis_size("node")
    here, node = lax.axis_index("local"), lax.axis_index("node")
    wide = columns // 2
    far = size // 2
    group = size // nodes
    core = node % 2

    order = ring_order(size)
    distances = ring_distances(size)
    table = jnp.asarray(index_table(size, nodes))
    idx = lax.dynamic_index_in_dim(table, node * size + here, 0, keepdims=False)

    def shift(array, distance):
        moves = [(order[i], order[(i + distance) % size]) for i in range(size)]
        return lax.ppermute(array, "local", moves)

    def swap(array, bit):
        return lax.ppermute(array, "node", [(n, n ^ bit) for n in range(nodes)])

    blocks, inverse_rms = normed_blocks(idx, tokens, norm_gain[None], size, depth // 2)
    mine_far = shift(blocks[far], far)
    other_far = swap(mine_far, 1)
    weights, turned = scaled_weights(w_quant, w_scale)
    firsts = sum_first(idx, size, mine_far, other_far, weights)
    mine = stack(
        [shift(blocks[-d % size], -d) if d else blocks[0] for d in distances[:-1]], firsts[:1]
    )
    other = swap(mine, 1)

    rows_turned = turn(idx, mine, other, mine_far, other_far)

    tables = rope_tables(length, HEAD_DIM)
    arrived = []
    for chunk in range(2):
        right, left = firsts[2 * chunk : 2 * chunk + 2]
        for distance in range(far - 1, -1, -1):
            from_left, from_right = shift(right, 1), shift(left, -1)
            if distance:
                places = distances.index(distance), distances.index(-distance)
                ties = [rows_turned] if distance == 1 else []
                right, left = sum_step(
                    idx, size, mine, other, places, weights, from_left, from_right, chunk, wide, ties
                )
        arrived.append((from_left, from_right))

    outputs, sets, dots = [], [], 0.0
    for chunk in range(2):
        output, product, *parts = attention(
            idx, size, mine, other, weights, *arrived[chunk], d_out, tables, chunk, wide, chunk + 1
        )
        outputs.append(output)
        sets += parts
        dots += jnp.sum(product, axis=-1, keepdims=True)
    bit = 1
    while bit < nodes:
        dots = dots + swap(dots, bit)
        bit *= 2

    half = length // 2
    gathered = [[block] for block in sets]
    moving = [(block, block) for block in sets]
    schedule = [(0, 1)]
    for step in range(2, far):
        schedule += [(0, step), (1, step - 1)]
    schedule += [(2, 1), (0, far), (1, far - 1), (1, far)]
    schedule += [(2, step) for step in range(2, far + 1)]

    share = width // nodes
    values_part = lax.dynamic_slice_in_dim(tokens, node * share, share, 1).astype(jnp.float32)
    gains_part = lax.dynamic_slice_in_dim(norm_gain, node * share, share, 0).astype(jnp.float32)
    inverse_rms = inverse_rms[:, :1]

    def start_term(part, ties):
        keep, send = term_last(
            idx, turned, lasts[part], gathered[1 + part][-2:], terms[1 + part], 1, wide, ties
        )
        return keep + swap(send, 1).astype(jnp.float32)

    def sum_nodes(summed):
        bit = 2
        while bit < nodes:
            pair = summed.reshape(-1, 2, group, *summed.shape[1:])
            own = (node // bit) % 2
            keep = lax.dynamic_index_in_dim(pair, own, 1, keepdims=False)
            send = lax.dynamic_index_in_dim(pair, 1 - own, 1, keepdims=False)
            summed = keep + swap(send.astype(jnp.bfloat16), bit).astype(jnp.float32)
            summed = summed.reshape(-1, *pair.shape[3:])
            bit *= 2
        return summed.astype(jnp.bfloat16)

    def relocate(summed):
        came = []
        for turn in range(group):
            block = lax.dynamic_index_in_dim(summed, (here + turn) % group, 0, keepdims=False)
            moves = [
                (n * size + s, (s // group) * size + n * group + (s + turn) % group)
                for n in range(nodes)
                for s in range(size)
            ]
            came.append(lax.ppermute(block, ("node", "local"), moves))
        return came

    def end_term(came, part):
        came = jnp.stack(came)
        upstream = jnp.concatenate(
            [
                lax.dynamic_index_in_dim(came, (here + group - i) % group, 0, keepdims=False)
                for i in range(group)
            ],
            axis=-1,
        ).astype(jnp.float32)
        rows = slice(part * half, (part + 1) * half)
        d_rows = (
            inverse_rms[rows] * gains_part * upstream
            - values_part[rows] * inverse_rms[rows] ** 2 * dots[rows] / width
        )
        return d_rows.astype(jnp.bfloat16)

    terms = [[], [], []]
    early = summed = None
    for ring, step in schedule:
        right, left = moving[ring]
        if step == far:
            ties = [[], [dots, *moving[2]], [summed]][ring]
            right, left = pass_on(right, left, True, ties)
        elif (ring, step) == (2, far - 1):
            right, left = pass_on(right, left, False, [early, first_grads])
        right, left = shift(right, 1), shift(left, -1)
        moving[ring] = right, left
        gathered[ring] += [right, left]
        chunk, part = min(ring, 1), max(ring - 1, 0)
        if step < far:
            pieces = gathered[ring] if step == 1 else [right, left]
            known = len(terms[ring])
            befores = terms[0][known : known + len(pieces)] if ring else []
            terms[ring] += term_step(turned, pieces, befores, part, chunk, wide)
        elif ring == 0:
            lasts = term_step(turned, [right, left], [], 0, 0, wide)
            first_grads = grads_chunk(
                size, rows_turned, gathered[0], 0, None, False, 0, wide, columns
            )
        elif ring == 1:
            early = start_term(0, [])
            half_grads = grads_chunk(
                size, rows_turned, gathered[1], 0, first_grads, False, 1, wide, columns
            )
            summed = sum_nodes(early)
    came = relocate(summed)
    late = start_term(1, came)
    d_tokens = jnp.concatenate([end_term(came, 0), end_term(relocate(sum_nodes(late)), 1)], axis=0)
    grads = grads_chunk(size, rows_turned, gathered[2], half, half_grads, True, 1, wide, columns)
    return (jnp.concatenate(outputs, axis=-1), d_tokens, grads)


def solution(mesh):
    placed = (
        P("local", None),
        P(),
        P(None, "local", "node"),
        P(None, "local", "node"),
        P("local", "node"),
    )
    return jax.shard_map(
        local,
        mesh=mesh,
        in_specs=placed,
        out_specs=(P("local", "node"), P("local", "node"), P(None, "local", "node")),
        check_vma=False,
    )
```

```python
import functools
import math

import jax
import jax.numpy as jnp
import numpy as np
from jax import lax
from jax.experimental import pallas as pl
from jax.experimental.pallas import tpu as pltpu
from jax.sharding import PartitionSpec as P

HEAD_DIM = 128
NORM_EPS = 1e-05
MIB = 1024 * 1024


def params(limit):
    return pltpu.CompilerParams(
        dimension_semantics=("arbitrary",), vmem_limit_bytes=limit * MIB
    )


def tied(kernel, inputs, ties):
    def inner(*refs):
        kernel(*refs[:inputs], *refs[inputs + ties :])

    return inner


def tie_specs(ties):
    return [pl.BlockSpec(memory_space=pl.ANY)] * len(ties)


def cost(flops, moved):
    return pl.CostEstimate(flops=flops, bytes_accessed=moved, transcendentals=0)


def mm(a, b):
    return jnp.dot(a, b, preferred_element_type=jnp.float32)


def mm_nt(a, b):
    return lax.dot_general(a, b, (((1,), (1,)), ((), ())), preferred_element_type=jnp.float32)


def mm_tn(a, b):
    return lax.dot_general(a, b, (((0,), (0,)), ((), ())), preferred_element_type=jnp.float32)


def rope_tables(length, width):
    position = jnp.arange(length).astype(jnp.float32)[:, None]
    frequency = jnp.exp(
        jnp.arange(width // 2).astype(jnp.float32) * (-2.0 * math.log(10000.0) / width)
    )
    angle = position * frequency[None, :]
    cosine, sine = jnp.cos(angle), jnp.sin(angle)
    return (
        jnp.concatenate([cosine, cosine], axis=-1),
        jnp.concatenate([-sine, sine], axis=-1),
    )


def ring_order(size):
    return [*range(0, size, 2), *reversed(range(1, size, 2))]


def ring_distances(size):
    far = size // 2
    distances = [0]
    for step in range(1, far):
        distances += [-step, step]
    return [*distances, far]


def index_table(size, nodes):
    order, group = ring_order(size), size // nodes
    rows = []
    for node in range(nodes):
        for here in range(size):
            place = order.index(here)
            seqs = [order[(place + distance) % size] for distance in ring_distances(size)]
            owner = [seq // group for seq in seqs]
            rows.append(
                [order[(place + distance) % size] for distance in range(size)]
                + [node % 2]
                + seqs
                + [owner_ % 2 ^ node % 2 for owner_ in owner]
                + [(o // 2) * group + seq % group for o, seq in zip(owner, seqs)]
                + [node >> level & 1 for level in range(1, nodes.bit_length() - 1)]
                + [(here + turn) % group for turn in range(group)]
            )
    return np.array(rows, np.int32)


def weights_kernel(quant, scale, out, turned):
    blocks = scale.shape[1]
    rows = quant.shape[1] // blocks
    scales = scale[0].astype(jnp.float32)
    for block in range(blocks):
        span = slice(block * rows, (block + 1) * rows)
        scaled = (quant[0, span].astype(jnp.float32) * scales[block : block + 1]).astype(jnp.bfloat16)
        out[0, span] = scaled
        turned[0, :, span] = scaled.T


def scaled_weights(w_quant, w_scale):
    _, depth, columns = w_quant.shape
    blocks = w_scale.shape[1]
    return pl.pallas_call(
        weights_kernel,
        grid=(3,),
        in_specs=[
            pl.BlockSpec((1, depth, columns), lambda m: (m, 0, 0)),
            pl.BlockSpec((1, blocks, columns), lambda m: (m, 0, 0)),
        ],
        out_specs=[
            pl.BlockSpec((1, depth, columns), lambda m: (m, 0, 0)),
            pl.BlockSpec((1, columns, depth), lambda m: (m, 0, 0)),
        ],
        out_shape=[
            jax.ShapeDtypeStruct((3, depth, columns), jnp.bfloat16),
            jax.ShapeDtypeStruct((3, columns, depth), jnp.bfloat16),
        ],
        compiler_params=params(20),
        cost_estimate=cost(3 * depth * columns, 18 * depth * columns),
        name="scaled_weights",
    )(w_quant, w_scale)


def normed_kernel(idx, tokens, gain, *refs):
    outs, gains = refs[:-1], refs[-1]
    width, part = tokens.shape[1], outs[0].shape[1]
    gains[...] = gain[...].astype(jnp.float32)
    values = tokens[...].astype(jnp.float32)
    inverse = lax.rsqrt(jnp.mean(values * values, axis=-1, keepdims=True) + NORM_EPS)
    size = len(outs) - 1
    for distance in range(size):
        start = pl.multiple_of(idx[distance] * (width // size) + idx[size] * part, part)
        block = tokens[:, pl.ds(start, part)].astype(jnp.float32)
        scale = gains[:, pl.ds(start, part)]
        outs[distance][...] = (block * inverse * scale).astype(jnp.bfloat16)
    outs[size][...] = jnp.broadcast_to(inverse, outs[size].shape)


def normed_blocks(idx, tokens, gain, size, part):
    length, width = tokens.shape
    tile = length // 4
    block = pl.BlockSpec((tile, part), lambda i, idx: (i, 0))
    *blocks, inverse = pl.pallas_call(
        normed_kernel,
        grid_spec=pltpu.PrefetchScalarGridSpec(
            num_scalar_prefetch=1,
            grid=(4,),
            in_specs=[
                pl.BlockSpec((tile, width), lambda i, idx: (i, 0)),
                pl.BlockSpec((1, width), lambda i, idx: (0, 0)),
            ],
            out_specs=[block] * size + [pl.BlockSpec((tile, 128), lambda i, idx: (i, 0))],
            scratch_shapes=[pltpu.VMEM((1, width), jnp.float32)],
        ),
        out_shape=[jax.ShapeDtypeStruct((length, part), jnp.bfloat16)] * size
        + [jax.ShapeDtypeStruct((length, 128), jnp.float32)],
        compiler_params=params(12),
        cost_estimate=cost(8 * length * width, 4 * length * width),
        name="normed_blocks",
    )(idx, tokens, gain)
    return blocks, inverse


def stack_kernel(*refs):
    for place, block in enumerate(refs[:-1]):
        refs[-1][place] = block[...]


def stack(blocks, ties):
    count, shape = len(blocks), blocks[0].shape
    block = pl.BlockSpec(shape, lambda i: (0, 0))
    return pl.pallas_call(
        tied(stack_kernel, count, len(ties)),
        grid=(1,),
        in_specs=[block] * count + tie_specs(ties),
        out_specs=pl.BlockSpec((count, *shape), lambda i: (0, 0, 0)),
        out_shape=jax.ShapeDtypeStruct((count, *shape), blocks[0].dtype),
        compiler_params=params(10),
        cost_estimate=cost(0, 4 * count * shape[0] * shape[1]),
        name="stack",
    )(*blocks, *ties)


def halve_kernel(right, left, right_out, left_out):
    half = right_out.shape[1]
    right_out[...] = right[:, :half]
    left_out[...] = left[:, half:]


def halve(right, left, ties):
    _, rows, wide = right.shape
    result = jax.ShapeDtypeStruct((3, rows // 2, wide), right.dtype)
    whole = pl.BlockSpec(memory_space=pltpu.VMEM)
    return pl.pallas_call(
        tied(halve_kernel, 2, len(ties)),
        in_specs=[whole, whole] + tie_specs(ties),
        out_specs=[whole, whole],
        out_shape=[result, result],
        compiler_params=pltpu.CompilerParams(vmem_limit_bytes=4 * MIB),
        cost_estimate=cost(0, 6 * rows * wide),
        name="halve",
    )(right, left, *ties)


def turn_kernel(count, idx, mine, other, mine_far, other_far, out):
    length, part = mine_far.shape
    for side, near, last in ((0, mine, mine_far), (1, other, other_far)):
        half = idx[count] * (1 - side) + (1 - idx[count]) * side
        rows = pl.ds(pl.multiple_of(half * part, part), part)
        for place in range(count):
            block = near[place] if place < count - 1 else last[...]
            out[rows, place * length : (place + 1) * length] = block.T


def turn(idx, mine, other, mine_far, other_far):
    near, length, part = mine.shape
    count = near + 1
    stack = pl.BlockSpec(mine.shape, lambda i, idx: (0, 0, 0))
    last = pl.BlockSpec((length, part), lambda i, idx: (0, 0))
    shape = (2 * part, count * length)
    return pl.pallas_call(
        functools.partial(turn_kernel, count),
        grid_spec=pltpu.PrefetchScalarGridSpec(
            num_scalar_prefetch=1,
            grid=(1,),
            in_specs=[stack, stack, last, last],
            out_specs=pl.BlockSpec(shape, lambda i, idx: (0, 0)),
        ),
        out_shape=jax.ShapeDtypeStruct(shape, jnp.bfloat16),
        compiler_params=params(12),
        cost_estimate=cost(2 * count * length * part, 8 * count * length * part),
        name="turn",
    )(idx, mine, other, mine_far, other_far)


def sum_first_kernel(idx, mine, other, weight, weight_other, *outs):
    half, wide = outs[0].shape[1:]
    for chunk in range(2):
        span = slice(chunk * wide, (chunk + 1) * wide)
        product = mm(mine[...], weight[0, :, span]) + mm(other[...], weight_other[0, :, span])
        outs[2 * chunk][0] = product[:half].astype(jnp.bfloat16)
        outs[2 * chunk + 1][0] = product[half:].astype(jnp.bfloat16)


def sum_step_kernel(
    idx, mine_r, other_r, mine_l, other_l, weight, weight_other, from_left, from_right, right, left
):
    length, part = right.shape[1], from_left.shape[1]
    product = mm(mine_r[0], weight[0]) + mm(other_r[0], weight_other[0])
    right[0, :part] = (product[:part] + from_left[0].astype(jnp.float32)).astype(jnp.bfloat16)
    if part < length:
        right[0, part:] = product[part:].astype(jnp.bfloat16)
    product = mm(mine_l[0], weight[0]) + mm(other_l[0], weight_other[0])
    rest = length - part
    left[0, rest:] = (product[rest:] + from_right[0].astype(jnp.float32)).astype(jnp.bfloat16)
    if rest:
        left[0, :rest] = product[:rest].astype(jnp.bfloat16)


def weight_halves(size, part, wide, chunk):
    return [
        pl.BlockSpec((1, part, wide), lambda m, idx: (m, idx[size], chunk)),
        pl.BlockSpec((1, part, wide), lambda m, idx: (m, 1 - idx[size], chunk)),
    ]


def sum_first(idx, size, mine, other, weights):
    length, part = mine.shape
    columns = weights.shape[2]
    half, wide = length // 2, columns // 2
    block = pl.BlockSpec((length, part), lambda m, idx: (0, 0))
    result = jax.ShapeDtypeStruct((3, half, wide), jnp.bfloat16)
    return pl.pallas_call(
        sum_first_kernel,
        grid_spec=pltpu.PrefetchScalarGridSpec(
            num_scalar_prefetch=1,
            grid=(3,),
            in_specs=[block, block, *weight_halves(size, part, columns, 0)],
            out_specs=[pl.BlockSpec((1, half, wide), lambda m, idx: (m, 0, 0))] * 4,
        ),
        out_shape=[result] * 4,
        compiler_params=params(12),
        cost_estimate=cost(12 * length * part * columns, 16 * part * columns),
        name="sum_first",
    )(idx, mine, other, weights, weights)


def sum_step(idx, size, mine, other, places, weights, from_left, from_right, chunk, wide, ties):
    _, length, part = mine.shape
    block_r = pl.BlockSpec((1, length, part), lambda m, idx: (places[0], 0, 0))
    block_l = pl.BlockSpec((1, length, part), lambda m, idx: (places[1], 0, 0))
    came = pl.BlockSpec((1, from_left.shape[1], wide), lambda m, idx: (m, 0, 0))
    whole = jax.ShapeDtypeStruct((3, length, wide), jnp.bfloat16)
    return pl.pallas_call(
        tied(sum_step_kernel, 9, len(ties)),
        grid_spec=pltpu.PrefetchScalarGridSpec(
            num_scalar_prefetch=1,
            grid=(3,),
            in_specs=[
                block_r,
                block_r,
                block_l,
                block_l,
                *weight_halves(size, part, wide, chunk),
                came,
                came,
                *tie_specs(ties),
            ],
            out_specs=[pl.BlockSpec((1, length, wide), lambda m, idx: (m, 0, 0))] * 2,
        ),
        out_shape=[whole, whole],
        compiler_params=params(12),
        cost_estimate=cost(24 * length * part * wide, 24 * part * wide),
        name="sum_step",
    )(idx, mine, other, mine, other, weights, weights, from_left, from_right, *ties)


def attention_kernel(
    idx, mine, other, weight, weight_other, from_left, from_right, d_out, cosine, sine,
    output, dots, pre,
):
    length = mine.shape[1]
    proj = [
        mm(mine[0], weight[m])
        + mm(other[0], weight_other[m])
        + (from_left[m].astype(jnp.float32) + from_right[m].astype(jnp.float32))
        for m in range(3)
    ]
    cos, sin = cosine[...], sine[...]
    half = HEAD_DIM // 2

    def rotate(tensor, angle):
        return tensor * cos + pltpu.roll(tensor, half, 1) * angle

    query = rotate(proj[0], sin).astype(jnp.bfloat16)
    key_rows = rotate(proj[1], sin).astype(jnp.bfloat16)
    value = proj[2].astype(jnp.bfloat16)
    scores = mm_nt(query, key_rows) * (1.0 / math.sqrt(HEAD_DIM))
    causal = lax.broadcasted_iota(jnp.int32, (length, length), 0) >= lax.broadcasted_iota(
        jnp.int32, (length, length), 1
    )
    scores = jnp.where(causal, scores, jnp.float32(-1e30))
    powers = jnp.exp(scores - jnp.max(scores, axis=-1, keepdims=True))
    probs = powers * (1.0 / jnp.sum(powers, axis=-1, keepdims=True))
    probs_low = probs.astype(jnp.bfloat16)
    output[...] = mm(probs_low, value).astype(jnp.bfloat16)
    cotangent = d_out[...]
    d_value = mm_tn(probs_low, cotangent).astype(jnp.bfloat16)
    d_probs = mm_nt(cotangent, value).astype(jnp.bfloat16).astype(jnp.float32)
    inner = jnp.sum(d_probs * probs, axis=-1, keepdims=True)
    d_scores = (probs * (d_probs - inner) * (1.0 / math.sqrt(HEAD_DIM))).astype(jnp.bfloat16)
    d_query = mm(d_scores, key_rows).astype(jnp.bfloat16).astype(jnp.float32)
    d_key = mm_tn(d_scores, query).astype(jnp.bfloat16).astype(jnp.float32)
    pre_query = rotate(d_query, -sin).astype(jnp.bfloat16)
    pre_key = rotate(d_key, -sin).astype(jnp.bfloat16)
    pre[0] = pre_query
    pre[1] = pre_key
    pre[2] = d_value
    product = (
        pre_query.astype(jnp.float32) * proj[0]
        + pre_key.astype(jnp.float32) * proj[1]
        + d_value.astype(jnp.float32) * proj[2]
    )

    @pl.when(pl.program_id(0) == 0)
    def _():
        dots[...] = product

    @pl.when(pl.program_id(0) > 0)
    def _():
        dots[...] += product


def attention(idx, size, mine, other, weights, from_left, from_right, d_out, tables, chunk, wide):
    _, length, part = mine.shape
    heads = wide // HEAD_DIM
    first = chunk * heads
    block = pl.BlockSpec((1, length, part), lambda h, idx: (0, 0, 0))
    table = pl.BlockSpec((length, HEAD_DIM), lambda h, idx: (0, 0))
    stack = pl.BlockSpec((3, length, HEAD_DIM), lambda h, idx: (0, 0, h))
    return pl.pallas_call(
        attention_kernel,
        grid_spec=pltpu.PrefetchScalarGridSpec(
            num_scalar_prefetch=1,
            grid=(heads,),
            in_specs=[
                block,
                block,
                pl.BlockSpec((3, part, HEAD_DIM), lambda h, idx: (0, idx[size], first + h)),
                pl.BlockSpec((3, part, HEAD_DIM), lambda h, idx: (0, 1 - idx[size], first + h)),
                stack,
                stack,
                pl.BlockSpec((length, HEAD_DIM), lambda h, idx: (0, first + h)),
                table,
                table,
            ],
            out_specs=[
                pl.BlockSpec((length, HEAD_DIM), lambda h, idx: (0, h)),
                table,
                stack,
            ],
        ),
        out_shape=[
            jax.ShapeDtypeStruct((length, wide), jnp.bfloat16),
            jax.ShapeDtypeStruct((length, HEAD_DIM), jnp.float32),
            jax.ShapeDtypeStruct((3, length, wide), jnp.bfloat16),
        ],
        compiler_params=params(16),
        cost_estimate=cost(12 * length * part * wide, 24 * part * wide),
        name="attention",
    )(idx, mine, other, weights, weights, from_left, from_right, d_out, *tables)


def grads_kernel(turned, *refs):
    blocks = jnp.concatenate([piece[0] for piece in refs[:-1]], axis=0)
    refs[-1][0] = mm(turned[...], blocks)


def grads_chunk(turned, pieces, before, chunk, wide, columns):
    depth, span = turned.shape
    ties = [] if before is None else [before]
    return pl.pallas_call(
        tied(grads_kernel, 1 + len(pieces), len(ties)),
        grid=(3,),
        in_specs=[
            pl.BlockSpec((depth, span), lambda m: (0, 0)),
            *[pl.BlockSpec((1, *piece.shape[1:]), lambda m: (m, 0, 0)) for piece in pieces],
            *tie_specs(ties),
        ],
        out_specs=pl.BlockSpec((1, depth, wide), lambda m: (m, 0, chunk)),
        out_shape=jax.ShapeDtypeStruct((3, depth, columns), jnp.float32),
        input_output_aliases={1 + len(pieces): 0} if ties else {},
        compiler_params=params(24),
        cost_estimate=cost(6 * span * depth * wide, 6 * span * wide + 12 * depth * wide),
        name="grads",
    )(turned, *pieces, *ties)


def back(pieces, turned, chunk):
    wide = pieces[0].shape[2]
    rows = [jnp.concatenate([piece[m] for m in range(3)], axis=1) for piece in pieces]
    weight = [turned[m, chunk * wide : (chunk + 1) * wide] for m in range(3)]
    return mm(jnp.concatenate(rows, axis=0), jnp.concatenate(weight, axis=0))


def term_step(turned, pieces, befores, chunk):
    depth, wide = turned.shape[2], pieces[0].shape[2]
    count, rows = len(pieces), pieces[0].shape[1]
    whole = pl.BlockSpec(memory_space=pltpu.VMEM)

    def kernel(turned_ref, *refs):
        total = back(refs[:count], turned_ref, chunk)
        for place in range(count):
            block = total[place * rows : (place + 1) * rows]
            if befores:
                block += refs[count + place][...]
            refs[len(refs) - count + place][...] = block

    return pl.pallas_call(
        kernel,
        in_specs=[whole] * (1 + count + len(befores)),
        out_specs=[whole] * count,
        out_shape=[jax.ShapeDtypeStruct((rows, depth), jnp.float32)] * count,
        compiler_params=pltpu.CompilerParams(vmem_limit_bytes=16 * MIB),
        cost_estimate=cost(6 * count * rows * depth * wide, 12 * count * rows * wide),
        name="term_step",
    )(turned, *pieces, *befores)


def term_last_kernel(count, idx, turned, *refs):
    befores, fars, nears = refs[:2], refs[2:4], refs[4 : 3 + count]
    keeps, sends = refs[-4:-2], refs[-2:]
    half = keeps[0].shape[1]
    last = back(fars, turned, 1)
    for place in range(count):
        for part in range(2):
            span = slice(part * half, (part + 1) * half)
            total = nears[place][span] if place < count - 1 else last[span] + befores[part][...]

            @pl.when(idx[2 * count + 1 + place] == 0)
            def _():
                keeps[part][idx[3 * count + 1 + place]] = total

            @pl.when(idx[2 * count + 1 + place] == 1)
            def _():
                sends[part][idx[3 * count + 1 + place]] = total.astype(jnp.bfloat16)


def term_last(idx, turned, befores, pieces, nears):
    count = len(nears) + 1
    rows, depth = nears[0].shape
    whole = pl.BlockSpec(memory_space=pltpu.VMEM)
    shape = (count // 2, rows // 2, depth)
    return pl.pallas_call(
        functools.partial(term_last_kernel, count),
        in_specs=[pl.BlockSpec(memory_space=pltpu.SMEM)] + [whole] * (count + 4),
        out_specs=[whole] * 4,
        out_shape=[jax.ShapeDtypeStruct(shape, jnp.float32)] * 2
        + [jax.ShapeDtypeStruct(shape, jnp.bfloat16)] * 2,
        compiler_params=pltpu.CompilerParams(vmem_limit_bytes=12 * MIB),
        cost_estimate=cost(rows * depth * depth, 12 * count * rows * depth),
        name="term_last",
    )(idx, turned, *befores, *pieces, *nears)


def split_kernel(column, group, idx, keep, came, keep_out, send_out):
    own = idx[column]
    for block in range(keep_out.shape[0]):
        high, low = block // group, block % group
        mine = (2 * high + own) * group + low
        other = (2 * high + 1 - own) * group + low
        keep_out[block] = keep[mine] + came[mine].astype(jnp.float32)
        send_out[block] = (keep[other] + came[other].astype(jnp.float32)).astype(jnp.bfloat16)


def split_sum(idx, column, group, keep, came):
    whole = pl.BlockSpec(memory_space=pltpu.VMEM)
    shape = (keep.shape[0] // 2, *keep.shape[1:])
    return pl.pallas_call(
        functools.partial(split_kernel, column, group),
        in_specs=[pl.BlockSpec(memory_space=pltpu.SMEM), whole, whole],
        out_specs=[whole, whole],
        out_shape=[
            jax.ShapeDtypeStruct(shape, jnp.float32),
            jax.ShapeDtypeStruct(shape, jnp.bfloat16),
        ],
        compiler_params=pltpu.CompilerParams(vmem_limit_bytes=4 * MIB),
        cost_estimate=cost(0, 8 * keep.shape[0] * keep.shape[1] * keep.shape[2]),
        name="split_sum",
    )(idx, keep, came)


def order_kernel(column, idx, keep, came, *outs):
    for turn, out in enumerate(outs):
        block = idx[column + turn]
        out[...] = (keep[block] + came[block].astype(jnp.float32)).astype(jnp.bfloat16)


def order_sum(idx, column, keep, came):
    whole = pl.BlockSpec(memory_space=pltpu.VMEM)
    count = keep.shape[0]
    return pl.pallas_call(
        functools.partial(order_kernel, column),
        in_specs=[pl.BlockSpec(memory_space=pltpu.SMEM), whole, whole],
        out_specs=[whole] * count,
        out_shape=[jax.ShapeDtypeStruct(keep.shape[1:], jnp.bfloat16)] * count,
        compiler_params=pltpu.CompilerParams(vmem_limit_bytes=4 * MIB),
        cost_estimate=cost(0, 8 * count * keep.shape[1] * keep.shape[2]),
        name="order_sum",
    )(idx, keep, came)


def local(tokens, norm_gain, w_quant, w_scale, d_out):
    length, width = tokens.shape
    depth, columns = w_quant.shape[1:]
    size, nodes = lax.axis_size("local"), lax.axis_size("node")
    here, node = lax.axis_index("local"), lax.axis_index("node")
    wide = columns // 2
    far = size // 2
    group = size // nodes
    core = node % 2

    order = ring_order(size)
    distances = ring_distances(size)
    table = jnp.asarray(index_table(size, nodes))
    idx = lax.dynamic_index_in_dim(table, node * size + here, 0, keepdims=False)

    def shift(array, distance):
        moves = [(order[i], order[(i + distance) % size]) for i in range(size)]
        return lax.ppermute(array, "local", moves)

    def swap(array, bit):
        return lax.ppermute(array, "node", [(n, n ^ bit) for n in range(nodes)])

    blocks, inverse_rms = normed_blocks(idx, tokens, norm_gain[None], size, depth // 2)
    mine_far = shift(blocks[far], far)
    other_far = swap(mine_far, 1)
    weights, turned = scaled_weights(w_quant, w_scale)
    firsts = sum_first(idx, size, mine_far, other_far, weights)
    mine = stack(
        [shift(blocks[-d % size], -d) if d else blocks[0] for d in distances[:-1]], firsts[:1]
    )
    other = swap(mine, 1)

    rows_turned = turn(idx, mine, other, mine_far, other_far)

    tables = rope_tables(length, HEAD_DIM)
    arrived = []
    for chunk in range(2):
        right, left = firsts[2 * chunk : 2 * chunk + 2]
        for distance in range(far - 1, -1, -1):
            from_left, from_right = shift(right, 1), shift(left, -1)
            if distance:
                places = distances.index(distance), distances.index(-distance)
                ties = [rows_turned] if distance == 1 else []
                right, left = sum_step(
                    idx, size, mine, other, places, weights, from_left, from_right, chunk, wide, ties
                )
        arrived.append((from_left, from_right))

    outputs, sets, dots = [], [], 0.0
    for chunk in range(2):
        output, product, pre = attention(
            idx, size, mine, other, weights, *arrived[chunk], d_out, tables, chunk, wide
        )
        outputs.append(output)
        sets.append(pre)
        dots += jnp.sum(product, axis=-1, keepdims=True)
    bit = 1
    while bit < nodes:
        dots = dots + swap(dots, bit)
        bit *= 2

    half = length // 2
    share = width // nodes
    values_part = lax.dynamic_slice_in_dim(tokens, node * share, share, 1).astype(jnp.float32)
    gains_part = lax.dynamic_slice_in_dim(norm_gain, node * share, share, 0).astype(jnp.float32)
    inverse_rms = inverse_rms[:, :1]

    def to_place(keep, send):
        column = 4 * size + 1
        bit = 1
        while 2 * bit < nodes:
            keep, send = split_sum(idx, column, group, keep, swap(send, bit))
            column += 1
            bit *= 2
        came = []
        for turn, block in enumerate(order_sum(idx, column, keep, swap(send, bit))):
            moves = [
                (n * size + s, (s // group) * size + n * group + (s + turn) % group)
                for n in range(nodes)
                for s in range(size)
            ]
            came.append(lax.ppermute(block, ("node", "local"), moves))
        return came

    def end_term(came, part):
        came = jnp.stack(came)
        upstream = jnp.concatenate(
            [
                lax.dynamic_index_in_dim(came, (here + group - i) % group, 0, keepdims=False)
                for i in range(group)
            ],
            axis=-1,
        ).astype(jnp.float32)
        rows = slice(part * half, (part + 1) * half)
        d_rows = (
            inverse_rms[rows] * gains_part * upstream
            - values_part[rows] * inverse_rms[rows] ** 2 * dots[rows] / width
        )
        return d_rows.astype(jnp.bfloat16)

    gathered = [[block] for block in sets]
    moving = [(block, block) for block in sets]
    terms = [[], []]
    for step in range(1, far + 1):
        for chunk in range(2):
            right, left = moving[chunk]
            if step == far:
                early = [dots] if chunk == 0 else terms[1][: size - 3]
                right, left = halve(right, left, early)
            right, left = shift(right, 1), shift(left, -1)
            moving[chunk] = right, left
            gathered[chunk] += [right, left]
            if step < far:
                pieces = gathered[chunk] if step == 1 else [right, left]
                known = len(terms[chunk])
                befores = terms[0][known : known + len(pieces)] if chunk else []
                terms[chunk] += term_step(turned, pieces, befores, chunk)
            elif chunk == 0:
                lasts = term_step(turned, [right, left], [], 0)
    keep_0, keep_1, send_0, send_1 = term_last(idx, turned, lasts, gathered[1][-2:], terms[1])
    first, second = to_place(keep_0, send_0), to_place(keep_1, send_1)
    d_tokens = jnp.concatenate([end_term(first, 0), end_term(second, 1)], axis=0)
    grads = grads_chunk(rows_turned, gathered[0], None, 0, wide, columns)
    grads = grads_chunk(rows_turned, gathered[1], grads, 1, wide, columns)
    return (jnp.concatenate(outputs, axis=-1), d_tokens, grads)


def solution(mesh):
    placed = (
        P("local", None),
        P(),
        P(None, "local", "node"),
        P(None, "local", "node"),
        P("local", "node"),
    )
    return jax.shard_map(
        local,
        mesh=mesh,
        in_specs=placed,
        out_specs=(P("local", "node"), P("local", "node"), P(None, "local", "node")),
        check_vma=False,
    )
```

```python
import functools
import math

import jax
import jax.numpy as jnp
import numpy as np
from jax import lax
from jax.experimental import pallas as pl
from jax.experimental.pallas import tpu as pltpu
from jax.sharding import PartitionSpec as P

HEAD_DIM = 128
NORM_EPS = 1e-05
MIB = 1024 * 1024


def params(limit):
    return pltpu.CompilerParams(
        dimension_semantics=("arbitrary",), vmem_limit_bytes=limit * MIB
    )


def tied(kernel, inputs, ties):
    def inner(*refs):
        kernel(*refs[:inputs], *refs[inputs + ties :])

    return inner


def tie_specs(ties):
    return [pl.BlockSpec(memory_space=pl.ANY)] * len(ties)


def cost(flops, moved):
    return pl.CostEstimate(flops=flops, bytes_accessed=moved, transcendentals=0)


def mm(a, b):
    return jnp.dot(a, b, preferred_element_type=jnp.float32)


def mm_nt(a, b):
    return lax.dot_general(a, b, (((1,), (1,)), ((), ())), preferred_element_type=jnp.float32)


def mm_tn(a, b):
    return lax.dot_general(a, b, (((0,), (0,)), ((), ())), preferred_element_type=jnp.float32)


def rope_tables(length, width):
    position = jnp.arange(length).astype(jnp.float32)[:, None]
    frequency = jnp.exp(
        jnp.arange(width // 2).astype(jnp.float32) * (-2.0 * math.log(10000.0) / width)
    )
    angle = position * frequency[None, :]
    cosine, sine = jnp.cos(angle), jnp.sin(angle)
    return (
        jnp.concatenate([cosine, cosine], axis=-1),
        jnp.concatenate([-sine, sine], axis=-1),
    )


def ring_order(size):
    return [*range(0, size, 2), *reversed(range(1, size, 2))]


def ring_distances(size):
    far = size // 2
    distances = [0]
    for step in range(1, far):
        distances += [-step, step]
    return [*distances, far]


def index_table(size, nodes):
    order, group = ring_order(size), size // nodes
    rows = []
    for node in range(nodes):
        for here in range(size):
            place = order.index(here)
            seqs = [order[(place + distance) % size] for distance in ring_distances(size)]
            owner = [seq // group for seq in seqs]
            rows.append(
                [order[(place + distance) % size] for distance in range(size)]
                + [node % 2]
                + seqs
                + [owner_ % 2 ^ node % 2 for owner_ in owner]
                + [(o // 2) * group + seq % group for o, seq in zip(owner, seqs)]
                + [node >> level & 1 for level in range(1, nodes.bit_length() - 1)]
                + [(here + turn) % group for turn in range(group)]
                + [(here - turn) % group for turn in range(group)]
                + [node]
            )
    return np.array(rows, np.int32)


def weights_kernel(quant, scale, out, turned):
    blocks = scale.shape[1]
    rows = quant.shape[1] // blocks
    scales = scale[0].astype(jnp.float32)
    for block in range(blocks):
        span = slice(block * rows, (block + 1) * rows)
        scaled = (quant[0, span].astype(jnp.float32) * scales[block : block + 1]).astype(jnp.bfloat16)
        out[0, span] = scaled
        turned[0, :, span] = scaled.T


def scaled_weights(w_quant, w_scale):
    _, depth, columns = w_quant.shape
    blocks = w_scale.shape[1]
    return pl.pallas_call(
        weights_kernel,
        grid=(3,),
        in_specs=[
            pl.BlockSpec((1, depth, columns), lambda m: (m, 0, 0)),
            pl.BlockSpec((1, blocks, columns), lambda m: (m, 0, 0)),
        ],
        out_specs=[
            pl.BlockSpec((1, depth, columns), lambda m: (m, 0, 0)),
            pl.BlockSpec((1, columns, depth), lambda m: (m, 0, 0)),
        ],
        out_shape=[
            jax.ShapeDtypeStruct((3, depth, columns), jnp.bfloat16),
            jax.ShapeDtypeStruct((3, columns, depth), jnp.bfloat16),
        ],
        compiler_params=params(20),
        cost_estimate=cost(3 * depth * columns, 18 * depth * columns),
        name="scaled_weights",
    )(w_quant, w_scale)


def normed_kernel(idx, tokens, gain, *refs):
    outs, gains = refs[:-1], refs[-1]
    width, part = tokens.shape[1], outs[0].shape[1]
    gains[...] = gain[...].astype(jnp.float32)
    values = tokens[...].astype(jnp.float32)
    inverse = lax.rsqrt(jnp.mean(values * values, axis=-1, keepdims=True) + NORM_EPS)
    size = len(outs) - 1
    for distance in range(size):
        start = pl.multiple_of(idx[distance] * (width // size) + idx[size] * part, part)
        block = tokens[:, pl.ds(start, part)].astype(jnp.float32)
        scale = gains[:, pl.ds(start, part)]
        outs[distance][...] = (block * inverse * scale).astype(jnp.bfloat16)
    outs[size][...] = jnp.broadcast_to(inverse, outs[size].shape)


def normed_blocks(idx, tokens, gain, size, part):
    length, width = tokens.shape
    tile = length // 4
    block = pl.BlockSpec((tile, part), lambda i, idx: (i, 0))
    *blocks, inverse = pl.pallas_call(
        normed_kernel,
        grid_spec=pltpu.PrefetchScalarGridSpec(
            num_scalar_prefetch=1,
            grid=(4,),
            in_specs=[
                pl.BlockSpec((tile, width), lambda i, idx: (i, 0)),
                pl.BlockSpec((1, width), lambda i, idx: (0, 0)),
            ],
            out_specs=[block] * size + [pl.BlockSpec((tile, 128), lambda i, idx: (i, 0))],
            scratch_shapes=[pltpu.VMEM((1, width), jnp.float32)],
        ),
        out_shape=[jax.ShapeDtypeStruct((length, part), jnp.bfloat16)] * size
        + [jax.ShapeDtypeStruct((length, 128), jnp.float32)],
        compiler_params=params(12),
        cost_estimate=cost(8 * length * width, 4 * length * width),
        name="normed_blocks",
    )(idx, tokens, gain)
    return blocks, inverse


def stack_kernel(*refs):
    for place, block in enumerate(refs[:-1]):
        refs[-1][place] = block[...]


def stack(blocks, ties):
    count, shape = len(blocks), blocks[0].shape
    block = pl.BlockSpec(shape, lambda i: (0, 0))
    return pl.pallas_call(
        tied(stack_kernel, count, len(ties)),
        grid=(1,),
        in_specs=[block] * count + tie_specs(ties),
        out_specs=pl.BlockSpec((count, *shape), lambda i: (0, 0, 0)),
        out_shape=jax.ShapeDtypeStruct((count, *shape), blocks[0].dtype),
        compiler_params=params(10),
        cost_estimate=cost(0, 4 * count * shape[0] * shape[1]),
        name="stack",
    )(*blocks, *ties)


def halve_kernel(right, left, right_out, left_out):
    half = right_out.shape[1]
    right_out[...] = right[:, :half]
    left_out[...] = left[:, half:]


def halve(right, left, ties):
    _, rows, wide = right.shape
    result = jax.ShapeDtypeStruct((3, rows // 2, wide), right.dtype)
    whole = pl.BlockSpec(memory_space=pltpu.VMEM)
    return pl.pallas_call(
        tied(halve_kernel, 2, len(ties)),
        in_specs=[whole, whole] + tie_specs(ties),
        out_specs=[whole, whole],
        out_shape=[result, result],
        compiler_params=pltpu.CompilerParams(vmem_limit_bytes=4 * MIB),
        cost_estimate=cost(0, 6 * rows * wide),
        name="halve",
    )(right, left, *ties)


def turn_kernel(count, idx, mine, other, mine_far, other_far, out):
    length, part = mine_far.shape
    for side, near, last in ((0, mine, mine_far), (1, other, other_far)):
        half = idx[count] * (1 - side) + (1 - idx[count]) * side
        rows = pl.ds(pl.multiple_of(half * part, part), part)
        for place in range(count):
            block = near[place] if place < count - 1 else last[...]
            out[rows, place * length : (place + 1) * length] = block.T


def turn(idx, mine, other, mine_far, other_far):
    near, length, part = mine.shape
    count = near + 1
    stack = pl.BlockSpec(mine.shape, lambda i, idx: (0, 0, 0))
    last = pl.BlockSpec((length, part), lambda i, idx: (0, 0))
    shape = (2 * part, count * length)
    return pl.pallas_call(
        functools.partial(turn_kernel, count),
        grid_spec=pltpu.PrefetchScalarGridSpec(
            num_scalar_prefetch=1,
            grid=(1,),
            in_specs=[stack, stack, last, last],
            out_specs=pl.BlockSpec(shape, lambda i, idx: (0, 0)),
        ),
        out_shape=jax.ShapeDtypeStruct(shape, jnp.bfloat16),
        compiler_params=params(12),
        cost_estimate=cost(2 * count * length * part, 8 * count * length * part),
        name="turn",
    )(idx, mine, other, mine_far, other_far)


def sum_first_kernel(idx, mine, other, weight, weight_other, *outs):
    half, wide = outs[0].shape[1:]
    for chunk in range(2):
        span = slice(chunk * wide, (chunk + 1) * wide)
        product = mm(mine[...], weight[0, :, span]) + mm(other[...], weight_other[0, :, span])
        outs[2 * chunk][0] = product[:half].astype(jnp.bfloat16)
        outs[2 * chunk + 1][0] = product[half:].astype(jnp.bfloat16)


def sum_step_kernel(
    idx, mine_r, other_r, mine_l, other_l, weight, weight_other, from_left, from_right, right, left
):
    length, part = right.shape[1], from_left.shape[1]
    product = mm(mine_r[0], weight[0]) + mm(other_r[0], weight_other[0])
    right[0, :part] = (product[:part] + from_left[0].astype(jnp.float32)).astype(jnp.bfloat16)
    if part < length:
        right[0, part:] = product[part:].astype(jnp.bfloat16)
    product = mm(mine_l[0], weight[0]) + mm(other_l[0], weight_other[0])
    rest = length - part
    left[0, rest:] = (product[rest:] + from_right[0].astype(jnp.float32)).astype(jnp.bfloat16)
    if rest:
        left[0, :rest] = product[:rest].astype(jnp.bfloat16)


def weight_halves(size, part, wide, chunk):
    return [
        pl.BlockSpec((1, part, wide), lambda m, idx: (m, idx[size], chunk)),
        pl.BlockSpec((1, part, wide), lambda m, idx: (m, 1 - idx[size], chunk)),
    ]


def sum_first(idx, size, mine, other, weights):
    length, part = mine.shape
    columns = weights.shape[2]
    half, wide = length // 2, columns // 2
    block = pl.BlockSpec((length, part), lambda m, idx: (0, 0))
    result = jax.ShapeDtypeStruct((3, half, wide), jnp.bfloat16)
    return pl.pallas_call(
        sum_first_kernel,
        grid_spec=pltpu.PrefetchScalarGridSpec(
            num_scalar_prefetch=1,
            grid=(3,),
            in_specs=[block, block, *weight_halves(size, part, columns, 0)],
            out_specs=[pl.BlockSpec((1, half, wide), lambda m, idx: (m, 0, 0))] * 4,
        ),
        out_shape=[result] * 4,
        compiler_params=params(12),
        cost_estimate=cost(12 * length * part * columns, 16 * part * columns),
        name="sum_first",
    )(idx, mine, other, weights, weights)


def sum_step(idx, size, mine, other, places, weights, from_left, from_right, chunk, wide, ties):
    _, length, part = mine.shape
    block_r = pl.BlockSpec((1, length, part), lambda m, idx: (places[0], 0, 0))
    block_l = pl.BlockSpec((1, length, part), lambda m, idx: (places[1], 0, 0))
    came = pl.BlockSpec((1, from_left.shape[1], wide), lambda m, idx: (m, 0, 0))
    whole = jax.ShapeDtypeStruct((3, length, wide), jnp.bfloat16)
    return pl.pallas_call(
        tied(sum_step_kernel, 9, len(ties)),
        grid_spec=pltpu.PrefetchScalarGridSpec(
            num_scalar_prefetch=1,
            grid=(3,),
            in_specs=[
                block_r,
                block_r,
                block_l,
                block_l,
                *weight_halves(size, part, wide, chunk),
                came,
                came,
                *tie_specs(ties),
            ],
            out_specs=[pl.BlockSpec((1, length, wide), lambda m, idx: (m, 0, 0))] * 2,
        ),
        out_shape=[whole, whole],
        compiler_params=params(12),
        cost_estimate=cost(24 * length * part * wide, 24 * part * wide),
        name="sum_step",
    )(idx, mine, other, mine, other, weights, weights, from_left, from_right, *ties)


def attention_kernel(
    idx, mine, other, weight, weight_other, from_left, from_right, d_out, cosine, sine,
    output, dots, pre,
):
    length = mine.shape[1]
    proj = [
        mm(mine[0], weight[m])
        + mm(other[0], weight_other[m])
        + (from_left[m].astype(jnp.float32) + from_right[m].astype(jnp.float32))
        for m in range(3)
    ]
    cos, sin = cosine[...], sine[...]
    half = HEAD_DIM // 2

    def rotate(tensor, angle):
        return tensor * cos + pltpu.roll(tensor, half, 1) * angle

    query = rotate(proj[0], sin).astype(jnp.bfloat16)
    key_rows = rotate(proj[1], sin).astype(jnp.bfloat16)
    value = proj[2].astype(jnp.bfloat16)
    scores = mm_nt(query, key_rows) * (1.0 / math.sqrt(HEAD_DIM))
    causal = lax.broadcasted_iota(jnp.int32, (length, length), 0) >= lax.broadcasted_iota(
        jnp.int32, (length, length), 1
    )
    scores = jnp.where(causal, scores, jnp.float32(-1e30))
    powers = jnp.exp(scores - jnp.max(scores, axis=-1, keepdims=True))
    probs = powers * (1.0 / jnp.sum(powers, axis=-1, keepdims=True))
    probs_low = probs.astype(jnp.bfloat16)
    output[...] = mm(probs_low, value).astype(jnp.bfloat16)
    cotangent = d_out[...]
    d_value = mm_tn(probs_low, cotangent).astype(jnp.bfloat16)
    d_probs = mm_nt(cotangent, value).astype(jnp.bfloat16).astype(jnp.float32)
    inner = jnp.sum(d_probs * probs, axis=-1, keepdims=True)
    d_scores = (probs * (d_probs - inner) * (1.0 / math.sqrt(HEAD_DIM))).astype(jnp.bfloat16)
    d_query = mm(d_scores, key_rows).astype(jnp.bfloat16).astype(jnp.float32)
    d_key = mm_tn(d_scores, query).astype(jnp.bfloat16).astype(jnp.float32)
    pre_query = rotate(d_query, -sin).astype(jnp.bfloat16)
    pre_key = rotate(d_key, -sin).astype(jnp.bfloat16)
    pre[0] = pre_query
    pre[1] = pre_key
    pre[2] = d_value
    product = (
        pre_query.astype(jnp.float32) * proj[0]
        + pre_key.astype(jnp.float32) * proj[1]
        + d_value.astype(jnp.float32) * proj[2]
    )

    @pl.when(pl.program_id(0) == 0)
    def _():
        dots[...] = product

    @pl.when(pl.program_id(0) > 0)
    def _():
        dots[...] += product


def attention(idx, size, mine, other, weights, from_left, from_right, d_out, tables, chunk, wide):
    _, length, part = mine.shape
    heads = wide // HEAD_DIM
    first = chunk * heads
    block = pl.BlockSpec((1, length, part), lambda h, idx: (0, 0, 0))
    table = pl.BlockSpec((length, HEAD_DIM), lambda h, idx: (0, 0))
    stack = pl.BlockSpec((3, length, HEAD_DIM), lambda h, idx: (0, 0, h))
    return pl.pallas_call(
        attention_kernel,
        grid_spec=pltpu.PrefetchScalarGridSpec(
            num_scalar_prefetch=1,
            grid=(heads,),
            in_specs=[
                block,
                block,
                pl.BlockSpec((3, part, HEAD_DIM), lambda h, idx: (0, idx[size], first + h)),
                pl.BlockSpec((3, part, HEAD_DIM), lambda h, idx: (0, 1 - idx[size], first + h)),
                stack,
                stack,
                pl.BlockSpec((length, HEAD_DIM), lambda h, idx: (0, first + h)),
                table,
                table,
            ],
            out_specs=[
                pl.BlockSpec((length, HEAD_DIM), lambda h, idx: (0, h)),
                table,
                stack,
            ],
        ),
        out_shape=[
            jax.ShapeDtypeStruct((length, wide), jnp.bfloat16),
            jax.ShapeDtypeStruct((length, HEAD_DIM), jnp.float32),
            jax.ShapeDtypeStruct((3, length, wide), jnp.bfloat16),
        ],
        compiler_params=params(16),
        cost_estimate=cost(12 * length * part * wide, 24 * part * wide),
        name="attention",
    )(idx, mine, other, weights, weights, from_left, from_right, d_out, *tables)


def grads_kernel(turned, *refs):
    blocks = jnp.concatenate([piece[0] for piece in refs[:-1]], axis=0)
    refs[-1][0] = mm(turned[...], blocks)


def grads_chunk(turned, pieces, before, ties, chunk, wide, columns):
    depth, span = turned.shape
    aliases = {} if before is None else {1 + len(pieces): 0}
    ties = ties if before is None else [before, *ties]
    return pl.pallas_call(
        tied(grads_kernel, 1 + len(pieces), len(ties)),
        grid=(3,),
        in_specs=[
            pl.BlockSpec((depth, span), lambda m: (0, 0)),
            *[pl.BlockSpec((1, *piece.shape[1:]), lambda m: (m, 0, 0)) for piece in pieces],
            *tie_specs(ties),
        ],
        out_specs=pl.BlockSpec((1, depth, wide), lambda m: (m, 0, chunk)),
        out_shape=jax.ShapeDtypeStruct((3, depth, columns), jnp.float32),
        input_output_aliases=aliases,
        compiler_params=params(24),
        cost_estimate=cost(6 * span * depth * wide, 6 * span * wide + 12 * depth * wide),
        name="grads",
    )(turned, *pieces, *ties)


def back(pieces, turned, chunk):
    wide = pieces[0].shape[2]
    rows = [jnp.concatenate([piece[m] for m in range(3)], axis=1) for piece in pieces]
    weight = [turned[m, chunk * wide : (chunk + 1) * wide] for m in range(3)]
    return mm(jnp.concatenate(rows, axis=0), jnp.concatenate(weight, axis=0))


def term_step(turned, pieces, befores, chunk):
    depth, wide = turned.shape[2], pieces[0].shape[2]
    count, rows = len(pieces), pieces[0].shape[1]
    whole = pl.BlockSpec(memory_space=pltpu.VMEM)

    def kernel(turned_ref, *refs):
        total = back(refs[:count], turned_ref, chunk)
        for place in range(count):
            block = total[place * rows : (place + 1) * rows]
            if befores:
                block += refs[count + place][...]
            refs[len(refs) - count + place][...] = block

    return pl.pallas_call(
        kernel,
        in_specs=[whole] * (1 + count + len(befores)),
        out_specs=[whole] * count,
        out_shape=[jax.ShapeDtypeStruct((rows, depth), jnp.float32)] * count,
        compiler_params=pltpu.CompilerParams(vmem_limit_bytes=16 * MIB),
        cost_estimate=cost(6 * count * rows * depth * wide, 12 * count * rows * wide),
        name="term_step",
    )(turned, *pieces, *befores)


def term_last_kernel(count, idx, turned, *refs):
    befores, fars, nears = refs[:2], refs[2:4], refs[4 : 3 + count]
    keeps, sends = refs[-4:-2], refs[-2:]
    half = keeps[0].shape[1]
    last = back(fars, turned, 1)
    for place in range(count):
        for part in range(2):
            span = slice(part * half, (part + 1) * half)
            total = nears[place][span] if place < count - 1 else last[span] + befores[part][...]

            @pl.when(idx[2 * count + 1 + place] == 0)
            def _():
                keeps[part][idx[3 * count + 1 + place]] = total

            @pl.when(idx[2 * count + 1 + place] == 1)
            def _():
                sends[part][idx[3 * count + 1 + place]] = total.astype(jnp.bfloat16)


def term_last(idx, turned, befores, pieces, nears):
    count = len(nears) + 1
    rows, depth = nears[0].shape
    whole = pl.BlockSpec(memory_space=pltpu.VMEM)
    shape = (count // 2, rows // 2, depth)
    return pl.pallas_call(
        functools.partial(term_last_kernel, count),
        in_specs=[pl.BlockSpec(memory_space=pltpu.SMEM)] + [whole] * (count + 4),
        out_specs=[whole] * 4,
        out_shape=[jax.ShapeDtypeStruct(shape, jnp.float32)] * 2
        + [jax.ShapeDtypeStruct(shape, jnp.bfloat16)] * 2,
        compiler_params=pltpu.CompilerParams(vmem_limit_bytes=12 * MIB),
        cost_estimate=cost(rows * depth * depth, 12 * count * rows * depth),
        name="term_last",
    )(idx, turned, *befores, *pieces, *nears)


def split_kernel(column, group, idx, keep, came, keep_out, send_out):
    own = idx[column]
    for block in range(keep_out.shape[0]):
        high, low = block // group, block % group
        mine = (2 * high + own) * group + low
        other = (2 * high + 1 - own) * group + low
        keep_out[block] = keep[mine] + came[mine].astype(jnp.float32)
        send_out[block] = (keep[other] + came[other].astype(jnp.float32)).astype(jnp.bfloat16)


def split_sum(idx, column, group, keep, came):
    whole = pl.BlockSpec(memory_space=pltpu.VMEM)
    shape = (keep.shape[0] // 2, *keep.shape[1:])
    return pl.pallas_call(
        functools.partial(split_kernel, column, group),
        in_specs=[pl.BlockSpec(memory_space=pltpu.SMEM), whole, whole],
        out_specs=[whole, whole],
        out_shape=[
            jax.ShapeDtypeStruct(shape, jnp.float32),
            jax.ShapeDtypeStruct(shape, jnp.bfloat16),
        ],
        compiler_params=pltpu.CompilerParams(vmem_limit_bytes=4 * MIB),
        cost_estimate=cost(0, 8 * keep.shape[0] * keep.shape[1] * keep.shape[2]),
        name="split_sum",
    )(idx, keep, came)


def order_kernel(column, idx, keep, came, *outs):
    for turn, out in enumerate(outs):
        block = idx[column + turn]
        out[...] = (keep[block] + came[block].astype(jnp.float32)).astype(jnp.bfloat16)


def order_sum(idx, column, keep, came):
    whole = pl.BlockSpec(memory_space=pltpu.VMEM)
    count = keep.shape[0]
    return pl.pallas_call(
        functools.partial(order_kernel, column),
        in_specs=[pl.BlockSpec(memory_space=pltpu.SMEM), whole, whole],
        out_specs=[whole] * count,
        out_shape=[jax.ShapeDtypeStruct(keep.shape[1:], jnp.bfloat16)] * count,
        compiler_params=pltpu.CompilerParams(vmem_limit_bytes=4 * MIB),
        cost_estimate=cost(0, 8 * count * keep.shape[1] * keep.shape[2]),
        name="order_sum",
    )(idx, keep, came)


def finish_kernel(column, width, idx, tokens, gain, inverse, dots, *refs):
    came, out, gains = refs[:-2], refs[-2], refs[-1]
    rows, depth = came[0].shape
    group = out.shape[1] // depth
    gains[...] = gain[...].astype(jnp.float32)
    for turn in range(group):
        features = pl.ds(pl.multiple_of(idx[column + turn] * depth, depth), depth)
        for part in range(len(came) // group):
            span = slice(part * rows, (part + 1) * rows)
            scale = inverse[span, :1]
            upstream = came[part * group + turn][...].astype(jnp.float32)
            values = tokens[span, features].astype(jnp.float32)
            common = scale * scale * dots[span] / width
            out[span, features] = (
                scale * gains[:, features] * upstream - values * common
            ).astype(jnp.bfloat16)


def finish(idx, column, tokens, gain, inverse, dots, came, share):
    length, width = tokens.shape
    node = column + share // came[0].shape[1]
    whole = pl.BlockSpec(memory_space=pltpu.VMEM)
    return pl.pallas_call(
        functools.partial(finish_kernel, column, width),
        grid_spec=pltpu.PrefetchScalarGridSpec(
            num_scalar_prefetch=1,
            grid=(1,),
            in_specs=[
                pl.BlockSpec((length, share), lambda i, idx: (0, idx[node])),
                pl.BlockSpec((1, share), lambda i, idx: (0, idx[node])),
                *[whole] * (2 + len(came)),
            ],
            out_specs=pl.BlockSpec((length, share), lambda i, idx: (0, 0)),
            scratch_shapes=[pltpu.VMEM((1, share), jnp.float32)],
        ),
        out_shape=jax.ShapeDtypeStruct((length, share), jnp.bfloat16),
        compiler_params=params(12),
        cost_estimate=cost(8 * length * share, 6 * length * share),
        name="finish",
    )(idx, tokens, gain, inverse, dots, *came)


def local(tokens, norm_gain, w_quant, w_scale, d_out):
    length, width = tokens.shape
    depth, columns = w_quant.shape[1:]
    size, nodes = lax.axis_size("local"), lax.axis_size("node")
    here, node = lax.axis_index("local"), lax.axis_index("node")
    wide = columns // 2
    far = size // 2
    group = size // nodes
    core = node % 2

    order = ring_order(size)
    distances = ring_distances(size)
    table = jnp.asarray(index_table(size, nodes))
    idx = lax.dynamic_index_in_dim(table, node * size + here, 0, keepdims=False)

    def shift(array, distance):
        moves = [(order[i], order[(i + distance) % size]) for i in range(size)]
        return lax.ppermute(array, "local", moves)

    def swap(array, bit):
        return lax.ppermute(array, "node", [(n, n ^ bit) for n in range(nodes)])

    blocks, inverse_rms = normed_blocks(idx, tokens, norm_gain[None], size, depth // 2)
    mine_far = shift(blocks[far], far)
    other_far = swap(mine_far, 1)
    weights, turned = scaled_weights(w_quant, w_scale)
    firsts = sum_first(idx, size, mine_far, other_far, weights)
    mine = stack(
        [shift(blocks[-d % size], -d) if d else blocks[0] for d in distances[:-1]], firsts[:1]
    )
    other = swap(mine, 1)

    rows_turned = turn(idx, mine, other, mine_far, other_far)

    tables = rope_tables(length, HEAD_DIM)
    arrived = []
    for chunk in range(2):
        right, left = firsts[2 * chunk : 2 * chunk + 2]
        for distance in range(far - 1, -1, -1):
            from_left, from_right = shift(right, 1), shift(left, -1)
            if distance:
                places = distances.index(distance), distances.index(-distance)
                ties = [rows_turned] if distance == 1 else []
                right, left = sum_step(
                    idx, size, mine, other, places, weights, from_left, from_right, chunk, wide, ties
                )
        arrived.append((from_left, from_right))

    outputs, sets, dots = [], [], 0.0
    for chunk in range(2):
        output, product, pre = attention(
            idx, size, mine, other, weights, *arrived[chunk], d_out, tables, chunk, wide
        )
        outputs.append(output)
        sets.append(pre)
        dots += jnp.sum(product, axis=-1, keepdims=True)
    bit = 1
    while bit < nodes:
        dots = dots + swap(dots, bit)
        bit *= 2

    def sum_nodes(keep, send):
        column = 4 * size + 1
        bit = 1
        while 2 * bit < nodes:
            keep, send = split_sum(idx, column, group, keep, swap(send, bit))
            column += 1
            bit *= 2
        return order_sum(idx, column, keep, swap(send, bit))

    def relocate(blocks):
        came = []
        for turn, block in enumerate(blocks):
            moves = [
                (n * size + s, (s // group) * size + n * group + (s + turn) % group)
                for n in range(nodes)
                for s in range(size)
            ]
            came.append(lax.ppermute(block, ("node", "local"), moves))
        return came

    gathered = [[block] for block in sets]
    moving = [(block, block) for block in sets]
    terms = [[], []]
    for step in range(1, far + 1):
        for chunk in range(2):
            right, left = moving[chunk]
            if step == far:
                early = [dots] if chunk == 0 else terms[1][: size - 3]
                right, left = halve(right, left, early)
            right, left = shift(right, 1), shift(left, -1)
            moving[chunk] = right, left
            gathered[chunk] += [right, left]
            if step < far:
                pieces = gathered[chunk] if step == 1 else [right, left]
                known = len(terms[chunk])
                befores = terms[0][known : known + len(pieces)] if chunk else []
                terms[chunk] += term_step(turned, pieces, befores, chunk)
            elif chunk == 0:
                lasts = term_step(turned, [right, left], [], 0)
    keep_0, keep_1, send_0, send_1 = term_last(idx, turned, lasts, gathered[1][-2:], terms[1])
    first, second = sum_nodes(keep_0, send_0), sum_nodes(keep_1, send_1)
    came = [*relocate(first), *relocate(second)]
    column = idx.shape[0] - 1 - group
    d_tokens = finish(
        idx, column, tokens, norm_gain[None], inverse_rms, dots, came, width // nodes
    )
    sums = [first[0], second[0]]
    grads = grads_chunk(rows_turned, gathered[0], None, sums, 0, wide, columns)
    grads = grads_chunk(rows_turned, gathered[1], grads, [], 1, wide, columns)
    return (jnp.concatenate(outputs, axis=-1), d_tokens, grads)


def solution(mesh):
    placed = (
        P("local", None),
        P(),
        P(None, "local", "node"),
        P(None, "local", "node"),
        P("local", "node"),
    )
    return jax.shard_map(
        local,
        mesh=mesh,
        in_specs=placed,
        out_specs=(P("local", "node"), P("local", "node"), P(None, "local", "node")),
        check_vma=False,
    )
```

```python
import functools
import math

import jax
import jax.numpy as jnp
import numpy as np
from jax import lax
from jax.experimental import pallas as pl
from jax.experimental.pallas import tpu as pltpu
from jax.sharding import PartitionSpec as P

HEAD_DIM = 128
NORM_EPS = 1e-05
MIB = 1024 * 1024


def params(limit):
    return pltpu.CompilerParams(
        dimension_semantics=("arbitrary",), vmem_limit_bytes=limit * MIB
    )


def tied(kernel, inputs, ties):
    def inner(*refs):
        kernel(*refs[:inputs], *refs[inputs + ties :])

    return inner


def tie_specs(ties):
    return [pl.BlockSpec(memory_space=pl.ANY)] * len(ties)


def cost(flops, moved):
    return pl.CostEstimate(flops=flops, bytes_accessed=moved, transcendentals=0)


def mm(a, b):
    return jnp.dot(a, b, preferred_element_type=jnp.float32)


def mm_nt(a, b):
    return lax.dot_general(a, b, (((1,), (1,)), ((), ())), preferred_element_type=jnp.float32)


def mm_tn(a, b):
    return lax.dot_general(a, b, (((0,), (0,)), ((), ())), preferred_element_type=jnp.float32)


def rope_tables(length, width):
    position = jnp.arange(length).astype(jnp.float32)[:, None]
    frequency = jnp.exp(
        jnp.arange(width // 2).astype(jnp.float32) * (-2.0 * math.log(10000.0) / width)
    )
    angle = position * frequency[None, :]
    cosine, sine = jnp.cos(angle), jnp.sin(angle)
    return (
        jnp.concatenate([cosine, cosine], axis=-1),
        jnp.concatenate([-sine, sine], axis=-1),
    )


def ring_order(size):
    return [*range(0, size, 2), *reversed(range(1, size, 2))]


def ring_distances(size):
    far = size // 2
    distances = [0]
    for step in range(1, far):
        distances += [-step, step]
    return [*distances, far]


def index_table(size, nodes):
    order, group = ring_order(size), size // nodes
    rows = []
    for node in range(nodes):
        for here in range(size):
            place = order.index(here)
            seqs = [order[(place + distance) % size] for distance in ring_distances(size)]
            owner = [seq // group for seq in seqs]
            rows.append(
                [order[(place + distance) % size] for distance in range(size)]
                + [node % 2]
                + seqs
                + [owner_ % 2 ^ node % 2 for owner_ in owner]
                + [(o // 2) * group + seq % group for o, seq in zip(owner, seqs)]
                + [node >> level & 1 for level in range(1, nodes.bit_length() - 1)]
                + [(here + turn) % group for turn in range(group)]
                + [(here - turn) % group for turn in range(group)]
                + [node]
            )
    return np.array(rows, np.int32)


def weights_kernel(quant, scale, out, turned):
    blocks = scale.shape[1]
    rows = quant.shape[1] // blocks
    scales = scale[0].astype(jnp.float32)
    for block in range(blocks):
        span = slice(block * rows, (block + 1) * rows)
        scaled = (quant[0, span].astype(jnp.float32) * scales[block : block + 1]).astype(jnp.bfloat16)
        out[0, span] = scaled
        turned[0, :, span] = scaled.T


def scaled_weights(w_quant, w_scale):
    _, depth, columns = w_quant.shape
    blocks = w_scale.shape[1]
    return pl.pallas_call(
        weights_kernel,
        grid=(3,),
        in_specs=[
            pl.BlockSpec((1, depth, columns), lambda m: (m, 0, 0)),
            pl.BlockSpec((1, blocks, columns), lambda m: (m, 0, 0)),
        ],
        out_specs=[
            pl.BlockSpec((1, depth, columns), lambda m: (m, 0, 0)),
            pl.BlockSpec((1, columns, depth), lambda m: (m, 0, 0)),
        ],
        out_shape=[
            jax.ShapeDtypeStruct((3, depth, columns), jnp.bfloat16),
            jax.ShapeDtypeStruct((3, columns, depth), jnp.bfloat16),
        ],
        compiler_params=params(20),
        cost_estimate=cost(3 * depth * columns, 18 * depth * columns),
        name="scaled_weights",
    )(w_quant, w_scale)


def normed_kernel(split, idx, tokens, gain, *refs):
    outs, gains = refs[:-1], refs[-1]
    width, part = tokens.shape[1], outs[0].shape[1]
    gains[...] = gain[...].astype(jnp.float32)
    values = tokens[...].astype(jnp.float32)
    inverse = lax.rsqrt(jnp.mean(values * values, axis=-1, keepdims=True) + NORM_EPS)
    size = len(outs) - 1
    share = idx[size] if split == 2 else 2 * idx[size] + idx[4 * size + 1]
    for distance in range(size):
        start = pl.multiple_of(idx[distance] * (width // size) + share * part, part)
        block = tokens[:, pl.ds(start, part)].astype(jnp.float32)
        scale = gains[:, pl.ds(start, part)]
        outs[distance][...] = (block * inverse * scale).astype(jnp.bfloat16)
    outs[size][...] = jnp.broadcast_to(inverse, outs[size].shape)


def normed_blocks(idx, tokens, gain, size, split):
    length, width = tokens.shape
    part = width // (size * split)
    tile = length // 4
    block = pl.BlockSpec((tile, part), lambda i, idx: (i, 0))
    *blocks, inverse = pl.pallas_call(
        functools.partial(normed_kernel, split),
        grid_spec=pltpu.PrefetchScalarGridSpec(
            num_scalar_prefetch=1,
            grid=(4,),
            in_specs=[
                pl.BlockSpec((tile, width), lambda i, idx: (i, 0)),
                pl.BlockSpec((1, width), lambda i, idx: (0, 0)),
            ],
            out_specs=[block] * size + [pl.BlockSpec((tile, 128), lambda i, idx: (i, 0))],
            scratch_shapes=[pltpu.VMEM((1, width), jnp.float32)],
        ),
        out_shape=[jax.ShapeDtypeStruct((length, part), jnp.bfloat16)] * size
        + [jax.ShapeDtypeStruct((length, 128), jnp.float32)],
        compiler_params=params(12),
        cost_estimate=cost(8 * length * width, 4 * length * width),
        name="normed_blocks",
    )(idx, tokens, gain)
    return blocks, inverse


def stack_kernel(*refs):
    for place, block in enumerate(refs[:-1]):
        refs[-1][place] = block[...]


def stack(blocks, ties):
    count, shape = len(blocks), blocks[0].shape
    block = pl.BlockSpec(shape, lambda i: (0, 0))
    return pl.pallas_call(
        tied(stack_kernel, count, len(ties)),
        grid=(1,),
        in_specs=[block] * count + tie_specs(ties),
        out_specs=pl.BlockSpec((count, *shape), lambda i: (0, 0, 0)),
        out_shape=jax.ShapeDtypeStruct((count, *shape), blocks[0].dtype),
        compiler_params=params(10),
        cost_estimate=cost(0, 4 * count * shape[0] * shape[1]),
        name="stack",
    )(*blocks, *ties)


def join_kernel(column, idx, own, came, out):
    part = own.shape[-1]
    out[..., pl.ds(pl.multiple_of(idx[column] * part, part), part)] = own[...]
    out[..., pl.ds(pl.multiple_of((1 - idx[column]) * part, part), part)] = came[...]


def join(idx, column, own, came):
    whole = pl.BlockSpec(memory_space=pltpu.VMEM)
    shape = (*own.shape[:-1], 2 * own.shape[-1])
    return pl.pallas_call(
        functools.partial(join_kernel, column),
        in_specs=[pl.BlockSpec(memory_space=pltpu.SMEM), whole, whole],
        out_specs=whole,
        out_shape=jax.ShapeDtypeStruct(shape, own.dtype),
        compiler_params=pltpu.CompilerParams(vmem_limit_bytes=4 * MIB),
        cost_estimate=cost(0, 4 * math.prod(shape)),
        name="join",
    )(idx, own, came)


def halve_kernel(right, left, right_out, left_out):
    half = right_out.shape[1]
    right_out[...] = right[:, :half]
    left_out[...] = left[:, half:]


def halve(right, left, ties):
    _, rows, wide = right.shape
    result = jax.ShapeDtypeStruct((3, rows // 2, wide), right.dtype)
    whole = pl.BlockSpec(memory_space=pltpu.VMEM)
    return pl.pallas_call(
        tied(halve_kernel, 2, len(ties)),
        in_specs=[whole, whole] + tie_specs(ties),
        out_specs=[whole, whole],
        out_shape=[result, result],
        compiler_params=pltpu.CompilerParams(vmem_limit_bytes=4 * MIB),
        cost_estimate=cost(0, 6 * rows * wide),
        name="halve",
    )(right, left, *ties)


def turn_kernel(count, idx, mine, other, mine_far, other_far, out):
    length, part = mine_far.shape
    for side, near, last in ((0, mine, mine_far), (1, other, other_far)):
        half = idx[count] * (1 - side) + (1 - idx[count]) * side
        rows = pl.ds(pl.multiple_of(half * part, part), part)
        for place in range(count):
            block = near[place] if place < count - 1 else last[...]
            out[rows, place * length : (place + 1) * length] = block.T


def turn(idx, mine, other, mine_far, other_far):
    near, length, part = mine.shape
    count = near + 1
    stack = pl.BlockSpec(mine.shape, lambda i, idx: (0, 0, 0))
    last = pl.BlockSpec((length, part), lambda i, idx: (0, 0))
    shape = (2 * part, count * length)
    return pl.pallas_call(
        functools.partial(turn_kernel, count),
        grid_spec=pltpu.PrefetchScalarGridSpec(
            num_scalar_prefetch=1,
            grid=(1,),
            in_specs=[stack, stack, last, last],
            out_specs=pl.BlockSpec(shape, lambda i, idx: (0, 0)),
        ),
        out_shape=jax.ShapeDtypeStruct(shape, jnp.bfloat16),
        compiler_params=params(12),
        cost_estimate=cost(2 * count * length * part, 8 * count * length * part),
        name="turn",
    )(idx, mine, other, mine_far, other_far)


def sum_first_kernel(idx, mine, other, weight, weight_other, *outs):
    half, wide = outs[0].shape[1:]
    for chunk in range(2):
        span = slice(chunk * wide, (chunk + 1) * wide)
        product = mm(mine[...], weight[0, :, span]) + mm(other[...], weight_other[0, :, span])
        outs[2 * chunk][0] = product[:half].astype(jnp.bfloat16)
        outs[2 * chunk + 1][0] = product[half:].astype(jnp.bfloat16)


def sum_step_kernel(
    idx, mine_r, other_r, mine_l, other_l, weight, weight_other, from_left, from_right, right, left
):
    length, part = right.shape[1], from_left.shape[1]
    product = mm(mine_r[0], weight[0]) + mm(other_r[0], weight_other[0])
    right[0, :part] = (product[:part] + from_left[0].astype(jnp.float32)).astype(jnp.bfloat16)
    if part < length:
        right[0, part:] = product[part:].astype(jnp.bfloat16)
    product = mm(mine_l[0], weight[0]) + mm(other_l[0], weight_other[0])
    rest = length - part
    left[0, rest:] = (product[rest:] + from_right[0].astype(jnp.float32)).astype(jnp.bfloat16)
    if rest:
        left[0, :rest] = product[:rest].astype(jnp.bfloat16)


def weight_halves(size, part, wide, chunk):
    return [
        pl.BlockSpec((1, part, wide), lambda m, idx: (m, idx[size], chunk)),
        pl.BlockSpec((1, part, wide), lambda m, idx: (m, 1 - idx[size], chunk)),
    ]


def sum_first(idx, size, mine, other, weights):
    length, part = mine.shape
    columns = weights.shape[2]
    half, wide = length // 2, columns // 2
    block = pl.BlockSpec((length, part), lambda m, idx: (0, 0))
    result = jax.ShapeDtypeStruct((3, half, wide), jnp.bfloat16)
    return pl.pallas_call(
        sum_first_kernel,
        grid_spec=pltpu.PrefetchScalarGridSpec(
            num_scalar_prefetch=1,
            grid=(3,),
            in_specs=[block, block, *weight_halves(size, part, columns, 0)],
            out_specs=[pl.BlockSpec((1, half, wide), lambda m, idx: (m, 0, 0))] * 4,
        ),
        out_shape=[result] * 4,
        compiler_params=params(12),
        cost_estimate=cost(12 * length * part * columns, 16 * part * columns),
        name="sum_first",
    )(idx, mine, other, weights, weights)


def sum_step(idx, size, mine, other, places, weights, from_left, from_right, chunk, wide, ties):
    _, length, part = mine.shape
    block_r = pl.BlockSpec((1, length, part), lambda m, idx: (places[0], 0, 0))
    block_l = pl.BlockSpec((1, length, part), lambda m, idx: (places[1], 0, 0))
    came = pl.BlockSpec((1, from_left.shape[1], wide), lambda m, idx: (m, 0, 0))
    whole = jax.ShapeDtypeStruct((3, length, wide), jnp.bfloat16)
    return pl.pallas_call(
        tied(sum_step_kernel, 9, len(ties)),
        grid_spec=pltpu.PrefetchScalarGridSpec(
            num_scalar_prefetch=1,
            grid=(3,),
            in_specs=[
                block_r,
                block_r,
                block_l,
                block_l,
                *weight_halves(size, part, wide, chunk),
                came,
                came,
                *tie_specs(ties),
            ],
            out_specs=[pl.BlockSpec((1, length, wide), lambda m, idx: (m, 0, 0))] * 2,
        ),
        out_shape=[whole, whole],
        compiler_params=params(12),
        cost_estimate=cost(24 * length * part * wide, 24 * part * wide),
        name="sum_step",
    )(idx, mine, other, mine, other, weights, weights, from_left, from_right, *ties)


def attention_kernel(
    idx, mine, other, weight, weight_other, from_left, from_right, d_out, cosine, sine,
    output, dots, pre,
):
    length = mine.shape[1]
    proj = [
        mm(mine[0], weight[m])
        + mm(other[0], weight_other[m])
        + (from_left[m].astype(jnp.float32) + from_right[m].astype(jnp.float32))
        for m in range(3)
    ]
    cos, sin = cosine[...], sine[...]
    half = HEAD_DIM // 2

    def rotate(tensor, angle):
        return tensor * cos + pltpu.roll(tensor, half, 1) * angle

    query = rotate(proj[0], sin).astype(jnp.bfloat16)
    key_rows = rotate(proj[1], sin).astype(jnp.bfloat16)
    value = proj[2].astype(jnp.bfloat16)
    scores = mm_nt(query, key_rows) * (1.0 / math.sqrt(HEAD_DIM))
    causal = lax.broadcasted_iota(jnp.int32, (length, length), 0) >= lax.broadcasted_iota(
        jnp.int32, (length, length), 1
    )
    scores = jnp.where(causal, scores, jnp.float32(-1e30))
    powers = jnp.exp(scores - jnp.max(scores, axis=-1, keepdims=True))
    probs = powers * (1.0 / jnp.sum(powers, axis=-1, keepdims=True))
    probs_low = probs.astype(jnp.bfloat16)
    output[...] = mm(probs_low, value).astype(jnp.bfloat16)
    cotangent = d_out[...]
    d_value = mm_tn(probs_low, cotangent).astype(jnp.bfloat16)
    d_probs = mm_nt(cotangent, value).astype(jnp.bfloat16).astype(jnp.float32)
    inner = jnp.sum(d_probs * probs, axis=-1, keepdims=True)
    d_scores = (probs * (d_probs - inner) * (1.0 / math.sqrt(HEAD_DIM))).astype(jnp.bfloat16)
    d_query = mm(d_scores, key_rows).astype(jnp.bfloat16).astype(jnp.float32)
    d_key = mm_tn(d_scores, query).astype(jnp.bfloat16).astype(jnp.float32)
    pre_query = rotate(d_query, -sin).astype(jnp.bfloat16)
    pre_key = rotate(d_key, -sin).astype(jnp.bfloat16)
    pre[0] = pre_query
    pre[1] = pre_key
    pre[2] = d_value
    product = (
        pre_query.astype(jnp.float32) * proj[0]
        + pre_key.astype(jnp.float32) * proj[1]
        + d_value.astype(jnp.float32) * proj[2]
    )

    @pl.when(pl.program_id(0) == 0)
    def _():
        dots[...] = product

    @pl.when(pl.program_id(0) > 0)
    def _():
        dots[...] += product


def attention(idx, size, mine, other, weights, from_left, from_right, d_out, tables, chunk, wide):
    _, length, part = mine.shape
    heads = wide // HEAD_DIM
    first = chunk * heads
    block = pl.BlockSpec((1, length, part), lambda h, idx: (0, 0, 0))
    table = pl.BlockSpec((length, HEAD_DIM), lambda h, idx: (0, 0))
    stack = pl.BlockSpec((3, length, HEAD_DIM), lambda h, idx: (0, 0, h))
    return pl.pallas_call(
        attention_kernel,
        grid_spec=pltpu.PrefetchScalarGridSpec(
            num_scalar_prefetch=1,
            grid=(heads,),
            in_specs=[
                block,
                block,
                pl.BlockSpec((3, part, HEAD_DIM), lambda h, idx: (0, idx[size], first + h)),
                pl.BlockSpec((3, part, HEAD_DIM), lambda h, idx: (0, 1 - idx[size], first + h)),
                stack,
                stack,
                pl.BlockSpec((length, HEAD_DIM), lambda h, idx: (0, first + h)),
                table,
                table,
            ],
            out_specs=[
                pl.BlockSpec((length, HEAD_DIM), lambda h, idx: (0, h)),
                table,
                stack,
            ],
        ),
        out_shape=[
            jax.ShapeDtypeStruct((length, wide), jnp.bfloat16),
            jax.ShapeDtypeStruct((length, HEAD_DIM), jnp.float32),
            jax.ShapeDtypeStruct((3, length, wide), jnp.bfloat16),
        ],
        compiler_params=params(16),
        cost_estimate=cost(12 * length * part * wide, 24 * part * wide),
        name="attention",
    )(idx, mine, other, weights, weights, from_left, from_right, d_out, *tables)


def grads_kernel(turned, *refs):
    blocks = jnp.concatenate([piece[0] for piece in refs[:-1]], axis=0)
    refs[-1][0] = mm(turned[...], blocks)


def grads_chunk(turned, pieces, before, ties, chunk, wide, columns):
    depth, span = turned.shape
    aliases = {} if before is None else {1 + len(pieces): 0}
    ties = ties if before is None else [before, *ties]
    return pl.pallas_call(
        tied(grads_kernel, 1 + len(pieces), len(ties)),
        grid=(3,),
        in_specs=[
            pl.BlockSpec((depth, span), lambda m: (0, 0)),
            *[pl.BlockSpec((1, *piece.shape[1:]), lambda m: (m, 0, 0)) for piece in pieces],
            *tie_specs(ties),
        ],
        out_specs=pl.BlockSpec((1, depth, wide), lambda m: (m, 0, chunk)),
        out_shape=jax.ShapeDtypeStruct((3, depth, columns), jnp.float32),
        input_output_aliases=aliases,
        compiler_params=params(24),
        cost_estimate=cost(6 * span * depth * wide, 6 * span * wide + 12 * depth * wide),
        name="grads",
    )(turned, *pieces, *ties)


def back(pieces, turned, chunk):
    wide = pieces[0].shape[2]
    rows = [jnp.concatenate([piece[m] for m in range(3)], axis=1) for piece in pieces]
    weight = [turned[m, chunk * wide : (chunk + 1) * wide] for m in range(3)]
    return mm(jnp.concatenate(rows, axis=0), jnp.concatenate(weight, axis=0))


def term_step(turned, pieces, befores, chunk):
    depth, wide = turned.shape[2], pieces[0].shape[2]
    count, rows = len(pieces), pieces[0].shape[1]
    whole = pl.BlockSpec(memory_space=pltpu.VMEM)

    def kernel(turned_ref, *refs):
        total = back(refs[:count], turned_ref, chunk)
        for place in range(count):
            block = total[place * rows : (place + 1) * rows]
            if befores:
                block += refs[count + place][...]
            refs[len(refs) - count + place][...] = block

    return pl.pallas_call(
        kernel,
        in_specs=[whole] * (1 + count + len(befores)),
        out_specs=[whole] * count,
        out_shape=[jax.ShapeDtypeStruct((rows, depth), jnp.float32)] * count,
        compiler_params=pltpu.CompilerParams(vmem_limit_bytes=16 * MIB),
        cost_estimate=cost(6 * count * rows * depth * wide, 12 * count * rows * wide),
        name="term_step",
    )(turned, *pieces, *befores)


def term_last_kernel(count, idx, turned, *refs):
    befores, fars, nears = refs[:2], refs[2:4], refs[4 : 3 + count]
    keeps, sends = refs[-4:-2], refs[-2:]
    half = keeps[0].shape[1]
    last = back(fars, turned, 1)
    for place in range(count):
        for part in range(2):
            span = slice(part * half, (part + 1) * half)
            total = nears[place][span] if place < count - 1 else last[span] + befores[part][...]

            @pl.when(idx[2 * count + 1 + place] == 0)
            def _():
                keeps[part][idx[3 * count + 1 + place]] = total

            @pl.when(idx[2 * count + 1 + place] == 1)
            def _():
                sends[part][idx[3 * count + 1 + place]] = total.astype(jnp.bfloat16)


def term_last(idx, turned, befores, pieces, nears, ties):
    count = len(nears) + 1
    rows, depth = nears[0].shape
    whole = pl.BlockSpec(memory_space=pltpu.VMEM)
    shape = (count // 2, rows // 2, depth)
    return pl.pallas_call(
        tied(functools.partial(term_last_kernel, count), count + 5, len(ties)),
        in_specs=[pl.BlockSpec(memory_space=pltpu.SMEM)]
        + [whole] * (count + 4)
        + tie_specs(ties),
        out_specs=[whole] * 4,
        out_shape=[jax.ShapeDtypeStruct(shape, jnp.float32)] * 2
        + [jax.ShapeDtypeStruct(shape, jnp.bfloat16)] * 2,
        compiler_params=pltpu.CompilerParams(vmem_limit_bytes=12 * MIB),
        cost_estimate=cost(rows * depth * depth, 12 * count * rows * depth),
        name="term_last",
    )(idx, turned, *befores, *pieces, *nears, *ties)


def split_kernel(column, group, idx, keep, came, keep_out, send_out):
    own = idx[column]
    for block in range(keep_out.shape[0]):
        high, low = block // group, block % group
        mine = (2 * high + own) * group + low
        other = (2 * high + 1 - own) * group + low
        keep_out[block] = keep[mine] + came[mine].astype(jnp.float32)
        send_out[block] = (keep[other] + came[other].astype(jnp.float32)).astype(jnp.bfloat16)


def split_sum(idx, column, group, keep, came):
    whole = pl.BlockSpec(memory_space=pltpu.VMEM)
    shape = (keep.shape[0] // 2, *keep.shape[1:])
    return pl.pallas_call(
        functools.partial(split_kernel, column, group),
        in_specs=[pl.BlockSpec(memory_space=pltpu.SMEM), whole, whole],
        out_specs=[whole, whole],
        out_shape=[
            jax.ShapeDtypeStruct(shape, jnp.float32),
            jax.ShapeDtypeStruct(shape, jnp.bfloat16),
        ],
        compiler_params=pltpu.CompilerParams(vmem_limit_bytes=4 * MIB),
        cost_estimate=cost(0, 8 * keep.shape[0] * keep.shape[1] * keep.shape[2]),
        name="split_sum",
    )(idx, keep, came)


def order_kernel(column, idx, keep, came, *outs):
    for turn, out in enumerate(outs):
        block = idx[column + turn]
        out[...] = (keep[block] + came[block].astype(jnp.float32)).astype(jnp.bfloat16)


def order_sum(idx, column, keep, came):
    whole = pl.BlockSpec(memory_space=pltpu.VMEM)
    count = keep.shape[0]
    return pl.pallas_call(
        functools.partial(order_kernel, column),
        in_specs=[pl.BlockSpec(memory_space=pltpu.SMEM), whole, whole],
        out_specs=[whole] * count,
        out_shape=[jax.ShapeDtypeStruct(keep.shape[1:], jnp.bfloat16)] * count,
        compiler_params=pltpu.CompilerParams(vmem_limit_bytes=4 * MIB),
        cost_estimate=cost(0, 8 * count * keep.shape[1] * keep.shape[2]),
        name="order_sum",
    )(idx, keep, came)


def finish_kernel(column, width, idx, tokens, gain, inverse, dots, *refs):
    came, out, gains = refs[:-2], refs[-2], refs[-1]
    rows, depth = came[0].shape
    group = out.shape[1] // depth
    gains[...] = gain[...].astype(jnp.float32)
    for turn in range(group):
        features = pl.ds(pl.multiple_of(idx[column + turn] * depth, depth), depth)
        for part in range(len(came) // group):
            span = slice(part * rows, (part + 1) * rows)
            scale = inverse[span, :1]
            upstream = came[part * group + turn][...].astype(jnp.float32)
            values = tokens[span, features].astype(jnp.float32)
            common = scale * scale * dots[span] / width
            out[span, features] = (
                scale * gains[:, features] * upstream - values * common
            ).astype(jnp.bfloat16)


def finish(idx, column, tokens, gain, inverse, dots, came, share):
    length, width = tokens.shape
    node = column + share // came[0].shape[1]
    whole = pl.BlockSpec(memory_space=pltpu.VMEM)
    return pl.pallas_call(
        functools.partial(finish_kernel, column, width),
        grid_spec=pltpu.PrefetchScalarGridSpec(
            num_scalar_prefetch=1,
            grid=(1,),
            in_specs=[
                pl.BlockSpec((length, share), lambda i, idx: (0, idx[node])),
                pl.BlockSpec((1, share), lambda i, idx: (0, idx[node])),
                *[whole] * (2 + len(came)),
            ],
            out_specs=pl.BlockSpec((length, share), lambda i, idx: (0, 0)),
            scratch_shapes=[pltpu.VMEM((1, share), jnp.float32)],
        ),
        out_shape=jax.ShapeDtypeStruct((length, share), jnp.bfloat16),
        compiler_params=params(12),
        cost_estimate=cost(8 * length * share, 6 * length * share),
        name="finish",
    )(idx, tokens, gain, inverse, dots, *came)


def local(tokens, norm_gain, w_quant, w_scale, d_out):
    length, width = tokens.shape
    depth, columns = w_quant.shape[1:]
    size, nodes = lax.axis_size("local"), lax.axis_size("node")
    here, node = lax.axis_index("local"), lax.axis_index("node")
    wide = columns // 2
    far = size // 2
    group = size // nodes
    core = node % 2

    order = ring_order(size)
    distances = ring_distances(size)
    table = jnp.asarray(index_table(size, nodes))
    idx = lax.dynamic_index_in_dim(table, node * size + here, 0, keepdims=False)

    def shift(array, distance):
        moves = [(order[i], order[(i + distance) % size]) for i in range(size)]
        return lax.ppermute(array, "local", moves)

    def swap(array, bit):
        return lax.ppermute(array, "node", [(n, n ^ bit) for n in range(nodes)])

    split = 4 if nodes >= 4 and depth % 512 == 0 else 2

    def whole_half(block):
        return join(idx, 4 * size + 1, block, swap(block, 2)) if split == 4 else block

    blocks, inverse_rms = normed_blocks(idx, tokens, norm_gain[None], size, split)
    mine_far = whole_half(shift(blocks[far], far))
    other_far = swap(mine_far, 1)
    weights, turned = scaled_weights(w_quant, w_scale)
    firsts = sum_first(idx, size, mine_far, other_far, weights)
    nears = [shift(blocks[-d % size], -d) if d else blocks[0] for d in distances[:-1]]
    mine = whole_half(stack(nears, firsts[:1]))
    other = swap(mine, 1)

    rows_turned = turn(idx, mine, other, mine_far, other_far)

    tables = rope_tables(length, HEAD_DIM)
    arrived = []
    for chunk in range(2):
        right, left = firsts[2 * chunk : 2 * chunk + 2]
        for distance in range(far - 1, -1, -1):
            from_left, from_right = shift(right, 1), shift(left, -1)
            if distance:
                places = distances.index(distance), distances.index(-distance)
                ties = [rows_turned] if distance == 1 else []
                right, left = sum_step(
                    idx, size, mine, other, places, weights, from_left, from_right, chunk, wide, ties
                )
        arrived.append((from_left, from_right))

    outputs, sets, dots = [], [], 0.0
    for chunk in range(2):
        output, product, pre = attention(
            idx, size, mine, other, weights, *arrived[chunk], d_out, tables, chunk, wide
        )
        outputs.append(output)
        sets.append(pre)
        dots += jnp.sum(product, axis=-1, keepdims=True)
    bit = 1
    while bit < nodes:
        dots = dots + swap(dots, bit)
        bit *= 2

    def sum_nodes(keep, send):
        column = 4 * size + 1
        bit = 1
        while 2 * bit < nodes:
            keep, send = split_sum(idx, column, group, keep, swap(send, bit))
            column += 1
            bit *= 2
        return order_sum(idx, column, keep, swap(send, bit))

    def relocate(blocks):
        came = []
        for turn, block in enumerate(blocks):
            moves = [
                (n * size + s, (s // group) * size + n * group + (s + turn) % group)
                for n in range(nodes)
                for s in range(size)
            ]
            came.append(lax.ppermute(block, ("node", "local"), moves))
        return came

    gathered = [[block] for block in sets]
    moving = [(block, block) for block in sets]
    terms = [[], []]
    for step in range(1, far + 1):
        for chunk in range(2):
            right, left = moving[chunk]
            if step == far:
                early = [dots] if chunk == 0 else terms[1][: size - 3]
                right, left = halve(right, left, early)
            right, left = shift(right, 1), shift(left, -1)
            moving[chunk] = right, left
            gathered[chunk] += [right, left]
            if step < far:
                pieces = gathered[chunk] if step == 1 else [right, left]
                known = len(terms[chunk])
                befores = terms[0][known : known + len(pieces)] if chunk else []
                terms[chunk] += term_step(turned, pieces, befores, chunk)
            elif chunk == 0:
                lasts = term_step(turned, [right, left], [], 0)
    grads = grads_chunk(rows_turned, gathered[0], None, [], 0, wide, columns)
    keep_0, keep_1, send_0, send_1 = term_last(
        idx, turned, lasts, gathered[1][-2:], terms[1], [grads]
    )
    first, second = sum_nodes(keep_0, send_0), sum_nodes(keep_1, send_1)
    came = [*relocate(first), *relocate(second)]
    column = idx.shape[0] - 1 - group
    d_tokens = finish(
        idx, column, tokens, norm_gain[None], inverse_rms, dots, came, width // nodes
    )
    sums = [first[0], second[0]]
    grads = grads_chunk(rows_turned, gathered[1], grads, sums, 1, wide, columns)
    return (jnp.concatenate(outputs, axis=-1), d_tokens, grads)


def solution(mesh):
    placed = (
        P("local", None),
        P(),
        P(None, "local", "node"),
        P(None, "local", "node"),
        P("local", "node"),
    )
    return jax.shard_map(
        local,
        mesh=mesh,
        in_specs=placed,
        out_specs=(P("local", "node"), P("local", "node"), P(None, "local", "node")),
        check_vma=False,
    )
```

```python
import functools
import math

import jax
import jax.numpy as jnp
import numpy as np
from jax import lax
from jax.experimental import pallas as pl
from jax.experimental.pallas import tpu as pltpu
from jax.sharding import PartitionSpec as P

HEAD_DIM = 128
NORM_EPS = 1e-05
MIB = 1024 * 1024


def params(limit):
    return pltpu.CompilerParams(
        dimension_semantics=("arbitrary",), vmem_limit_bytes=limit * MIB
    )


def tied(kernel, inputs, ties):
    def inner(*refs):
        kernel(*refs[:inputs], *refs[inputs + ties :])

    return inner


def tie_specs(ties):
    return [pl.BlockSpec(memory_space=pl.ANY)] * len(ties)


def cost(flops, moved):
    return pl.CostEstimate(flops=flops, bytes_accessed=moved, transcendentals=0)


def mm(a, b):
    return jnp.dot(a, b, preferred_element_type=jnp.float32)


def mm_nt(a, b):
    return lax.dot_general(a, b, (((1,), (1,)), ((), ())), preferred_element_type=jnp.float32)


def mm_tn(a, b):
    return lax.dot_general(a, b, (((0,), (0,)), ((), ())), preferred_element_type=jnp.float32)


def rope_tables(length, width):
    position = jnp.arange(length).astype(jnp.float32)[:, None]
    frequency = jnp.exp(
        jnp.arange(width // 2).astype(jnp.float32) * (-2.0 * math.log(10000.0) / width)
    )
    angle = position * frequency[None, :]
    cosine, sine = jnp.cos(angle), jnp.sin(angle)
    return (
        jnp.concatenate([cosine, cosine], axis=-1),
        jnp.concatenate([-sine, sine], axis=-1),
    )


def ring_order(size):
    return [*range(0, size, 2), *reversed(range(1, size, 2))]


def ring_distances(size):
    far = size // 2
    distances = [0]
    for step in range(1, far):
        distances += [-step, step]
    return [*distances, far]


def index_table(size, nodes):
    order, group = ring_order(size), size // nodes
    rows = []
    for node in range(nodes):
        for here in range(size):
            place = order.index(here)
            seqs = [order[(place + distance) % size] for distance in ring_distances(size)]
            owner = [seq // group for seq in seqs]
            rows.append(
                [order[(place + distance) % size] for distance in range(size)]
                + [node % 2]
                + seqs
                + [owner_ % 2 ^ node % 2 for owner_ in owner]
                + [(o // 2) * group + seq % group for o, seq in zip(owner, seqs)]
                + [node >> level & 1 for level in range(1, nodes.bit_length() - 1)]
                + [(here + turn) % group for turn in range(group)]
                + [(here - turn) % group for turn in range(group)]
                + [node]
            )
    return np.array(rows, np.int32)


def weights_kernel(quant, scale, out, turned):
    blocks = scale.shape[1]
    rows = quant.shape[1] // blocks
    scales = scale[0].astype(jnp.float32)
    for block in range(blocks):
        span = slice(block * rows, (block + 1) * rows)
        scaled = (quant[0, span].astype(jnp.float32) * scales[block : block + 1]).astype(jnp.bfloat16)
        out[0, span] = scaled
        turned[0, :, span] = scaled.T


def scaled_weights(w_quant, w_scale):
    _, depth, columns = w_quant.shape
    blocks = w_scale.shape[1]
    return pl.pallas_call(
        weights_kernel,
        grid=(3,),
        in_specs=[
            pl.BlockSpec((1, depth, columns), lambda m: (m, 0, 0)),
            pl.BlockSpec((1, blocks, columns), lambda m: (m, 0, 0)),
        ],
        out_specs=[
            pl.BlockSpec((1, depth, columns), lambda m: (m, 0, 0)),
            pl.BlockSpec((1, columns, depth), lambda m: (m, 0, 0)),
        ],
        out_shape=[
            jax.ShapeDtypeStruct((3, depth, columns), jnp.bfloat16),
            jax.ShapeDtypeStruct((3, columns, depth), jnp.bfloat16),
        ],
        compiler_params=params(20),
        cost_estimate=cost(3 * depth * columns, 18 * depth * columns),
        name="scaled_weights",
    )(w_quant, w_scale)


def normed_kernel(idx, tokens, gain, *refs):
    outs, gains = refs[:-1], refs[-1]
    width, part = tokens.shape[1], outs[0].shape[1]
    gains[...] = gain[...].astype(jnp.float32)
    values = tokens[...].astype(jnp.float32)
    inverse = lax.rsqrt(jnp.mean(values * values, axis=-1, keepdims=True) + NORM_EPS)
    size = len(outs) - 1
    for distance in range(size):
        start = pl.multiple_of(idx[distance] * (width // size) + idx[size] * part, part)
        block = tokens[:, pl.ds(start, part)].astype(jnp.float32)
        scale = gains[:, pl.ds(start, part)]
        outs[distance][...] = (block * inverse * scale).astype(jnp.bfloat16)
    outs[size][...] = jnp.broadcast_to(inverse, outs[size].shape)


def normed_blocks(idx, tokens, gain, size, part):
    length, width = tokens.shape
    tile = length // 4
    block = pl.BlockSpec((tile, part), lambda i, idx: (i, 0))
    *blocks, inverse = pl.pallas_call(
        normed_kernel,
        grid_spec=pltpu.PrefetchScalarGridSpec(
            num_scalar_prefetch=1,
            grid=(4,),
            in_specs=[
                pl.BlockSpec((tile, width), lambda i, idx: (i, 0)),
                pl.BlockSpec((1, width), lambda i, idx: (0, 0)),
            ],
            out_specs=[block] * size + [pl.BlockSpec((tile, 128), lambda i, idx: (i, 0))],
            scratch_shapes=[pltpu.VMEM((1, width), jnp.float32)],
        ),
        out_shape=[jax.ShapeDtypeStruct((length, part), jnp.bfloat16)] * size
        + [jax.ShapeDtypeStruct((length, 128), jnp.float32)],
        compiler_params=params(12),
        cost_estimate=cost(8 * length * width, 4 * length * width),
        name="normed_blocks",
    )(idx, tokens, gain)
    return blocks, inverse


def stack_kernel(*refs):
    for place, block in enumerate(refs[:-1]):
        refs[-1][place] = block[...]


def stack(blocks, ties):
    count, shape = len(blocks), blocks[0].shape
    block = pl.BlockSpec(shape, lambda i: (0, 0))
    return pl.pallas_call(
        tied(stack_kernel, count, len(ties)),
        grid=(1,),
        in_specs=[block] * count + tie_specs(ties),
        out_specs=pl.BlockSpec((count, *shape), lambda i: (0, 0, 0)),
        out_shape=jax.ShapeDtypeStruct((count, *shape), blocks[0].dtype),
        compiler_params=params(10),
        cost_estimate=cost(0, 4 * count * shape[0] * shape[1]),
        name="stack",
    )(*blocks, *ties)


def halve_kernel(right, left, right_out, left_out):
    half = right_out.shape[1]
    right_out[...] = right[:, :half]
    left_out[...] = left[:, half:]


def halve(right, left):
    _, rows, wide = right.shape
    result = jax.ShapeDtypeStruct((3, rows // 2, wide), right.dtype)
    whole = pl.BlockSpec(memory_space=pltpu.VMEM)
    return pl.pallas_call(
        halve_kernel,
        in_specs=[whole, whole],
        out_specs=[whole, whole],
        out_shape=[result, result],
        compiler_params=pltpu.CompilerParams(vmem_limit_bytes=4 * MIB),
        cost_estimate=cost(0, 6 * rows * wide),
        name="halve",
    )(right, left)


def turn_kernel(count, idx, mine, other, mine_far, other_far, out):
    length, part = mine_far.shape
    for side, near, last in ((0, mine, mine_far), (1, other, other_far)):
        half = idx[count] * (1 - side) + (1 - idx[count]) * side
        rows = pl.ds(pl.multiple_of(half * part, part), part)
        for place in range(count):
            block = near[place] if place < count - 1 else last[...]
            out[rows, place * length : (place + 1) * length] = block.T


def turn(idx, mine, other, mine_far, other_far):
    near, length, part = mine.shape
    count = near + 1
    stack = pl.BlockSpec(mine.shape, lambda i, idx: (0, 0, 0))
    last = pl.BlockSpec((length, part), lambda i, idx: (0, 0))
    shape = (2 * part, count * length)
    return pl.pallas_call(
        functools.partial(turn_kernel, count),
        grid_spec=pltpu.PrefetchScalarGridSpec(
            num_scalar_prefetch=1,
            grid=(1,),
            in_specs=[stack, stack, last, last],
            out_specs=pl.BlockSpec(shape, lambda i, idx: (0, 0)),
        ),
        out_shape=jax.ShapeDtypeStruct(shape, jnp.bfloat16),
        compiler_params=params(12),
        cost_estimate=cost(2 * count * length * part, 8 * count * length * part),
        name="turn",
    )(idx, mine, other, mine_far, other_far)


def sum_first_kernel(idx, mine, other, weight, weight_other, *outs):
    half, wide = outs[0].shape[1:]
    for chunk in range(2):
        span = slice(chunk * wide, (chunk + 1) * wide)
        product = mm(mine[...], weight[0, :, span]) + mm(other[...], weight_other[0, :, span])
        outs[2 * chunk][0] = product[:half].astype(jnp.bfloat16)
        outs[2 * chunk + 1][0] = product[half:].astype(jnp.bfloat16)


def sum_step_kernel(
    idx, mine_r, other_r, mine_l, other_l, weight, weight_other, from_left, from_right, right, left
):
    length, part = right.shape[1], from_left.shape[1]
    product = mm(mine_r[0], weight[0]) + mm(other_r[0], weight_other[0])
    right[0, :part] = (product[:part] + from_left[0].astype(jnp.float32)).astype(jnp.bfloat16)
    if part < length:
        right[0, part:] = product[part:].astype(jnp.bfloat16)
    product = mm(mine_l[0], weight[0]) + mm(other_l[0], weight_other[0])
    rest = length - part
    left[0, rest:] = (product[rest:] + from_right[0].astype(jnp.float32)).astype(jnp.bfloat16)
    if rest:
        left[0, :rest] = product[:rest].astype(jnp.bfloat16)


def weight_halves(size, part, wide, chunk):
    return [
        pl.BlockSpec((1, part, wide), lambda m, idx: (m, idx[size], chunk)),
        pl.BlockSpec((1, part, wide), lambda m, idx: (m, 1 - idx[size], chunk)),
    ]


def sum_first(idx, size, mine, other, weights):
    length, part = mine.shape
    columns = weights.shape[2]
    half, wide = length // 2, columns // 2
    block = pl.BlockSpec((length, part), lambda m, idx: (0, 0))
    result = jax.ShapeDtypeStruct((3, half, wide), jnp.bfloat16)
    return pl.pallas_call(
        sum_first_kernel,
        grid_spec=pltpu.PrefetchScalarGridSpec(
            num_scalar_prefetch=1,
            grid=(3,),
            in_specs=[block, block, *weight_halves(size, part, columns, 0)],
            out_specs=[pl.BlockSpec((1, half, wide), lambda m, idx: (m, 0, 0))] * 4,
        ),
        out_shape=[result] * 4,
        compiler_params=params(12),
        cost_estimate=cost(12 * length * part * columns, 16 * part * columns),
        name="sum_first",
    )(idx, mine, other, weights, weights)


def sum_step(idx, size, mine, other, places, weights, from_left, from_right, chunk, wide, ties):
    _, length, part = mine.shape
    block_r = pl.BlockSpec((1, length, part), lambda m, idx: (places[0], 0, 0))
    block_l = pl.BlockSpec((1, length, part), lambda m, idx: (places[1], 0, 0))
    came = pl.BlockSpec((1, from_left.shape[1], wide), lambda m, idx: (m, 0, 0))
    whole = jax.ShapeDtypeStruct((3, length, wide), jnp.bfloat16)
    return pl.pallas_call(
        tied(sum_step_kernel, 9, len(ties)),
        grid_spec=pltpu.PrefetchScalarGridSpec(
            num_scalar_prefetch=1,
            grid=(3,),
            in_specs=[
                block_r,
                block_r,
                block_l,
                block_l,
                *weight_halves(size, part, wide, chunk),
                came,
                came,
                *tie_specs(ties),
            ],
            out_specs=[pl.BlockSpec((1, length, wide), lambda m, idx: (m, 0, 0))] * 2,
        ),
        out_shape=[whole, whole],
        compiler_params=params(12),
        cost_estimate=cost(24 * length * part * wide, 24 * part * wide),
        name="sum_step",
    )(idx, mine, other, mine, other, weights, weights, from_left, from_right, *ties)


def attention_kernel(
    idx, mine, other, weight, weight_other, from_left, from_right, d_out, cosine, sine,
    output, dots, pre,
):
    length = mine.shape[1]
    proj = [
        mm(mine[0], weight[m])
        + mm(other[0], weight_other[m])
        + (from_left[m].astype(jnp.float32) + from_right[m].astype(jnp.float32))
        for m in range(3)
    ]
    cos, sin = cosine[...], sine[...]
    half = HEAD_DIM // 2

    def rotate(tensor, angle):
        return tensor * cos + pltpu.roll(tensor, half, 1) * angle

    query = rotate(proj[0], sin).astype(jnp.bfloat16)
    key_rows = rotate(proj[1], sin).astype(jnp.bfloat16)
    value = proj[2].astype(jnp.bfloat16)
    scores = mm_nt(query, key_rows) * (1.0 / math.sqrt(HEAD_DIM))
    causal = lax.broadcasted_iota(jnp.int32, (length, length), 0) >= lax.broadcasted_iota(
        jnp.int32, (length, length), 1
    )
    scores = jnp.where(causal, scores, jnp.float32(-1e30))
    powers = jnp.exp(scores - jnp.max(scores, axis=-1, keepdims=True))
    probs = powers * (1.0 / jnp.sum(powers, axis=-1, keepdims=True))
    probs_low = probs.astype(jnp.bfloat16)
    output[...] = mm(probs_low, value).astype(jnp.bfloat16)
    cotangent = d_out[...]
    d_value = mm_tn(probs_low, cotangent).astype(jnp.bfloat16)
    d_probs = mm_nt(cotangent, value).astype(jnp.bfloat16).astype(jnp.float32)
    inner = jnp.sum(d_probs * probs, axis=-1, keepdims=True)
    d_scores = (probs * (d_probs - inner) * (1.0 / math.sqrt(HEAD_DIM))).astype(jnp.bfloat16)
    d_query = mm(d_scores, key_rows).astype(jnp.bfloat16).astype(jnp.float32)
    d_key = mm_tn(d_scores, query).astype(jnp.bfloat16).astype(jnp.float32)
    pre_query = rotate(d_query, -sin).astype(jnp.bfloat16)
    pre_key = rotate(d_key, -sin).astype(jnp.bfloat16)
    pre[0] = pre_query
    pre[1] = pre_key
    pre[2] = d_value
    product = (
        pre_query.astype(jnp.float32) * proj[0]
        + pre_key.astype(jnp.float32) * proj[1]
        + d_value.astype(jnp.float32) * proj[2]
    )

    @pl.when(pl.program_id(0) == 0)
    def _():
        dots[...] = product

    @pl.when(pl.program_id(0) > 0)
    def _():
        dots[...] += product


def attention(idx, size, mine, other, weights, from_left, from_right, d_out, tables, chunk, wide):
    _, length, part = mine.shape
    heads = wide // HEAD_DIM
    first = chunk * heads
    block = pl.BlockSpec((1, length, part), lambda h, idx: (0, 0, 0))
    table = pl.BlockSpec((length, HEAD_DIM), lambda h, idx: (0, 0))
    stack = pl.BlockSpec((3, length, HEAD_DIM), lambda h, idx: (0, 0, h))
    return pl.pallas_call(
        attention_kernel,
        grid_spec=pltpu.PrefetchScalarGridSpec(
            num_scalar_prefetch=1,
            grid=(heads,),
            in_specs=[
                block,
                block,
                pl.BlockSpec((3, part, HEAD_DIM), lambda h, idx: (0, idx[size], first + h)),
                pl.BlockSpec((3, part, HEAD_DIM), lambda h, idx: (0, 1 - idx[size], first + h)),
                stack,
                stack,
                pl.BlockSpec((length, HEAD_DIM), lambda h, idx: (0, first + h)),
                table,
                table,
            ],
            out_specs=[
                pl.BlockSpec((length, HEAD_DIM), lambda h, idx: (0, h)),
                table,
                stack,
            ],
        ),
        out_shape=[
            jax.ShapeDtypeStruct((length, wide), jnp.bfloat16),
            jax.ShapeDtypeStruct((length, HEAD_DIM), jnp.float32),
            jax.ShapeDtypeStruct((3, length, wide), jnp.bfloat16),
        ],
        compiler_params=params(16),
        cost_estimate=cost(12 * length * part * wide, 24 * part * wide),
        name="attention",
    )(idx, mine, other, weights, weights, from_left, from_right, d_out, *tables)


def grads_kernel(turned, *refs):
    blocks = jnp.concatenate([piece[0] for piece in refs[:-1]], axis=0)
    refs[-1][0] = mm(turned[...], blocks)


def grads_chunk(turned, pieces, before, ties, chunk, wide, columns):
    depth, span = turned.shape
    aliases = {} if before is None else {1 + len(pieces): 0}
    ties = ties if before is None else [before, *ties]
    return pl.pallas_call(
        tied(grads_kernel, 1 + len(pieces), len(ties)),
        grid=(3,),
        in_specs=[
            pl.BlockSpec((depth, span), lambda m: (0, 0)),
            *[pl.BlockSpec((1, *piece.shape[1:]), lambda m: (m, 0, 0)) for piece in pieces],
            *tie_specs(ties),
        ],
        out_specs=pl.BlockSpec((1, depth, wide), lambda m: (m, 0, chunk)),
        out_shape=jax.ShapeDtypeStruct((3, depth, columns), jnp.float32),
        input_output_aliases=aliases,
        compiler_params=params(24),
        cost_estimate=cost(6 * span * depth * wide, 6 * span * wide + 12 * depth * wide),
        name="grads",
    )(turned, *pieces, *ties)


def back(pieces, turned, chunk):
    wide = pieces[0].shape[2]
    rows = [jnp.concatenate([piece[m] for m in range(3)], axis=1) for piece in pieces]
    weight = [turned[m, chunk * wide : (chunk + 1) * wide] for m in range(3)]
    return mm(jnp.concatenate(rows, axis=0), jnp.concatenate(weight, axis=0))


def term_step(turned, pieces, befores, chunk):
    depth, wide = turned.shape[2], pieces[0].shape[2]
    count, rows = len(pieces), pieces[0].shape[1]
    whole = pl.BlockSpec(memory_space=pltpu.VMEM)

    def kernel(turned_ref, *refs):
        total = back(refs[:count], turned_ref, chunk)
        for place in range(count):
            block = total[place * rows : (place + 1) * rows]
            if befores:
                block += refs[count + place][...]
            refs[len(refs) - count + place][...] = block

    return pl.pallas_call(
        kernel,
        in_specs=[whole] * (1 + count + len(befores)),
        out_specs=[whole] * count,
        out_shape=[jax.ShapeDtypeStruct((rows, depth), jnp.float32)] * count,
        compiler_params=pltpu.CompilerParams(vmem_limit_bytes=16 * MIB),
        cost_estimate=cost(6 * count * rows * depth * wide, 12 * count * rows * wide),
        name="term_step",
    )(turned, *pieces, *befores)


def term_last_kernel(count, idx, turned, *refs):
    befores, fars, nears = refs[:2], refs[2:4], refs[4 : 3 + count]
    keeps, sends = refs[-4:-2], refs[-2:]
    half = keeps[0].shape[1]
    last = back(fars, turned, 1)
    for place in range(count):
        for part in range(2):
            span = slice(part * half, (part + 1) * half)
            total = nears[place][span] if place < count - 1 else last[span] + befores[part][...]

            @pl.when(idx[2 * count + 1 + place] == 0)
            def _():
                keeps[part][idx[3 * count + 1 + place]] = total

            @pl.when(idx[2 * count + 1 + place] == 1)
            def _():
                sends[part][idx[3 * count + 1 + place]] = total.astype(jnp.bfloat16)


def term_last(idx, turned, befores, pieces, nears):
    count = len(nears) + 1
    rows, depth = nears[0].shape
    whole = pl.BlockSpec(memory_space=pltpu.VMEM)
    shape = (count // 2, rows // 2, depth)
    return pl.pallas_call(
        functools.partial(term_last_kernel, count),
        in_specs=[pl.BlockSpec(memory_space=pltpu.SMEM)] + [whole] * (count + 4),
        out_specs=[whole] * 4,
        out_shape=[jax.ShapeDtypeStruct(shape, jnp.float32)] * 2
        + [jax.ShapeDtypeStruct(shape, jnp.bfloat16)] * 2,
        compiler_params=pltpu.CompilerParams(vmem_limit_bytes=12 * MIB),
        cost_estimate=cost(rows * depth * depth, 12 * count * rows * depth),
        name="term_last",
    )(idx, turned, *befores, *pieces, *nears)


def split_kernel(column, group, idx, keep, came, keep_out, send_out):
    own = idx[column]
    for block in range(keep_out.shape[0]):
        high, low = block // group, block % group
        mine = (2 * high + own) * group + low
        other = (2 * high + 1 - own) * group + low
        keep_out[block] = keep[mine] + came[mine].astype(jnp.float32)
        send_out[block] = (keep[other] + came[other].astype(jnp.float32)).astype(jnp.bfloat16)


def split_sum(idx, column, group, keep, came):
    whole = pl.BlockSpec(memory_space=pltpu.VMEM)
    shape = (keep.shape[0] // 2, *keep.shape[1:])
    return pl.pallas_call(
        functools.partial(split_kernel, column, group),
        in_specs=[pl.BlockSpec(memory_space=pltpu.SMEM), whole, whole],
        out_specs=[whole, whole],
        out_shape=[
            jax.ShapeDtypeStruct(shape, jnp.float32),
            jax.ShapeDtypeStruct(shape, jnp.bfloat16),
        ],
        compiler_params=pltpu.CompilerParams(vmem_limit_bytes=4 * MIB),
        cost_estimate=cost(0, 8 * keep.shape[0] * keep.shape[1] * keep.shape[2]),
        name="split_sum",
    )(idx, keep, came)


def order_kernel(column, idx, keep, came, *outs):
    for turn, out in enumerate(outs):
        block = idx[column + turn]
        out[...] = (keep[block] + came[block].astype(jnp.float32)).astype(jnp.bfloat16)


def order_sum(idx, column, keep, came):
    whole = pl.BlockSpec(memory_space=pltpu.VMEM)
    count = keep.shape[0]
    return pl.pallas_call(
        functools.partial(order_kernel, column),
        in_specs=[pl.BlockSpec(memory_space=pltpu.SMEM), whole, whole],
        out_specs=[whole] * count,
        out_shape=[jax.ShapeDtypeStruct(keep.shape[1:], jnp.bfloat16)] * count,
        compiler_params=pltpu.CompilerParams(vmem_limit_bytes=4 * MIB),
        cost_estimate=cost(0, 8 * count * keep.shape[1] * keep.shape[2]),
        name="order_sum",
    )(idx, keep, came)


def finish_kernel(column, width, idx, tokens, gain, inverse, dots, *refs):
    came, out, gains = refs[:-2], refs[-2], refs[-1]
    rows, depth = came[0].shape
    group = out.shape[1] // depth
    gains[...] = gain[...].astype(jnp.float32)
    for turn in range(group):
        features = pl.ds(pl.multiple_of(idx[column + turn] * depth, depth), depth)
        for part in range(len(came) // group):
            span = slice(part * rows, (part + 1) * rows)
            scale = inverse[span, :1]
            upstream = came[part * group + turn][...].astype(jnp.float32)
            values = tokens[span, features].astype(jnp.float32)
            common = scale * scale * dots[span] / width
            out[span, features] = (
                scale * gains[:, features] * upstream - values * common
            ).astype(jnp.bfloat16)


def finish(idx, column, tokens, gain, inverse, dots, came, share):
    length, width = tokens.shape
    node = column + share // came[0].shape[1]
    whole = pl.BlockSpec(memory_space=pltpu.VMEM)
    return pl.pallas_call(
        functools.partial(finish_kernel, column, width),
        grid_spec=pltpu.PrefetchScalarGridSpec(
            num_scalar_prefetch=1,
            grid=(1,),
            in_specs=[
                pl.BlockSpec((length, share), lambda i, idx: (0, idx[node])),
                pl.BlockSpec((1, share), lambda i, idx: (0, idx[node])),
                *[whole] * (2 + len(came)),
            ],
            out_specs=pl.BlockSpec((length, share), lambda i, idx: (0, 0)),
            scratch_shapes=[pltpu.VMEM((1, share), jnp.float32)],
        ),
        out_shape=jax.ShapeDtypeStruct((length, share), jnp.bfloat16),
        compiler_params=params(12),
        cost_estimate=cost(8 * length * share, 6 * length * share),
        name="finish",
    )(idx, tokens, gain, inverse, dots, *came)


def local(tokens, norm_gain, w_quant, w_scale, d_out):
    length, width = tokens.shape
    depth, columns = w_quant.shape[1:]
    size, nodes = lax.axis_size("local"), lax.axis_size("node")
    here, node = lax.axis_index("local"), lax.axis_index("node")
    wide = columns // 2
    far = size // 2
    group = size // nodes
    core = node % 2

    order = ring_order(size)
    distances = ring_distances(size)
    table = jnp.asarray(index_table(size, nodes))
    idx = lax.dynamic_index_in_dim(table, node * size + here, 0, keepdims=False)

    def shift(array, distance):
        moves = [(order[i], order[(i + distance) % size]) for i in range(size)]
        return lax.ppermute(array, "local", moves)

    def swap(array, bit):
        return lax.ppermute(array, "node", [(n, n ^ bit) for n in range(nodes)])

    blocks, inverse_rms = normed_blocks(idx, tokens, norm_gain[None], size, depth // 2)
    mine_far = shift(blocks[far], far)
    other_far = swap(mine_far, 1)
    weights, turned = scaled_weights(w_quant, w_scale)
    firsts = sum_first(idx, size, mine_far, other_far, weights)
    mine = stack(
        [shift(blocks[-d % size], -d) if d else blocks[0] for d in distances[:-1]], firsts[:1]
    )
    other = swap(mine, 1)

    rows_turned = turn(idx, mine, other, mine_far, other_far)

    tables = rope_tables(length, HEAD_DIM)
    arrived = []
    for chunk in range(2):
        right, left = firsts[2 * chunk : 2 * chunk + 2]
        for distance in range(far - 1, -1, -1):
            from_left, from_right = shift(right, 1), shift(left, -1)
            if distance:
                places = distances.index(distance), distances.index(-distance)
                ties = [rows_turned] if distance == 1 else []
                right, left = sum_step(
                    idx, size, mine, other, places, weights, from_left, from_right, chunk, wide, ties
                )
        arrived.append((from_left, from_right))

    outputs, sets, dots = [], [], 0.0
    for chunk in range(2):
        output, product, pre = attention(
            idx, size, mine, other, weights, *arrived[chunk], d_out, tables, chunk, wide
        )
        outputs.append(output)
        sets.append(pre)
        dots += jnp.sum(product, axis=-1, keepdims=True)
    bit = 1
    while bit < nodes:
        dots = dots + swap(dots, bit)
        bit *= 2

    def sum_nodes(keep, send):
        column = 4 * size + 1
        bit = 1
        while 2 * bit < nodes:
            keep, send = split_sum(idx, column, group, keep, swap(send, bit))
            column += 1
            bit *= 2
        return order_sum(idx, column, keep, swap(send, bit))

    def relocate(blocks):
        came = []
        for turn, block in enumerate(blocks):
            moves = [
                (n * size + s, (s // group) * size + n * group + (s + turn) % group)
                for n in range(nodes)
                for s in range(size)
            ]
            came.append(lax.ppermute(block, ("node", "local"), moves))
        return came

    gathered = [[block] for block in sets]
    moving = [(block, block) for block in sets]
    terms = [[], []]
    for step in range(1, far + 1):
        for chunk in range(2):
            right, left = moving[chunk]
            if step == far:
                right, left = halve(right, left)
            right, left = shift(right, 1), shift(left, -1)
            moving[chunk] = right, left
            gathered[chunk] += [right, left]
            if step < far:
                pieces = gathered[chunk] if step == 1 else [right, left]
                known = len(terms[chunk])
                befores = terms[0][known : known + len(pieces)] if chunk else []
                terms[chunk] += term_step(turned, pieces, befores, chunk)
            elif chunk == 0:
                lasts = term_step(turned, [right, left], [], 0)
    keep_0, keep_1, send_0, send_1 = term_last(idx, turned, lasts, gathered[1][-2:], terms[1])
    first, second = sum_nodes(keep_0, send_0), sum_nodes(keep_1, send_1)
    came = [*relocate(first), *relocate(second)]
    column = idx.shape[0] - 1 - group
    d_tokens = finish(
        idx, column, tokens, norm_gain[None], inverse_rms, dots, came, width // nodes
    )
    sums = [first[0], second[0]]
    grads = grads_chunk(rows_turned, gathered[0], None, sums, 0, wide, columns)
    grads = grads_chunk(rows_turned, gathered[1], grads, [], 1, wide, columns)
    return (jnp.concatenate(outputs, axis=-1), d_tokens, grads)


def solution(mesh):
    placed = (
        P("local", None),
        P(),
        P(None, "local", "node"),
        P(None, "local", "node"),
        P("local", "node"),
    )
    return jax.shard_map(
        local,
        mesh=mesh,
        in_specs=placed,
        out_specs=(P("local", "node"), P("local", "node"), P(None, "local", "node")),
        check_vma=False,
    )
```

```python
import functools
import math

import jax
import jax.numpy as jnp
import numpy as np
from jax import lax
from jax.experimental import pallas as pl
from jax.experimental.pallas import tpu as pltpu
from jax.sharding import PartitionSpec as P

HEAD_DIM = 128
NORM_EPS = 1e-05
MIB = 1024 * 1024


def params(limit):
    return pltpu.CompilerParams(
        dimension_semantics=("arbitrary",), vmem_limit_bytes=limit * MIB
    )


def tied(kernel, inputs, ties):
    def inner(*refs):
        kernel(*refs[:inputs], *refs[inputs + ties :])

    return inner


def tie_specs(ties):
    return [pl.BlockSpec(memory_space=pl.ANY)] * len(ties)


def cost(flops, moved):
    return pl.CostEstimate(flops=flops, bytes_accessed=moved, transcendentals=0)


def mm(a, b):
    return jnp.dot(a, b, preferred_element_type=jnp.float32)


def mm_nt(a, b):
    return lax.dot_general(a, b, (((1,), (1,)), ((), ())), preferred_element_type=jnp.float32)


def mm_tn(a, b):
    return lax.dot_general(a, b, (((0,), (0,)), ((), ())), preferred_element_type=jnp.float32)


def rope_tables(length, width):
    position = jnp.arange(length).astype(jnp.float32)[:, None]
    frequency = jnp.exp(
        jnp.arange(width // 2).astype(jnp.float32) * (-2.0 * math.log(10000.0) / width)
    )
    angle = position * frequency[None, :]
    cosine, sine = jnp.cos(angle), jnp.sin(angle)
    return (
        jnp.concatenate([cosine, cosine], axis=-1),
        jnp.concatenate([-sine, sine], axis=-1),
    )


def ring_order(size):
    return [*range(0, size, 2), *reversed(range(1, size, 2))]


def ring_distances(size):
    far = size // 2
    distances = [0]
    for step in range(1, far):
        distances += [-step, step]
    return [*distances, far]


def group_of(nodes):
    bits = nodes.bit_length() - 1
    return [sum((node >> bit & 1) << (bits - 1 - bit) for bit in range(bits)) for node in range(nodes)]


def index_table(size, nodes):
    order, group = ring_order(size), size // nodes
    rows = []
    for node in range(nodes):
        for here in range(size):
            place = order.index(here)
            seqs = [order[(place + distance) % size] for distance in ring_distances(size)]
            owner = [group_of(nodes).index(seq // group) for seq in seqs]
            rows.append(
                [order[(place + distance) % size] for distance in range(size)]
                + [node % 2]
                + seqs
                + [owner_ % 2 ^ node % 2 for owner_ in owner]
                + [(o // 2) * group + seq % group for o, seq in zip(owner, seqs)]
                + [node >> level & 1 for level in range(1, nodes.bit_length() - 1)]
                + [(here + turn) % group for turn in range(group)]
                + [(here - turn) % group for turn in range(group)]
                + [node]
            )
    return np.array(rows, np.int32)


def weights_kernel(quant, scale, out, turned):
    blocks = scale.shape[1]
    rows = quant.shape[1] // blocks
    scales = scale[0].astype(jnp.float32)
    for block in range(blocks):
        span = slice(block * rows, (block + 1) * rows)
        scaled = (quant[0, span].astype(jnp.float32) * scales[block : block + 1]).astype(jnp.bfloat16)
        out[0, span] = scaled
        turned[0, :, span] = scaled.T


def scaled_weights(w_quant, w_scale):
    _, depth, columns = w_quant.shape
    blocks = w_scale.shape[1]
    return pl.pallas_call(
        weights_kernel,
        grid=(3,),
        in_specs=[
            pl.BlockSpec((1, depth, columns), lambda m: (m, 0, 0)),
            pl.BlockSpec((1, blocks, columns), lambda m: (m, 0, 0)),
        ],
        out_specs=[
            pl.BlockSpec((1, depth, columns), lambda m: (m, 0, 0)),
            pl.BlockSpec((1, columns, depth), lambda m: (m, 0, 0)),
        ],
        out_shape=[
            jax.ShapeDtypeStruct((3, depth, columns), jnp.bfloat16),
            jax.ShapeDtypeStruct((3, columns, depth), jnp.bfloat16),
        ],
        compiler_params=params(20),
        cost_estimate=cost(3 * depth * columns, 18 * depth * columns),
        name="scaled_weights",
    )(w_quant, w_scale)


def normed_kernel(idx, tokens, gain, *refs):
    outs, gains = refs[:-1], refs[-1]
    width, part = tokens.shape[1], outs[0].shape[1]
    gains[...] = gain[...].astype(jnp.float32)
    values = tokens[...].astype(jnp.float32)
    inverse = lax.rsqrt(jnp.mean(values * values, axis=-1, keepdims=True) + NORM_EPS)
    size = len(outs) - 1
    for distance in range(size):
        start = pl.multiple_of(idx[distance] * (width // size) + idx[size] * part, part)
        block = tokens[:, pl.ds(start, part)].astype(jnp.float32)
        scale = gains[:, pl.ds(start, part)]
        outs[distance][...] = (block * inverse * scale).astype(jnp.bfloat16)
    outs[size][...] = jnp.broadcast_to(inverse, outs[size].shape)


def normed_blocks(idx, tokens, gain, size, part):
    length, width = tokens.shape
    tile = length // 4
    block = pl.BlockSpec((tile, part), lambda i, idx: (i, 0))
    *blocks, inverse = pl.pallas_call(
        normed_kernel,
        grid_spec=pltpu.PrefetchScalarGridSpec(
            num_scalar_prefetch=1,
            grid=(4,),
            in_specs=[
                pl.BlockSpec((tile, width), lambda i, idx: (i, 0)),
                pl.BlockSpec((1, width), lambda i, idx: (0, 0)),
            ],
            out_specs=[block] * size + [pl.BlockSpec((tile, 128), lambda i, idx: (i, 0))],
            scratch_shapes=[pltpu.VMEM((1, width), jnp.float32)],
        ),
        out_shape=[jax.ShapeDtypeStruct((length, part), jnp.bfloat16)] * size
        + [jax.ShapeDtypeStruct((length, 128), jnp.float32)],
        compiler_params=params(12),
        cost_estimate=cost(8 * length * width, 4 * length * width),
        name="normed_blocks",
    )(idx, tokens, gain)
    return blocks, inverse


def stack_kernel(*refs):
    for place, block in enumerate(refs[:-1]):
        refs[-1][place] = block[...]


def stack(blocks, ties):
    count, shape = len(blocks), blocks[0].shape
    block = pl.BlockSpec(shape, lambda i: (0, 0))
    return pl.pallas_call(
        tied(stack_kernel, count, len(ties)),
        grid=(1,),
        in_specs=[block] * count + tie_specs(ties),
        out_specs=pl.BlockSpec((count, *shape), lambda i: (0, 0, 0)),
        out_shape=jax.ShapeDtypeStruct((count, *shape), blocks[0].dtype),
        compiler_params=params(10),
        cost_estimate=cost(0, 4 * count * shape[0] * shape[1]),
        name="stack",
    )(*blocks, *ties)


def halve_kernel(right, left, right_out, left_out):
    half = right_out.shape[1]
    right_out[...] = right[:, :half]
    left_out[...] = left[:, half:]


def halve(right, left, ties):
    _, rows, wide = right.shape
    result = jax.ShapeDtypeStruct((3, rows // 2, wide), right.dtype)
    whole = pl.BlockSpec(memory_space=pltpu.VMEM)
    return pl.pallas_call(
        tied(halve_kernel, 2, len(ties)),
        in_specs=[whole, whole] + tie_specs(ties),
        out_specs=[whole, whole],
        out_shape=[result, result],
        compiler_params=pltpu.CompilerParams(vmem_limit_bytes=4 * MIB),
        cost_estimate=cost(0, 6 * rows * wide),
        name="halve",
    )(right, left, *ties)


def turn_kernel(count, idx, mine, other, mine_far, other_far, out):
    length, part = mine_far.shape
    for side, near, last in ((0, mine, mine_far), (1, other, other_far)):
        half = idx[count] * (1 - side) + (1 - idx[count]) * side
        rows = pl.ds(pl.multiple_of(half * part, part), part)
        for place in range(count):
            block = near[place] if place < count - 1 else last[...]
            out[rows, place * length : (place + 1) * length] = block.T


def turn(idx, mine, other, mine_far, other_far):
    near, length, part = mine.shape
    count = near + 1
    stack = pl.BlockSpec(mine.shape, lambda i, idx: (0, 0, 0))
    last = pl.BlockSpec((length, part), lambda i, idx: (0, 0))
    shape = (2 * part, count * length)
    return pl.pallas_call(
        functools.partial(turn_kernel, count),
        grid_spec=pltpu.PrefetchScalarGridSpec(
            num_scalar_prefetch=1,
            grid=(1,),
            in_specs=[stack, stack, last, last],
            out_specs=pl.BlockSpec(shape, lambda i, idx: (0, 0)),
        ),
        out_shape=jax.ShapeDtypeStruct(shape, jnp.bfloat16),
        compiler_params=params(12),
        cost_estimate=cost(2 * count * length * part, 8 * count * length * part),
        name="turn",
    )(idx, mine, other, mine_far, other_far)


def sum_first_kernel(idx, mine, other, weight, weight_other, *outs):
    half, wide = outs[0].shape[1:]
    for chunk in range(2):
        span = slice(chunk * wide, (chunk + 1) * wide)
        product = mm(mine[...], weight[0, :, span]) + mm(other[...], weight_other[0, :, span])
        outs[2 * chunk][0] = product[:half].astype(jnp.bfloat16)
        outs[2 * chunk + 1][0] = product[half:].astype(jnp.bfloat16)


def sum_step_kernel(
    idx, mine_r, other_r, mine_l, other_l, weight, weight_other, from_left, from_right, right, left
):
    length, part = right.shape[1], from_left.shape[1]
    product = mm(mine_r[0], weight[0]) + mm(other_r[0], weight_other[0])
    right[0, :part] = (product[:part] + from_left[0].astype(jnp.float32)).astype(jnp.bfloat16)
    if part < length:
        right[0, part:] = product[part:].astype(jnp.bfloat16)
    product = mm(mine_l[0], weight[0]) + mm(other_l[0], weight_other[0])
    rest = length - part
    left[0, rest:] = (product[rest:] + from_right[0].astype(jnp.float32)).astype(jnp.bfloat16)
    if rest:
        left[0, :rest] = product[:rest].astype(jnp.bfloat16)


def weight_halves(size, part, wide, chunk):
    return [
        pl.BlockSpec((1, part, wide), lambda m, idx: (m, idx[size], chunk)),
        pl.BlockSpec((1, part, wide), lambda m, idx: (m, 1 - idx[size], chunk)),
    ]


def sum_first(idx, size, mine, other, weights):
    length, part = mine.shape
    columns = weights.shape[2]
    half, wide = length // 2, columns // 2
    block = pl.BlockSpec((length, part), lambda m, idx: (0, 0))
    result = jax.ShapeDtypeStruct((3, half, wide), jnp.bfloat16)
    return pl.pallas_call(
        sum_first_kernel,
        grid_spec=pltpu.PrefetchScalarGridSpec(
            num_scalar_prefetch=1,
            grid=(3,),
            in_specs=[block, block, *weight_halves(size, part, columns, 0)],
            out_specs=[pl.BlockSpec((1, half, wide), lambda m, idx: (m, 0, 0))] * 4,
        ),
        out_shape=[result] * 4,
        compiler_params=params(12),
        cost_estimate=cost(12 * length * part * columns, 16 * part * columns),
        name="sum_first",
    )(idx, mine, other, weights, weights)


def sum_step(idx, size, mine, other, places, weights, from_left, from_right, chunk, wide, ties):
    _, length, part = mine.shape
    block_r = pl.BlockSpec((1, length, part), lambda m, idx: (places[0], 0, 0))
    block_l = pl.BlockSpec((1, length, part), lambda m, idx: (places[1], 0, 0))
    came = pl.BlockSpec((1, from_left.shape[1], wide), lambda m, idx: (m, 0, 0))
    whole = jax.ShapeDtypeStruct((3, length, wide), jnp.bfloat16)
    return pl.pallas_call(
        tied(sum_step_kernel, 9, len(ties)),
        grid_spec=pltpu.PrefetchScalarGridSpec(
            num_scalar_prefetch=1,
            grid=(3,),
            in_specs=[
                block_r,
                block_r,
                block_l,
                block_l,
                *weight_halves(size, part, wide, chunk),
                came,
                came,
                *tie_specs(ties),
            ],
            out_specs=[pl.BlockSpec((1, length, wide), lambda m, idx: (m, 0, 0))] * 2,
        ),
        out_shape=[whole, whole],
        compiler_params=params(12),
        cost_estimate=cost(24 * length * part * wide, 24 * part * wide),
        name="sum_step",
    )(idx, mine, other, mine, other, weights, weights, from_left, from_right, *ties)


def attention_kernel(
    idx, mine, other, weight, weight_other, from_left, from_right, d_out, cosine, sine,
    output, dots, pre,
):
    length = mine.shape[1]
    proj = [
        mm(mine[0], weight[m])
        + mm(other[0], weight_other[m])
        + (from_left[m].astype(jnp.float32) + from_right[m].astype(jnp.float32))
        for m in range(3)
    ]
    cos, sin = cosine[...], sine[...]
    half = HEAD_DIM // 2

    def rotate(tensor, angle):
        return tensor * cos + pltpu.roll(tensor, half, 1) * angle

    query = rotate(proj[0], sin).astype(jnp.bfloat16)
    key_rows = rotate(proj[1], sin).astype(jnp.bfloat16)
    value = proj[2].astype(jnp.bfloat16)
    scores = mm_nt(query, key_rows) * (1.0 / math.sqrt(HEAD_DIM))
    causal = lax.broadcasted_iota(jnp.int32, (length, length), 0) >= lax.broadcasted_iota(
        jnp.int32, (length, length), 1
    )
    scores = jnp.where(causal, scores, jnp.float32(-1e30))
    powers = jnp.exp(scores - jnp.max(scores, axis=-1, keepdims=True))
    probs = powers * (1.0 / jnp.sum(powers, axis=-1, keepdims=True))
    probs_low = probs.astype(jnp.bfloat16)
    output[...] = mm(probs_low, value).astype(jnp.bfloat16)
    cotangent = d_out[...]
    d_value = mm_tn(probs_low, cotangent).astype(jnp.bfloat16)
    d_probs = mm_nt(cotangent, value).astype(jnp.bfloat16).astype(jnp.float32)
    inner = jnp.sum(d_probs * probs, axis=-1, keepdims=True)
    d_scores = (probs * (d_probs - inner) * (1.0 / math.sqrt(HEAD_DIM))).astype(jnp.bfloat16)
    d_query = mm(d_scores, key_rows).astype(jnp.bfloat16).astype(jnp.float32)
    d_key = mm_tn(d_scores, query).astype(jnp.bfloat16).astype(jnp.float32)
    pre_query = rotate(d_query, -sin).astype(jnp.bfloat16)
    pre_key = rotate(d_key, -sin).astype(jnp.bfloat16)
    pre[0] = pre_query
    pre[1] = pre_key
    pre[2] = d_value
    product = (
        pre_query.astype(jnp.float32) * proj[0]
        + pre_key.astype(jnp.float32) * proj[1]
        + d_value.astype(jnp.float32) * proj[2]
    )

    @pl.when(pl.program_id(0) == 0)
    def _():
        dots[...] = product

    @pl.when(pl.program_id(0) > 0)
    def _():
        dots[...] += product


def attention(idx, size, mine, other, weights, from_left, from_right, d_out, tables, chunk, wide):
    _, length, part = mine.shape
    heads = wide // HEAD_DIM
    first = chunk * heads
    block = pl.BlockSpec((1, length, part), lambda h, idx: (0, 0, 0))
    table = pl.BlockSpec((length, HEAD_DIM), lambda h, idx: (0, 0))
    stack = pl.BlockSpec((3, length, HEAD_DIM), lambda h, idx: (0, 0, h))
    return pl.pallas_call(
        attention_kernel,
        grid_spec=pltpu.PrefetchScalarGridSpec(
            num_scalar_prefetch=1,
            grid=(heads,),
            in_specs=[
                block,
                block,
                pl.BlockSpec((3, part, HEAD_DIM), lambda h, idx: (0, idx[size], first + h)),
                pl.BlockSpec((3, part, HEAD_DIM), lambda h, idx: (0, 1 - idx[size], first + h)),
                stack,
                stack,
                pl.BlockSpec((length, HEAD_DIM), lambda h, idx: (0, first + h)),
                table,
                table,
            ],
            out_specs=[
                pl.BlockSpec((length, HEAD_DIM), lambda h, idx: (0, h)),
                table,
                stack,
            ],
        ),
        out_shape=[
            jax.ShapeDtypeStruct((length, wide), jnp.bfloat16),
            jax.ShapeDtypeStruct((length, HEAD_DIM), jnp.float32),
            jax.ShapeDtypeStruct((3, length, wide), jnp.bfloat16),
        ],
        compiler_params=params(16),
        cost_estimate=cost(12 * length * part * wide, 24 * part * wide),
        name="attention",
    )(idx, mine, other, weights, weights, from_left, from_right, d_out, *tables)


def grads_kernel(turned, *refs):
    blocks = jnp.concatenate([piece[0] for piece in refs[:-1]], axis=0)
    refs[-1][0] = mm(turned[...], blocks)


def grads_chunk(turned, pieces, before, ties, chunk, wide, columns):
    depth, span = turned.shape
    aliases = {} if before is None else {1 + len(pieces): 0}
    ties = ties if before is None else [before, *ties]
    return pl.pallas_call(
        tied(grads_kernel, 1 + len(pieces), len(ties)),
        grid=(3,),
        in_specs=[
            pl.BlockSpec((depth, span), lambda m: (0, 0)),
            *[pl.BlockSpec((1, *piece.shape[1:]), lambda m: (m, 0, 0)) for piece in pieces],
            *tie_specs(ties),
        ],
        out_specs=pl.BlockSpec((1, depth, wide), lambda m: (m, 0, chunk)),
        out_shape=jax.ShapeDtypeStruct((3, depth, columns), jnp.float32),
        input_output_aliases=aliases,
        compiler_params=params(24),
        cost_estimate=cost(6 * span * depth * wide, 6 * span * wide + 12 * depth * wide),
        name="grads",
    )(turned, *pieces, *ties)


def back(pieces, turned, chunk):
    wide = pieces[0].shape[2]
    rows = [jnp.concatenate([piece[m] for m in range(3)], axis=1) for piece in pieces]
    weight = [turned[m, chunk * wide : (chunk + 1) * wide] for m in range(3)]
    return mm(jnp.concatenate(rows, axis=0), jnp.concatenate(weight, axis=0))


def term_step(turned, pieces, befores, chunk):
    depth, wide = turned.shape[2], pieces[0].shape[2]
    count, rows = len(pieces), pieces[0].shape[1]
    whole = pl.BlockSpec(memory_space=pltpu.VMEM)

    def kernel(turned_ref, *refs):
        total = back(refs[:count], turned_ref, chunk)
        for place in range(count):
            block = total[place * rows : (place + 1) * rows]
            if befores:
                block += refs[count + place][...]
            refs[len(refs) - count + place][...] = block

    return pl.pallas_call(
        kernel,
        in_specs=[whole] * (1 + count + len(befores)),
        out_specs=[whole] * count,
        out_shape=[jax.ShapeDtypeStruct((rows, depth), jnp.float32)] * count,
        compiler_params=pltpu.CompilerParams(vmem_limit_bytes=16 * MIB),
        cost_estimate=cost(6 * count * rows * depth * wide, 12 * count * rows * wide),
        name="term_step",
    )(turned, *pieces, *befores)


def term_last_kernel(count, idx, turned, *refs):
    befores, fars, nears = refs[:2], refs[2:4], refs[4 : 3 + count]
    keeps, sends = refs[-4:-2], refs[-2:]
    half = keeps[0].shape[1]
    last = back(fars, turned, 1)
    for place in range(count):
        for part in range(2):
            span = slice(part * half, (part + 1) * half)
            total = nears[place][span] if place < count - 1 else last[span] + befores[part][...]

            @pl.when(idx[2 * count + 1 + place] == 0)
            def _():
                keeps[part][idx[3 * count + 1 + place]] = total

            @pl.when(idx[2 * count + 1 + place] == 1)
            def _():
                sends[part][idx[3 * count + 1 + place]] = total.astype(jnp.bfloat16)


def term_last(idx, turned, befores, pieces, nears):
    count = len(nears) + 1
    rows, depth = nears[0].shape
    whole = pl.BlockSpec(memory_space=pltpu.VMEM)
    shape = (count // 2, rows // 2, depth)
    return pl.pallas_call(
        functools.partial(term_last_kernel, count),
        in_specs=[pl.BlockSpec(memory_space=pltpu.SMEM)] + [whole] * (count + 4),
        out_specs=[whole] * 4,
        out_shape=[jax.ShapeDtypeStruct(shape, jnp.float32)] * 2
        + [jax.ShapeDtypeStruct(shape, jnp.bfloat16)] * 2,
        compiler_params=pltpu.CompilerParams(vmem_limit_bytes=12 * MIB),
        cost_estimate=cost(rows * depth * depth, 12 * count * rows * depth),
        name="term_last",
    )(idx, turned, *befores, *pieces, *nears)


def split_kernel(column, group, idx, keep, came, keep_out, send_out):
    own = idx[column]
    for block in range(keep_out.shape[0]):
        high, low = block // group, block % group
        mine = (2 * high + own) * group + low
        other = (2 * high + 1 - own) * group + low
        keep_out[block] = keep[mine] + came[mine].astype(jnp.float32)
        send_out[block] = (keep[other] + came[other].astype(jnp.float32)).astype(jnp.bfloat16)


def split_sum(idx, column, group, keep, came):
    whole = pl.BlockSpec(memory_space=pltpu.VMEM)
    shape = (keep.shape[0] // 2, *keep.shape[1:])
    return pl.pallas_call(
        functools.partial(split_kernel, column, group),
        in_specs=[pl.BlockSpec(memory_space=pltpu.SMEM), whole, whole],
        out_specs=[whole, whole],
        out_shape=[
            jax.ShapeDtypeStruct(shape, jnp.float32),
            jax.ShapeDtypeStruct(shape, jnp.bfloat16),
        ],
        compiler_params=pltpu.CompilerParams(vmem_limit_bytes=4 * MIB),
        cost_estimate=cost(0, 8 * keep.shape[0] * keep.shape[1] * keep.shape[2]),
        name="split_sum",
    )(idx, keep, came)


def order_kernel(column, idx, keep, came, *outs):
    for turn, out in enumerate(outs):
        block = idx[column + turn]
        out[...] = (keep[block] + came[block].astype(jnp.float32)).astype(jnp.bfloat16)


def order_sum(idx, column, keep, came):
    whole = pl.BlockSpec(memory_space=pltpu.VMEM)
    count = keep.shape[0]
    return pl.pallas_call(
        functools.partial(order_kernel, column),
        in_specs=[pl.BlockSpec(memory_space=pltpu.SMEM), whole, whole],
        out_specs=[whole] * count,
        out_shape=[jax.ShapeDtypeStruct(keep.shape[1:], jnp.bfloat16)] * count,
        compiler_params=pltpu.CompilerParams(vmem_limit_bytes=4 * MIB),
        cost_estimate=cost(0, 8 * count * keep.shape[1] * keep.shape[2]),
        name="order_sum",
    )(idx, keep, came)


def finish_kernel(column, width, idx, tokens, gain, inverse, dots, *refs):
    came, out, gains = refs[:-2], refs[-2], refs[-1]
    rows, depth = came[0].shape
    group = out.shape[1] // depth
    gains[...] = gain[...].astype(jnp.float32)
    for turn in range(group):
        features = pl.ds(pl.multiple_of(idx[column + turn] * depth, depth), depth)
        for part in range(len(came) // group):
            span = slice(part * rows, (part + 1) * rows)
            scale = inverse[span, :1]
            upstream = came[part * group + turn][...].astype(jnp.float32)
            values = tokens[span, features].astype(jnp.float32)
            common = scale * scale * dots[span] / width
            out[span, features] = (
                scale * gains[:, features] * upstream - values * common
            ).astype(jnp.bfloat16)


def finish(idx, column, tokens, gain, inverse, dots, came, share):
    length, width = tokens.shape
    node = column + share // came[0].shape[1]
    whole = pl.BlockSpec(memory_space=pltpu.VMEM)
    return pl.pallas_call(
        functools.partial(finish_kernel, column, width),
        grid_spec=pltpu.PrefetchScalarGridSpec(
            num_scalar_prefetch=1,
            grid=(1,),
            in_specs=[
                pl.BlockSpec((length, share), lambda i, idx: (0, idx[node])),
                pl.BlockSpec((1, share), lambda i, idx: (0, idx[node])),
                *[whole] * (2 + len(came)),
            ],
            out_specs=pl.BlockSpec((length, share), lambda i, idx: (0, 0)),
            scratch_shapes=[pltpu.VMEM((1, share), jnp.float32)],
        ),
        out_shape=jax.ShapeDtypeStruct((length, share), jnp.bfloat16),
        compiler_params=params(12),
        cost_estimate=cost(8 * length * share, 6 * length * share),
        name="finish",
    )(idx, tokens, gain, inverse, dots, *came)


def local(tokens, norm_gain, w_quant, w_scale, d_out):
    length, width = tokens.shape
    depth, columns = w_quant.shape[1:]
    size, nodes = lax.axis_size("local"), lax.axis_size("node")
    here, node = lax.axis_index("local"), lax.axis_index("node")
    wide = columns // 2
    far = size // 2
    group, groups = size // nodes, group_of(nodes)

    order = ring_order(size)
    distances = ring_distances(size)
    table = jnp.asarray(index_table(size, nodes))
    idx = lax.dynamic_index_in_dim(table, node * size + here, 0, keepdims=False)

    def shift(array, distance):
        moves = [(order[i], order[(i + distance) % size]) for i in range(size)]
        return lax.ppermute(array, "local", moves)

    def swap(array, bit):
        return lax.ppermute(array, "node", [(n, n ^ bit) for n in range(nodes)])

    blocks, inverse_rms = normed_blocks(idx, tokens, norm_gain[None], size, depth // 2)
    mine_far = shift(blocks[far], far)
    other_far = swap(mine_far, 1)
    weights, turned = scaled_weights(w_quant, w_scale)
    firsts = sum_first(idx, size, mine_far, other_far, weights)
    mine = stack(
        [shift(blocks[-d % size], -d) if d else blocks[0] for d in distances[:-1]], firsts[:1]
    )
    other = swap(mine, 1)

    rows_turned = turn(idx, mine, other, mine_far, other_far)

    tables = rope_tables(length, HEAD_DIM)
    arrived = []
    for chunk in range(2):
        right, left = firsts[2 * chunk : 2 * chunk + 2]
        for distance in range(far - 1, -1, -1):
            from_left, from_right = shift(right, 1), shift(left, -1)
            if distance:
                places = distances.index(distance), distances.index(-distance)
                ties = [rows_turned] if distance == 1 else []
                right, left = sum_step(
                    idx, size, mine, other, places, weights, from_left, from_right, chunk, wide, ties
                )
        arrived.append((from_left, from_right))

    outputs, sets, dots = [], [], 0.0
    for chunk in range(2):
        output, product, pre = attention(
            idx, size, mine, other, weights, *arrived[chunk], d_out, tables, chunk, wide
        )
        outputs.append(output)
        sets.append(pre)
        dots += jnp.sum(product, axis=-1, keepdims=True)
    bit = 1
    while bit < nodes:
        dots = dots + swap(dots, bit)
        bit *= 2

    def sum_nodes(keep, send):
        column = 4 * size + 1
        bit = 1
        while 2 * bit < nodes:
            keep, send = split_sum(idx, column, group, keep, swap(send, bit))
            column += 1
            bit *= 2
        return order_sum(idx, column, keep, swap(send, bit))

    def relocate(blocks):
        came = []
        for turn, block in enumerate(blocks):
            moves = [
                (n * size + s, (s // group) * size + groups[n] * group + (s + turn) % group)
                for n in range(nodes)
                for s in range(size)
            ]
            came.append(lax.ppermute(block, ("node", "local"), moves))
        return came

    gathered = [[block] for block in sets]
    moving = [(block, block) for block in sets]
    terms = [[], []]
    for step in range(1, far + 1):
        for chunk in range(2):
            right, left = moving[chunk]
            if step == far:
                right, left = halve(right, left, [] if chunk else [dots])
            right, left = shift(right, 1), shift(left, -1)
            moving[chunk] = right, left
            gathered[chunk] += [right, left]
            if step < far:
                pieces = gathered[chunk] if step == 1 else [right, left]
                known = len(terms[chunk])
                befores = terms[0][known : known + len(pieces)] if chunk else []
                terms[chunk] += term_step(turned, pieces, befores, chunk)
            elif chunk == 0:
                lasts = term_step(turned, [right, left], [], 0)
    keep_0, keep_1, send_0, send_1 = term_last(idx, turned, lasts, gathered[1][-2:], terms[1])
    first, second = sum_nodes(keep_0, send_0), sum_nodes(keep_1, send_1)
    came = [*relocate(first), *relocate(second)]
    column = idx.shape[0] - 1 - group
    d_tokens = finish(
        idx, column, tokens, norm_gain[None], inverse_rms, dots, came, width // nodes
    )
    sums = [first[0], second[0]]
    grads = grads_chunk(rows_turned, gathered[0], None, sums, 0, wide, columns)
    grads = grads_chunk(rows_turned, gathered[1], grads, [], 1, wide, columns)
    return (jnp.concatenate(outputs, axis=-1), d_tokens, grads)


def solution(mesh):
    placed = (
        P("local", None),
        P(),
        P(None, "local", "node"),
        P(None, "local", "node"),
        P("local", "node"),
    )
    return jax.shard_map(
        local,
        mesh=mesh,
        in_specs=placed,
        out_specs=(P("local", "node"), P("local", "node"), P(None, "local", "node")),
        check_vma=False,
    )
```

```python
import functools
import math

import jax
import jax.numpy as jnp
import numpy as np
from jax import lax
from jax.experimental import pallas as pl
from jax.experimental.pallas import tpu as pltpu
from jax.sharding import PartitionSpec as P

HEAD_DIM = 128
NORM_EPS = 1e-05
MIB = 1024 * 1024


def params(limit):
    return pltpu.CompilerParams(
        dimension_semantics=("arbitrary",), vmem_limit_bytes=limit * MIB
    )


def tied(kernel, inputs, ties):
    def inner(*refs):
        kernel(*refs[:inputs], *refs[inputs + ties :])

    return inner


def tie_specs(ties):
    return [pl.BlockSpec(memory_space=pl.ANY)] * len(ties)


def cost(flops, moved):
    return pl.CostEstimate(flops=flops, bytes_accessed=moved, transcendentals=0)


def mm(a, b):
    return jnp.dot(a, b, preferred_element_type=jnp.float32)


def mm_nt(a, b):
    return lax.dot_general(a, b, (((1,), (1,)), ((), ())), preferred_element_type=jnp.float32)


def mm_tn(a, b):
    return lax.dot_general(a, b, (((0,), (0,)), ((), ())), preferred_element_type=jnp.float32)


def rope_tables(length, width):
    position = jnp.arange(length).astype(jnp.float32)[:, None]
    frequency = jnp.exp(
        jnp.arange(width // 2).astype(jnp.float32) * (-2.0 * math.log(10000.0) / width)
    )
    angle = position * frequency[None, :]
    cosine, sine = jnp.cos(angle), jnp.sin(angle)
    return (
        jnp.concatenate([cosine, cosine], axis=-1),
        jnp.concatenate([-sine, sine], axis=-1),
    )


def ring_order(size):
    return [*range(0, size, 2), *reversed(range(1, size, 2))]


def ring_distances(size):
    far = size // 2
    distances = [0]
    for step in range(1, far):
        distances += [-step, step]
    return [*distances, far]


def index_table(size, nodes):
    order, group = ring_order(size), size // nodes
    rows = []
    for node in range(nodes):
        for here in range(size):
            place = order.index(here)
            seqs = [order[(place + distance) % size] for distance in ring_distances(size)]
            owner = [seq // group for seq in seqs]
            rows.append(
                [order[(place + distance) % size] for distance in range(size)]
                + [node % 2]
                + seqs
                + [owner_ % 2 ^ node % 2 for owner_ in owner]
                + [(o // 2) * group + seq % group for o, seq in zip(owner, seqs)]
                + [node >> level & 1 for level in range(1, nodes.bit_length() - 1)]
                + [(here + turn) % group for turn in range(group)]
                + [(here - turn) % group for turn in range(group)]
                + [node]
            )
    return np.array(rows, np.int32)


def weights_kernel(quant, scale, out, turned):
    blocks = scale.shape[1]
    rows = quant.shape[1] // blocks
    scales = scale[0].astype(jnp.float32)
    for block in range(blocks):
        span = slice(block * rows, (block + 1) * rows)
        scaled = (quant[0, span].astype(jnp.float32) * scales[block : block + 1]).astype(jnp.bfloat16)
        out[0, span] = scaled
        turned[0, :, span] = scaled.T


def scaled_weights(w_quant, w_scale):
    _, depth, columns = w_quant.shape
    blocks = w_scale.shape[1]
    return pl.pallas_call(
        weights_kernel,
        grid=(3,),
        in_specs=[
            pl.BlockSpec((1, depth, columns), lambda m: (m, 0, 0)),
            pl.BlockSpec((1, blocks, columns), lambda m: (m, 0, 0)),
        ],
        out_specs=[
            pl.BlockSpec((1, depth, columns), lambda m: (m, 0, 0)),
            pl.BlockSpec((1, columns, depth), lambda m: (m, 0, 0)),
        ],
        out_shape=[
            jax.ShapeDtypeStruct((3, depth, columns), jnp.bfloat16),
            jax.ShapeDtypeStruct((3, columns, depth), jnp.bfloat16),
        ],
        compiler_params=params(20),
        cost_estimate=cost(3 * depth * columns, 18 * depth * columns),
        name="scaled_weights",
    )(w_quant, w_scale)


def normed_kernel(idx, tokens, gain, *refs):
    outs, gains = refs[:-1], refs[-1]
    width, part = tokens.shape[1], outs[0].shape[1]
    gains[...] = gain[...].astype(jnp.float32)
    values = tokens[...].astype(jnp.float32)
    inverse = lax.rsqrt(jnp.mean(values * values, axis=-1, keepdims=True) + NORM_EPS)
    size = len(outs) - 1
    for distance in range(size):
        start = pl.multiple_of(idx[distance] * (width // size) + idx[size] * part, part)
        block = tokens[:, pl.ds(start, part)].astype(jnp.float32)
        scale = gains[:, pl.ds(start, part)]
        outs[distance][...] = (block * inverse * scale).astype(jnp.bfloat16)
    outs[size][...] = jnp.broadcast_to(inverse, outs[size].shape)


def normed_blocks(idx, tokens, gain, size, part):
    length, width = tokens.shape
    tile = length // 4
    block = pl.BlockSpec((tile, part), lambda i, idx: (i, 0))
    *blocks, inverse = pl.pallas_call(
        normed_kernel,
        grid_spec=pltpu.PrefetchScalarGridSpec(
            num_scalar_prefetch=1,
            grid=(4,),
            in_specs=[
                pl.BlockSpec((tile, width), lambda i, idx: (i, 0)),
                pl.BlockSpec((1, width), lambda i, idx: (0, 0)),
            ],
            out_specs=[block] * size + [pl.BlockSpec((tile, 128), lambda i, idx: (i, 0))],
            scratch_shapes=[pltpu.VMEM((1, width), jnp.float32)],
        ),
        out_shape=[jax.ShapeDtypeStruct((length, part), jnp.bfloat16)] * size
        + [jax.ShapeDtypeStruct((length, 128), jnp.float32)],
        compiler_params=params(12),
        cost_estimate=cost(8 * length * width, 4 * length * width),
        name="normed_blocks",
    )(idx, tokens, gain)
    return blocks, inverse


def stack_kernel(*refs):
    for place, block in enumerate(refs[:-1]):
        refs[-1][place] = block[...]


def stack(blocks, ties):
    count, shape = len(blocks), blocks[0].shape
    block = pl.BlockSpec(shape, lambda i: (0, 0))
    return pl.pallas_call(
        tied(stack_kernel, count, len(ties)),
        grid=(1,),
        in_specs=[block] * count + tie_specs(ties),
        out_specs=pl.BlockSpec((count, *shape), lambda i: (0, 0, 0)),
        out_shape=jax.ShapeDtypeStruct((count, *shape), blocks[0].dtype),
        compiler_params=params(10),
        cost_estimate=cost(0, 4 * count * shape[0] * shape[1]),
        name="stack",
    )(*blocks, *ties)


def halve_kernel(right, left, right_out, left_out):
    half = right_out.shape[1]
    right_out[...] = right[:, :half]
    left_out[...] = left[:, half:]


def halve(right, left, ties):
    _, rows, wide = right.shape
    result = jax.ShapeDtypeStruct((3, rows // 2, wide), right.dtype)
    whole = pl.BlockSpec(memory_space=pltpu.VMEM)
    return pl.pallas_call(
        tied(halve_kernel, 2, len(ties)),
        in_specs=[whole, whole] + tie_specs(ties),
        out_specs=[whole, whole],
        out_shape=[result, result],
        compiler_params=pltpu.CompilerParams(vmem_limit_bytes=4 * MIB),
        cost_estimate=cost(0, 6 * rows * wide),
        name="halve",
    )(right, left, *ties)


def turn_kernel(count, idx, mine, other, mine_far, other_far, out):
    length, part = mine_far.shape
    for side, near, last in ((0, mine, mine_far), (1, other, other_far)):
        half = idx[count] * (1 - side) + (1 - idx[count]) * side
        rows = pl.ds(pl.multiple_of(half * part, part), part)
        for place in range(count):
            block = near[place] if place < count - 1 else last[...]
            out[rows, place * length : (place + 1) * length] = block.T


def turn(idx, mine, other, mine_far, other_far):
    near, length, part = mine.shape
    count = near + 1
    stack = pl.BlockSpec(mine.shape, lambda i, idx: (0, 0, 0))
    last = pl.BlockSpec((length, part), lambda i, idx: (0, 0))
    shape = (2 * part, count * length)
    return pl.pallas_call(
        functools.partial(turn_kernel, count),
        grid_spec=pltpu.PrefetchScalarGridSpec(
            num_scalar_prefetch=1,
            grid=(1,),
            in_specs=[stack, stack, last, last],
            out_specs=pl.BlockSpec(shape, lambda i, idx: (0, 0)),
        ),
        out_shape=jax.ShapeDtypeStruct(shape, jnp.bfloat16),
        compiler_params=params(12),
        cost_estimate=cost(2 * count * length * part, 8 * count * length * part),
        name="turn",
    )(idx, mine, other, mine_far, other_far)


def sum_first_kernel(idx, mine, other, weight, weight_other, *outs):
    half, wide = outs[0].shape[1:]
    for chunk in range(2):
        span = slice(chunk * wide, (chunk + 1) * wide)
        product = mm(mine[...], weight[0, :, span]) + mm(other[...], weight_other[0, :, span])
        outs[2 * chunk][0] = product[:half].astype(jnp.bfloat16)
        outs[2 * chunk + 1][0] = product[half:].astype(jnp.bfloat16)


def sum_step_kernel(
    idx, mine_r, other_r, mine_l, other_l, weight, weight_other, from_left, from_right, right, left
):
    length, part = right.shape[1], from_left.shape[1]
    product = mm(mine_r[0], weight[0]) + mm(other_r[0], weight_other[0])
    right[0, :part] = (product[:part] + from_left[0].astype(jnp.float32)).astype(jnp.bfloat16)
    if part < length:
        right[0, part:] = product[part:].astype(jnp.bfloat16)
    product = mm(mine_l[0], weight[0]) + mm(other_l[0], weight_other[0])
    rest = length - part
    left[0, rest:] = (product[rest:] + from_right[0].astype(jnp.float32)).astype(jnp.bfloat16)
    if rest:
        left[0, :rest] = product[:rest].astype(jnp.bfloat16)


def weight_halves(size, part, wide, chunk):
    return [
        pl.BlockSpec((1, part, wide), lambda m, idx: (m, idx[size], chunk)),
        pl.BlockSpec((1, part, wide), lambda m, idx: (m, 1 - idx[size], chunk)),
    ]


def sum_first(idx, size, mine, other, weights):
    length, part = mine.shape
    columns = weights.shape[2]
    half, wide = length // 2, columns // 2
    block = pl.BlockSpec((length, part), lambda m, idx: (0, 0))
    result = jax.ShapeDtypeStruct((3, half, wide), jnp.bfloat16)
    return pl.pallas_call(
        sum_first_kernel,
        grid_spec=pltpu.PrefetchScalarGridSpec(
            num_scalar_prefetch=1,
            grid=(3,),
            in_specs=[block, block, *weight_halves(size, part, columns, 0)],
            out_specs=[pl.BlockSpec((1, half, wide), lambda m, idx: (m, 0, 0))] * 4,
        ),
        out_shape=[result] * 4,
        compiler_params=params(12),
        cost_estimate=cost(12 * length * part * columns, 16 * part * columns),
        name="sum_first",
    )(idx, mine, other, weights, weights)


def sum_step(idx, size, mine, other, places, weights, from_left, from_right, chunk, wide, ties):
    _, length, part = mine.shape
    block_r = pl.BlockSpec((1, length, part), lambda m, idx: (places[0], 0, 0))
    block_l = pl.BlockSpec((1, length, part), lambda m, idx: (places[1], 0, 0))
    came = pl.BlockSpec((1, from_left.shape[1], wide), lambda m, idx: (m, 0, 0))
    whole = jax.ShapeDtypeStruct((3, length, wide), jnp.bfloat16)
    return pl.pallas_call(
        tied(sum_step_kernel, 9, len(ties)),
        grid_spec=pltpu.PrefetchScalarGridSpec(
            num_scalar_prefetch=1,
            grid=(3,),
            in_specs=[
                block_r,
                block_r,
                block_l,
                block_l,
                *weight_halves(size, part, wide, chunk),
                came,
                came,
                *tie_specs(ties),
            ],
            out_specs=[pl.BlockSpec((1, length, wide), lambda m, idx: (m, 0, 0))] * 2,
        ),
        out_shape=[whole, whole],
        compiler_params=params(12),
        cost_estimate=cost(24 * length * part * wide, 24 * part * wide),
        name="sum_step",
    )(idx, mine, other, mine, other, weights, weights, from_left, from_right, *ties)


def attention_kernel(
    idx, mine, other, weight, weight_other, from_left, from_right, d_out, cosine, sine,
    output, dots, pre,
):
    length = mine.shape[1]
    proj = [
        mm(mine[0], weight[m])
        + mm(other[0], weight_other[m])
        + (from_left[m].astype(jnp.float32) + from_right[m].astype(jnp.float32))
        for m in range(3)
    ]
    cos, sin = cosine[...], sine[...]
    half = HEAD_DIM // 2

    def rotate(tensor, angle):
        return tensor * cos + pltpu.roll(tensor, half, 1) * angle

    query = rotate(proj[0], sin).astype(jnp.bfloat16)
    key_rows = rotate(proj[1], sin).astype(jnp.bfloat16)
    value = proj[2].astype(jnp.bfloat16)
    scores = mm_nt(query, key_rows) * (1.0 / math.sqrt(HEAD_DIM))
    causal = lax.broadcasted_iota(jnp.int32, (length, length), 0) >= lax.broadcasted_iota(
        jnp.int32, (length, length), 1
    )
    scores = jnp.where(causal, scores, jnp.float32(-1e30))
    powers = jnp.exp(scores - jnp.max(scores, axis=-1, keepdims=True))
    probs = powers * (1.0 / jnp.sum(powers, axis=-1, keepdims=True))
    probs_low = probs.astype(jnp.bfloat16)
    output[...] = mm(probs_low, value).astype(jnp.bfloat16)
    cotangent = d_out[...]
    d_value = mm_tn(probs_low, cotangent).astype(jnp.bfloat16)
    d_probs = mm_nt(cotangent, value).astype(jnp.bfloat16).astype(jnp.float32)
    inner = jnp.sum(d_probs * probs, axis=-1, keepdims=True)
    d_scores = (probs * (d_probs - inner) * (1.0 / math.sqrt(HEAD_DIM))).astype(jnp.bfloat16)
    d_query = mm(d_scores, key_rows).astype(jnp.bfloat16).astype(jnp.float32)
    d_key = mm_tn(d_scores, query).astype(jnp.bfloat16).astype(jnp.float32)
    pre_query = rotate(d_query, -sin).astype(jnp.bfloat16)
    pre_key = rotate(d_key, -sin).astype(jnp.bfloat16)
    pre[0] = pre_query
    pre[1] = pre_key
    pre[2] = d_value
    product = (
        pre_query.astype(jnp.float32) * proj[0]
        + pre_key.astype(jnp.float32) * proj[1]
        + d_value.astype(jnp.float32) * proj[2]
    )

    @pl.when(pl.program_id(0) == 0)
    def _():
        dots[...] = product

    @pl.when(pl.program_id(0) > 0)
    def _():
        dots[...] += product


def attention(idx, size, mine, other, weights, from_left, from_right, d_out, tables, chunk, wide):
    _, length, part = mine.shape
    heads = wide // HEAD_DIM
    first = chunk * heads
    block = pl.BlockSpec((1, length, part), lambda h, idx: (0, 0, 0))
    table = pl.BlockSpec((length, HEAD_DIM), lambda h, idx: (0, 0))
    stack = pl.BlockSpec((3, length, HEAD_DIM), lambda h, idx: (0, 0, h))
    return pl.pallas_call(
        attention_kernel,
        grid_spec=pltpu.PrefetchScalarGridSpec(
            num_scalar_prefetch=1,
            grid=(heads,),
            in_specs=[
                block,
                block,
                pl.BlockSpec((3, part, HEAD_DIM), lambda h, idx: (0, idx[size], first + h)),
                pl.BlockSpec((3, part, HEAD_DIM), lambda h, idx: (0, 1 - idx[size], first + h)),
                stack,
                stack,
                pl.BlockSpec((length, HEAD_DIM), lambda h, idx: (0, first + h)),
                table,
                table,
            ],
            out_specs=[
                pl.BlockSpec((length, HEAD_DIM), lambda h, idx: (0, h)),
                table,
                stack,
            ],
        ),
        out_shape=[
            jax.ShapeDtypeStruct((length, wide), jnp.bfloat16),
            jax.ShapeDtypeStruct((length, HEAD_DIM), jnp.float32),
            jax.ShapeDtypeStruct((3, length, wide), jnp.bfloat16),
        ],
        compiler_params=params(16),
        cost_estimate=cost(12 * length * part * wide, 24 * part * wide),
        name="attention",
    )(idx, mine, other, weights, weights, from_left, from_right, d_out, *tables)


def grads_kernel(turned, *refs):
    blocks = jnp.concatenate([piece[0] for piece in refs[:-1]], axis=0)
    refs[-1][0] = mm(turned[...], blocks)


def grads_chunk(turned, pieces, before, ties, chunk, wide, columns):
    depth, span = turned.shape
    aliases = {} if before is None else {1 + len(pieces): 0}
    ties = ties if before is None else [before, *ties]
    return pl.pallas_call(
        tied(grads_kernel, 1 + len(pieces), len(ties)),
        grid=(3,),
        in_specs=[
            pl.BlockSpec((depth, span), lambda m: (0, 0)),
            *[pl.BlockSpec((1, *piece.shape[1:]), lambda m: (m, 0, 0)) for piece in pieces],
            *tie_specs(ties),
        ],
        out_specs=pl.BlockSpec((1, depth, wide), lambda m: (m, 0, chunk)),
        out_shape=jax.ShapeDtypeStruct((3, depth, columns), jnp.float32),
        input_output_aliases=aliases,
        compiler_params=params(24),
        cost_estimate=cost(6 * span * depth * wide, 6 * span * wide + 12 * depth * wide),
        name="grads",
    )(turned, *pieces, *ties)


def back(pieces, turned, chunk):
    wide = pieces[0].shape[2]
    rows = [jnp.concatenate([piece[m] for m in range(3)], axis=1) for piece in pieces]
    weight = [turned[m, chunk * wide : (chunk + 1) * wide] for m in range(3)]
    return mm(jnp.concatenate(rows, axis=0), jnp.concatenate(weight, axis=0))


def term_step(turned, pieces, befores, chunk):
    depth, wide = turned.shape[2], pieces[0].shape[2]
    count, rows = len(pieces), pieces[0].shape[1]
    whole = pl.BlockSpec(memory_space=pltpu.VMEM)

    def kernel(turned_ref, *refs):
        total = back(refs[:count], turned_ref, chunk)
        for place in range(count):
            block = total[place * rows : (place + 1) * rows]
            if befores:
                block += refs[count + place][...]
            refs[len(refs) - count + place][...] = block

    return pl.pallas_call(
        kernel,
        in_specs=[whole] * (1 + count + len(befores)),
        out_specs=[whole] * count,
        out_shape=[jax.ShapeDtypeStruct((rows, depth), jnp.float32)] * count,
        compiler_params=pltpu.CompilerParams(vmem_limit_bytes=16 * MIB),
        cost_estimate=cost(6 * count * rows * depth * wide, 12 * count * rows * wide),
        name="term_step",
    )(turned, *pieces, *befores)


def term_last_kernel(count, idx, turned, *refs):
    befores, fars, nears = refs[:2], refs[2:4], refs[4 : 3 + count]
    keeps, sends = refs[-4:-2], refs[-2:]
    half = keeps[0].shape[1]
    last = back(fars, turned, 1)
    for place in range(count):
        for part in range(2):
            span = slice(part * half, (part + 1) * half)
            total = nears[place][span] if place < count - 1 else last[span] + befores[part][...]

            @pl.when(idx[2 * count + 1 + place] == 0)
            def _():
                keeps[part][idx[3 * count + 1 + place]] = total

            @pl.when(idx[2 * count + 1 + place] == 1)
            def _():
                sends[part][idx[3 * count + 1 + place]] = total.astype(jnp.bfloat16)


def term_last(idx, turned, befores, pieces, nears):
    count = len(nears) + 1
    rows, depth = nears[0].shape
    whole = pl.BlockSpec(memory_space=pltpu.VMEM)
    shape = (count // 2, rows // 2, depth)
    return pl.pallas_call(
        functools.partial(term_last_kernel, count),
        in_specs=[pl.BlockSpec(memory_space=pltpu.SMEM)] + [whole] * (count + 4),
        out_specs=[whole] * 4,
        out_shape=[jax.ShapeDtypeStruct(shape, jnp.float32)] * 2
        + [jax.ShapeDtypeStruct(shape, jnp.bfloat16)] * 2,
        compiler_params=pltpu.CompilerParams(vmem_limit_bytes=12 * MIB),
        cost_estimate=cost(rows * depth * depth, 12 * count * rows * depth),
        name="term_last",
    )(idx, turned, *befores, *pieces, *nears)


def split_kernel(column, group, idx, keep, came, keep_out, send_out):
    own = idx[column]
    for block in range(keep_out.shape[0]):
        high, low = block // group, block % group
        mine = (2 * high + own) * group + low
        other = (2 * high + 1 - own) * group + low
        keep_out[block] = keep[mine] + came[mine].astype(jnp.float32)
        send_out[block] = (keep[other] + came[other].astype(jnp.float32)).astype(jnp.bfloat16)


def split_sum(idx, column, group, keep, came):
    whole = pl.BlockSpec(memory_space=pltpu.VMEM)
    shape = (keep.shape[0] // 2, *keep.shape[1:])
    return pl.pallas_call(
        functools.partial(split_kernel, column, group),
        in_specs=[pl.BlockSpec(memory_space=pltpu.SMEM), whole, whole],
        out_specs=[whole, whole],
        out_shape=[
            jax.ShapeDtypeStruct(shape, jnp.float32),
            jax.ShapeDtypeStruct(shape, jnp.bfloat16),
        ],
        compiler_params=pltpu.CompilerParams(vmem_limit_bytes=4 * MIB),
        cost_estimate=cost(0, 8 * keep.shape[0] * keep.shape[1] * keep.shape[2]),
        name="split_sum",
    )(idx, keep, came)


def order_kernel(column, idx, keep, came, *outs):
    for turn, out in enumerate(outs):
        block = idx[column + turn]
        out[...] = (keep[block] + came[block].astype(jnp.float32)).astype(jnp.bfloat16)


def order_sum(idx, column, keep, came):
    whole = pl.BlockSpec(memory_space=pltpu.VMEM)
    count = keep.shape[0]
    return pl.pallas_call(
        functools.partial(order_kernel, column),
        in_specs=[pl.BlockSpec(memory_space=pltpu.SMEM), whole, whole],
        out_specs=[whole] * count,
        out_shape=[jax.ShapeDtypeStruct(keep.shape[1:], jnp.bfloat16)] * count,
        compiler_params=pltpu.CompilerParams(vmem_limit_bytes=4 * MIB),
        cost_estimate=cost(0, 8 * count * keep.shape[1] * keep.shape[2]),
        name="order_sum",
    )(idx, keep, came)


def finish_kernel(column, width, idx, tokens, gain, inverse, dots, *refs):
    came, out, gains = refs[:-2], refs[-2], refs[-1]
    rows, depth = came[0].shape
    group = out.shape[1] // depth
    gains[...] = gain[...].astype(jnp.float32)
    for turn in range(group):
        features = pl.ds(pl.multiple_of(idx[column + turn] * depth, depth), depth)
        for part in range(len(came) // group):
            span = slice(part * rows, (part + 1) * rows)
            scale = inverse[span, :1]
            upstream = came[part * group + turn][...].astype(jnp.float32)
            values = tokens[span, features].astype(jnp.float32)
            common = scale * scale * dots[span] / width
            out[span, features] = (
                scale * gains[:, features] * upstream - values * common
            ).astype(jnp.bfloat16)


def finish(idx, column, tokens, gain, inverse, dots, came, share):
    length, width = tokens.shape
    node = column + share // came[0].shape[1]
    whole = pl.BlockSpec(memory_space=pltpu.VMEM)
    return pl.pallas_call(
        functools.partial(finish_kernel, column, width),
        grid_spec=pltpu.PrefetchScalarGridSpec(
            num_scalar_prefetch=1,
            grid=(1,),
            in_specs=[
                pl.BlockSpec((length, share), lambda i, idx: (0, idx[node])),
                pl.BlockSpec((1, share), lambda i, idx: (0, idx[node])),
                *[whole] * (2 + len(came)),
            ],
            out_specs=pl.BlockSpec((length, share), lambda i, idx: (0, 0)),
            scratch_shapes=[pltpu.VMEM((1, share), jnp.float32)],
        ),
        out_shape=jax.ShapeDtypeStruct((length, share), jnp.bfloat16),
        compiler_params=params(12),
        cost_estimate=cost(8 * length * share, 6 * length * share),
        name="finish",
    )(idx, tokens, gain, inverse, dots, *came)


def local(tokens, norm_gain, w_quant, w_scale, d_out):
    length, width = tokens.shape
    depth, columns = w_quant.shape[1:]
    size, nodes = lax.axis_size("local"), lax.axis_size("node")
    here, node = lax.axis_index("local"), lax.axis_index("node")
    wide = columns // 2
    far = size // 2
    group = size // nodes
    core = node % 2

    order = ring_order(size)
    distances = ring_distances(size)
    table = jnp.asarray(index_table(size, nodes))
    idx = lax.dynamic_index_in_dim(table, node * size + here, 0, keepdims=False)

    def shift(array, distance):
        moves = [(order[i], order[(i + distance) % size]) for i in range(size)]
        return lax.ppermute(array, "local", moves)

    def swap(array, bit):
        return lax.ppermute(array, "node", [(n, n ^ bit) for n in range(nodes)])

    blocks, inverse_rms = normed_blocks(idx, tokens, norm_gain[None], size, depth // 2)
    mine_far = shift(blocks[far], far)
    other_far = swap(mine_far, 1)
    weights, turned = scaled_weights(w_quant, w_scale)
    firsts = sum_first(idx, size, mine_far, other_far, weights)
    mine = stack(
        [shift(blocks[-d % size], -d) if d else blocks[0] for d in distances[:-1]], firsts[:1]
    )
    other = swap(mine, 1)

    rows_turned = turn(idx, mine, other, mine_far, other_far)

    tables = rope_tables(length, HEAD_DIM)
    arrived = []
    for chunk in range(2):
        right, left = firsts[2 * chunk : 2 * chunk + 2]
        for distance in range(far - 1, -1, -1):
            from_left, from_right = shift(right, 1), shift(left, -1)
            if distance:
                places = distances.index(distance), distances.index(-distance)
                ties = [rows_turned] if distance == 1 else []
                right, left = sum_step(
                    idx, size, mine, other, places, weights, from_left, from_right, chunk, wide, ties
                )
        arrived.append((from_left, from_right))

    outputs, sets, dots = [], [], 0.0
    for chunk in range(2):
        output, product, pre = attention(
            idx, size, mine, other, weights, *arrived[chunk], d_out, tables, chunk, wide
        )
        outputs.append(output)
        sets.append(pre)
        dots += jnp.sum(product, axis=-1, keepdims=True)
    bit = 1
    while bit < nodes:
        dots = dots + swap(dots, bit)
        bit *= 2

    def sum_nodes(keep, send):
        column = 4 * size + 1
        bit = 1
        while 2 * bit < nodes:
            keep, send = split_sum(idx, column, group, keep, swap(send, bit))
            column += 1
            bit *= 2
        return order_sum(idx, column, keep, swap(send, bit))

    def relocate(blocks):
        came = []
        for turn, block in enumerate(blocks):
            moves = [
                (n * size + s, (s // group) * size + n * group + (s + turn) % group)
                for n in range(nodes)
                for s in range(size)
            ]
            came.append(lax.ppermute(block, ("node", "local"), moves))
        return came

    gathered = [[block] for block in sets]
    moving = [(block, block) for block in sets]
    terms = [[], []]
    for step in range(1, far + 1):
        for chunk in range(2):
            right, left = moving[chunk]
            if step == far:
                early = [dots] if chunk == 0 else terms[1][: size - 3]
                right, left = halve(right, left, early)
            right, left = shift(right, 1), shift(left, -1)
            moving[chunk] = right, left
            gathered[chunk] += [right, left]
            if step < far:
                pieces = gathered[chunk] if step == 1 else [right, left]
                known = len(terms[chunk])
                befores = terms[0][known : known + len(pieces)] if chunk else []
                terms[chunk] += term_step(turned, pieces, befores, chunk)
            elif chunk == 0:
                lasts = term_step(turned, [right, left], [], 0)
    keep_0, keep_1, send_0, send_1 = term_last(idx, turned, lasts, gathered[1][-2:], terms[1])
    first, second = sum_nodes(keep_0, send_0), sum_nodes(keep_1, send_1)
    came = [*relocate(first), *relocate(second)]
    column = idx.shape[0] - 1 - group
    d_tokens = finish(
        idx, column, tokens, norm_gain[None], inverse_rms, dots, came, width // nodes
    )
    grads = grads_chunk(rows_turned, gathered[0], None, [keep_1], 0, wide, columns)
    sums = [first[0], second[0]]
    grads = grads_chunk(rows_turned, gathered[1], grads, sums, 1, wide, columns)
    return (jnp.concatenate(outputs, axis=-1), d_tokens, grads)


def solution(mesh):
    placed = (
        P("local", None),
        P(),
        P(None, "local", "node"),
        P(None, "local", "node"),
        P("local", "node"),
    )
    return jax.shard_map(
        local,
        mesh=mesh,
        in_specs=placed,
        out_specs=(P("local", "node"), P("local", "node"), P(None, "local", "node")),
        check_vma=False,
    )
```

```python
import functools
import math

import jax
import jax.numpy as jnp
import numpy as np
from jax import lax
from jax.experimental import pallas as pl
from jax.experimental.pallas import tpu as pltpu
from jax.sharding import PartitionSpec as P

HEAD_DIM = 128
NORM_EPS = 1e-05
MIB = 1024 * 1024


def params(limit):
    return pltpu.CompilerParams(
        dimension_semantics=("arbitrary",), vmem_limit_bytes=limit * MIB
    )


def tied(kernel, inputs, ties):
    def inner(*refs):
        kernel(*refs[:inputs], *refs[inputs + ties :])

    return inner


def tie_specs(ties):
    return [pl.BlockSpec(memory_space=pl.ANY)] * len(ties)


def cost(flops, moved):
    return pl.CostEstimate(flops=flops, bytes_accessed=moved, transcendentals=0)


def mm(a, b):
    return jnp.dot(a, b, preferred_element_type=jnp.float32)


def mm_nt(a, b):
    return lax.dot_general(a, b, (((1,), (1,)), ((), ())), preferred_element_type=jnp.float32)


def mm_tn(a, b):
    return lax.dot_general(a, b, (((0,), (0,)), ((), ())), preferred_element_type=jnp.float32)


def rope_tables(length, width):
    position = jnp.arange(length).astype(jnp.float32)[:, None]
    frequency = jnp.exp(
        jnp.arange(width // 2).astype(jnp.float32) * (-2.0 * math.log(10000.0) / width)
    )
    angle = position * frequency[None, :]
    cosine, sine = jnp.cos(angle), jnp.sin(angle)
    return (
        jnp.concatenate([cosine, cosine], axis=-1),
        jnp.concatenate([-sine, sine], axis=-1),
    )


def ring_order(size):
    return [*range(0, size, 2), *reversed(range(1, size, 2))]


def ring_distances(size):
    far = size // 2
    distances = [0]
    for step in range(1, far):
        distances += [-step, step]
    return [*distances, far]


def group_of(nodes):
    bits = nodes.bit_length() - 1
    return [sum((node >> bit & 1) << (bits - 1 - bit) for bit in range(bits)) for node in range(nodes)]


def index_table(size, nodes):
    order, group = ring_order(size), size // nodes
    rows = []
    for node in range(nodes):
        for here in range(size):
            place = order.index(here)
            seqs = [order[(place + distance) % size] for distance in ring_distances(size)]
            owner = [group_of(nodes).index(seq // group) for seq in seqs]
            rows.append(
                [order[(place + distance) % size] for distance in range(size)]
                + [node % 2]
                + seqs
                + [owner_ % 2 ^ node % 2 for owner_ in owner]
                + [(o // 2) * group + seq % group for o, seq in zip(owner, seqs)]
                + [node >> level & 1 for level in range(1, nodes.bit_length() - 1)]
                + [(here + turn) % group for turn in range(group)]
                + [(here - turn) % group for turn in range(group)]
                + [node]
            )
    return np.array(rows, np.int32)


def weights_kernel(quant, scale, out, turned):
    blocks = scale.shape[1]
    rows = quant.shape[1] // blocks
    scales = scale[0].astype(jnp.float32)
    for block in range(blocks):
        span = slice(block * rows, (block + 1) * rows)
        scaled = (quant[0, span].astype(jnp.float32) * scales[block : block + 1]).astype(jnp.bfloat16)
        out[0, span] = scaled
        turned[0, :, span] = scaled.T


def scaled_weights(w_quant, w_scale):
    _, depth, columns = w_quant.shape
    blocks = w_scale.shape[1]
    return pl.pallas_call(
        weights_kernel,
        grid=(3,),
        in_specs=[
            pl.BlockSpec((1, depth, columns), lambda m: (m, 0, 0)),
            pl.BlockSpec((1, blocks, columns), lambda m: (m, 0, 0)),
        ],
        out_specs=[
            pl.BlockSpec((1, depth, columns), lambda m: (m, 0, 0)),
            pl.BlockSpec((1, columns, depth), lambda m: (m, 0, 0)),
        ],
        out_shape=[
            jax.ShapeDtypeStruct((3, depth, columns), jnp.bfloat16),
            jax.ShapeDtypeStruct((3, columns, depth), jnp.bfloat16),
        ],
        compiler_params=params(20),
        cost_estimate=cost(3 * depth * columns, 18 * depth * columns),
        name="scaled_weights",
    )(w_quant, w_scale)


def normed_kernel(idx, tokens, gain, *refs):
    outs, gains = refs[:-1], refs[-1]
    width, part = tokens.shape[1], outs[0].shape[1]
    gains[...] = gain[...].astype(jnp.float32)
    values = tokens[...].astype(jnp.float32)
    inverse = lax.rsqrt(jnp.mean(values * values, axis=-1, keepdims=True) + NORM_EPS)
    size = len(outs) - 1
    for distance in range(size):
        start = pl.multiple_of(idx[distance] * (width // size) + idx[size] * part, part)
        block = tokens[:, pl.ds(start, part)].astype(jnp.float32)
        scale = gains[:, pl.ds(start, part)]
        outs[distance][...] = (block * inverse * scale).astype(jnp.bfloat16)
    outs[size][...] = jnp.broadcast_to(inverse, outs[size].shape)


def normed_blocks(idx, tokens, gain, size, part):
    length, width = tokens.shape
    tile = length // 4
    block = pl.BlockSpec((tile, part), lambda i, idx: (i, 0))
    *blocks, inverse = pl.pallas_call(
        normed_kernel,
        grid_spec=pltpu.PrefetchScalarGridSpec(
            num_scalar_prefetch=1,
            grid=(4,),
            in_specs=[
                pl.BlockSpec((tile, width), lambda i, idx: (i, 0)),
                pl.BlockSpec((1, width), lambda i, idx: (0, 0)),
            ],
            out_specs=[block] * size + [pl.BlockSpec((tile, 128), lambda i, idx: (i, 0))],
            scratch_shapes=[pltpu.VMEM((1, width), jnp.float32)],
        ),
        out_shape=[jax.ShapeDtypeStruct((length, part), jnp.bfloat16)] * size
        + [jax.ShapeDtypeStruct((length, 128), jnp.float32)],
        compiler_params=params(12),
        cost_estimate=cost(8 * length * width, 4 * length * width),
        name="normed_blocks",
    )(idx, tokens, gain)
    return blocks, inverse


def stack_kernel(*refs):
    for place, block in enumerate(refs[:-1]):
        refs[-1][place] = block[...]


def stack(blocks, ties):
    count, shape = len(blocks), blocks[0].shape
    block = pl.BlockSpec(shape, lambda i: (0, 0))
    return pl.pallas_call(
        tied(stack_kernel, count, len(ties)),
        grid=(1,),
        in_specs=[block] * count + tie_specs(ties),
        out_specs=pl.BlockSpec((count, *shape), lambda i: (0, 0, 0)),
        out_shape=jax.ShapeDtypeStruct((count, *shape), blocks[0].dtype),
        compiler_params=params(10),
        cost_estimate=cost(0, 4 * count * shape[0] * shape[1]),
        name="stack",
    )(*blocks, *ties)


def halve_kernel(right, left, right_out, left_out):
    half = right_out.shape[1]
    right_out[...] = right[:, :half]
    left_out[...] = left[:, half:]


def halve(right, left, ties):
    _, rows, wide = right.shape
    result = jax.ShapeDtypeStruct((3, rows // 2, wide), right.dtype)
    whole = pl.BlockSpec(memory_space=pltpu.VMEM)
    return pl.pallas_call(
        tied(halve_kernel, 2, len(ties)),
        in_specs=[whole, whole] + tie_specs(ties),
        out_specs=[whole, whole],
        out_shape=[result, result],
        compiler_params=pltpu.CompilerParams(vmem_limit_bytes=4 * MIB),
        cost_estimate=cost(0, 6 * rows * wide),
        name="halve",
    )(right, left, *ties)


def turn_kernel(count, idx, mine, other, mine_far, other_far, out):
    length, part = mine_far.shape
    for side, near, last in ((0, mine, mine_far), (1, other, other_far)):
        half = idx[count] * (1 - side) + (1 - idx[count]) * side
        rows = pl.ds(pl.multiple_of(half * part, part), part)
        for place in range(count):
            block = near[place] if place < count - 1 else last[...]
            out[rows, place * length : (place + 1) * length] = block.T


def turn(idx, mine, other, mine_far, other_far):
    near, length, part = mine.shape
    count = near + 1
    stack = pl.BlockSpec(mine.shape, lambda i, idx: (0, 0, 0))
    last = pl.BlockSpec((length, part), lambda i, idx: (0, 0))
    shape = (2 * part, count * length)
    return pl.pallas_call(
        functools.partial(turn_kernel, count),
        grid_spec=pltpu.PrefetchScalarGridSpec(
            num_scalar_prefetch=1,
            grid=(1,),
            in_specs=[stack, stack, last, last],
            out_specs=pl.BlockSpec(shape, lambda i, idx: (0, 0)),
        ),
        out_shape=jax.ShapeDtypeStruct(shape, jnp.bfloat16),
        compiler_params=params(12),
        cost_estimate=cost(2 * count * length * part, 8 * count * length * part),
        name="turn",
    )(idx, mine, other, mine_far, other_far)


def sum_first_kernel(idx, mine, other, weight, weight_other, *outs):
    half, wide = outs[0].shape[1:]
    for chunk in range(2):
        span = slice(chunk * wide, (chunk + 1) * wide)
        product = mm(mine[...], weight[0, :, span]) + mm(other[...], weight_other[0, :, span])
        outs[2 * chunk][0] = product[:half].astype(jnp.bfloat16)
        outs[2 * chunk + 1][0] = product[half:].astype(jnp.bfloat16)


def sum_step_kernel(
    idx, mine_r, other_r, mine_l, other_l, weight, weight_other, from_left, from_right, right, left
):
    length, part = right.shape[1], from_left.shape[1]
    product = mm(mine_r[0], weight[0]) + mm(other_r[0], weight_other[0])
    right[0, :part] = (product[:part] + from_left[0].astype(jnp.float32)).astype(jnp.bfloat16)
    if part < length:
        right[0, part:] = product[part:].astype(jnp.bfloat16)
    product = mm(mine_l[0], weight[0]) + mm(other_l[0], weight_other[0])
    rest = length - part
    left[0, rest:] = (product[rest:] + from_right[0].astype(jnp.float32)).astype(jnp.bfloat16)
    if rest:
        left[0, :rest] = product[:rest].astype(jnp.bfloat16)


def weight_halves(size, part, wide, chunk):
    return [
        pl.BlockSpec((1, part, wide), lambda m, idx: (m, idx[size], chunk)),
        pl.BlockSpec((1, part, wide), lambda m, idx: (m, 1 - idx[size], chunk)),
    ]


def sum_first(idx, size, mine, other, weights):
    length, part = mine.shape
    columns = weights.shape[2]
    half, wide = length // 2, columns // 2
    block = pl.BlockSpec((length, part), lambda m, idx: (0, 0))
    result = jax.ShapeDtypeStruct((3, half, wide), jnp.bfloat16)
    return pl.pallas_call(
        sum_first_kernel,
        grid_spec=pltpu.PrefetchScalarGridSpec(
            num_scalar_prefetch=1,
            grid=(3,),
            in_specs=[block, block, *weight_halves(size, part, columns, 0)],
            out_specs=[pl.BlockSpec((1, half, wide), lambda m, idx: (m, 0, 0))] * 4,
        ),
        out_shape=[result] * 4,
        compiler_params=params(12),
        cost_estimate=cost(12 * length * part * columns, 16 * part * columns),
        name="sum_first",
    )(idx, mine, other, weights, weights)


def sum_step(idx, size, mine, other, places, weights, from_left, from_right, chunk, wide, ties):
    _, length, part = mine.shape
    block_r = pl.BlockSpec((1, length, part), lambda m, idx: (places[0], 0, 0))
    block_l = pl.BlockSpec((1, length, part), lambda m, idx: (places[1], 0, 0))
    came = pl.BlockSpec((1, from_left.shape[1], wide), lambda m, idx: (m, 0, 0))
    whole = jax.ShapeDtypeStruct((3, length, wide), jnp.bfloat16)
    return pl.pallas_call(
        tied(sum_step_kernel, 9, len(ties)),
        grid_spec=pltpu.PrefetchScalarGridSpec(
            num_scalar_prefetch=1,
            grid=(3,),
            in_specs=[
                block_r,
                block_r,
                block_l,
                block_l,
                *weight_halves(size, part, wide, chunk),
                came,
                came,
                *tie_specs(ties),
            ],
            out_specs=[pl.BlockSpec((1, length, wide), lambda m, idx: (m, 0, 0))] * 2,
        ),
        out_shape=[whole, whole],
        compiler_params=params(12),
        cost_estimate=cost(24 * length * part * wide, 24 * part * wide),
        name="sum_step",
    )(idx, mine, other, mine, other, weights, weights, from_left, from_right, *ties)


def attention_kernel(
    idx, mine, other, weight, weight_other, from_left, from_right, d_out, cosine, sine,
    output, dots, pre,
):
    length = mine.shape[1]
    proj = [
        mm(mine[0], weight[m])
        + mm(other[0], weight_other[m])
        + (from_left[m].astype(jnp.float32) + from_right[m].astype(jnp.float32))
        for m in range(3)
    ]
    cos, sin = cosine[...], sine[...]
    half = HEAD_DIM // 2

    def rotate(tensor, angle):
        return tensor * cos + pltpu.roll(tensor, half, 1) * angle

    query = rotate(proj[0], sin).astype(jnp.bfloat16)
    key_rows = rotate(proj[1], sin).astype(jnp.bfloat16)
    value = proj[2].astype(jnp.bfloat16)
    scores = mm_nt(query, key_rows) * (1.0 / math.sqrt(HEAD_DIM))
    causal = lax.broadcasted_iota(jnp.int32, (length, length), 0) >= lax.broadcasted_iota(
        jnp.int32, (length, length), 1
    )
    scores = jnp.where(causal, scores, jnp.float32(-1e30))
    powers = jnp.exp(scores - jnp.max(scores, axis=-1, keepdims=True))
    probs = powers * (1.0 / jnp.sum(powers, axis=-1, keepdims=True))
    probs_low = probs.astype(jnp.bfloat16)
    output[...] = mm(probs_low, value).astype(jnp.bfloat16)
    cotangent = d_out[...]
    d_value = mm_tn(probs_low, cotangent).astype(jnp.bfloat16)
    d_probs = mm_nt(cotangent, value).astype(jnp.bfloat16).astype(jnp.float32)
    inner = jnp.sum(d_probs * probs, axis=-1, keepdims=True)
    d_scores = (probs * (d_probs - inner) * (1.0 / math.sqrt(HEAD_DIM))).astype(jnp.bfloat16)
    d_query = mm(d_scores, key_rows).astype(jnp.bfloat16).astype(jnp.float32)
    d_key = mm_tn(d_scores, query).astype(jnp.bfloat16).astype(jnp.float32)
    pre_query = rotate(d_query, -sin).astype(jnp.bfloat16)
    pre_key = rotate(d_key, -sin).astype(jnp.bfloat16)
    pre[0] = pre_query
    pre[1] = pre_key
    pre[2] = d_value
    product = (
        pre_query.astype(jnp.float32) * proj[0]
        + pre_key.astype(jnp.float32) * proj[1]
        + d_value.astype(jnp.float32) * proj[2]
    )

    @pl.when(pl.program_id(0) == 0)
    def _():
        dots[...] = product

    @pl.when(pl.program_id(0) > 0)
    def _():
        dots[...] += product


def attention(idx, size, mine, other, weights, from_left, from_right, d_out, tables, chunk, wide):
    _, length, part = mine.shape
    heads = wide // HEAD_DIM
    first = chunk * heads
    block = pl.BlockSpec((1, length, part), lambda h, idx: (0, 0, 0))
    table = pl.BlockSpec((length, HEAD_DIM), lambda h, idx: (0, 0))
    stack = pl.BlockSpec((3, length, HEAD_DIM), lambda h, idx: (0, 0, h))
    return pl.pallas_call(
        attention_kernel,
        grid_spec=pltpu.PrefetchScalarGridSpec(
            num_scalar_prefetch=1,
            grid=(heads,),
            in_specs=[
                block,
                block,
                pl.BlockSpec((3, part, HEAD_DIM), lambda h, idx: (0, idx[size], first + h)),
                pl.BlockSpec((3, part, HEAD_DIM), lambda h, idx: (0, 1 - idx[size], first + h)),
                stack,
                stack,
                pl.BlockSpec((length, HEAD_DIM), lambda h, idx: (0, first + h)),
                table,
                table,
            ],
            out_specs=[
                pl.BlockSpec((length, HEAD_DIM), lambda h, idx: (0, h)),
                table,
                stack,
            ],
        ),
        out_shape=[
            jax.ShapeDtypeStruct((length, wide), jnp.bfloat16),
            jax.ShapeDtypeStruct((length, HEAD_DIM), jnp.float32),
            jax.ShapeDtypeStruct((3, length, wide), jnp.bfloat16),
        ],
        compiler_params=params(16),
        cost_estimate=cost(12 * length * part * wide, 24 * part * wide),
        name="attention",
    )(idx, mine, other, weights, weights, from_left, from_right, d_out, *tables)


def grads_kernel(turned, *refs):
    blocks = jnp.concatenate([piece[0] for piece in refs[:-1]], axis=0)
    refs[-1][0] = mm(turned[...], blocks)


def grads_chunk(turned, pieces, before, ties, chunk, wide, columns):
    depth, span = turned.shape
    aliases = {} if before is None else {1 + len(pieces): 0}
    ties = ties if before is None else [before, *ties]
    return pl.pallas_call(
        tied(grads_kernel, 1 + len(pieces), len(ties)),
        grid=(3,),
        in_specs=[
            pl.BlockSpec((depth, span), lambda m: (0, 0)),
            *[pl.BlockSpec((1, *piece.shape[1:]), lambda m: (m, 0, 0)) for piece in pieces],
            *tie_specs(ties),
        ],
        out_specs=pl.BlockSpec((1, depth, wide), lambda m: (m, 0, chunk)),
        out_shape=jax.ShapeDtypeStruct((3, depth, columns), jnp.float32),
        input_output_aliases=aliases,
        compiler_params=params(24),
        cost_estimate=cost(6 * span * depth * wide, 6 * span * wide + 12 * depth * wide),
        name="grads",
    )(turned, *pieces, *ties)


def back(pieces, turned, chunk):
    wide = pieces[0].shape[2]
    rows = [jnp.concatenate([piece[m] for m in range(3)], axis=1) for piece in pieces]
    weight = [turned[m, chunk * wide : (chunk + 1) * wide] for m in range(3)]
    return mm(jnp.concatenate(rows, axis=0), jnp.concatenate(weight, axis=0))


def term_step(turned, pieces, befores, chunk):
    depth, wide = turned.shape[2], pieces[0].shape[2]
    count, rows = len(pieces), pieces[0].shape[1]
    whole = pl.BlockSpec(memory_space=pltpu.VMEM)

    def kernel(turned_ref, *refs):
        total = back(refs[:count], turned_ref, chunk)
        for place in range(count):
            block = total[place * rows : (place + 1) * rows]
            if befores:
                block += refs[count + place][...]
            refs[len(refs) - count + place][...] = block

    return pl.pallas_call(
        kernel,
        in_specs=[whole] * (1 + count + len(befores)),
        out_specs=[whole] * count,
        out_shape=[jax.ShapeDtypeStruct((rows, depth), jnp.float32)] * count,
        compiler_params=pltpu.CompilerParams(vmem_limit_bytes=16 * MIB),
        cost_estimate=cost(6 * count * rows * depth * wide, 12 * count * rows * wide),
        name="term_step",
    )(turned, *pieces, *befores)


def term_last_kernel(count, idx, turned, *refs):
    befores, fars, nears = refs[:2], refs[2:4], refs[4 : 3 + count]
    keeps, sends = refs[-4:-2], refs[-2:]
    half = keeps[0].shape[1]
    last = back(fars, turned, 1)
    for place in range(count):
        for part in range(2):
            span = slice(part * half, (part + 1) * half)
            total = nears[place][span] if place < count - 1 else last[span] + befores[part][...]

            @pl.when(idx[2 * count + 1 + place] == 0)
            def _():
                keeps[part][idx[3 * count + 1 + place]] = total

            @pl.when(idx[2 * count + 1 + place] == 1)
            def _():
                sends[part][idx[3 * count + 1 + place]] = total.astype(jnp.bfloat16)


def term_last(idx, turned, befores, pieces, nears):
    count = len(nears) + 1
    rows, depth = nears[0].shape
    whole = pl.BlockSpec(memory_space=pltpu.VMEM)
    shape = (count // 2, rows // 2, depth)
    return pl.pallas_call(
        functools.partial(term_last_kernel, count),
        in_specs=[pl.BlockSpec(memory_space=pltpu.SMEM)] + [whole] * (count + 4),
        out_specs=[whole] * 4,
        out_shape=[jax.ShapeDtypeStruct(shape, jnp.float32)] * 2
        + [jax.ShapeDtypeStruct(shape, jnp.bfloat16)] * 2,
        compiler_params=pltpu.CompilerParams(vmem_limit_bytes=12 * MIB),
        cost_estimate=cost(rows * depth * depth, 12 * count * rows * depth),
        name="term_last",
    )(idx, turned, *befores, *pieces, *nears)


def split_kernel(column, group, idx, keep, came, keep_out, send_out):
    own = idx[column]
    for block in range(keep_out.shape[0]):
        high, low = block // group, block % group
        mine = (2 * high + own) * group + low
        other = (2 * high + 1 - own) * group + low
        keep_out[block] = keep[mine] + came[mine].astype(jnp.float32)
        send_out[block] = (keep[other] + came[other].astype(jnp.float32)).astype(jnp.bfloat16)


def split_sum(idx, column, group, keep, came):
    whole = pl.BlockSpec(memory_space=pltpu.VMEM)
    shape = (keep.shape[0] // 2, *keep.shape[1:])
    return pl.pallas_call(
        functools.partial(split_kernel, column, group),
        in_specs=[pl.BlockSpec(memory_space=pltpu.SMEM), whole, whole],
        out_specs=[whole, whole],
        out_shape=[
            jax.ShapeDtypeStruct(shape, jnp.float32),
            jax.ShapeDtypeStruct(shape, jnp.bfloat16),
        ],
        compiler_params=pltpu.CompilerParams(vmem_limit_bytes=4 * MIB),
        cost_estimate=cost(0, 8 * keep.shape[0] * keep.shape[1] * keep.shape[2]),
        name="split_sum",
    )(idx, keep, came)


def order_kernel(column, idx, keep, came, *outs):
    for turn, out in enumerate(outs):
        block = idx[column + turn]
        out[...] = (keep[block] + came[block].astype(jnp.float32)).astype(jnp.bfloat16)


def order_sum(idx, column, keep, came):
    whole = pl.BlockSpec(memory_space=pltpu.VMEM)
    count = keep.shape[0]
    return pl.pallas_call(
        functools.partial(order_kernel, column),
        in_specs=[pl.BlockSpec(memory_space=pltpu.SMEM), whole, whole],
        out_specs=[whole] * count,
        out_shape=[jax.ShapeDtypeStruct(keep.shape[1:], jnp.bfloat16)] * count,
        compiler_params=pltpu.CompilerParams(vmem_limit_bytes=4 * MIB),
        cost_estimate=cost(0, 8 * count * keep.shape[1] * keep.shape[2]),
        name="order_sum",
    )(idx, keep, came)


def finish_kernel(column, width, idx, tokens, gain, inverse, dots, *refs):
    came, out, gains = refs[:-2], refs[-2], refs[-1]
    rows, depth = came[0].shape
    group = out.shape[1] // depth
    gains[...] = gain[...].astype(jnp.float32)
    for turn in range(group):
        features = pl.ds(pl.multiple_of(idx[column + turn] * depth, depth), depth)
        for part in range(len(came) // group):
            span = slice(part * rows, (part + 1) * rows)
            scale = inverse[span, :1]
            upstream = came[part * group + turn][...].astype(jnp.float32)
            values = tokens[span, features].astype(jnp.float32)
            common = scale * scale * dots[span] / width
            out[span, features] = (
                scale * gains[:, features] * upstream - values * common
            ).astype(jnp.bfloat16)


def finish(idx, column, tokens, gain, inverse, dots, came, share):
    length, width = tokens.shape
    node = column + share // came[0].shape[1]
    whole = pl.BlockSpec(memory_space=pltpu.VMEM)
    return pl.pallas_call(
        functools.partial(finish_kernel, column, width),
        grid_spec=pltpu.PrefetchScalarGridSpec(
            num_scalar_prefetch=1,
            grid=(1,),
            in_specs=[
                pl.BlockSpec((length, share), lambda i, idx: (0, idx[node])),
                pl.BlockSpec((1, share), lambda i, idx: (0, idx[node])),
                *[whole] * (2 + len(came)),
            ],
            out_specs=pl.BlockSpec((length, share), lambda i, idx: (0, 0)),
            scratch_shapes=[pltpu.VMEM((1, share), jnp.float32)],
        ),
        out_shape=jax.ShapeDtypeStruct((length, share), jnp.bfloat16),
        compiler_params=params(12),
        cost_estimate=cost(8 * length * share, 6 * length * share),
        name="finish",
    )(idx, tokens, gain, inverse, dots, *came)


def local(tokens, norm_gain, w_quant, w_scale, d_out):
    length, width = tokens.shape
    depth, columns = w_quant.shape[1:]
    size, nodes = lax.axis_size("local"), lax.axis_size("node")
    here, node = lax.axis_index("local"), lax.axis_index("node")
    wide = columns // 2
    far = size // 2
    group, groups = size // nodes, group_of(nodes)

    order = ring_order(size)
    distances = ring_distances(size)
    table = jnp.asarray(index_table(size, nodes))
    idx = lax.dynamic_index_in_dim(table, node * size + here, 0, keepdims=False)

    def shift(array, distance):
        moves = [(order[i], order[(i + distance) % size]) for i in range(size)]
        return lax.ppermute(array, "local", moves)

    def swap(array, bit):
        return lax.ppermute(array, "node", [(n, n ^ bit) for n in range(nodes)])

    blocks, inverse_rms = normed_blocks(idx, tokens, norm_gain[None], size, depth // 2)
    mine_far = shift(blocks[far], far)
    other_far = swap(mine_far, 1)
    weights, turned = scaled_weights(w_quant, w_scale)
    firsts = sum_first(idx, size, mine_far, other_far, weights)
    mine = stack(
        [shift(blocks[-d % size], -d) if d else blocks[0] for d in distances[:-1]], firsts[:1]
    )
    other = swap(mine, 1)

    rows_turned = turn(idx, mine, other, mine_far, other_far)

    tables = rope_tables(length, HEAD_DIM)
    arrived = []
    for chunk in range(2):
        right, left = firsts[2 * chunk : 2 * chunk + 2]
        for distance in range(far - 1, -1, -1):
            from_left, from_right = shift(right, 1), shift(left, -1)
            if distance:
                places = distances.index(distance), distances.index(-distance)
                ties = [rows_turned] if distance == 1 else []
                right, left = sum_step(
                    idx, size, mine, other, places, weights, from_left, from_right, chunk, wide, ties
                )
        arrived.append((from_left, from_right))

    outputs, sets, dots = [], [], 0.0
    for chunk in range(2):
        output, product, pre = attention(
            idx, size, mine, other, weights, *arrived[chunk], d_out, tables, chunk, wide
        )
        outputs.append(output)
        sets.append(pre)
        dots += jnp.sum(product, axis=-1, keepdims=True)
    bit = 1
    while bit < nodes:
        dots = dots + swap(dots, bit)
        bit *= 2

    def sum_nodes(keep, send):
        column = 4 * size + 1
        bit = 1
        while 2 * bit < nodes:
            keep, send = split_sum(idx, column, group, keep, swap(send, bit))
            column += 1
            bit *= 2
        return order_sum(idx, column, keep, swap(send, bit))

    def relocate(blocks):
        came = []
        for turn, block in enumerate(blocks):
            moves = [
                (n * size + s, (s // group) * size + groups[n] * group + (s + turn) % group)
                for n in range(nodes)
                for s in range(size)
            ]
            came.append(lax.ppermute(block, ("node", "local"), moves))
        return came

    gathered = [[block] for block in sets]
    moving = [(block, block) for block in sets]
    terms = [[], []]
    for step in range(1, far + 1):
        for chunk in range(2):
            right, left = moving[chunk]
            if step == far:
                early = [dots] if chunk == 0 else terms[1][: size - 3]
                right, left = halve(right, left, early)
            right, left = shift(right, 1), shift(left, -1)
            moving[chunk] = right, left
            gathered[chunk] += [right, left]
            if step < far:
                pieces = gathered[chunk] if step == 1 else [right, left]
                known = len(terms[chunk])
                befores = terms[0][known : known + len(pieces)] if chunk else []
                terms[chunk] += term_step(turned, pieces, befores, chunk)
            elif chunk == 0:
                lasts = term_step(turned, [right, left], [], 0)
    keep_0, keep_1, send_0, send_1 = term_last(idx, turned, lasts, gathered[1][-2:], terms[1])
    first, second = sum_nodes(keep_0, send_0), sum_nodes(keep_1, send_1)
    came = [*relocate(first), *relocate(second)]
    column = idx.shape[0] - 1 - group
    d_tokens = finish(
        idx, column, tokens, norm_gain[None], inverse_rms, dots, came, width // nodes
    )
    grads = grads_chunk(rows_turned, gathered[0], None, [keep_1], 0, wide, columns)
    sums = [first[0], second[0]]
    grads = grads_chunk(rows_turned, gathered[1], grads, sums, 1, wide, columns)
    return (jnp.concatenate(outputs, axis=-1), d_tokens, grads)


def solution(mesh):
    placed = (
        P("local", None),
        P(),
        P(None, "local", "node"),
        P(None, "local", "node"),
        P("local", "node"),
    )
    return jax.shard_map(
        local,
        mesh=mesh,
        in_specs=placed,
        out_specs=(P("local", "node"), P("local", "node"), P(None, "local", "node")),
        check_vma=False,
    )
```

```python
import functools
import math

import jax
import jax.numpy as jnp
import numpy as np
from jax import lax
from jax.experimental import pallas as pl
from jax.experimental.pallas import tpu as pltpu
from jax.sharding import PartitionSpec as P

HEAD_DIM = 128
NORM_EPS = 1e-05
MIB = 1024 * 1024


def params(limit):
    return pltpu.CompilerParams(
        dimension_semantics=("arbitrary",), vmem_limit_bytes=limit * MIB
    )


def tied(kernel, inputs, ties):
    def inner(*refs):
        kernel(*refs[:inputs], *refs[inputs + ties :])

    return inner


def tie_specs(ties):
    return [pl.BlockSpec(memory_space=pl.ANY)] * len(ties)


def cost(flops, moved):
    return pl.CostEstimate(flops=flops, bytes_accessed=moved, transcendentals=0)


def mm(a, b):
    return jnp.dot(a, b, preferred_element_type=jnp.float32)


def mm_nt(a, b):
    return lax.dot_general(a, b, (((1,), (1,)), ((), ())), preferred_element_type=jnp.float32)


def mm_tn(a, b):
    return lax.dot_general(a, b, (((0,), (0,)), ((), ())), preferred_element_type=jnp.float32)


def rope_tables(length, width):
    position = jnp.arange(length).astype(jnp.float32)[:, None]
    frequency = jnp.exp(
        jnp.arange(width // 2).astype(jnp.float32) * (-2.0 * math.log(10000.0) / width)
    )
    angle = position * frequency[None, :]
    cosine, sine = jnp.cos(angle), jnp.sin(angle)
    return (
        jnp.concatenate([cosine, cosine], axis=-1),
        jnp.concatenate([-sine, sine], axis=-1),
    )


def ring_order(size):
    return [*range(0, size, 2), *reversed(range(1, size, 2))]


def ring_distances(size):
    far = size // 2
    distances = [0]
    for step in range(1, far):
        distances += [-step, step]
    return [*distances, far]


def group_of(nodes):
    bits = nodes.bit_length() - 1
    return [sum((node >> bit & 1) << (bits - 1 - bit) for bit in range(bits)) for node in range(nodes)]


def index_table(size, nodes):
    order, group = ring_order(size), size // nodes
    rows = []
    for node in range(nodes):
        for here in range(size):
            place = order.index(here)
            seqs = [order[(place + distance) % size] for distance in ring_distances(size)]
            owner = [group_of(nodes).index(seq // group) for seq in seqs]
            rows.append(
                [order[(place + distance) % size] for distance in range(size)]
                + [node % 2]
                + seqs
                + [owner_ % 2 ^ node % 2 for owner_ in owner]
                + [(o // 2) * group + seq % group for o, seq in zip(owner, seqs)]
                + [node >> level & 1 for level in range(1, nodes.bit_length() - 1)]
                + [(here + turn) % group for turn in range(group)]
                + [(here - turn) % group for turn in range(group)]
                + [node]
            )
    return np.array(rows, np.int32)


def weights_kernel(quant, scale, out, turned):
    blocks = scale.shape[1]
    rows = quant.shape[1] // blocks
    scales = scale[0].astype(jnp.float32)
    for block in range(blocks):
        span = slice(block * rows, (block + 1) * rows)
        scaled = (quant[0, span].astype(jnp.float32) * scales[block : block + 1]).astype(jnp.bfloat16)
        out[0, span] = scaled
        turned[0, :, span] = scaled.T


def scaled_weights(w_quant, w_scale):
    _, depth, columns = w_quant.shape
    blocks = w_scale.shape[1]
    return pl.pallas_call(
        weights_kernel,
        grid=(3,),
        in_specs=[
            pl.BlockSpec((1, depth, columns), lambda m: (m, 0, 0)),
            pl.BlockSpec((1, blocks, columns), lambda m: (m, 0, 0)),
        ],
        out_specs=[
            pl.BlockSpec((1, depth, columns), lambda m: (m, 0, 0)),
            pl.BlockSpec((1, columns, depth), lambda m: (m, 0, 0)),
        ],
        out_shape=[
            jax.ShapeDtypeStruct((3, depth, columns), jnp.bfloat16),
            jax.ShapeDtypeStruct((3, columns, depth), jnp.bfloat16),
        ],
        compiler_params=params(20),
        cost_estimate=cost(3 * depth * columns, 18 * depth * columns),
        name="scaled_weights",
    )(w_quant, w_scale)


def normed_kernel(idx, tokens, gain, *refs):
    outs, gains = refs[:-1], refs[-1]
    width, part = tokens.shape[1], outs[0].shape[1]
    gains[...] = gain[...].astype(jnp.float32)
    values = tokens[...].astype(jnp.float32)
    inverse = lax.rsqrt(jnp.mean(values * values, axis=-1, keepdims=True) + NORM_EPS)
    size = len(outs) - 1
    for distance in range(size):
        start = pl.multiple_of(idx[distance] * (width // size) + idx[size] * part, part)
        block = tokens[:, pl.ds(start, part)].astype(jnp.float32)
        scale = gains[:, pl.ds(start, part)]
        outs[distance][...] = (block * inverse * scale).astype(jnp.bfloat16)
    outs[size][...] = jnp.broadcast_to(inverse, outs[size].shape)


def normed_blocks(idx, tokens, gain, size, part):
    length, width = tokens.shape
    tile = length // 4
    block = pl.BlockSpec((tile, part), lambda i, idx: (i, 0))
    *blocks, inverse = pl.pallas_call(
        normed_kernel,
        grid_spec=pltpu.PrefetchScalarGridSpec(
            num_scalar_prefetch=1,
            grid=(4,),
            in_specs=[
                pl.BlockSpec((tile, width), lambda i, idx: (i, 0)),
                pl.BlockSpec((1, width), lambda i, idx: (0, 0)),
            ],
            out_specs=[block] * size + [pl.BlockSpec((tile, 128), lambda i, idx: (i, 0))],
            scratch_shapes=[pltpu.VMEM((1, width), jnp.float32)],
        ),
        out_shape=[jax.ShapeDtypeStruct((length, part), jnp.bfloat16)] * size
        + [jax.ShapeDtypeStruct((length, 128), jnp.float32)],
        compiler_params=params(12),
        cost_estimate=cost(8 * length * width, 4 * length * width),
        name="normed_blocks",
    )(idx, tokens, gain)
    return blocks, inverse


def stack_kernel(*refs):
    for place, block in enumerate(refs[:-1]):
        refs[-1][place] = block[...]


def stack(blocks, ties):
    count, shape = len(blocks), blocks[0].shape
    block = pl.BlockSpec(shape, lambda i: (0, 0))
    return pl.pallas_call(
        tied(stack_kernel, count, len(ties)),
        grid=(1,),
        in_specs=[block] * count + tie_specs(ties),
        out_specs=pl.BlockSpec((count, *shape), lambda i: (0, 0, 0)),
        out_shape=jax.ShapeDtypeStruct((count, *shape), blocks[0].dtype),
        compiler_params=params(10),
        cost_estimate=cost(0, 4 * count * shape[0] * shape[1]),
        name="stack",
    )(*blocks, *ties)


def halve_kernel(right, left, right_out, left_out):
    half = right_out.shape[1]
    right_out[...] = right[:, :half]
    left_out[...] = left[:, half:]


def halve(right, left, ties):
    _, rows, wide = right.shape
    result = jax.ShapeDtypeStruct((3, rows // 2, wide), right.dtype)
    whole = pl.BlockSpec(memory_space=pltpu.VMEM)
    return pl.pallas_call(
        tied(halve_kernel, 2, len(ties)),
        in_specs=[whole, whole] + tie_specs(ties),
        out_specs=[whole, whole],
        out_shape=[result, result],
        compiler_params=pltpu.CompilerParams(vmem_limit_bytes=4 * MIB),
        cost_estimate=cost(0, 6 * rows * wide),
        name="halve",
    )(right, left, *ties)


def turn_kernel(count, idx, mine, other, mine_far, other_far, out):
    length, part = mine_far.shape
    for side, near, last in ((0, mine, mine_far), (1, other, other_far)):
        half = idx[count] * (1 - side) + (1 - idx[count]) * side
        rows = pl.ds(pl.multiple_of(half * part, part), part)
        for place in range(count):
            block = near[place] if place < count - 1 else last[...]
            out[rows, place * length : (place + 1) * length] = block.T


def turn(idx, mine, other, mine_far, other_far):
    near, length, part = mine.shape
    count = near + 1
    stack = pl.BlockSpec(mine.shape, lambda i, idx: (0, 0, 0))
    last = pl.BlockSpec((length, part), lambda i, idx: (0, 0))
    shape = (2 * part, count * length)
    return pl.pallas_call(
        functools.partial(turn_kernel, count),
        grid_spec=pltpu.PrefetchScalarGridSpec(
            num_scalar_prefetch=1,
            grid=(1,),
            in_specs=[stack, stack, last, last],
            out_specs=pl.BlockSpec(shape, lambda i, idx: (0, 0)),
        ),
        out_shape=jax.ShapeDtypeStruct(shape, jnp.bfloat16),
        compiler_params=params(12),
        cost_estimate=cost(2 * count * length * part, 8 * count * length * part),
        name="turn",
    )(idx, mine, other, mine_far, other_far)


def sum_first_kernel(idx, mine, other, weight, weight_other, *outs):
    half, wide = outs[0].shape[1:]
    for chunk in range(2):
        span = slice(chunk * wide, (chunk + 1) * wide)
        product = mm(mine[...], weight[0, :, span]) + mm(other[...], weight_other[0, :, span])
        outs[2 * chunk][0] = product[:half].astype(jnp.bfloat16)
        outs[2 * chunk + 1][0] = product[half:].astype(jnp.bfloat16)


def sum_step_kernel(
    idx, mine_r, other_r, mine_l, other_l, weight, weight_other, from_left, from_right, right, left
):
    length, part = right.shape[1], from_left.shape[1]
    product = mm(mine_r[0], weight[0]) + mm(other_r[0], weight_other[0])
    right[0, :part] = (product[:part] + from_left[0].astype(jnp.float32)).astype(jnp.bfloat16)
    if part < length:
        right[0, part:] = product[part:].astype(jnp.bfloat16)
    product = mm(mine_l[0], weight[0]) + mm(other_l[0], weight_other[0])
    rest = length - part
    left[0, rest:] = (product[rest:] + from_right[0].astype(jnp.float32)).astype(jnp.bfloat16)
    if rest:
        left[0, :rest] = product[:rest].astype(jnp.bfloat16)


def weight_halves(size, part, wide, chunk):
    return [
        pl.BlockSpec((1, part, wide), lambda m, idx: (m, idx[size], chunk)),
        pl.BlockSpec((1, part, wide), lambda m, idx: (m, 1 - idx[size], chunk)),
    ]


def sum_first(idx, size, mine, other, weights):
    length, part = mine.shape
    columns = weights.shape[2]
    half, wide = length // 2, columns // 2
    block = pl.BlockSpec((length, part), lambda m, idx: (0, 0))
    result = jax.ShapeDtypeStruct((3, half, wide), jnp.bfloat16)
    return pl.pallas_call(
        sum_first_kernel,
        grid_spec=pltpu.PrefetchScalarGridSpec(
            num_scalar_prefetch=1,
            grid=(3,),
            in_specs=[block, block, *weight_halves(size, part, columns, 0)],
            out_specs=[pl.BlockSpec((1, half, wide), lambda m, idx: (m, 0, 0))] * 4,
        ),
        out_shape=[result] * 4,
        compiler_params=params(12),
        cost_estimate=cost(12 * length * part * columns, 16 * part * columns),
        name="sum_first",
    )(idx, mine, other, weights, weights)


def sum_step(idx, size, mine, other, places, weights, from_left, from_right, chunk, wide, ties):
    _, length, part = mine.shape
    block_r = pl.BlockSpec((1, length, part), lambda m, idx: (places[0], 0, 0))
    block_l = pl.BlockSpec((1, length, part), lambda m, idx: (places[1], 0, 0))
    came = pl.BlockSpec((1, from_left.shape[1], wide), lambda m, idx: (m, 0, 0))
    whole = jax.ShapeDtypeStruct((3, length, wide), jnp.bfloat16)
    return pl.pallas_call(
        tied(sum_step_kernel, 9, len(ties)),
        grid_spec=pltpu.PrefetchScalarGridSpec(
            num_scalar_prefetch=1,
            grid=(3,),
            in_specs=[
                block_r,
                block_r,
                block_l,
                block_l,
                *weight_halves(size, part, wide, chunk),
                came,
                came,
                *tie_specs(ties),
            ],
            out_specs=[pl.BlockSpec((1, length, wide), lambda m, idx: (m, 0, 0))] * 2,
        ),
        out_shape=[whole, whole],
        compiler_params=params(12),
        cost_estimate=cost(24 * length * part * wide, 24 * part * wide),
        name="sum_step",
    )(idx, mine, other, mine, other, weights, weights, from_left, from_right, *ties)


def attention_kernel(
    idx, mine, other, weight, weight_other, from_left, from_right, d_out, cosine, sine,
    output, dots, pre,
):
    length = mine.shape[1]
    proj = [
        mm(mine[0], weight[m])
        + mm(other[0], weight_other[m])
        + (from_left[m].astype(jnp.float32) + from_right[m].astype(jnp.float32))
        for m in range(3)
    ]
    cos, sin = cosine[...], sine[...]
    half = HEAD_DIM // 2

    def rotate(tensor, angle):
        return tensor * cos + pltpu.roll(tensor, half, 1) * angle

    query = rotate(proj[0], sin).astype(jnp.bfloat16)
    key_rows = rotate(proj[1], sin).astype(jnp.bfloat16)
    value = proj[2].astype(jnp.bfloat16)
    scores = mm_nt(query, key_rows) * (1.0 / math.sqrt(HEAD_DIM))
    causal = lax.broadcasted_iota(jnp.int32, (length, length), 0) >= lax.broadcasted_iota(
        jnp.int32, (length, length), 1
    )
    scores = jnp.where(causal, scores, jnp.float32(-1e30))
    powers = jnp.exp(scores - jnp.max(scores, axis=-1, keepdims=True))
    probs = powers * (1.0 / jnp.sum(powers, axis=-1, keepdims=True))
    probs_low = probs.astype(jnp.bfloat16)
    output[...] = mm(probs_low, value).astype(jnp.bfloat16)
    cotangent = d_out[...]
    d_value = mm_tn(probs_low, cotangent).astype(jnp.bfloat16)
    d_probs = mm_nt(cotangent, value).astype(jnp.bfloat16).astype(jnp.float32)
    inner = jnp.sum(d_probs * probs, axis=-1, keepdims=True)
    d_scores = (probs * (d_probs - inner) * (1.0 / math.sqrt(HEAD_DIM))).astype(jnp.bfloat16)
    d_query = mm(d_scores, key_rows).astype(jnp.bfloat16).astype(jnp.float32)
    d_key = mm_tn(d_scores, query).astype(jnp.bfloat16).astype(jnp.float32)
    pre_query = rotate(d_query, -sin).astype(jnp.bfloat16)
    pre_key = rotate(d_key, -sin).astype(jnp.bfloat16)
    pre[0] = pre_query
    pre[1] = pre_key
    pre[2] = d_value
    product = (
        pre_query.astype(jnp.float32) * proj[0]
        + pre_key.astype(jnp.float32) * proj[1]
        + d_value.astype(jnp.float32) * proj[2]
    )

    @pl.when(pl.program_id(0) == 0)
    def _():
        dots[...] = product

    @pl.when(pl.program_id(0) > 0)
    def _():
        dots[...] += product


def attention(idx, size, mine, other, weights, from_left, from_right, d_out, tables, chunk, wide):
    _, length, part = mine.shape
    heads = wide // HEAD_DIM
    first = chunk * heads
    block = pl.BlockSpec((1, length, part), lambda h, idx: (0, 0, 0))
    table = pl.BlockSpec((length, HEAD_DIM), lambda h, idx: (0, 0))
    stack = pl.BlockSpec((3, length, HEAD_DIM), lambda h, idx: (0, 0, h))
    return pl.pallas_call(
        attention_kernel,
        grid_spec=pltpu.PrefetchScalarGridSpec(
            num_scalar_prefetch=1,
            grid=(heads,),
            in_specs=[
                block,
                block,
                pl.BlockSpec((3, part, HEAD_DIM), lambda h, idx: (0, idx[size], first + h)),
                pl.BlockSpec((3, part, HEAD_DIM), lambda h, idx: (0, 1 - idx[size], first + h)),
                stack,
                stack,
                pl.BlockSpec((length, HEAD_DIM), lambda h, idx: (0, first + h)),
                table,
                table,
            ],
            out_specs=[
                pl.BlockSpec((length, HEAD_DIM), lambda h, idx: (0, h)),
                table,
                stack,
            ],
        ),
        out_shape=[
            jax.ShapeDtypeStruct((length, wide), jnp.bfloat16),
            jax.ShapeDtypeStruct((length, HEAD_DIM), jnp.float32),
            jax.ShapeDtypeStruct((3, length, wide), jnp.bfloat16),
        ],
        compiler_params=params(16),
        cost_estimate=cost(12 * length * part * wide, 24 * part * wide),
        name="attention",
    )(idx, mine, other, weights, weights, from_left, from_right, d_out, *tables)


def grads_kernel(turned, *refs):
    pieces, out, token = refs[:-2], refs[-2], refs[-1]
    blocks = jnp.concatenate([piece[0] for piece in pieces], axis=0)
    out[0] = mm(turned[...], blocks)
    token[...] = jnp.zeros_like(token)


def grads_chunk(turned, pieces, before, ties, chunk, wide, columns):
    depth, span = turned.shape
    aliases = {} if before is None else {1 + len(pieces): 0}
    ties = ties if before is None else [before, *ties]
    return pl.pallas_call(
        tied(grads_kernel, 1 + len(pieces), len(ties)),
        grid=(3,),
        in_specs=[
            pl.BlockSpec((depth, span), lambda m: (0, 0)),
            *[pl.BlockSpec((1, *piece.shape[1:]), lambda m: (m, 0, 0)) for piece in pieces],
            *tie_specs(ties),
        ],
        out_specs=[
            pl.BlockSpec((1, depth, wide), lambda m: (m, 0, chunk)),
            pl.BlockSpec((8, 128), lambda m: (0, 0)),
        ],
        out_shape=[
            jax.ShapeDtypeStruct((3, depth, columns), jnp.float32),
            jax.ShapeDtypeStruct((8, 128), jnp.float32),
        ],
        input_output_aliases=aliases,
        compiler_params=params(24),
        cost_estimate=cost(6 * span * depth * wide, 6 * span * wide + 12 * depth * wide),
        name="grads",
    )(turned, *pieces, *ties)


def back(pieces, turned, chunk):
    wide = pieces[0].shape[2]
    rows = [jnp.concatenate([piece[m] for m in range(3)], axis=1) for piece in pieces]
    weight = [turned[m, chunk * wide : (chunk + 1) * wide] for m in range(3)]
    return mm(jnp.concatenate(rows, axis=0), jnp.concatenate(weight, axis=0))


def term_step(turned, pieces, befores, chunk):
    depth, wide = turned.shape[2], pieces[0].shape[2]
    count, rows = len(pieces), pieces[0].shape[1]
    whole = pl.BlockSpec(memory_space=pltpu.VMEM)

    def kernel(turned_ref, *refs):
        total = back(refs[:count], turned_ref, chunk)
        for place in range(count):
            block = total[place * rows : (place + 1) * rows]
            if befores:
                block += refs[count + place][...]
            refs[len(refs) - count + place][...] = block

    return pl.pallas_call(
        kernel,
        in_specs=[whole] * (1 + count + len(befores)),
        out_specs=[whole] * count,
        out_shape=[jax.ShapeDtypeStruct((rows, depth), jnp.float32)] * count,
        compiler_params=pltpu.CompilerParams(vmem_limit_bytes=16 * MIB),
        cost_estimate=cost(6 * count * rows * depth * wide, 12 * count * rows * wide),
        name="term_step",
    )(turned, *pieces, *befores)


def term_last_kernel(count, idx, turned, *refs):
    befores, fars, nears = refs[:2], refs[2:4], refs[4 : 3 + count]
    keeps, sends = refs[-4:-2], refs[-2:]
    half = keeps[0].shape[1]
    last = back(fars, turned, 1)
    for place in range(count):
        for part in range(2):
            span = slice(part * half, (part + 1) * half)
            total = nears[place][span] if place < count - 1 else last[span] + befores[part][...]

            @pl.when(idx[2 * count + 1 + place] == 0)
            def _():
                keeps[part][idx[3 * count + 1 + place]] = total

            @pl.when(idx[2 * count + 1 + place] == 1)
            def _():
                sends[part][idx[3 * count + 1 + place]] = total.astype(jnp.bfloat16)


def term_last(idx, turned, befores, pieces, nears, ties):
    count = len(nears) + 1
    rows, depth = nears[0].shape
    whole = pl.BlockSpec(memory_space=pltpu.VMEM)
    shape = (count // 2, rows // 2, depth)
    return pl.pallas_call(
        tied(functools.partial(term_last_kernel, count), count + 5, len(ties)),
        in_specs=[pl.BlockSpec(memory_space=pltpu.SMEM)]
        + [whole] * (count + 4)
        + tie_specs(ties),
        out_specs=[whole] * 4,
        out_shape=[jax.ShapeDtypeStruct(shape, jnp.float32)] * 2
        + [jax.ShapeDtypeStruct(shape, jnp.bfloat16)] * 2,
        compiler_params=pltpu.CompilerParams(vmem_limit_bytes=12 * MIB),
        cost_estimate=cost(rows * depth * depth, 12 * count * rows * depth),
        name="term_last",
    )(idx, turned, *befores, *pieces, *nears, *ties)


def split_kernel(column, group, idx, keep, came, keep_out, send_out):
    own = idx[column]
    for block in range(keep_out.shape[0]):
        high, low = block // group, block % group
        mine = (2 * high + own) * group + low
        other = (2 * high + 1 - own) * group + low
        keep_out[block] = keep[mine] + came[mine].astype(jnp.float32)
        send_out[block] = (keep[other] + came[other].astype(jnp.float32)).astype(jnp.bfloat16)


def split_sum(idx, column, group, keep, came):
    whole = pl.BlockSpec(memory_space=pltpu.VMEM)
    shape = (keep.shape[0] // 2, *keep.shape[1:])
    return pl.pallas_call(
        functools.partial(split_kernel, column, group),
        in_specs=[pl.BlockSpec(memory_space=pltpu.SMEM), whole, whole],
        out_specs=[whole, whole],
        out_shape=[
            jax.ShapeDtypeStruct(shape, jnp.float32),
            jax.ShapeDtypeStruct(shape, jnp.bfloat16),
        ],
        compiler_params=pltpu.CompilerParams(vmem_limit_bytes=4 * MIB),
        cost_estimate=cost(0, 8 * keep.shape[0] * keep.shape[1] * keep.shape[2]),
        name="split_sum",
    )(idx, keep, came)


def order_kernel(column, idx, keep, came, *outs):
    for turn, out in enumerate(outs):
        block = idx[column + turn]
        out[...] = (keep[block] + came[block].astype(jnp.float32)).astype(jnp.bfloat16)


def order_sum(idx, column, keep, came):
    whole = pl.BlockSpec(memory_space=pltpu.VMEM)
    count = keep.shape[0]
    return pl.pallas_call(
        functools.partial(order_kernel, column),
        in_specs=[pl.BlockSpec(memory_space=pltpu.SMEM), whole, whole],
        out_specs=[whole] * count,
        out_shape=[jax.ShapeDtypeStruct(keep.shape[1:], jnp.bfloat16)] * count,
        compiler_params=pltpu.CompilerParams(vmem_limit_bytes=4 * MIB),
        cost_estimate=cost(0, 8 * count * keep.shape[1] * keep.shape[2]),
        name="order_sum",
    )(idx, keep, came)


def finish_kernel(column, width, idx, tokens, gain, inverse, dots, *refs):
    came, out, gains = refs[:-2], refs[-2], refs[-1]
    rows, depth = came[0].shape
    group = out.shape[1] // depth
    gains[...] = gain[...].astype(jnp.float32)
    for turn in range(group):
        features = pl.ds(pl.multiple_of(idx[column + turn] * depth, depth), depth)
        for part in range(len(came) // group):
            span = slice(part * rows, (part + 1) * rows)
            scale = inverse[span, :1]
            upstream = came[part * group + turn][...].astype(jnp.float32)
            values = tokens[span, features].astype(jnp.float32)
            common = scale * scale * dots[span] / width
            out[span, features] = (
                scale * gains[:, features] * upstream - values * common
            ).astype(jnp.bfloat16)


def finish(idx, column, tokens, gain, inverse, dots, came, share):
    length, width = tokens.shape
    node = column + share // came[0].shape[1]
    whole = pl.BlockSpec(memory_space=pltpu.VMEM)
    return pl.pallas_call(
        functools.partial(finish_kernel, column, width),
        grid_spec=pltpu.PrefetchScalarGridSpec(
            num_scalar_prefetch=1,
            grid=(1,),
            in_specs=[
                pl.BlockSpec((length, share), lambda i, idx: (0, idx[node])),
                pl.BlockSpec((1, share), lambda i, idx: (0, idx[node])),
                *[whole] * (2 + len(came)),
            ],
            out_specs=pl.BlockSpec((length, share), lambda i, idx: (0, 0)),
            scratch_shapes=[pltpu.VMEM((1, share), jnp.float32)],
        ),
        out_shape=jax.ShapeDtypeStruct((length, share), jnp.bfloat16),
        compiler_params=params(12),
        cost_estimate=cost(8 * length * share, 6 * length * share),
        name="finish",
    )(idx, tokens, gain, inverse, dots, *came)


def local(tokens, norm_gain, w_quant, w_scale, d_out):
    length, width = tokens.shape
    depth, columns = w_quant.shape[1:]
    size, nodes = lax.axis_size("local"), lax.axis_size("node")
    here, node = lax.axis_index("local"), lax.axis_index("node")
    wide = columns // 2
    far = size // 2
    group, groups = size // nodes, group_of(nodes)

    order = ring_order(size)
    distances = ring_distances(size)
    table = jnp.asarray(index_table(size, nodes))
    idx = lax.dynamic_index_in_dim(table, node * size + here, 0, keepdims=False)

    def shift(array, distance):
        moves = [(order[i], order[(i + distance) % size]) for i in range(size)]
        return lax.ppermute(array, "local", moves)

    def swap(array, bit):
        return lax.ppermute(array, "node", [(n, n ^ bit) for n in range(nodes)])

    blocks, inverse_rms = normed_blocks(idx, tokens, norm_gain[None], size, depth // 2)
    mine_far = shift(blocks[far], far)
    other_far = swap(mine_far, 1)
    weights, turned = scaled_weights(w_quant, w_scale)
    firsts = sum_first(idx, size, mine_far, other_far, weights)
    mine = stack(
        [shift(blocks[-d % size], -d) if d else blocks[0] for d in distances[:-1]], firsts[:1]
    )
    other = swap(mine, 1)

    rows_turned = turn(idx, mine, other, mine_far, other_far)

    tables = rope_tables(length, HEAD_DIM)
    arrived = []
    for chunk in range(2):
        right, left = firsts[2 * chunk : 2 * chunk + 2]
        for distance in range(far - 1, -1, -1):
            from_left, from_right = shift(right, 1), shift(left, -1)
            if distance:
                places = distances.index(distance), distances.index(-distance)
                ties = [rows_turned] if distance == 1 else []
                right, left = sum_step(
                    idx, size, mine, other, places, weights, from_left, from_right, chunk, wide, ties
                )
        arrived.append((from_left, from_right))

    outputs, sets, dots = [], [], 0.0
    for chunk in range(2):
        output, product, pre = attention(
            idx, size, mine, other, weights, *arrived[chunk], d_out, tables, chunk, wide
        )
        outputs.append(output)
        sets.append(pre)
        dots += jnp.sum(product, axis=-1, keepdims=True)
    bit = 1
    while bit < nodes:
        dots = dots + swap(dots, bit)
        bit *= 2

    def sum_nodes(keep, send):
        column = 4 * size + 1
        bit = 1
        while 2 * bit < nodes:
            keep, send = split_sum(idx, column, group, keep, swap(send, bit))
            column += 1
            bit *= 2
        return order_sum(idx, column, keep, swap(send, bit))

    def relocate(blocks):
        came = []
        for turn, block in enumerate(blocks):
            moves = [
                (n * size + s, (s // group) * size + groups[n] * group + (s + turn) % group)
                for n in range(nodes)
                for s in range(size)
            ]
            came.append(lax.ppermute(block, ("node", "local"), moves))
        return came

    gathered = [[block] for block in sets]
    moving = [(block, block) for block in sets]
    terms = [[], []]
    for step in range(1, far + 1):
        for chunk in range(2):
            right, left = moving[chunk]
            if step == far:
                early = [dots] if chunk == 0 else terms[1][: size - 3]
                right, left = halve(right, left, early)
            right, left = shift(right, 1), shift(left, -1)
            moving[chunk] = right, left
            gathered[chunk] += [right, left]
            if step < far:
                pieces = gathered[chunk] if step == 1 else [right, left]
                known = len(terms[chunk])
                befores = terms[0][known : known + len(pieces)] if chunk else []
                terms[chunk] += term_step(turned, pieces, befores, chunk)
            elif chunk == 0:
                lasts = term_step(turned, [right, left], [], 0)
    grads, done = grads_chunk(rows_turned, gathered[0], None, [], 0, wide, columns)
    keep_0, keep_1, send_0, send_1 = term_last(
        idx, turned, lasts, gathered[1][-2:], terms[1], [done]
    )
    first, second = sum_nodes(keep_0, send_0), sum_nodes(keep_1, send_1)
    came = [*relocate(first), *relocate(second)]
    column = idx.shape[0] - 1 - group
    d_tokens = finish(
        idx, column, tokens, norm_gain[None], inverse_rms, dots, came, width // nodes
    )
    grads, _ = grads_chunk(rows_turned, gathered[1], grads, [keep_1], 1, wide, columns)
    return (jnp.concatenate(outputs, axis=-1), d_tokens, grads)


def solution(mesh):
    placed = (
        P("local", None),
        P(),
        P(None, "local", "node"),
        P(None, "local", "node"),
        P("local", "node"),
    )
    return jax.shard_map(
        local,
        mesh=mesh,
        in_specs=placed,
        out_specs=(P("local", "node"), P("local", "node"), P(None, "local", "node")),
        check_vma=False,
    )
```

```python
import functools
import math

import jax
import jax.numpy as jnp
import numpy as np
from jax import lax
from jax.experimental import pallas as pl
from jax.experimental.pallas import tpu as pltpu
from jax.sharding import PartitionSpec as P

HEAD_DIM = 128
NORM_EPS = 1e-05
MIB = 1024 * 1024


def params(limit):
    return pltpu.CompilerParams(
        dimension_semantics=("arbitrary",), vmem_limit_bytes=limit * MIB
    )


def tied(kernel, inputs, ties):
    def inner(*refs):
        kernel(*refs[:inputs], *refs[inputs + ties :])

    return inner


def tie_specs(ties):
    return [pl.BlockSpec(memory_space=pl.ANY)] * len(ties)


def cost(flops, moved):
    return pl.CostEstimate(flops=flops, bytes_accessed=moved, transcendentals=0)


def mm(a, b):
    return jnp.dot(a, b, preferred_element_type=jnp.float32)


def mm_nt(a, b):
    return lax.dot_general(a, b, (((1,), (1,)), ((), ())), preferred_element_type=jnp.float32)


def mm_tn(a, b):
    return lax.dot_general(a, b, (((0,), (0,)), ((), ())), preferred_element_type=jnp.float32)


def rope_tables(length, width):
    position = jnp.arange(length).astype(jnp.float32)[:, None]
    frequency = jnp.exp(
        jnp.arange(width // 2).astype(jnp.float32) * (-2.0 * math.log(10000.0) / width)
    )
    angle = position * frequency[None, :]
    cosine, sine = jnp.cos(angle), jnp.sin(angle)
    return (
        jnp.concatenate([cosine, cosine], axis=-1),
        jnp.concatenate([-sine, sine], axis=-1),
    )


def ring_order(size):
    return [*range(0, size, 2), *reversed(range(1, size, 2))]


def ring_distances(size):
    far = size // 2
    distances = [0]
    for step in range(1, far):
        distances += [-step, step]
    return [*distances, far]


def group_of(nodes):
    bits = nodes.bit_length() - 1
    return [sum((node >> bit & 1) << (bits - 1 - bit) for bit in range(bits)) for node in range(nodes)]


def index_table(size, nodes):
    order, group = ring_order(size), size // nodes
    rows = []
    for node in range(nodes):
        for here in range(size):
            place = order.index(here)
            seqs = [order[(place + distance) % size] for distance in ring_distances(size)]
            owner = [group_of(nodes).index(seq // group) for seq in seqs]
            rows.append(
                [order[(place + distance) % size] for distance in range(size)]
                + [node % 2]
                + seqs
                + [owner_ % 2 ^ node % 2 for owner_ in owner]
                + [(o // 2) * group + seq % group for o, seq in zip(owner, seqs)]
                + [node >> level & 1 for level in range(1, nodes.bit_length() - 1)]
                + [(here + turn) % group for turn in range(group)]
                + [(here - turn) % group for turn in range(group)]
                + [node]
            )
    return np.array(rows, np.int32)


def weights_kernel(quant, scale, out, turned):
    blocks = scale.shape[1]
    rows = quant.shape[1] // blocks
    scales = scale[0].astype(jnp.float32)
    for block in range(blocks):
        span = slice(block * rows, (block + 1) * rows)
        scaled = (quant[0, span].astype(jnp.float32) * scales[block : block + 1]).astype(jnp.bfloat16)
        out[0, span] = scaled
        turned[0, :, span] = scaled.T


def scaled_weights(w_quant, w_scale):
    _, depth, columns = w_quant.shape
    blocks = w_scale.shape[1]
    return pl.pallas_call(
        weights_kernel,
        grid=(3,),
        in_specs=[
            pl.BlockSpec((1, depth, columns), lambda m: (m, 0, 0)),
            pl.BlockSpec((1, blocks, columns), lambda m: (m, 0, 0)),
        ],
        out_specs=[
            pl.BlockSpec((1, depth, columns), lambda m: (m, 0, 0)),
            pl.BlockSpec((1, columns, depth), lambda m: (m, 0, 0)),
        ],
        out_shape=[
            jax.ShapeDtypeStruct((3, depth, columns), jnp.bfloat16),
            jax.ShapeDtypeStruct((3, columns, depth), jnp.bfloat16),
        ],
        compiler_params=params(20),
        cost_estimate=cost(3 * depth * columns, 18 * depth * columns),
        name="scaled_weights",
    )(w_quant, w_scale)


def normed_kernel(idx, tokens, gain, *refs):
    outs, gains = refs[:-1], refs[-1]
    width, part = tokens.shape[1], outs[0].shape[1]
    gains[...] = gain[...].astype(jnp.float32)
    values = tokens[...].astype(jnp.float32)
    inverse = lax.rsqrt(jnp.mean(values * values, axis=-1, keepdims=True) + NORM_EPS)
    size = len(outs) - 1
    for distance in range(size):
        start = pl.multiple_of(idx[distance] * (width // size) + idx[size] * part, part)
        block = tokens[:, pl.ds(start, part)].astype(jnp.float32)
        scale = gains[:, pl.ds(start, part)]
        outs[distance][...] = (block * inverse * scale).astype(jnp.bfloat16)
    outs[size][...] = jnp.broadcast_to(inverse, outs[size].shape)


def normed_blocks(idx, tokens, gain, size, part):
    length, width = tokens.shape
    tile = length // 4
    block = pl.BlockSpec((tile, part), lambda i, idx: (i, 0))
    *blocks, inverse = pl.pallas_call(
        normed_kernel,
        grid_spec=pltpu.PrefetchScalarGridSpec(
            num_scalar_prefetch=1,
            grid=(4,),
            in_specs=[
                pl.BlockSpec((tile, width), lambda i, idx: (i, 0)),
                pl.BlockSpec((1, width), lambda i, idx: (0, 0)),
            ],
            out_specs=[block] * size + [pl.BlockSpec((tile, 128), lambda i, idx: (i, 0))],
            scratch_shapes=[pltpu.VMEM((1, width), jnp.float32)],
        ),
        out_shape=[jax.ShapeDtypeStruct((length, part), jnp.bfloat16)] * size
        + [jax.ShapeDtypeStruct((length, 128), jnp.float32)],
        compiler_params=params(12),
        cost_estimate=cost(8 * length * width, 4 * length * width),
        name="normed_blocks",
    )(idx, tokens, gain)
    return blocks, inverse


def stack_kernel(*refs):
    for place, block in enumerate(refs[:-1]):
        refs[-1][place] = block[...]


def stack(blocks, ties):
    count, shape = len(blocks), blocks[0].shape
    block = pl.BlockSpec(shape, lambda i: (0, 0))
    return pl.pallas_call(
        tied(stack_kernel, count, len(ties)),
        grid=(1,),
        in_specs=[block] * count + tie_specs(ties),
        out_specs=pl.BlockSpec((count, *shape), lambda i: (0, 0, 0)),
        out_shape=jax.ShapeDtypeStruct((count, *shape), blocks[0].dtype),
        compiler_params=params(10),
        cost_estimate=cost(0, 4 * count * shape[0] * shape[1]),
        name="stack",
    )(*blocks, *ties)


def halve_kernel(right, left, right_out, left_out):
    half = right_out.shape[1]
    right_out[...] = right[:, :half]
    left_out[...] = left[:, half:]


def halve(right, left, ties):
    _, rows, wide = right.shape
    result = jax.ShapeDtypeStruct((3, rows // 2, wide), right.dtype)
    whole = pl.BlockSpec(memory_space=pltpu.VMEM)
    return pl.pallas_call(
        tied(halve_kernel, 2, len(ties)),
        in_specs=[whole, whole] + tie_specs(ties),
        out_specs=[whole, whole],
        out_shape=[result, result],
        compiler_params=pltpu.CompilerParams(vmem_limit_bytes=4 * MIB),
        cost_estimate=cost(0, 6 * rows * wide),
        name="halve",
    )(right, left, *ties)


def turn_kernel(count, idx, mine, other, mine_far, other_far, out):
    length, part = mine_far.shape
    for side, near, last in ((0, mine, mine_far), (1, other, other_far)):
        half = idx[count] * (1 - side) + (1 - idx[count]) * side
        rows = pl.ds(pl.multiple_of(half * part, part), part)
        for place in range(count):
            block = near[place] if place < count - 1 else last[...]
            out[rows, place * length : (place + 1) * length] = block.T


def turn(idx, mine, other, mine_far, other_far):
    near, length, part = mine.shape
    count = near + 1
    stack = pl.BlockSpec(mine.shape, lambda i, idx: (0, 0, 0))
    last = pl.BlockSpec((length, part), lambda i, idx: (0, 0))
    shape = (2 * part, count * length)
    return pl.pallas_call(
        functools.partial(turn_kernel, count),
        grid_spec=pltpu.PrefetchScalarGridSpec(
            num_scalar_prefetch=1,
            grid=(1,),
            in_specs=[stack, stack, last, last],
            out_specs=pl.BlockSpec(shape, lambda i, idx: (0, 0)),
        ),
        out_shape=jax.ShapeDtypeStruct(shape, jnp.bfloat16),
        compiler_params=params(12),
        cost_estimate=cost(2 * count * length * part, 8 * count * length * part),
        name="turn",
    )(idx, mine, other, mine_far, other_far)


def sum_first_kernel(idx, mine, other, weight, weight_other, *outs):
    half, wide = outs[0].shape[1:]
    for chunk in range(2):
        span = slice(chunk * wide, (chunk + 1) * wide)
        product = mm(mine[...], weight[0, :, span]) + mm(other[...], weight_other[0, :, span])
        outs[2 * chunk][0] = product[:half].astype(jnp.bfloat16)
        outs[2 * chunk + 1][0] = product[half:].astype(jnp.bfloat16)


def sum_step_kernel(
    idx, mine_r, other_r, mine_l, other_l, weight, weight_other, from_left, from_right, right, left
):
    length, part = right.shape[1], from_left.shape[1]
    product = mm(mine_r[0], weight[0]) + mm(other_r[0], weight_other[0])
    right[0, :part] = (product[:part] + from_left[0].astype(jnp.float32)).astype(jnp.bfloat16)
    if part < length:
        right[0, part:] = product[part:].astype(jnp.bfloat16)
    product = mm(mine_l[0], weight[0]) + mm(other_l[0], weight_other[0])
    rest = length - part
    left[0, rest:] = (product[rest:] + from_right[0].astype(jnp.float32)).astype(jnp.bfloat16)
    if rest:
        left[0, :rest] = product[:rest].astype(jnp.bfloat16)


def weight_halves(size, part, wide, chunk):
    return [
        pl.BlockSpec((1, part, wide), lambda m, idx: (m, idx[size], chunk)),
        pl.BlockSpec((1, part, wide), lambda m, idx: (m, 1 - idx[size], chunk)),
    ]


def sum_first(idx, size, mine, other, weights):
    length, part = mine.shape
    columns = weights.shape[2]
    half, wide = length // 2, columns // 2
    block = pl.BlockSpec((length, part), lambda m, idx: (0, 0))
    result = jax.ShapeDtypeStruct((3, half, wide), jnp.bfloat16)
    return pl.pallas_call(
        sum_first_kernel,
        grid_spec=pltpu.PrefetchScalarGridSpec(
            num_scalar_prefetch=1,
            grid=(3,),
            in_specs=[block, block, *weight_halves(size, part, columns, 0)],
            out_specs=[pl.BlockSpec((1, half, wide), lambda m, idx: (m, 0, 0))] * 4,
        ),
        out_shape=[result] * 4,
        compiler_params=params(12),
        cost_estimate=cost(12 * length * part * columns, 16 * part * columns),
        name="sum_first",
    )(idx, mine, other, weights, weights)


def sum_step(idx, size, mine, other, places, weights, from_left, from_right, chunk, wide, ties):
    _, length, part = mine.shape
    block_r = pl.BlockSpec((1, length, part), lambda m, idx: (places[0], 0, 0))
    block_l = pl.BlockSpec((1, length, part), lambda m, idx: (places[1], 0, 0))
    came = pl.BlockSpec((1, from_left.shape[1], wide), lambda m, idx: (m, 0, 0))
    whole = jax.ShapeDtypeStruct((3, length, wide), jnp.bfloat16)
    return pl.pallas_call(
        tied(sum_step_kernel, 9, len(ties)),
        grid_spec=pltpu.PrefetchScalarGridSpec(
            num_scalar_prefetch=1,
            grid=(3,),
            in_specs=[
                block_r,
                block_r,
                block_l,
                block_l,
                *weight_halves(size, part, wide, chunk),
                came,
                came,
                *tie_specs(ties),
            ],
            out_specs=[pl.BlockSpec((1, length, wide), lambda m, idx: (m, 0, 0))] * 2,
        ),
        out_shape=[whole, whole],
        compiler_params=params(12),
        cost_estimate=cost(24 * length * part * wide, 24 * part * wide),
        name="sum_step",
    )(idx, mine, other, mine, other, weights, weights, from_left, from_right, *ties)


def attention_kernel(
    idx, mine, other, weight, weight_other, from_left, from_right, d_out, cosine, sine,
    output, dots, pre,
):
    length = mine.shape[1]
    proj = [
        mm(mine[0], weight[m])
        + mm(other[0], weight_other[m])
        + (from_left[m].astype(jnp.float32) + from_right[m].astype(jnp.float32))
        for m in range(3)
    ]
    cos, sin = cosine[...], sine[...]
    half = HEAD_DIM // 2

    def rotate(tensor, angle):
        return tensor * cos + pltpu.roll(tensor, half, 1) * angle

    query = rotate(proj[0], sin).astype(jnp.bfloat16)
    key_rows = rotate(proj[1], sin).astype(jnp.bfloat16)
    value = proj[2].astype(jnp.bfloat16)
    scores = mm_nt(query, key_rows) * (1.0 / math.sqrt(HEAD_DIM))
    causal = lax.broadcasted_iota(jnp.int32, (length, length), 0) >= lax.broadcasted_iota(
        jnp.int32, (length, length), 1
    )
    scores = jnp.where(causal, scores, jnp.float32(-1e30))
    powers = jnp.exp(scores - jnp.max(scores, axis=-1, keepdims=True))
    probs = powers * (1.0 / jnp.sum(powers, axis=-1, keepdims=True))
    probs_low = probs.astype(jnp.bfloat16)
    output[...] = mm(probs_low, value).astype(jnp.bfloat16)
    cotangent = d_out[...]
    d_value = mm_tn(probs_low, cotangent).astype(jnp.bfloat16)
    d_probs = mm_nt(cotangent, value).astype(jnp.bfloat16).astype(jnp.float32)
    inner = jnp.sum(d_probs * probs, axis=-1, keepdims=True)
    d_scores = (probs * (d_probs - inner) * (1.0 / math.sqrt(HEAD_DIM))).astype(jnp.bfloat16)
    d_query = mm(d_scores, key_rows).astype(jnp.bfloat16).astype(jnp.float32)
    d_key = mm_tn(d_scores, query).astype(jnp.bfloat16).astype(jnp.float32)
    pre_query = rotate(d_query, -sin).astype(jnp.bfloat16)
    pre_key = rotate(d_key, -sin).astype(jnp.bfloat16)
    pre[0] = pre_query
    pre[1] = pre_key
    pre[2] = d_value
    product = (
        pre_query.astype(jnp.float32) * proj[0]
        + pre_key.astype(jnp.float32) * proj[1]
        + d_value.astype(jnp.float32) * proj[2]
    )

    @pl.when(pl.program_id(0) == 0)
    def _():
        dots[...] = product

    @pl.when(pl.program_id(0) > 0)
    def _():
        dots[...] += product


def attention(idx, size, mine, other, weights, from_left, from_right, d_out, tables, chunk, wide):
    _, length, part = mine.shape
    heads = wide // HEAD_DIM
    first = chunk * heads
    block = pl.BlockSpec((1, length, part), lambda h, idx: (0, 0, 0))
    table = pl.BlockSpec((length, HEAD_DIM), lambda h, idx: (0, 0))
    stack = pl.BlockSpec((3, length, HEAD_DIM), lambda h, idx: (0, 0, h))
    return pl.pallas_call(
        attention_kernel,
        grid_spec=pltpu.PrefetchScalarGridSpec(
            num_scalar_prefetch=1,
            grid=(heads,),
            in_specs=[
                block,
                block,
                pl.BlockSpec((3, part, HEAD_DIM), lambda h, idx: (0, idx[size], first + h)),
                pl.BlockSpec((3, part, HEAD_DIM), lambda h, idx: (0, 1 - idx[size], first + h)),
                stack,
                stack,
                pl.BlockSpec((length, HEAD_DIM), lambda h, idx: (0, first + h)),
                table,
                table,
            ],
            out_specs=[
                pl.BlockSpec((length, HEAD_DIM), lambda h, idx: (0, h)),
                table,
                stack,
            ],
        ),
        out_shape=[
            jax.ShapeDtypeStruct((length, wide), jnp.bfloat16),
            jax.ShapeDtypeStruct((length, HEAD_DIM), jnp.float32),
            jax.ShapeDtypeStruct((3, length, wide), jnp.bfloat16),
        ],
        compiler_params=params(16),
        cost_estimate=cost(12 * length * part * wide, 24 * part * wide),
        name="attention",
    )(idx, mine, other, weights, weights, from_left, from_right, d_out, *tables)


def grads_kernel(turned, *refs):
    pieces, out, token = refs[:-2], refs[-2], refs[-1]
    blocks = jnp.concatenate([piece[0] for piece in pieces], axis=0)
    out[0] = mm(turned[...], blocks)
    token[...] = jnp.zeros_like(token)


def grads_chunk(turned, pieces, before, ties, chunk, wide, columns):
    depth, span = turned.shape
    aliases = {} if before is None else {1 + len(pieces): 0}
    ties = ties if before is None else [before, *ties]
    return pl.pallas_call(
        tied(grads_kernel, 1 + len(pieces), len(ties)),
        grid=(3,),
        in_specs=[
            pl.BlockSpec((depth, span), lambda m: (0, 0)),
            *[pl.BlockSpec((1, *piece.shape[1:]), lambda m: (m, 0, 0)) for piece in pieces],
            *tie_specs(ties),
        ],
        out_specs=[
            pl.BlockSpec((1, depth, wide), lambda m: (m, 0, chunk)),
            pl.BlockSpec((8, 128), lambda m: (0, 0)),
        ],
        out_shape=[
            jax.ShapeDtypeStruct((3, depth, columns), jnp.float32),
            jax.ShapeDtypeStruct((8, 128), jnp.float32),
        ],
        input_output_aliases=aliases,
        compiler_params=params(24),
        cost_estimate=cost(6 * span * depth * wide, 6 * span * wide + 12 * depth * wide),
        name="grads",
    )(turned, *pieces, *ties)


def back(pieces, turned, chunk):
    wide = pieces[0].shape[2]
    rows = [jnp.concatenate([piece[m] for m in range(3)], axis=1) for piece in pieces]
    weight = [turned[m, chunk * wide : (chunk + 1) * wide] for m in range(3)]
    return mm(jnp.concatenate(rows, axis=0), jnp.concatenate(weight, axis=0))


def term_step(turned, pieces, befores, chunk):
    depth, wide = turned.shape[2], pieces[0].shape[2]
    count, rows = len(pieces), pieces[0].shape[1]
    whole = pl.BlockSpec(memory_space=pltpu.VMEM)

    def kernel(turned_ref, *refs):
        total = back(refs[:count], turned_ref, chunk)
        for place in range(count):
            block = total[place * rows : (place + 1) * rows]
            if befores:
                block += refs[count + place][...]
            refs[len(refs) - count + place][...] = block

    return pl.pallas_call(
        kernel,
        in_specs=[whole] * (1 + count + len(befores)),
        out_specs=[whole] * count,
        out_shape=[jax.ShapeDtypeStruct((rows, depth), jnp.float32)] * count,
        compiler_params=pltpu.CompilerParams(vmem_limit_bytes=16 * MIB),
        cost_estimate=cost(6 * count * rows * depth * wide, 12 * count * rows * wide),
        name="term_step",
    )(turned, *pieces, *befores)


def term_last_kernel(count, idx, turned, *refs):
    befores, fars, nears = refs[:2], refs[2:4], refs[4 : 3 + count]
    keeps, sends = refs[-4:-2], refs[-2:]
    half = keeps[0].shape[1]
    last = back(fars, turned, 1)
    for place in range(count):
        for part in range(2):
            span = slice(part * half, (part + 1) * half)
            total = nears[place][span] if place < count - 1 else last[span] + befores[part][...]

            @pl.when(idx[2 * count + 1 + place] == 0)
            def _():
                keeps[part][idx[3 * count + 1 + place]] = total

            @pl.when(idx[2 * count + 1 + place] == 1)
            def _():
                sends[part][idx[3 * count + 1 + place]] = total.astype(jnp.bfloat16)


def term_last(idx, turned, befores, pieces, nears, ties):
    count = len(nears) + 1
    rows, depth = nears[0].shape
    whole = pl.BlockSpec(memory_space=pltpu.VMEM)
    shape = (count // 2, rows // 2, depth)
    return pl.pallas_call(
        tied(functools.partial(term_last_kernel, count), count + 5, len(ties)),
        in_specs=[pl.BlockSpec(memory_space=pltpu.SMEM)]
        + [whole] * (count + 4)
        + tie_specs(ties),
        out_specs=[whole] * 4,
        out_shape=[jax.ShapeDtypeStruct(shape, jnp.float32)] * 2
        + [jax.ShapeDtypeStruct(shape, jnp.bfloat16)] * 2,
        compiler_params=pltpu.CompilerParams(vmem_limit_bytes=12 * MIB),
        cost_estimate=cost(rows * depth * depth, 12 * count * rows * depth),
        name="term_last",
    )(idx, turned, *befores, *pieces, *nears, *ties)


def split_kernel(column, group, idx, keep, came, keep_out, send_out):
    own = idx[column]
    for block in range(keep_out.shape[0]):
        high, low = block // group, block % group
        mine = (2 * high + own) * group + low
        other = (2 * high + 1 - own) * group + low
        keep_out[block] = keep[mine] + came[mine].astype(jnp.float32)
        send_out[block] = (keep[other] + came[other].astype(jnp.float32)).astype(jnp.bfloat16)


def split_sum(idx, column, group, keep, came):
    whole = pl.BlockSpec(memory_space=pltpu.VMEM)
    shape = (keep.shape[0] // 2, *keep.shape[1:])
    return pl.pallas_call(
        functools.partial(split_kernel, column, group),
        in_specs=[pl.BlockSpec(memory_space=pltpu.SMEM), whole, whole],
        out_specs=[whole, whole],
        out_shape=[
            jax.ShapeDtypeStruct(shape, jnp.float32),
            jax.ShapeDtypeStruct(shape, jnp.bfloat16),
        ],
        compiler_params=pltpu.CompilerParams(vmem_limit_bytes=4 * MIB),
        cost_estimate=cost(0, 8 * keep.shape[0] * keep.shape[1] * keep.shape[2]),
        name="split_sum",
    )(idx, keep, came)


def order_kernel(column, idx, keep, came, *outs):
    for turn, out in enumerate(outs):
        block = idx[column + turn]
        out[...] = (keep[block] + came[block].astype(jnp.float32)).astype(jnp.bfloat16)


def order_sum(idx, column, keep, came, ties):
    whole = pl.BlockSpec(memory_space=pltpu.VMEM)
    count = keep.shape[0]
    return pl.pallas_call(
        tied(functools.partial(order_kernel, column), 3, len(ties)),
        in_specs=[pl.BlockSpec(memory_space=pltpu.SMEM), whole, whole, *tie_specs(ties)],
        out_specs=[whole] * count,
        out_shape=[jax.ShapeDtypeStruct(keep.shape[1:], jnp.bfloat16)] * count,
        compiler_params=pltpu.CompilerParams(vmem_limit_bytes=4 * MIB),
        cost_estimate=cost(0, 8 * count * keep.shape[1] * keep.shape[2]),
        name="order_sum",
    )(idx, keep, came, *ties)


def finish_kernel(column, width, idx, tokens, gain, inverse, dots, *refs):
    came, out, gains = refs[:-2], refs[-2], refs[-1]
    rows, depth = came[0].shape
    group = out.shape[1] // depth
    gains[...] = gain[...].astype(jnp.float32)
    for turn in range(group):
        features = pl.ds(pl.multiple_of(idx[column + turn] * depth, depth), depth)
        for part in range(len(came) // group):
            span = slice(part * rows, (part + 1) * rows)
            scale = inverse[span, :1]
            upstream = came[part * group + turn][...].astype(jnp.float32)
            values = tokens[span, features].astype(jnp.float32)
            common = scale * scale * dots[span] / width
            out[span, features] = (
                scale * gains[:, features] * upstream - values * common
            ).astype(jnp.bfloat16)


def finish(idx, column, tokens, gain, inverse, dots, came, share):
    length, width = tokens.shape
    node = column + share // came[0].shape[1]
    whole = pl.BlockSpec(memory_space=pltpu.VMEM)
    return pl.pallas_call(
        functools.partial(finish_kernel, column, width),
        grid_spec=pltpu.PrefetchScalarGridSpec(
            num_scalar_prefetch=1,
            grid=(1,),
            in_specs=[
                pl.BlockSpec((length, share), lambda i, idx: (0, idx[node])),
                pl.BlockSpec((1, share), lambda i, idx: (0, idx[node])),
                *[whole] * (2 + len(came)),
            ],
            out_specs=pl.BlockSpec((length, share), lambda i, idx: (0, 0)),
            scratch_shapes=[pltpu.VMEM((1, share), jnp.float32)],
        ),
        out_shape=jax.ShapeDtypeStruct((length, share), jnp.bfloat16),
        compiler_params=params(12),
        cost_estimate=cost(8 * length * share, 6 * length * share),
        name="finish",
    )(idx, tokens, gain, inverse, dots, *came)


def local(tokens, norm_gain, w_quant, w_scale, d_out):
    length, width = tokens.shape
    depth, columns = w_quant.shape[1:]
    size, nodes = lax.axis_size("local"), lax.axis_size("node")
    here, node = lax.axis_index("local"), lax.axis_index("node")
    wide = columns // 2
    far = size // 2
    group, groups = size // nodes, group_of(nodes)

    order = ring_order(size)
    distances = ring_distances(size)
    table = jnp.asarray(index_table(size, nodes))
    idx = lax.dynamic_index_in_dim(table, node * size + here, 0, keepdims=False)

    def shift(array, distance):
        moves = [(order[i], order[(i + distance) % size]) for i in range(size)]
        return lax.ppermute(array, "local", moves)

    def swap(array, bit):
        return lax.ppermute(array, "node", [(n, n ^ bit) for n in range(nodes)])

    blocks, inverse_rms = normed_blocks(idx, tokens, norm_gain[None], size, depth // 2)
    mine_far = shift(blocks[far], far)
    other_far = swap(mine_far, 1)
    weights, turned = scaled_weights(w_quant, w_scale)
    firsts = sum_first(idx, size, mine_far, other_far, weights)
    mine = stack(
        [shift(blocks[-d % size], -d) if d else blocks[0] for d in distances[:-1]], firsts[:1]
    )
    other = swap(mine, 1)

    rows_turned = turn(idx, mine, other, mine_far, other_far)

    tables = rope_tables(length, HEAD_DIM)
    arrived = []
    for chunk in range(2):
        right, left = firsts[2 * chunk : 2 * chunk + 2]
        for distance in range(far - 1, -1, -1):
            from_left, from_right = shift(right, 1), shift(left, -1)
            if distance:
                places = distances.index(distance), distances.index(-distance)
                ties = [rows_turned] if distance == 1 else []
                right, left = sum_step(
                    idx, size, mine, other, places, weights, from_left, from_right, chunk, wide, ties
                )
        arrived.append((from_left, from_right))

    outputs, sets, dots = [], [], 0.0
    for chunk in range(2):
        output, product, pre = attention(
            idx, size, mine, other, weights, *arrived[chunk], d_out, tables, chunk, wide
        )
        outputs.append(output)
        sets.append(pre)
        dots += jnp.sum(product, axis=-1, keepdims=True)
    bit = 1
    while bit < nodes:
        dots = dots + swap(dots, bit)
        bit *= 2

    def sum_nodes(keep, send, ties):
        column = 4 * size + 1
        bit = 1
        while 2 * bit < nodes:
            keep, send = split_sum(idx, column, group, keep, swap(send, bit))
            column += 1
            bit *= 2
        return order_sum(idx, column, keep, swap(send, bit), ties)

    def relocate(blocks):
        came = []
        for turn, block in enumerate(blocks):
            moves = [
                (n * size + s, (s // group) * size + groups[n] * group + (s + turn) % group)
                for n in range(nodes)
                for s in range(size)
            ]
            came.append(lax.ppermute(block, ("node", "local"), moves))
        return came

    gathered = [[block] for block in sets]
    moving = [(block, block) for block in sets]
    terms = [[], []]
    for step in range(1, far + 1):
        for chunk in range(2):
            right, left = moving[chunk]
            if step == far:
                early = [dots] if chunk == 0 else terms[1][: size - 3]
                right, left = halve(right, left, early)
            right, left = shift(right, 1), shift(left, -1)
            moving[chunk] = right, left
            gathered[chunk] += [right, left]
            if step < far:
                pieces = gathered[chunk] if step == 1 else [right, left]
                known = len(terms[chunk])
                befores = terms[0][known : known + len(pieces)] if chunk else []
                terms[chunk] += term_step(turned, pieces, befores, chunk)
            elif chunk == 0:
                lasts = term_step(turned, [right, left], [], 0)
    grads, done = grads_chunk(rows_turned, gathered[0], None, [], 0, wide, columns)
    keep_0, keep_1, send_0, send_1 = term_last(
        idx, turned, lasts, gathered[1][-2:], terms[1], [done]
    )
    grads, done = grads_chunk(rows_turned, gathered[1], grads, [keep_1], 1, wide, columns)
    first, second = sum_nodes(keep_0, send_0, [done]), sum_nodes(keep_1, send_1, [done])
    came = [*relocate(first), *relocate(second)]
    column = idx.shape[0] - 1 - group
    d_tokens = finish(
        idx, column, tokens, norm_gain[None], inverse_rms, dots, came, width // nodes
    )
    return (jnp.concatenate(outputs, axis=-1), d_tokens, grads)


def solution(mesh):
    placed = (
        P("local", None),
        P(),
        P(None, "local", "node"),
        P(None, "local", "node"),
        P("local", "node"),
    )
    return jax.shard_map(
        local,
        mesh=mesh,
        in_specs=placed,
        out_specs=(P("local", "node"), P("local", "node"), P(None, "local", "node")),
        check_vma=False,
    )
```

```python
import functools
import math

import jax
import jax.numpy as jnp
import numpy as np
from jax import lax
from jax.experimental import pallas as pl
from jax.experimental.pallas import tpu as pltpu
from jax.sharding import PartitionSpec as P

HEAD_DIM = 128
NORM_EPS = 1e-05
MIB = 1024 * 1024


def params(limit):
    return pltpu.CompilerParams(
        dimension_semantics=("arbitrary",), vmem_limit_bytes=limit * MIB
    )


def tied(kernel, inputs, ties):
    def inner(*refs):
        kernel(*refs[:inputs], *refs[inputs + ties :])

    return inner


def tie_specs(ties):
    return [pl.BlockSpec(memory_space=pl.ANY)] * len(ties)


def cost(flops, moved):
    return pl.CostEstimate(flops=flops, bytes_accessed=moved, transcendentals=0)


def mm(a, b):
    return jnp.dot(a, b, preferred_element_type=jnp.float32)


def mm_nt(a, b):
    return lax.dot_general(a, b, (((1,), (1,)), ((), ())), preferred_element_type=jnp.float32)


def mm_tn(a, b):
    return lax.dot_general(a, b, (((0,), (0,)), ((), ())), preferred_element_type=jnp.float32)


def rope_tables(length, width):
    position = jnp.arange(length).astype(jnp.float32)[:, None]
    frequency = jnp.exp(
        jnp.arange(width // 2).astype(jnp.float32) * (-2.0 * math.log(10000.0) / width)
    )
    angle = position * frequency[None, :]
    cosine, sine = jnp.cos(angle), jnp.sin(angle)
    return (
        jnp.concatenate([cosine, cosine], axis=-1),
        jnp.concatenate([-sine, sine], axis=-1),
    )


def ring_order(size):
    return [*range(0, size, 2), *reversed(range(1, size, 2))]


def ring_distances(size):
    far = size // 2
    distances = [0]
    for step in range(1, far):
        distances += [-step, step]
    return [*distances, far]


def group_of(nodes):
    bits = nodes.bit_length() - 1
    return [sum((node >> bit & 1) << (bits - 1 - bit) for bit in range(bits)) for node in range(nodes)]


def index_table(size, nodes):
    order, group = ring_order(size), size // nodes
    rows = []
    for node in range(nodes):
        for here in range(size):
            place = order.index(here)
            seqs = [order[(place + distance) % size] for distance in ring_distances(size)]
            owner = [group_of(nodes).index(seq // group) for seq in seqs]
            rows.append(
                [order[(place + distance) % size] for distance in range(size)]
                + [node % 2]
                + seqs
                + [owner_ % 2 ^ node % 2 for owner_ in owner]
                + [(o // 2) * group + seq % group for o, seq in zip(owner, seqs)]
                + [node >> level & 1 for level in range(1, nodes.bit_length() - 1)]
                + [(here + turn) % group for turn in range(group)]
                + [(here - turn) % group for turn in range(group)]
                + [node]
            )
    return np.array(rows, np.int32)


def weights_kernel(quant, scale, out, turned):
    blocks = scale.shape[1]
    rows = quant.shape[1] // blocks
    scales = scale[0].astype(jnp.float32)
    for block in range(blocks):
        span = slice(block * rows, (block + 1) * rows)
        scaled = (quant[0, span].astype(jnp.float32) * scales[block : block + 1]).astype(jnp.bfloat16)
        out[0, span] = scaled
        turned[0, :, span] = scaled.T


def scaled_weights(w_quant, w_scale):
    _, depth, columns = w_quant.shape
    blocks = w_scale.shape[1]
    return pl.pallas_call(
        weights_kernel,
        grid=(3,),
        in_specs=[
            pl.BlockSpec((1, depth, columns), lambda m: (m, 0, 0)),
            pl.BlockSpec((1, blocks, columns), lambda m: (m, 0, 0)),
        ],
        out_specs=[
            pl.BlockSpec((1, depth, columns), lambda m: (m, 0, 0)),
            pl.BlockSpec((1, columns, depth), lambda m: (m, 0, 0)),
        ],
        out_shape=[
            jax.ShapeDtypeStruct((3, depth, columns), jnp.bfloat16),
            jax.ShapeDtypeStruct((3, columns, depth), jnp.bfloat16),
        ],
        compiler_params=params(20),
        cost_estimate=cost(3 * depth * columns, 18 * depth * columns),
        name="scaled_weights",
    )(w_quant, w_scale)


def normed_kernel(idx, tokens, gain, *refs):
    outs, gains = refs[:-1], refs[-1]
    width, part = tokens.shape[1], outs[0].shape[1]
    gains[...] = gain[...].astype(jnp.float32)
    values = tokens[...].astype(jnp.float32)
    inverse = lax.rsqrt(jnp.mean(values * values, axis=-1, keepdims=True) + NORM_EPS)
    size = len(outs) - 1
    for distance in range(size):
        start = pl.multiple_of(idx[distance] * (width // size) + idx[size] * part, part)
        block = tokens[:, pl.ds(start, part)].astype(jnp.float32)
        scale = gains[:, pl.ds(start, part)]
        outs[distance][...] = (block * inverse * scale).astype(jnp.bfloat16)
    outs[size][...] = jnp.broadcast_to(inverse, outs[size].shape)


def normed_blocks(idx, tokens, gain, size, part):
    length, width = tokens.shape
    tile = length // 4
    block = pl.BlockSpec((tile, part), lambda i, idx: (i, 0))
    *blocks, inverse = pl.pallas_call(
        normed_kernel,
        grid_spec=pltpu.PrefetchScalarGridSpec(
            num_scalar_prefetch=1,
            grid=(4,),
            in_specs=[
                pl.BlockSpec((tile, width), lambda i, idx: (i, 0)),
                pl.BlockSpec((1, width), lambda i, idx: (0, 0)),
            ],
            out_specs=[block] * size + [pl.BlockSpec((tile, 128), lambda i, idx: (i, 0))],
            scratch_shapes=[pltpu.VMEM((1, width), jnp.float32)],
        ),
        out_shape=[jax.ShapeDtypeStruct((length, part), jnp.bfloat16)] * size
        + [jax.ShapeDtypeStruct((length, 128), jnp.float32)],
        compiler_params=params(12),
        cost_estimate=cost(8 * length * width, 4 * length * width),
        name="normed_blocks",
    )(idx, tokens, gain)
    return blocks, inverse


def stack_kernel(*refs):
    for place, block in enumerate(refs[:-1]):
        refs[-1][place] = block[...]


def stack(blocks, ties):
    count, shape = len(blocks), blocks[0].shape
    block = pl.BlockSpec(shape, lambda i: (0, 0))
    return pl.pallas_call(
        tied(stack_kernel, count, len(ties)),
        grid=(1,),
        in_specs=[block] * count + tie_specs(ties),
        out_specs=pl.BlockSpec((count, *shape), lambda i: (0, 0, 0)),
        out_shape=jax.ShapeDtypeStruct((count, *shape), blocks[0].dtype),
        compiler_params=params(10),
        cost_estimate=cost(0, 4 * count * shape[0] * shape[1]),
        name="stack",
    )(*blocks, *ties)


def halve_kernel(right, left, right_out, left_out):
    half = right_out.shape[1]
    right_out[...] = right[:, :half]
    left_out[...] = left[:, half:]


def halve(right, left, ties):
    _, rows, wide = right.shape
    result = jax.ShapeDtypeStruct((3, rows // 2, wide), right.dtype)
    whole = pl.BlockSpec(memory_space=pltpu.VMEM)
    return pl.pallas_call(
        tied(halve_kernel, 2, len(ties)),
        in_specs=[whole, whole] + tie_specs(ties),
        out_specs=[whole, whole],
        out_shape=[result, result],
        compiler_params=pltpu.CompilerParams(vmem_limit_bytes=4 * MIB),
        cost_estimate=cost(0, 6 * rows * wide),
        name="halve",
    )(right, left, *ties)


def turn_kernel(count, idx, mine, other, mine_far, other_far, out):
    length, part = mine_far.shape
    for side, near, last in ((0, mine, mine_far), (1, other, other_far)):
        half = idx[count] * (1 - side) + (1 - idx[count]) * side
        rows = pl.ds(pl.multiple_of(half * part, part), part)
        for place in range(count):
            block = near[place] if place < count - 1 else last[...]
            out[rows, place * length : (place + 1) * length] = block.T


def turn(idx, mine, other, mine_far, other_far):
    near, length, part = mine.shape
    count = near + 1
    stack = pl.BlockSpec(mine.shape, lambda i, idx: (0, 0, 0))
    last = pl.BlockSpec((length, part), lambda i, idx: (0, 0))
    shape = (2 * part, count * length)
    return pl.pallas_call(
        functools.partial(turn_kernel, count),
        grid_spec=pltpu.PrefetchScalarGridSpec(
            num_scalar_prefetch=1,
            grid=(1,),
            in_specs=[stack, stack, last, last],
            out_specs=pl.BlockSpec(shape, lambda i, idx: (0, 0)),
        ),
        out_shape=jax.ShapeDtypeStruct(shape, jnp.bfloat16),
        compiler_params=params(12),
        cost_estimate=cost(2 * count * length * part, 8 * count * length * part),
        name="turn",
    )(idx, mine, other, mine_far, other_far)


def sum_first_kernel(idx, mine, other, weight, weight_other, *outs):
    half, wide = outs[0].shape[1:]
    for chunk in range(2):
        span = slice(chunk * wide, (chunk + 1) * wide)
        product = mm(mine[...], weight[0, :, span]) + mm(other[...], weight_other[0, :, span])
        outs[2 * chunk][0] = product[:half].astype(jnp.bfloat16)
        outs[2 * chunk + 1][0] = product[half:].astype(jnp.bfloat16)


def sum_step_kernel(
    idx, mine_r, other_r, mine_l, other_l, weight, weight_other, from_left, from_right, right, left
):
    length, part = right.shape[1], from_left.shape[1]
    product = mm(mine_r[0], weight[0]) + mm(other_r[0], weight_other[0])
    right[0, :part] = (product[:part] + from_left[0].astype(jnp.float32)).astype(jnp.bfloat16)
    if part < length:
        right[0, part:] = product[part:].astype(jnp.bfloat16)
    product = mm(mine_l[0], weight[0]) + mm(other_l[0], weight_other[0])
    rest = length - part
    left[0, rest:] = (product[rest:] + from_right[0].astype(jnp.float32)).astype(jnp.bfloat16)
    if rest:
        left[0, :rest] = product[:rest].astype(jnp.bfloat16)


def weight_halves(size, part, wide, chunk):
    return [
        pl.BlockSpec((1, part, wide), lambda m, idx: (m, idx[size], chunk)),
        pl.BlockSpec((1, part, wide), lambda m, idx: (m, 1 - idx[size], chunk)),
    ]


def sum_first(idx, size, mine, other, weights):
    length, part = mine.shape
    columns = weights.shape[2]
    half, wide = length // 2, columns // 2
    block = pl.BlockSpec((length, part), lambda m, idx: (0, 0))
    result = jax.ShapeDtypeStruct((3, half, wide), jnp.bfloat16)
    return pl.pallas_call(
        sum_first_kernel,
        grid_spec=pltpu.PrefetchScalarGridSpec(
            num_scalar_prefetch=1,
            grid=(3,),
            in_specs=[block, block, *weight_halves(size, part, columns, 0)],
            out_specs=[pl.BlockSpec((1, half, wide), lambda m, idx: (m, 0, 0))] * 4,
        ),
        out_shape=[result] * 4,
        compiler_params=params(12),
        cost_estimate=cost(12 * length * part * columns, 16 * part * columns),
        name="sum_first",
    )(idx, mine, other, weights, weights)


def sum_step(idx, size, mine, other, places, weights, from_left, from_right, chunk, wide, ties):
    _, length, part = mine.shape
    block_r = pl.BlockSpec((1, length, part), lambda m, idx: (places[0], 0, 0))
    block_l = pl.BlockSpec((1, length, part), lambda m, idx: (places[1], 0, 0))
    came = pl.BlockSpec((1, from_left.shape[1], wide), lambda m, idx: (m, 0, 0))
    whole = jax.ShapeDtypeStruct((3, length, wide), jnp.bfloat16)
    return pl.pallas_call(
        tied(sum_step_kernel, 9, len(ties)),
        grid_spec=pltpu.PrefetchScalarGridSpec(
            num_scalar_prefetch=1,
            grid=(3,),
            in_specs=[
                block_r,
                block_r,
                block_l,
                block_l,
                *weight_halves(size, part, wide, chunk),
                came,
                came,
                *tie_specs(ties),
            ],
            out_specs=[pl.BlockSpec((1, length, wide), lambda m, idx: (m, 0, 0))] * 2,
        ),
        out_shape=[whole, whole],
        compiler_params=params(12),
        cost_estimate=cost(24 * length * part * wide, 24 * part * wide),
        name="sum_step",
    )(idx, mine, other, mine, other, weights, weights, from_left, from_right, *ties)


def attention_kernel(
    idx, mine, other, weight, weight_other, from_left, from_right, d_out, cosine, sine,
    output, dots, pre,
):
    length = mine.shape[1]
    proj = [
        mm(mine[0], weight[m])
        + mm(other[0], weight_other[m])
        + (from_left[m].astype(jnp.float32) + from_right[m].astype(jnp.float32))
        for m in range(3)
    ]
    cos, sin = cosine[...], sine[...]
    half = HEAD_DIM // 2

    def rotate(tensor, angle):
        return tensor * cos + pltpu.roll(tensor, half, 1) * angle

    query = rotate(proj[0], sin).astype(jnp.bfloat16)
    key_rows = rotate(proj[1], sin).astype(jnp.bfloat16)
    value = proj[2].astype(jnp.bfloat16)
    scores = mm_nt(query, key_rows) * (1.0 / math.sqrt(HEAD_DIM))
    causal = lax.broadcasted_iota(jnp.int32, (length, length), 0) >= lax.broadcasted_iota(
        jnp.int32, (length, length), 1
    )
    scores = jnp.where(causal, scores, jnp.float32(-1e30))
    powers = jnp.exp(scores - jnp.max(scores, axis=-1, keepdims=True))
    probs = powers * (1.0 / jnp.sum(powers, axis=-1, keepdims=True))
    probs_low = probs.astype(jnp.bfloat16)
    output[...] = mm(probs_low, value).astype(jnp.bfloat16)
    cotangent = d_out[...]
    d_value = mm_tn(probs_low, cotangent).astype(jnp.bfloat16)
    d_probs = mm_nt(cotangent, value).astype(jnp.bfloat16).astype(jnp.float32)
    inner = jnp.sum(d_probs * probs, axis=-1, keepdims=True)
    d_scores = (probs * (d_probs - inner) * (1.0 / math.sqrt(HEAD_DIM))).astype(jnp.bfloat16)
    d_query = mm(d_scores, key_rows).astype(jnp.bfloat16).astype(jnp.float32)
    d_key = mm_tn(d_scores, query).astype(jnp.bfloat16).astype(jnp.float32)
    pre_query = rotate(d_query, -sin).astype(jnp.bfloat16)
    pre_key = rotate(d_key, -sin).astype(jnp.bfloat16)
    pre[0] = pre_query
    pre[1] = pre_key
    pre[2] = d_value
    product = (
        pre_query.astype(jnp.float32) * proj[0]
        + pre_key.astype(jnp.float32) * proj[1]
        + d_value.astype(jnp.float32) * proj[2]
    )

    @pl.when(pl.program_id(0) == 0)
    def _():
        dots[...] = product

    @pl.when(pl.program_id(0) > 0)
    def _():
        dots[...] += product


def attention(idx, size, mine, other, weights, from_left, from_right, d_out, tables, chunk, wide):
    _, length, part = mine.shape
    heads = wide // HEAD_DIM
    first = chunk * heads
    block = pl.BlockSpec((1, length, part), lambda h, idx: (0, 0, 0))
    table = pl.BlockSpec((length, HEAD_DIM), lambda h, idx: (0, 0))
    stack = pl.BlockSpec((3, length, HEAD_DIM), lambda h, idx: (0, 0, h))
    return pl.pallas_call(
        attention_kernel,
        grid_spec=pltpu.PrefetchScalarGridSpec(
            num_scalar_prefetch=1,
            grid=(heads,),
            in_specs=[
                block,
                block,
                pl.BlockSpec((3, part, HEAD_DIM), lambda h, idx: (0, idx[size], first + h)),
                pl.BlockSpec((3, part, HEAD_DIM), lambda h, idx: (0, 1 - idx[size], first + h)),
                stack,
                stack,
                pl.BlockSpec((length, HEAD_DIM), lambda h, idx: (0, first + h)),
                table,
                table,
            ],
            out_specs=[
                pl.BlockSpec((length, HEAD_DIM), lambda h, idx: (0, h)),
                table,
                stack,
            ],
        ),
        out_shape=[
            jax.ShapeDtypeStruct((length, wide), jnp.bfloat16),
            jax.ShapeDtypeStruct((length, HEAD_DIM), jnp.float32),
            jax.ShapeDtypeStruct((3, length, wide), jnp.bfloat16),
        ],
        compiler_params=params(16),
        cost_estimate=cost(12 * length * part * wide, 24 * part * wide),
        name="attention",
    )(idx, mine, other, weights, weights, from_left, from_right, d_out, *tables)


def grads_kernel(turned, *refs):
    pieces, out, token = refs[:-2], refs[-2], refs[-1]
    blocks = jnp.concatenate([piece[0] for piece in pieces], axis=0)
    out[0] = mm(turned[...], blocks)
    token[...] = jnp.zeros_like(token)


def grads_chunk(turned, pieces, before, ties, chunk, wide, columns):
    depth, span = turned.shape
    aliases = {} if before is None else {1 + len(pieces): 0}
    ties = ties if before is None else [before, *ties]
    return pl.pallas_call(
        tied(grads_kernel, 1 + len(pieces), len(ties)),
        grid=(3,),
        in_specs=[
            pl.BlockSpec((depth, span), lambda m: (0, 0)),
            *[pl.BlockSpec((1, *piece.shape[1:]), lambda m: (m, 0, 0)) for piece in pieces],
            *tie_specs(ties),
        ],
        out_specs=[
            pl.BlockSpec((1, depth, wide), lambda m: (m, 0, chunk)),
            pl.BlockSpec((8, 128), lambda m: (0, 0)),
        ],
        out_shape=[
            jax.ShapeDtypeStruct((3, depth, columns), jnp.float32),
            jax.ShapeDtypeStruct((8, 128), jnp.float32),
        ],
        input_output_aliases=aliases,
        compiler_params=params(24),
        cost_estimate=cost(6 * span * depth * wide, 6 * span * wide + 12 * depth * wide),
        name="grads",
    )(turned, *pieces, *ties)


def back(pieces, turned, chunk):
    wide = pieces[0].shape[2]
    rows = [jnp.concatenate([piece[m] for m in range(3)], axis=1) for piece in pieces]
    weight = [turned[m, chunk * wide : (chunk + 1) * wide] for m in range(3)]
    return mm(jnp.concatenate(rows, axis=0), jnp.concatenate(weight, axis=0))


def term_step(turned, pieces, befores, chunk):
    depth, wide = turned.shape[2], pieces[0].shape[2]
    count, rows = len(pieces), pieces[0].shape[1]
    whole = pl.BlockSpec(memory_space=pltpu.VMEM)

    def kernel(turned_ref, *refs):
        total = back(refs[:count], turned_ref, chunk)
        for place in range(count):
            block = total[place * rows : (place + 1) * rows]
            if befores:
                block += refs[count + place][...]
            refs[len(refs) - count + place][...] = block

    return pl.pallas_call(
        kernel,
        in_specs=[whole] * (1 + count + len(befores)),
        out_specs=[whole] * count,
        out_shape=[jax.ShapeDtypeStruct((rows, depth), jnp.float32)] * count,
        compiler_params=pltpu.CompilerParams(vmem_limit_bytes=16 * MIB),
        cost_estimate=cost(6 * count * rows * depth * wide, 12 * count * rows * wide),
        name="term_step",
    )(turned, *pieces, *befores)


def term_last_kernel(count, idx, turned, *refs):
    befores, fars, nears = refs[:2], refs[2:4], refs[4 : 3 + count]
    keeps, sends = refs[-4:-2], refs[-2:]
    half = keeps[0].shape[1]
    last = back(fars, turned, 1)
    for place in range(count):
        for part in range(2):
            span = slice(part * half, (part + 1) * half)
            total = nears[place][span] if place < count - 1 else last[span] + befores[part][...]

            @pl.when(idx[2 * count + 1 + place] == 0)
            def _():
                keeps[part][idx[3 * count + 1 + place]] = total

            @pl.when(idx[2 * count + 1 + place] == 1)
            def _():
                sends[part][idx[3 * count + 1 + place]] = total.astype(jnp.bfloat16)


def term_last(idx, turned, befores, pieces, nears, ties):
    count = len(nears) + 1
    rows, depth = nears[0].shape
    whole = pl.BlockSpec(memory_space=pltpu.VMEM)
    shape = (count // 2, rows // 2, depth)
    return pl.pallas_call(
        tied(functools.partial(term_last_kernel, count), count + 5, len(ties)),
        in_specs=[pl.BlockSpec(memory_space=pltpu.SMEM)]
        + [whole] * (count + 4)
        + tie_specs(ties),
        out_specs=[whole] * 4,
        out_shape=[jax.ShapeDtypeStruct(shape, jnp.float32)] * 2
        + [jax.ShapeDtypeStruct(shape, jnp.bfloat16)] * 2,
        compiler_params=pltpu.CompilerParams(vmem_limit_bytes=12 * MIB),
        cost_estimate=cost(rows * depth * depth, 12 * count * rows * depth),
        name="term_last",
    )(idx, turned, *befores, *pieces, *nears, *ties)


def split_kernel(column, group, idx, keep, came, keep_out, send_out):
    own = idx[column]
    for block in range(keep_out.shape[0]):
        high, low = block // group, block % group
        mine = (2 * high + own) * group + low
        other = (2 * high + 1 - own) * group + low
        keep_out[block] = keep[mine] + came[mine].astype(jnp.float32)
        send_out[block] = (keep[other] + came[other].astype(jnp.float32)).astype(jnp.bfloat16)


def split_sum(idx, column, group, keep, came):
    whole = pl.BlockSpec(memory_space=pltpu.VMEM)
    shape = (keep.shape[0] // 2, *keep.shape[1:])
    return pl.pallas_call(
        functools.partial(split_kernel, column, group),
        in_specs=[pl.BlockSpec(memory_space=pltpu.SMEM), whole, whole],
        out_specs=[whole, whole],
        out_shape=[
            jax.ShapeDtypeStruct(shape, jnp.float32),
            jax.ShapeDtypeStruct(shape, jnp.bfloat16),
        ],
        compiler_params=pltpu.CompilerParams(vmem_limit_bytes=4 * MIB),
        cost_estimate=cost(0, 8 * keep.shape[0] * keep.shape[1] * keep.shape[2]),
        name="split_sum",
    )(idx, keep, came)


def order_kernel(column, idx, keep_0, came_0, keep_1, came_1, *outs):
    half = keep_0.shape[1]
    for turn, out in enumerate(outs):
        block = idx[column + turn]
        out[:half] = (keep_0[block] + came_0[block].astype(jnp.float32)).astype(jnp.bfloat16)
        out[half:] = (keep_1[block] + came_1[block].astype(jnp.float32)).astype(jnp.bfloat16)


def order_sum(idx, column, halves, ties):
    whole = pl.BlockSpec(memory_space=pltpu.VMEM)
    count, rows, depth = halves[0].shape
    return pl.pallas_call(
        tied(functools.partial(order_kernel, column), 5, len(ties)),
        in_specs=[pl.BlockSpec(memory_space=pltpu.SMEM), *[whole] * 4, *tie_specs(ties)],
        out_specs=[whole] * count,
        out_shape=[jax.ShapeDtypeStruct((2 * rows, depth), jnp.bfloat16)] * count,
        compiler_params=pltpu.CompilerParams(vmem_limit_bytes=4 * MIB),
        cost_estimate=cost(0, 16 * count * rows * depth),
        name="order_sum",
    )(idx, *halves, *ties)


def finish_kernel(column, width, idx, tokens, gain, inverse, dots, *refs):
    came, out, gains = refs[:-2], refs[-2], refs[-1]
    rows, depth = came[0].shape
    group = out.shape[1] // depth
    gains[...] = gain[...].astype(jnp.float32)
    for turn in range(group):
        features = pl.ds(pl.multiple_of(idx[column + turn] * depth, depth), depth)
        for part in range(len(came) // group):
            span = slice(part * rows, (part + 1) * rows)
            scale = inverse[span, :1]
            upstream = came[part * group + turn][...].astype(jnp.float32)
            values = tokens[span, features].astype(jnp.float32)
            common = scale * scale * dots[span] / width
            out[span, features] = (
                scale * gains[:, features] * upstream - values * common
            ).astype(jnp.bfloat16)


def finish(idx, column, tokens, gain, inverse, dots, came, share):
    length, width = tokens.shape
    node = column + share // came[0].shape[1]
    whole = pl.BlockSpec(memory_space=pltpu.VMEM)
    return pl.pallas_call(
        functools.partial(finish_kernel, column, width),
        grid_spec=pltpu.PrefetchScalarGridSpec(
            num_scalar_prefetch=1,
            grid=(1,),
            in_specs=[
                pl.BlockSpec((length, share), lambda i, idx: (0, idx[node])),
                pl.BlockSpec((1, share), lambda i, idx: (0, idx[node])),
                *[whole] * (2 + len(came)),
            ],
            out_specs=pl.BlockSpec((length, share), lambda i, idx: (0, 0)),
            scratch_shapes=[pltpu.VMEM((1, share), jnp.float32)],
        ),
        out_shape=jax.ShapeDtypeStruct((length, share), jnp.bfloat16),
        compiler_params=params(12),
        cost_estimate=cost(8 * length * share, 6 * length * share),
        name="finish",
    )(idx, tokens, gain, inverse, dots, *came)


def local(tokens, norm_gain, w_quant, w_scale, d_out):
    length, width = tokens.shape
    depth, columns = w_quant.shape[1:]
    size, nodes = lax.axis_size("local"), lax.axis_size("node")
    here, node = lax.axis_index("local"), lax.axis_index("node")
    wide = columns // 2
    far = size // 2
    group, groups = size // nodes, group_of(nodes)

    order = ring_order(size)
    distances = ring_distances(size)
    table = jnp.asarray(index_table(size, nodes))
    idx = lax.dynamic_index_in_dim(table, node * size + here, 0, keepdims=False)

    def shift(array, distance):
        moves = [(order[i], order[(i + distance) % size]) for i in range(size)]
        return lax.ppermute(array, "local", moves)

    def swap(array, bit):
        return lax.ppermute(array, "node", [(n, n ^ bit) for n in range(nodes)])

    blocks, inverse_rms = normed_blocks(idx, tokens, norm_gain[None], size, depth // 2)
    mine_far = shift(blocks[far], far)
    other_far = swap(mine_far, 1)
    weights, turned = scaled_weights(w_quant, w_scale)
    firsts = sum_first(idx, size, mine_far, other_far, weights)
    mine = stack(
        [shift(blocks[-d % size], -d) if d else blocks[0] for d in distances[:-1]], firsts[:1]
    )
    other = swap(mine, 1)

    rows_turned = turn(idx, mine, other, mine_far, other_far)

    tables = rope_tables(length, HEAD_DIM)
    arrived = []
    for chunk in range(2):
        right, left = firsts[2 * chunk : 2 * chunk + 2]
        for distance in range(far - 1, -1, -1):
            from_left, from_right = shift(right, 1), shift(left, -1)
            if distance:
                places = distances.index(distance), distances.index(-distance)
                ties = [rows_turned] if distance == 1 else []
                right, left = sum_step(
                    idx, size, mine, other, places, weights, from_left, from_right, chunk, wide, ties
                )
        arrived.append((from_left, from_right))

    outputs, sets, dots = [], [], 0.0
    for chunk in range(2):
        output, product, pre = attention(
            idx, size, mine, other, weights, *arrived[chunk], d_out, tables, chunk, wide
        )
        outputs.append(output)
        sets.append(pre)
        dots += jnp.sum(product, axis=-1, keepdims=True)
    bit = 1
    while bit < nodes:
        dots = dots + swap(dots, bit)
        bit *= 2

    def sum_nodes(keep, send):
        column = 4 * size + 1
        bit = 1
        while 2 * bit < nodes:
            keep, send = split_sum(idx, column, group, keep, swap(send, bit))
            column += 1
            bit *= 2
        return keep, swap(send, bit)

    def relocate(blocks):
        came = []
        for turn, block in enumerate(blocks):
            moves = [
                (n * size + s, (s // group) * size + groups[n] * group + (s + turn) % group)
                for n in range(nodes)
                for s in range(size)
            ]
            came.append(lax.ppermute(block, ("node", "local"), moves))
        return came

    gathered = [[block] for block in sets]
    moving = [(block, block) for block in sets]
    terms = [[], []]
    for step in range(1, far + 1):
        for chunk in range(2):
            right, left = moving[chunk]
            if step == far:
                early = [dots] if chunk == 0 else terms[1][: size - 3]
                right, left = halve(right, left, early)
            right, left = shift(right, 1), shift(left, -1)
            moving[chunk] = right, left
            gathered[chunk] += [right, left]
            if step < far:
                pieces = gathered[chunk] if step == 1 else [right, left]
                known = len(terms[chunk])
                befores = terms[0][known : known + len(pieces)] if chunk else []
                terms[chunk] += term_step(turned, pieces, befores, chunk)
            elif chunk == 0:
                lasts = term_step(turned, [right, left], [], 0)
    grads, done = grads_chunk(rows_turned, gathered[0], None, [], 0, wide, columns)
    keep_0, keep_1, send_0, send_1 = term_last(
        idx, turned, lasts, gathered[1][-2:], terms[1], [done]
    )
    grads, done = grads_chunk(rows_turned, gathered[1], grads, [keep_1], 1, wide, columns)
    halves = [*sum_nodes(keep_0, send_0), *sum_nodes(keep_1, send_1)]
    column = idx.shape[0] - 1 - group
    came = relocate(order_sum(idx, column - group, halves, [done]))
    d_tokens = finish(
        idx, column, tokens, norm_gain[None], inverse_rms, dots, came, width // nodes
    )
    return (jnp.concatenate(outputs, axis=-1), d_tokens, grads)


def solution(mesh):
    placed = (
        P("local", None),
        P(),
        P(None, "local", "node"),
        P(None, "local", "node"),
        P("local", "node"),
    )
    return jax.shard_map(
        local,
        mesh=mesh,
        in_specs=placed,
        out_specs=(P("local", "node"), P("local", "node"), P(None, "local", "node")),
        check_vma=False,
    )
```
